32 devices in a mesh: ctx: 16 (over z, y, x), tp: 2 (over core).
Axes of the slice: x: 2, y: 2, z: 4, core: 2. Of those that a mesh axis runs over, the one named last changes fastest.
Arguments:
- projected: bfloat16 [4096, 3, 4096], P('ctx', None, 'tp'), may hold values from -6 to 6
- short_filter: float32 [3, 3, 4096], P(None, None, 'tp'), may hold values from -3 to 3
- residues: float32 [4096, 16], P('tp'), may hold values from -3 to 3
- rates: float32 [4096, 16], P('tp'), may hold values from 1.2207031e-06 to 0.05
- skip_gain: float32 [4096], P('tp'), may hold values from -3 to 3
- out_weight: bfloat16 [4096, 4096], P('tp', 'ctx'), may hold values from -0.09375 to 0.09375
Outputs:
- mixed: bfloat16 [4096, 4096], P('ctx', 'tp')
The draws below stay inside these ranges and needn't reach their ends.
All inputs are finite; a program needn't handle non-finite values.
Results may differ from the reference program's by a relative error of at most 0.019.
Values may be sent and summed in bfloat16 or wider, within the bound.
No kernel may reach another device: no remote copies, remote signals or barrier semaphores. Data moves between devices by JAX's collectives and lax.ppermute only.
A program may use at most 128 MiB of HBM per device.

```python
import math
import jax
import jax.numpy as jnp

D = 4096
ORDER = 16
SHORT = 3
TOKENS = 4096
N_TP = 2


def levels(key, dims, cuts, smallest, top_value):
    factor_of = 1.0
    for axis_at, shards_of in cuts:
        draws = jax.random.uniform(jax.random.fold_in(jax.random.fold_in(key, 6), axis_at), (shards_of,), jnp.float32, smallest / len(cuts), top_value / len(cuts))
        factor_of = factor_of * jnp.repeat(jnp.exp(draws), dims[axis_at] // shards_of).reshape((-1,) + (1,) * (len(dims) - 1 - axis_at))
    return factor_of


def normal_values(key, shape, spread, bound, cuts=(), held_as=jnp.bfloat16):
    factor_of = levels(key, shape, cuts, -0.22, 0.18) if cuts else 1.0
    result = jax.random.normal(key, shape, jnp.float32) * spread * factor_of
    return jnp.minimum(jnp.maximum(result, -bound), bound).astype(held_as)


def setup_inputs(seed: int = 0) -> dict:
    key_list = jax.random.split(jax.random.key(seed), 7)
    projected = normal_values(key_list[0], (TOKENS, SHORT, D), 1.0, 6.0, ((0, 16), (2, 2)))
    short_filter = normal_values(key_list[1], (SHORT, SHORT, D), 0.6, 3.0, ((2, 2),), jnp.float32)
    residues = normal_values(key_list[2], (D, ORDER), 0.5, 3.0, ((0, 2),), jnp.float32)
    rates = jnp.clip(jnp.exp(math.log(0.05) - 10.620351 * jax.random.uniform(key_list[3], (D, ORDER), jnp.float32) ** levels(key_list[3], (D, ORDER), ((0, 2),), -0.2, 0.2)), 1.220703097715159e-06, 0.05)
    skip_gain = normal_values(key_list[4], (D,), 0.5, 3.0, ((0, 2),), jnp.float32)
    out_weight = normal_values(key_list[5], (D, D), D ** -0.5, 0.09375, ((0, 2), (1, 16)))
    return dict(projected=projected, short_filter=short_filter, residues=residues, rates=rates, skip_gain=skip_gain, out_weight=out_weight)


def reference(projected, short_filter, residues, rates, skip_gain, out_weight):
    length = projected.shape[0]
    stream_data = projected.astype(jnp.float32)
    padded = jnp.concatenate([jnp.zeros((2,) + stream_data.shape[1:], jnp.float32), stream_data], axis=0)
    streams = short_filter[0][None] * padded[2:] + short_filter[1][None] * padded[1:-1] + short_filter[2][None] * padded[:-2]
    query_rows = streams[:, 0]
    gated_rows = streams[:, 1] * streams[:, 2]
    mode_coef = residues * jnp.sqrt(-jnp.expm1(-2.0 * rates))
    steps_float = jnp.arange(length).astype(rates.dtype)
    filt = jnp.zeros((length, residues.shape[0]), rates.dtype)
    for mode in range(residues.shape[1]):
        filt = filt + mode_coef[:, mode][None, :] * jnp.exp(-rates[:, mode][None, :] * steps_float[:, None])
    spectrum = jnp.fft.rfft(gated_rows, n=2 * length, axis=0) * jnp.fft.rfft(filt, n=2 * length, axis=0)
    long_out = jnp.fft.irfft(spectrum, n=2 * length, axis=0)[:length]
    long_out = long_out + skip_gain[None, :] * gated_rows
    hidden = (query_rows * long_out).astype(jnp.bfloat16)
    group_width = hidden.shape[1] // N_TP
    summed = jnp.zeros((length, out_weight.shape[1]), jnp.float32)
    for group in range(N_TP):
        lower = group * group_width
        partial_g = jnp.dot(hidden[:, lower:lower + group_width], out_weight[lower:lower + group_width, :], preferred_element_type=jnp.float32).astype(jnp.bfloat16)
        summed = summed + partial_g.astype(jnp.float32)
    return summed.astype(jnp.bfloat16)
```

```python
import functools

import jax
import jax.numpy as jnp
from jax import lax
from jax.experimental import pallas as pl
from jax.experimental.pallas import tpu as pltpu
from jax.sharding import PartitionSpec as P

LANES = 128
SEGS = 8
TOP = 8
VMEM_LIMIT = 40 * 1024 * 1024


def split_of(count):
    inner = 1
    while (2 * inner) ** 2 <= count and count % (2 * inner) == 0:
        inner *= 2
    return inner


def send_xor(value, count, group, step):
    pairs = [(p, p - p % group + ((p % group) ^ step)) for p in range(count)]
    return lax.ppermute(value, "ctx", pairs)


def send_along(value, count, group, steps, first=0):
    outer = count // group
    pairs = []
    for z in range(outer):
        if not 0 <= z + steps < outer:
            continue
        if (steps > 0 and z < first) or (steps < 0 and z > outer - 1 - first):
            continue
        pairs += [(z * group + e, (z + steps) * group + e) for e in range(group)]
    return lax.ppermute(value, "ctx", pairs)


def estimate(flops, bytes_accessed, transcendentals=0):
    return pl.CostEstimate(flops=flops, bytes_accessed=bytes_accessed, transcendentals=transcendentals)


def row(ref, r, lanes):
    return jnp.broadcast_to(ref[r : r + 1, lanes], (SEGS, LANES))


def lay_segments(dst, stream, halo, seg_len, lanes, group):
    pitch = seg_len + 1
    for s in range(SEGS):
        part = stream[0, s * seg_len : (s + 1) * seg_len, lanes].astype(jnp.float32)
        dst[group, TOP + s * pitch : TOP + s * pitch + seg_len, :] = part
    dst[group, TOP - 3 : TOP - 1, :] = halo


def taps(short, stream, lanes):
    return [jnp.broadcast_to(short[i, stream : stream + 1, lanes], (SEGS, LANES)) for i in range(3)]


def strided(ref, group, start, pitch):
    return ref[group, pl.ds(start, SEGS, stride=pitch), :]


def local_scan_body(place, key, value, halo, short, rates, *rest, seg_len, order, share):
    ends = rest[:share]
    gated, prefix = rest[share : share + 2]
    key_pos, value_pos, end_now = rest[share + 2 :]
    pitch = seg_len + 1
    groups = gated.shape[0]
    segment = lax.broadcasted_iota(jnp.int32, (SEGS, LANES), 0)
    for group in range(groups):
        lanes = slice(group * LANES, (group + 1) * LANES)
        lay_segments(key_pos, key, halo[1, :, lanes].astype(jnp.float32), seg_len, lanes, group)
        lay_segments(value_pos, value, halo[2, :, lanes].astype(jnp.float32), seg_len, lanes, group)

    for group in range(groups):
        lanes = slice(group * LANES, (group + 1) * LANES)
        key_taps = taps(short, 1, lanes)
        value_taps = taps(short, 2, lanes)
        decay = [jnp.exp(-row(rates, r, lanes)) for r in range(order)]

        def step(i, carry, group=group, key_taps=key_taps, value_taps=value_taps, decay=decay):
            k1, k2, v1, v2, *states = carry
            k0 = strided(key_pos, group, TOP + i, pitch)
            v0 = strided(value_pos, group, TOP + i, pitch)
            key_now = key_taps[0] * k0 + key_taps[1] * k1 + key_taps[2] * k2
            value_now = value_taps[0] * v0 + value_taps[1] * v1 + value_taps[2] * v2
            now = key_now * value_now
            gated[group, pl.ds(pl.multiple_of(i * SEGS, SEGS), SEGS), :] = now
            states = [d * h + now for d, h in zip(decay, states)]
            return (k0, k1, v0, v1, *states)

        zero = jnp.zeros((SEGS, LANES), jnp.float32)
        start = (
            strided(key_pos, group, TOP - 2, pitch),
            strided(key_pos, group, TOP - 3, pitch),
            strided(value_pos, group, TOP - 2, pitch),
            strided(value_pos, group, TOP - 3, pitch),
        ) + (zero,) * order
        states = lax.fori_loop(0, seg_len, step, start, unroll=8)[4:]
        for r in range(order):
            rate = row(rates, r, lanes)
            scan = states[r]
            for d in (1, 2, 4):
                moved = jnp.where(segment >= d, pltpu.roll(scan, d, 0), 0.0)
                scan = scan + jnp.exp(rate * (-1.0 * d * seg_len)) * moved
            prefix[group, r] = jnp.where(segment >= 1, pltpu.roll(scan, 1, 0), 0.0)
            end_now[r : r + 1, lanes] = scan[SEGS - 1 :, :]

    for j in range(share):

        @pl.when((pl.program_id(0) ^ place[0]) == j)
        def _(j=j):
            ends[j][...] = end_now[...]


def local_scan(place, streams, halo, short, rates, share):
    _, rows, chans = streams.shape
    order = rates.shape[0]
    wide = chans // share
    groups = wide // LANES
    seg_len = rows // SEGS
    pos_rows = TOP + SEGS * (seg_len + 1)
    end_shape = jax.ShapeDtypeStruct((order, wide), jnp.float32)
    return pl.pallas_call(
        functools.partial(local_scan_body, seg_len=seg_len, order=order, share=share),
        grid_spec=pltpu.PrefetchScalarGridSpec(
            num_scalar_prefetch=1,
            grid=(share,),
            in_specs=[
                pl.BlockSpec((1, rows, wide), lambda g, place: (1, 0, g)),
                pl.BlockSpec((1, rows, wide), lambda g, place: (2, 0, g)),
                pl.BlockSpec((3, 2, wide), lambda g, place: (0, 0, g)),
                pl.BlockSpec((3, 3, wide), lambda g, place: (0, 0, g)),
                pl.BlockSpec((order, wide), lambda g, place: (0, g)),
            ],
            out_specs=[pl.BlockSpec((order, wide), lambda g, place: (0, 0))] * share
            + [
                pl.BlockSpec((groups, rows, LANES), lambda g, place: (g, 0, 0)),
                pl.BlockSpec((groups, order, SEGS, LANES), lambda g, place: (g, 0, 0, 0)),
            ],
            scratch_shapes=[
                pltpu.VMEM((groups, pos_rows, LANES), jnp.float32),
                pltpu.VMEM((groups, pos_rows, LANES), jnp.float32),
                pltpu.VMEM((order, wide), jnp.float32),
            ],
        ),
        out_shape=[end_shape] * share
        + [
            jax.ShapeDtypeStruct((chans // LANES, rows, LANES), jnp.float32),
            jax.ShapeDtypeStruct((chans // LANES, order, SEGS, LANES), jnp.float32),
        ],
        compiler_params=pltpu.CompilerParams(vmem_limit_bytes=VMEM_LIMIT),
        cost_estimate=estimate(rows * chans * 50, rows * chans * 10),
        name="local_scan",
    )(place, streams, streams, halo, short, rates)


def plane_scan_body(place, rates, *rest, share, rows):
    ends = rest[:share]
    whole = rest[share]
    befores = rest[share + 1 : 2 * share + 1]
    by_place, before_place = rest[2 * share + 1 :]
    here = place[0]
    for j in range(share):
        by_place[here ^ j] = ends[j][...]
    decay = jnp.exp(rates[...] * (-1.0 * rows))
    state = jnp.zeros(rates.shape, jnp.float32)
    for at in range(share):
        before_place[at] = state
        state = decay * state + by_place[at]
    whole[...] = state
    for j in range(share):
        befores[j][...] = before_place[here ^ j]


def plane_scan(place, rates, ends, rows):
    share = len(ends)
    order, wide = ends[0].shape
    block = pl.BlockSpec((order, wide), lambda g, place: (0, 0))
    shape = jax.ShapeDtypeStruct((order, wide), jnp.float32)
    got = pl.pallas_call(
        functools.partial(plane_scan_body, share=share, rows=rows),
        grid_spec=pltpu.PrefetchScalarGridSpec(
            num_scalar_prefetch=1,
            grid=(1,),
            in_specs=[pl.BlockSpec((order, wide), lambda g, place: (0, place[0]))] + [block] * share,
            out_specs=[block] * (share + 1),
            scratch_shapes=[pltpu.VMEM((share, order, wide), jnp.float32)] * 2,
        ),
        out_shape=[shape] * (share + 1),
        cost_estimate=estimate(order * wide * 20, order * wide * 36),
        name="plane_scan",
    )(place, rates, *ends)
    return got[0], got[1:]


def line_scan_body(place, rates, *rest, share, rows, lines):
    befores = rest[:share]
    arrived = rest[share : share + lines]
    outs = rest[share + lines :]
    here = place[0]
    rate = rates[...] * (-1.0 * rows)
    decay = jnp.exp(rate * share)
    state = jnp.zeros(rate.shape, jnp.float32)
    for k in reversed(range(lines)):
        state = decay * state + arrived[k][...]
    for j in range(share):
        ahead = (here ^ j).astype(jnp.float32)
        outs[j][...] = befores[j][...] + jnp.exp(rate * ahead) * state


def line_scan(place, rates, befores, arrived, rows):
    share, lines = len(befores), len(arrived)
    order, wide = befores[0].shape
    block = pl.BlockSpec((order, wide), lambda g, place: (0, 0))
    return pl.pallas_call(
        functools.partial(line_scan_body, share=share, rows=rows, lines=lines),
        grid_spec=pltpu.PrefetchScalarGridSpec(
            num_scalar_prefetch=1,
            grid=(1,),
            in_specs=[pl.BlockSpec((order, wide), lambda g, place: (0, place[0]))]
            + [block] * (share + lines),
            out_specs=[block] * share,
        ),
        out_shape=[jax.ShapeDtypeStruct((order, wide), jnp.float32)] * share,
        cost_estimate=estimate(order * wide * 20, order * wide * 36),
        name="line_scan",
    )(place, rates, *befores, *arrived)


def hidden_body(place, query, halo, short, rates, coef, skip, gated, prefix, *rest, seg_len, order, share):
    starts = rest[:share]
    hidden = rest[share]
    query_pos, result_pos, start_by_place = rest[share + 1 :]
    pitch = seg_len + 1
    groups = gated.shape[0]
    now_at = pl.program_id(0)
    segment = lax.broadcasted_iota(jnp.int32, (SEGS, LANES), 0).astype(jnp.float32)

    @pl.when(now_at == 0)
    def _():
        for j in range(share):
            start_by_place[place[0] ^ j] = starts[j][...]

    for group in range(groups):
        lanes = slice(group * LANES, (group + 1) * LANES)
        lay_segments(query_pos, query, halo[0, :, lanes].astype(jnp.float32), seg_len, lanes, group)

    for group in range(groups):
        lanes = slice(group * LANES, (group + 1) * LANES)
        query_taps = taps(short, 0, lanes)
        gain = jnp.broadcast_to(skip[0:1, lanes], (SEGS, LANES))
        decay = [jnp.exp(-row(rates, r, lanes)) for r in range(order)]
        scale = [row(coef, r, lanes) for r in range(order)]
        states = []
        for r in range(order):
            ahead = jnp.exp(row(rates, r, lanes) * (segment * (-1.0 * seg_len)))
            before = jnp.broadcast_to(start_by_place[now_at, r : r + 1, lanes], (SEGS, LANES))
            states.append(prefix[group, r] + ahead * before)

        def step(i, carry, group=group, query_taps=query_taps, gain=gain, decay=decay, scale=scale):
            q1, q2, *states = carry
            q0 = strided(query_pos, group, TOP + i, pitch)
            now = gated[group, pl.ds(pl.multiple_of(i * SEGS, SEGS), SEGS), :]
            states = [d * h + now for d, h in zip(decay, states)]
            sums = [s * h for s, h in zip(scale, states)] + [gain * now]
            while len(sums) > 1:
                sums = [a + b for a, b in zip(sums[::2], sums[1::2])] + sums[len(sums) // 2 * 2 :]
            query_now = query_taps[0] * q0 + query_taps[1] * q1 + query_taps[2] * q2
            result_pos[group, pl.ds(TOP + i, SEGS, stride=pitch), :] = query_now * sums[0]
            return (q0, q1, *states)

        start = (
            strided(query_pos, group, TOP - 2, pitch),
            strided(query_pos, group, TOP - 3, pitch),
        ) + tuple(states)
        lax.fori_loop(0, seg_len, step, start, unroll=8)
        for s in range(SEGS):
            part = result_pos[group, TOP + s * pitch : TOP + s * pitch + seg_len, :]
            hidden[s * seg_len : (s + 1) * seg_len, lanes] = part.astype(hidden.dtype)


def hidden_rows(place, streams, halo, short, rates, coef, skip, gated, prefix, starts):
    _, rows, chans = streams.shape
    order = rates.shape[0]
    share = len(starts)
    wide = chans // share
    groups = wide // LANES
    seg_len = rows // SEGS
    pos_rows = TOP + SEGS * (seg_len + 1)
    return pl.pallas_call(
        functools.partial(hidden_body, seg_len=seg_len, order=order, share=share),
        grid_spec=pltpu.PrefetchScalarGridSpec(
            num_scalar_prefetch=1,
            grid=(share,),
            in_specs=[
                pl.BlockSpec((1, rows, wide), lambda g, place: (0, 0, g)),
                pl.BlockSpec((3, 2, wide), lambda g, place: (0, 0, g)),
                pl.BlockSpec((3, 3, wide), lambda g, place: (0, 0, g)),
                pl.BlockSpec((order, wide), lambda g, place: (0, g)),
                pl.BlockSpec((order, wide), lambda g, place: (0, g)),
                pl.BlockSpec((1, wide), lambda g, place: (0, g)),
                pl.BlockSpec((groups, rows, LANES), lambda g, place: (g, 0, 0)),
                pl.BlockSpec((groups, order, SEGS, LANES), lambda g, place: (g, 0, 0, 0)),
            ]
            + [pl.BlockSpec((order, wide), lambda g, place: (0, 0))] * share,
            out_specs=pl.BlockSpec((rows, wide), lambda g, place: (0, g)),
            scratch_shapes=[
                pltpu.VMEM((groups, pos_rows, LANES), jnp.float32),
                pltpu.VMEM((groups, pos_rows, LANES), jnp.float32),
                pltpu.VMEM((share, order, wide), jnp.float32),
            ],
        ),
        out_shape=jax.ShapeDtypeStruct((rows, chans), jnp.bfloat16),
        compiler_params=pltpu.CompilerParams(vmem_limit_bytes=VMEM_LIMIT),
        cost_estimate=estimate(rows * chans * 80, rows * chans * 10),
        name="hidden_rows",
    )(place, streams, halo, short, rates, coef, skip, gated, prefix, *starts)


def project_body(place, *refs, pieces, outer, blocks):
    hidden = refs[: sum(pieces)]
    weight = refs[sum(pieces) : sum(pieces) + 2 * outer - 1]
    outs = refs[sum(pieces) + 2 * outer - 1 : -4]
    held, cols, held_sem, cols_sem = refs[-4:]
    plane, half = place[0], place[1]
    away = [half * blocks + b - plane for b in range(blocks)]

    def col_copy(b, at):
        return pltpu.make_async_copy(weight[at], cols.at[b], cols_sem.at[b])

    def each_source(b, act):
        for at in range(2 * outer - 1):

            @pl.when(away[b] == at - (outer - 1))
            def _(at=at):
                act(col_copy(b, at))

    row_copies = []
    at = 0
    for j, count in enumerate(pieces):
        size = held.shape[1] // count
        row_copies.append(
            [
                pltpu.make_async_copy(
                    hidden[at + e], held.at[j, pl.ds(e * size, size)], held_sem.at[at + e]
                )
                for e in range(count)
            ]
        )
        at += count
    each_source(0, lambda copy: copy.start())
    for copy in row_copies[0]:
        copy.start()
    for b in range(1, blocks):
        each_source(b, lambda copy: copy.start())
    for copies in row_copies[1:]:
        for copy in copies:
            copy.start()
    width = cols.shape[2]
    for j in range(len(pieces)):
        for copy in row_copies[j]:
            copy.wait()
        for b in range(blocks):
            if j == 0:
                each_source(b, lambda copy: copy.wait())
            made = jnp.dot(held[j], cols[b], preferred_element_type=jnp.float32)
            outs[j][:, b * width : (b + 1) * width] = made.astype(jnp.bfloat16)


def project(place, hidden, weight, outer, blocks):
    pieces = tuple(len(part) for part in hidden)
    rows, depth = hidden[0][0].shape
    width = weight[0].shape[1]
    flat = [piece for part in hidden for piece in part]
    share = len(pieces)
    anywhere = pl.BlockSpec(memory_space=pl.ANY)
    return pl.pallas_call(
        functools.partial(project_body, pieces=pieces, outer=outer, blocks=blocks),
        in_specs=[pl.BlockSpec(memory_space=pltpu.SMEM)] + [anywhere] * (len(flat) + len(weight)),
        out_specs=[pl.BlockSpec(memory_space=pltpu.VMEM)] * share,
        out_shape=[jax.ShapeDtypeStruct((rows, blocks * width), jnp.bfloat16)] * share,
        scratch_shapes=[
            pltpu.VMEM((share, rows, depth), jnp.bfloat16),
            pltpu.VMEM((blocks, depth, width), jnp.bfloat16),
            pltpu.SemaphoreType.DMA((len(flat),)),
            pltpu.SemaphoreType.DMA((blocks,)),
        ],
        compiler_params=pltpu.CompilerParams(vmem_limit_bytes=VMEM_LIMIT),
        cost_estimate=estimate(
            2 * share * rows * depth * blocks * width,
            2 * depth * (share * rows + blocks * width) + 2 * share * rows * blocks * width,
        ),
        name="project",
    )(place, *flat, *weight)


def assemble_body(place, *refs, share, blocks, width):
    parts, out, sems = refs[:share], refs[share], refs[share + 1]
    copies = []
    for j in range(share):
        for b in range(blocks):
            column = pl.multiple_of((b * share + (place[0] ^ j)) * width, width)
            copies.append(
                pltpu.make_async_copy(
                    parts[j].at[:, pl.ds(b * width, width)],
                    out.at[:, pl.ds(column, width)],
                    sems.at[j * blocks + b],
                )
            )
    for copy in copies:
        copy.start()
    for copy in copies:
        copy.wait()


def assemble(place, parts, blocks, width):
    share = len(parts)
    rows = parts[0].shape[0]
    anywhere = pl.BlockSpec(memory_space=pl.ANY)
    return pl.pallas_call(
        functools.partial(assemble_body, share=share, blocks=blocks, width=width),
        in_specs=[pl.BlockSpec(memory_space=pltpu.SMEM)] + [anywhere] * share,
        out_specs=anywhere,
        out_shape=jax.ShapeDtypeStruct((rows, share * blocks * width), jnp.bfloat16),
        scratch_shapes=[pltpu.SemaphoreType.DMA((share * blocks,))],
        cost_estimate=estimate(0, 4 * rows * share * blocks * width),
        name="assemble",
    )(place, *parts)


def weight_line(out_weight, count, group):
    outer = count // group
    below, above = [out_weight], [out_weight]
    for k in range(1, outer):
        below.append(send_along(below[-1], count, group, 1, k - 1))
        above.append(send_along(above[-1], count, group, -1, k - 1))
    return below[:0:-1] + above


def plane_rows(hidden, count, group):
    if group != 4:
        return [[hidden]] + [[send_xor(hidden, count, group, j)] for j in range(1, group)]
    middle = hidden.shape[0] // 2
    top, bottom = hidden[:middle], hidden[middle:]
    top_1 = send_xor(top, count, group, 1)
    bottom_2 = send_xor(bottom, count, group, 2)
    bottom_1 = send_xor(bottom, count, group, 1)
    top_2 = send_xor(top, count, group, 2)
    top_3 = send_xor(top_1, count, group, 2)
    bottom_3 = send_xor(bottom_2, count, group, 1)
    return [[hidden], [top_1, bottom_1], [top_2, bottom_2], [top_3, bottom_3]]


def per_device(projected, short_filter, residues, rates, skip_gain, out_weight):
    count = lax.axis_size("ctx")
    halves = lax.axis_size("tp")
    here = lax.axis_index("ctx")
    half = lax.axis_index("tp")
    rows, _, chans = projected.shape
    order = rates.shape[1]

    streams = jnp.transpose(projected, (1, 0, 2))
    halo = lax.ppermute(streams[:, -2:], "ctx", [(p, p + 1) for p in range(count - 1)])
    group = split_of(count)
    outer = count // group
    line = weight_line(out_weight, count, group)

    rates_t = rates.T
    coef_t = (residues * jnp.sqrt(-jnp.expm1(-2.0 * rates))).T

    share = min(split_of(count), chans // LANES, 4)
    lines = count // share
    spot = jnp.full((1,), here % share, jnp.int32)
    *ends, gated, prefix = local_scan(spot, streams, halo, short_filter, rates_t, share)
    ends = [ends[0]] + [send_xor(ends[j], count, share, j) for j in range(1, share)]
    whole, befores = plane_scan(spot, rates_t, ends, rows)
    arrived = [send_along(whole, count, share, k) for k in range(1, lines)]
    starts = line_scan(spot, rates_t, befores, arrived, rows)
    starts = [starts[0]] + [send_xor(starts[j], count, share, j) for j in range(1, share)]
    hidden = hidden_rows(
        spot, streams, halo, short_filter, rates_t, coef_t, skip_gain[None], gated, prefix, starts
    )

    pieces = plane_rows(hidden, count, group)
    width = out_weight.shape[1]
    blocks = outer // halves
    plane = here // group
    if halves == 2 and width % LANES == 0:
        place = jnp.stack([plane, 1 - half]).astype(jnp.int32)
        given = project(place, pieces, line, outer, blocks)
        taken = [lax.ppermute(part, "tp", [(0, 1), (1, 0)]) for part in given]
        place = jnp.stack([plane, half]).astype(jnp.int32)
        kept = project(place, pieces, line, outer, blocks)
        mixed = [
            (a.astype(jnp.float32) + b.astype(jnp.float32)).astype(jnp.bfloat16)
            for a, b in zip(kept, taken)
        ]
    else:
        cols = lax.dynamic_slice_in_dim(jnp.stack(line), outer - 1 - plane, outer, 0)
        cols = jnp.moveaxis(cols, 0, 1).reshape(chans, outer * width)
        held = jnp.concatenate([piece for part in pieces for piece in part], axis=0)
        partial = jnp.dot(held, cols, preferred_element_type=jnp.float32).astype(jnp.bfloat16)
        summed = lax.psum_scatter(partial, "tp", scatter_dimension=1, tiled=True)
        mixed = list(summed.reshape(group, rows, blocks * width))
    mixed = [mixed[0]] + [send_xor(mixed[j], count, group, j) for j in range(1, group)]
    spot = jnp.full((1,), here % group, jnp.int32)
    if width % LANES == 0:
        return assemble(spot, mixed, blocks, width)
    stacked = jnp.stack(mixed).reshape(group, rows, blocks, width)
    by_place = jnp.take(stacked, jnp.arange(group) ^ spot[0], axis=0)
    return jnp.moveaxis(by_place, 0, 2).reshape(rows, blocks * group * width)


def solution(mesh):
    return jax.shard_map(
        per_device,
        mesh=mesh,
        in_specs=(
            P("ctx", None, "tp"),
            P(None, None, "tp"),
            P("tp", None),
            P("tp", None),
            P("tp"),
            P("tp", "ctx"),
        ),
        out_specs=P("ctx", "tp"),
        check_vma=False,
    )
```

```python
import functools

import jax
import jax.numpy as jnp
from jax import lax
from jax.experimental import pallas as pl
from jax.experimental.pallas import tpu as pltpu
from jax.sharding import PartitionSpec as P

LANES = 128
SEGS = 8
TOP = 8
VMEM_LIMIT = 16 * 1024 * 1024


def split_of(count):
    inner = 1
    while (2 * inner) ** 2 <= count and count % (2 * inner) == 0:
        inner *= 2
    return inner


def send_xor(value, count, group, step):
    pairs = [(p, p - p % group + ((p % group) ^ step)) for p in range(count)]
    return lax.ppermute(value, "ctx", pairs)


def send_along(value, count, group, steps, first=0):
    outer = count // group
    pairs = []
    for z in range(outer):
        if not 0 <= z + steps < outer:
            continue
        if (steps > 0 and z < first) or (steps < 0 and z > outer - 1 - first):
            continue
        pairs += [(z * group + e, (z + steps) * group + e) for e in range(group)]
    return lax.ppermute(value, "ctx", pairs)


def estimate(flops, bytes_accessed, transcendentals=0):
    return pl.CostEstimate(flops=flops, bytes_accessed=bytes_accessed, transcendentals=transcendentals)


def row(ref, r, lanes):
    return jnp.broadcast_to(ref[r : r + 1, lanes], (SEGS, LANES))


def lay_segments(dst, stream, halo, seg_len, lanes, group):
    pitch = seg_len + 1
    for s in range(SEGS):
        part = stream[0, s * seg_len : (s + 1) * seg_len, lanes].astype(jnp.float32)
        dst[group, TOP + s * pitch : TOP + s * pitch + seg_len, :] = part
    dst[group, TOP - 3 : TOP - 1, :] = halo


def taps(short, stream, lanes):
    return [jnp.broadcast_to(short[i, stream : stream + 1, lanes], (SEGS, LANES)) for i in range(3)]


def strided(ref, group, start, pitch):
    return ref[group, pl.ds(start, SEGS, stride=pitch), :]


def local_scan_body(place, key, value, halo, short, rates, *rest, seg_len, order, share):
    ends = rest[:share]
    gated, prefix = rest[share : share + 2]
    key_pos, value_pos, end_now = rest[share + 2 :]
    pitch = seg_len + 1
    groups = gated.shape[0]
    segment = lax.broadcasted_iota(jnp.int32, (SEGS, LANES), 0)
    for group in range(groups):
        lanes = slice(group * LANES, (group + 1) * LANES)
        lay_segments(key_pos, key, halo[1, :, lanes].astype(jnp.float32), seg_len, lanes, group)
        lay_segments(value_pos, value, halo[2, :, lanes].astype(jnp.float32), seg_len, lanes, group)

    for group in range(groups):
        lanes = slice(group * LANES, (group + 1) * LANES)
        key_taps = taps(short, 1, lanes)
        value_taps = taps(short, 2, lanes)
        decay = [jnp.exp(-row(rates, r, lanes)) for r in range(order)]

        def step(i, carry, group=group, key_taps=key_taps, value_taps=value_taps, decay=decay):
            k1, k2, v1, v2, *states = carry
            k0 = strided(key_pos, group, TOP + i, pitch)
            v0 = strided(value_pos, group, TOP + i, pitch)
            key_now = key_taps[0] * k0 + key_taps[1] * k1 + key_taps[2] * k2
            value_now = value_taps[0] * v0 + value_taps[1] * v1 + value_taps[2] * v2
            now = key_now * value_now
            gated[group, pl.ds(pl.multiple_of(i * SEGS, SEGS), SEGS), :] = now
            states = [d * h + now for d, h in zip(decay, states)]
            return (k0, k1, v0, v1, *states)

        zero = jnp.zeros((SEGS, LANES), jnp.float32)
        start = (
            strided(key_pos, group, TOP - 2, pitch),
            strided(key_pos, group, TOP - 3, pitch),
            strided(value_pos, group, TOP - 2, pitch),
            strided(value_pos, group, TOP - 3, pitch),
        ) + (zero,) * order
        states = lax.fori_loop(0, seg_len, step, start, unroll=8)[4:]
        for r in range(order):
            rate = row(rates, r, lanes)
            scan = states[r]
            for d in (1, 2, 4):
                moved = jnp.where(segment >= d, pltpu.roll(scan, d, 0), 0.0)
                scan = scan + jnp.exp(rate * (-1.0 * d * seg_len)) * moved
            prefix[group, r] = jnp.where(segment >= 1, pltpu.roll(scan, 1, 0), 0.0)
            end_now[r : r + 1, lanes] = scan[SEGS - 1 :, :]

    for j in range(share):

        @pl.when((pl.program_id(0) ^ place[0]) == j)
        def _(j=j):
            ends[j][...] = end_now[...]


def local_scan(place, streams, halo, short, rates, share):
    _, rows, chans = streams.shape
    order = rates.shape[0]
    wide = chans // share
    groups = wide // LANES
    seg_len = rows // SEGS
    pos_rows = TOP + SEGS * (seg_len + 1)
    end_shape = jax.ShapeDtypeStruct((order, wide), jnp.float32)
    return pl.pallas_call(
        functools.partial(local_scan_body, seg_len=seg_len, order=order, share=share),
        grid_spec=pltpu.PrefetchScalarGridSpec(
            num_scalar_prefetch=1,
            grid=(share,),
            in_specs=[
                pl.BlockSpec((1, rows, wide), lambda g, place: (1, 0, g)),
                pl.BlockSpec((1, rows, wide), lambda g, place: (2, 0, g)),
                pl.BlockSpec((3, 2, wide), lambda g, place: (0, 0, g)),
                pl.BlockSpec((3, 3, wide), lambda g, place: (0, 0, g)),
                pl.BlockSpec((order, wide), lambda g, place: (0, g)),
            ],
            out_specs=[pl.BlockSpec((order, wide), lambda g, place: (0, 0))] * share
            + [
                pl.BlockSpec((groups, rows, LANES), lambda g, place: (g, 0, 0)),
                pl.BlockSpec((groups, order, SEGS, LANES), lambda g, place: (g, 0, 0, 0)),
            ],
            scratch_shapes=[
                pltpu.VMEM((groups, pos_rows, LANES), jnp.float32),
                pltpu.VMEM((groups, pos_rows, LANES), jnp.float32),
                pltpu.VMEM((order, wide), jnp.float32),
            ],
        ),
        out_shape=[end_shape] * share
        + [
            jax.ShapeDtypeStruct((chans // LANES, rows, LANES), jnp.float32),
            jax.ShapeDtypeStruct((chans // LANES, order, SEGS, LANES), jnp.float32),
        ],
        compiler_params=pltpu.CompilerParams(vmem_limit_bytes=VMEM_LIMIT),
        cost_estimate=estimate(rows * chans * 50, rows * chans * 10),
        name="local_scan",
    )(place, streams, streams, halo, short, rates)


def plane_scan_body(place, rates, *rest, share, rows):
    ends = rest[:share]
    whole = rest[share]
    befores = rest[share + 1 : 2 * share + 1]
    by_place, before_place = rest[2 * share + 1 :]
    here = place[0]
    for j in range(share):
        by_place[here ^ j] = ends[j][...]
    decay = jnp.exp(rates[...] * (-1.0 * rows))
    state = jnp.zeros(rates.shape, jnp.float32)
    for at in range(share):
        before_place[at] = state
        state = decay * state + by_place[at]
    whole[...] = state
    for j in range(share):
        befores[j][...] = before_place[here ^ j]


def plane_scan(place, rates, ends, rows):
    share = len(ends)
    order, wide = ends[0].shape
    block = pl.BlockSpec((order, wide), lambda g, place: (0, 0))
    shape = jax.ShapeDtypeStruct((order, wide), jnp.float32)
    got = pl.pallas_call(
        functools.partial(plane_scan_body, share=share, rows=rows),
        grid_spec=pltpu.PrefetchScalarGridSpec(
            num_scalar_prefetch=1,
            grid=(1,),
            in_specs=[pl.BlockSpec((order, wide), lambda g, place: (0, place[0]))] + [block] * share,
            out_specs=[block] * (share + 1),
            scratch_shapes=[pltpu.VMEM((share, order, wide), jnp.float32)] * 2,
        ),
        out_shape=[shape] * (share + 1),
        cost_estimate=estimate(order * wide * 20, order * wide * 36),
        name="plane_scan",
    )(place, rates, *ends)
    return got[0], got[1:]


def line_scan_body(place, rates, *rest, share, rows, lines):
    befores = rest[:share]
    arrived = rest[share : share + lines]
    outs = rest[share + lines :]
    here = place[0]
    rate = rates[...] * (-1.0 * rows)
    decay = jnp.exp(rate * share)
    state = jnp.zeros(rate.shape, jnp.float32)
    for k in reversed(range(lines)):
        state = decay * state + arrived[k][...]
    for j in range(share):
        ahead = (here ^ j).astype(jnp.float32)
        outs[j][...] = befores[j][...] + jnp.exp(rate * ahead) * state


def line_scan(place, rates, befores, arrived, rows):
    share, lines = len(befores), len(arrived)
    order, wide = befores[0].shape
    block = pl.BlockSpec((order, wide), lambda g, place: (0, 0))
    return pl.pallas_call(
        functools.partial(line_scan_body, share=share, rows=rows, lines=lines),
        grid_spec=pltpu.PrefetchScalarGridSpec(
            num_scalar_prefetch=1,
            grid=(1,),
            in_specs=[pl.BlockSpec((order, wide), lambda g, place: (0, place[0]))]
            + [block] * (share + lines),
            out_specs=[block] * share,
        ),
        out_shape=[jax.ShapeDtypeStruct((order, wide), jnp.float32)] * share,
        cost_estimate=estimate(order * wide * 20, order * wide * 36),
        name="line_scan",
    )(place, rates, *befores, *arrived)


def hidden_body(place, query, halo, short, rates, coef, skip, gated, prefix, *rest, seg_len, order, share, first):
    starts = rest[:share]
    hidden = rest[share]
    query_pos, result_pos, start_by_place = rest[share + 1 :]
    pitch = seg_len + 1
    groups = gated.shape[0]
    now_at = pl.program_id(0) + first
    segment = lax.broadcasted_iota(jnp.int32, (SEGS, LANES), 0).astype(jnp.float32)

    @pl.when(pl.program_id(0) == 0)
    def _():
        for j in range(share):
            start_by_place[place[0] ^ j] = starts[j][...]

    for group in range(groups):
        lanes = slice(group * LANES, (group + 1) * LANES)
        lay_segments(query_pos, query, halo[0, :, lanes].astype(jnp.float32), seg_len, lanes, group)

    for group in range(groups):
        lanes = slice(group * LANES, (group + 1) * LANES)
        query_taps = taps(short, 0, lanes)
        gain = jnp.broadcast_to(skip[0:1, lanes], (SEGS, LANES))
        decay = [jnp.exp(-row(rates, r, lanes)) for r in range(order)]
        scale = [row(coef, r, lanes) for r in range(order)]
        states = []
        for r in range(order):
            ahead = jnp.exp(row(rates, r, lanes) * (segment * (-1.0 * seg_len)))
            before = jnp.broadcast_to(start_by_place[now_at, r : r + 1, lanes], (SEGS, LANES))
            states.append(prefix[group, r] + ahead * before)

        def step(i, carry, group=group, query_taps=query_taps, gain=gain, decay=decay, scale=scale):
            q1, q2, *states = carry
            q0 = strided(query_pos, group, TOP + i, pitch)
            now = gated[group, pl.ds(pl.multiple_of(i * SEGS, SEGS), SEGS), :]
            states = [d * h + now for d, h in zip(decay, states)]
            sums = [s * h for s, h in zip(scale, states)] + [gain * now]
            while len(sums) > 1:
                sums = [a + b for a, b in zip(sums[::2], sums[1::2])] + sums[len(sums) // 2 * 2 :]
            query_now = query_taps[0] * q0 + query_taps[1] * q1 + query_taps[2] * q2
            result_pos[group, pl.ds(TOP + i, SEGS, stride=pitch), :] = query_now * sums[0]
            return (q0, q1, *states)

        start = (
            strided(query_pos, group, TOP - 2, pitch),
            strided(query_pos, group, TOP - 3, pitch),
        ) + tuple(states)
        lax.fori_loop(0, seg_len, step, start, unroll=8)
        for s in range(SEGS):
            part = result_pos[group, TOP + s * pitch : TOP + s * pitch + seg_len, :]
            hidden[s * seg_len : (s + 1) * seg_len, lanes] = part.astype(hidden.dtype)


def hidden_rows(place, streams, halo, short, rates, coef, skip, gated, prefix, starts, part):
    _, rows, chans = streams.shape
    order = rates.shape[0]
    share = len(starts)
    wide = chans // share
    groups = wide // LANES
    seg_len = rows // SEGS
    steps = max(1, share // 2)
    first = part * steps
    pos_rows = TOP + SEGS * (seg_len + 1)
    return pl.pallas_call(
        functools.partial(hidden_body, seg_len=seg_len, order=order, share=share, first=first),
        grid_spec=pltpu.PrefetchScalarGridSpec(
            num_scalar_prefetch=1,
            grid=(steps,),
            in_specs=[
                pl.BlockSpec((1, rows, wide), lambda g, place: (0, 0, first + g)),
                pl.BlockSpec((3, 2, wide), lambda g, place: (0, 0, first + g)),
                pl.BlockSpec((3, 3, wide), lambda g, place: (0, 0, first + g)),
                pl.BlockSpec((order, wide), lambda g, place: (0, first + g)),
                pl.BlockSpec((order, wide), lambda g, place: (0, first + g)),
                pl.BlockSpec((1, wide), lambda g, place: (0, first + g)),
                pl.BlockSpec((groups, rows, LANES), lambda g, place: (first + g, 0, 0)),
                pl.BlockSpec((groups, order, SEGS, LANES), lambda g, place: (first + g, 0, 0, 0)),
            ]
            + [pl.BlockSpec((order, wide), lambda g, place: (0, 0))] * share,
            out_specs=pl.BlockSpec((rows, wide), lambda g, place: (0, g)),
            scratch_shapes=[
                pltpu.VMEM((groups, pos_rows, LANES), jnp.float32),
                pltpu.VMEM((groups, pos_rows, LANES), jnp.float32),
                pltpu.VMEM((share, order, wide), jnp.float32),
            ],
        ),
        out_shape=jax.ShapeDtypeStruct((rows, steps * wide), jnp.bfloat16),
        compiler_params=pltpu.CompilerParams(vmem_limit_bytes=VMEM_LIMIT),
        cost_estimate=estimate(rows * chans * 40, rows * chans * 5),
        name="hidden_rows",
    )(place, streams, halo, short, rates, coef, skip, gated, prefix, *starts)


def project_body(place, *refs, pieces, outer, blocks):
    hidden = refs[: sum(pieces)]
    weight = refs[sum(pieces) : sum(pieces) + 2 * outer - 1]
    outs = refs[sum(pieces) + 2 * outer - 1 : -4]
    held, cols, held_sem, cols_sem = refs[-4:]
    plane, half = place[0], place[1]
    away = [half * blocks + b - plane for b in range(blocks)]

    def col_copy(b, at):
        return pltpu.make_async_copy(weight[at], cols.at[b], cols_sem.at[b])

    def each_source(b, act):
        for at in range(2 * outer - 1):

            @pl.when(away[b] == at - (outer - 1))
            def _(at=at):
                act(col_copy(b, at))

    row_copies = []
    at = 0
    for j, count in enumerate(pieces):
        size = held.shape[2] // count
        row_copies.append(
            [
                pltpu.make_async_copy(
                    hidden[at + e], held.at[j, :, pl.ds(e * size, size)], held_sem.at[at + e]
                )
                for e in range(count)
            ]
        )
        at += count
    each_source(0, lambda copy: copy.start())
    for copy in row_copies[0]:
        copy.start()
    for b in range(1, blocks):
        each_source(b, lambda copy: copy.start())
    for copies in row_copies[1:]:
        for copy in copies:
            copy.start()
    width = cols.shape[2]
    for j in range(len(pieces)):
        for copy in row_copies[j]:
            copy.wait()
        for b in range(blocks):
            if j == 0:
                each_source(b, lambda copy: copy.wait())
            made = jnp.dot(held[j], cols[b], preferred_element_type=jnp.float32)
            outs[j][:, b * width : (b + 1) * width] = made.astype(jnp.bfloat16)


def project(place, hidden, weight, outer, blocks):
    pieces = tuple(len(part) for part in hidden)
    rows = hidden[0][0].shape[0]
    depth, width = weight[0].shape
    flat = [piece for part in hidden for piece in part]
    share = len(pieces)
    anywhere = pl.BlockSpec(memory_space=pl.ANY)
    return pl.pallas_call(
        functools.partial(project_body, pieces=pieces, outer=outer, blocks=blocks),
        in_specs=[pl.BlockSpec(memory_space=pltpu.SMEM)] + [anywhere] * (len(flat) + len(weight)),
        out_specs=[pl.BlockSpec(memory_space=pltpu.VMEM)] * share,
        out_shape=[jax.ShapeDtypeStruct((rows, blocks * width), jnp.bfloat16)] * share,
        scratch_shapes=[
            pltpu.VMEM((share, rows, depth), jnp.bfloat16),
            pltpu.VMEM((blocks, depth, width), jnp.bfloat16),
            pltpu.SemaphoreType.DMA((len(flat),)),
            pltpu.SemaphoreType.DMA((blocks,)),
        ],
        compiler_params=pltpu.CompilerParams(vmem_limit_bytes=VMEM_LIMIT),
        cost_estimate=estimate(
            2 * share * rows * depth * blocks * width,
            2 * depth * (share * rows + blocks * width) + 2 * share * rows * blocks * width,
        ),
        name="project",
    )(place, *flat, *weight)


def assemble_body(place, *refs):
    parts, out = refs[:-1], refs[-1]
    for j, part in enumerate(parts):

        @pl.when(pl.program_id(1) == j)
        def _(part=part):
            out[...] = part[...]


def assemble(place, parts, blocks, width):
    share = len(parts)
    rows = parts[0].shape[0]
    return pl.pallas_call(
        assemble_body,
        grid_spec=pltpu.PrefetchScalarGridSpec(
            num_scalar_prefetch=1,
            grid=(blocks, share),
            in_specs=[pl.BlockSpec((rows, width), lambda b, j, place: (0, b))] * share,
            out_specs=pl.BlockSpec((rows, width), lambda b, j, place: (0, b * share + (place[0] ^ j))),
        ),
        out_shape=jax.ShapeDtypeStruct((rows, share * blocks * width), jnp.bfloat16),
        cost_estimate=estimate(0, 4 * rows * share * blocks * width),
        name="assemble",
    )(place, *parts)


def after(value, *others):
    return lax.optimization_barrier((value, *others))[0]


def weight_step(below, above, count, group, k):
    return send_along(below, count, group, 1, k), send_along(above, count, group, -1, k)


def plane_rows(hidden, count, group):
    if group != 4:
        return [hidden] + [[send_xor(part, count, group, j) for part in hidden] for j in range(1, group)]
    first, second = hidden
    first_1 = send_xor(first, count, group, 1)
    first_2 = send_xor(first, count, group, 2)
    second_2 = send_xor(second, count, group, 2)
    second_1 = send_xor(second, count, group, 1)
    first_3 = send_xor(first_1, count, group, 2)
    second_3 = send_xor(second_2, count, group, 1)
    return [[first, second], [first_1, second_1], [first_2, second_2], [first_3, second_3]]


def per_device(projected, short_filter, residues, rates, skip_gain, out_weight):
    count = lax.axis_size("ctx")
    halves = lax.axis_size("tp")
    here = lax.axis_index("ctx")
    half = lax.axis_index("tp")
    rows, _, chans = projected.shape
    order = rates.shape[1]

    streams = jnp.transpose(projected, (1, 0, 2))
    halo = lax.ppermute(streams[:, -2:], "ctx", [(p, p + 1) for p in range(count - 1)])
    group = split_of(count)
    outer = count // group
    below, above = [out_weight], [out_weight]

    def weight_on(*others):
        k = len(below) - 1
        if k < outer - 1:
            down, up = weight_step(after(below[-1], *others), after(above[-1], *others), count, group, k)
            below.append(down)
            above.append(up)

    weight_on(halo)
    rates_t = rates.T
    coef_t = (residues * jnp.sqrt(-jnp.expm1(-2.0 * rates))).T

    share = min(split_of(count), chans // LANES, 4)
    lines = count // share
    spot = jnp.full((1,), here % share, jnp.int32)
    *ends, gated, prefix = local_scan(spot, streams, halo, short_filter, rates_t, share)
    ends = [ends[0]] + [send_xor(ends[j], count, share, j) for j in range(1, share)]
    whole, befores = plane_scan(spot, rates_t, ends, rows)
    arrived = [send_along(whole, count, share, k) for k in range(1, lines)]
    starts = line_scan(spot, rates_t, befores, arrived, rows)
    weight_on(starts[0])
    starts = [starts[0]] + [send_xor(starts[j], count, share, j) for j in range(1, share)]
    hidden = [
        hidden_rows(
            spot, streams, halo, short_filter, rates_t, coef_t, skip_gain[None], gated, prefix, starts, part
        )
        for part in range(2)
    ]

    pieces = plane_rows(hidden, count, group)
    for _ in range(3, outer):
        weight_on(pieces[1][0])
    weight_on(pieces[1][0])
    line = below[:0:-1] + above
    width = out_weight.shape[1]
    blocks = outer // halves
    plane = here // group
    if halves == 2 and width % LANES == 0:
        place = jnp.stack([plane, 1 - half]).astype(jnp.int32)
        given = project(place, pieces, line, outer, blocks)
        taken = [lax.ppermute(part, "tp", [(0, 1), (1, 0)]) for part in given]
        place = jnp.stack([plane, half]).astype(jnp.int32)
        kept = project(place, pieces, line, outer, blocks)
        mixed = [
            (a.astype(jnp.float32) + b.astype(jnp.float32)).astype(jnp.bfloat16)
            for a, b in zip(kept, taken)
        ]
    else:
        cols = lax.dynamic_slice_in_dim(jnp.stack(line), outer - 1 - plane, outer, 0)
        cols = jnp.moveaxis(cols, 0, 1).reshape(chans, outer * width)
        held = jnp.concatenate([jnp.concatenate(part, axis=1) for part in pieces], axis=0)
        partial = jnp.dot(held, cols, preferred_element_type=jnp.float32).astype(jnp.bfloat16)
        summed = lax.psum_scatter(partial, "tp", scatter_dimension=1, tiled=True)
        mixed = list(summed.reshape(group, rows, blocks * width))
    mixed = [mixed[0]] + [send_xor(mixed[j], count, group, j) for j in range(1, group)]
    spot = jnp.full((1,), here % group, jnp.int32)
    if width % LANES == 0:
        return assemble(spot, mixed, blocks, width)
    stacked = jnp.stack(mixed).reshape(group, rows, blocks, width)
    by_place = jnp.take(stacked, jnp.arange(group) ^ spot[0], axis=0)
    return jnp.moveaxis(by_place, 0, 2).reshape(rows, blocks * group * width)


def solution(mesh):
    return jax.shard_map(
        per_device,
        mesh=mesh,
        in_specs=(
            P("ctx", None, "tp"),
            P(None, None, "tp"),
            P("tp", None),
            P("tp", None),
            P("tp"),
            P("tp", "ctx"),
        ),
        out_specs=P("ctx", "tp"),
        check_vma=False,
    )
```

```python
import functools

import jax
import jax.numpy as jnp
from jax import lax
from jax.experimental import pallas as pl
from jax.experimental.pallas import tpu as pltpu
from jax.sharding import PartitionSpec as P

LANES = 128
SEGS = 8
TOP = 8
VMEM_LIMIT = 16 * 1024 * 1024
SMALL_LIMIT = 4 * 1024 * 1024
WHOLE_LIMIT = 50 * 1024 * 1024


def split_of(count):
    inner = 1
    while (2 * inner) ** 2 <= count and count % (2 * inner) == 0:
        inner *= 2
    return inner


def send_xor(value, count, group, step):
    pairs = [(p, p - p % group + ((p % group) ^ step)) for p in range(count)]
    return lax.ppermute(value, "ctx", pairs)


def send_along(value, count, group, steps, first=0):
    outer = count // group
    pairs = []
    for z in range(outer):
        if not 0 <= z + steps < outer:
            continue
        if (steps > 0 and z < first) or (steps < 0 and z > outer - 1 - first):
            continue
        pairs += [(z * group + e, (z + steps) * group + e) for e in range(group)]
    return lax.ppermute(value, "ctx", pairs)


def estimate(flops, bytes_accessed, transcendentals=0):
    return pl.CostEstimate(flops=flops, bytes_accessed=bytes_accessed, transcendentals=transcendentals)


def row(ref, r, lanes):
    return jnp.broadcast_to(ref[r : r + 1, lanes], (SEGS, LANES))


def lay_segments(dst, stream, halo, seg_len, lanes, group):
    pitch = seg_len + 1
    for s in range(SEGS):
        part = stream[0, s * seg_len : (s + 1) * seg_len, lanes].astype(jnp.float32)
        dst[group, TOP + s * pitch : TOP + s * pitch + seg_len, :] = part
    dst[group, TOP - 3 : TOP - 1, :] = halo


def taps(short, stream, lanes):
    return [jnp.broadcast_to(short[i, stream : stream + 1, lanes], (SEGS, LANES)) for i in range(3)]


def strided(ref, group, start, pitch):
    return ref[group, pl.ds(start, SEGS, stride=pitch), :]


def local_scan_body(place, streams, halo, short_all, rates_all, *rest, seg_len, order, share):
    ends = rest[:share]
    gated, prefix = rest[share : share + 2]
    key_pos, value_pos, end_now, held, short_held, rates_held, held_sem, small_sem = rest[share + 2 :]
    now_at = pl.program_id(0)
    wide = end_now.shape[1]
    small = [
        pltpu.make_async_copy(short_all, short_held, small_sem.at[0]),
        pltpu.make_async_copy(rates_all, rates_held, small_sem.at[1]),
    ]

    def stream_copy(at):
        columns = pl.ds(at * wide, wide)
        return pltpu.make_async_copy(
            streams.at[pl.ds(1, 2), :, columns], held.at[:, :, columns], held_sem.at[at]
        )

    @pl.when(now_at == 0)
    def _():
        stream_copy(0).start()
        for copy in small:
            copy.start()
        for at in range(1, share):
            stream_copy(at).start()
        for copy in small:
            copy.wait()

    for at in range(share):

        @pl.when(now_at == at)
        def _(at=at):
            stream_copy(at).wait()

    columns = pl.ds(pl.multiple_of(now_at * wide, LANES), wide)
    key = held.at[pl.ds(0, 1), :, columns]
    value = held.at[pl.ds(1, 1), :, columns]
    short = short_held.at[:, :, columns]
    rates = rates_held.at[:, columns]
    pitch = seg_len + 1
    groups = gated.shape[0]
    segment = lax.broadcasted_iota(jnp.int32, (SEGS, LANES), 0)
    for group in range(groups):
        lanes = slice(group * LANES, (group + 1) * LANES)
        lay_segments(key_pos, key, halo[1, :, lanes].astype(jnp.float32), seg_len, lanes, group)
        lay_segments(value_pos, value, halo[2, :, lanes].astype(jnp.float32), seg_len, lanes, group)

    for group in range(groups):
        lanes = slice(group * LANES, (group + 1) * LANES)
        key_taps = taps(short, 1, lanes)
        value_taps = taps(short, 2, lanes)
        decay = [jnp.exp(-row(rates, r, lanes)) for r in range(order)]

        def step(i, carry, group=group, key_taps=key_taps, value_taps=value_taps, decay=decay):
            k1, k2, v1, v2, *states = carry
            k0 = strided(key_pos, group, TOP + i, pitch)
            v0 = strided(value_pos, group, TOP + i, pitch)
            key_now = key_taps[0] * k0 + key_taps[1] * k1 + key_taps[2] * k2
            value_now = value_taps[0] * v0 + value_taps[1] * v1 + value_taps[2] * v2
            now = key_now * value_now
            gated[group, pl.ds(pl.multiple_of(i * SEGS, SEGS), SEGS), :] = now
            states = [d * h + now for d, h in zip(decay, states)]
            return (k0, k1, v0, v1, *states)

        zero = jnp.zeros((SEGS, LANES), jnp.float32)
        start = (
            strided(key_pos, group, TOP - 2, pitch),
            strided(key_pos, group, TOP - 3, pitch),
            strided(value_pos, group, TOP - 2, pitch),
            strided(value_pos, group, TOP - 3, pitch),
        ) + (zero,) * order
        states = lax.fori_loop(0, seg_len, step, start, unroll=8)[4:]
        for r in range(order):
            rate = row(rates, r, lanes)
            scan = states[r]
            for d in (1, 2, 4):
                moved = jnp.where(segment >= d, pltpu.roll(scan, d, 0), 0.0)
                scan = scan + jnp.exp(rate * (-1.0 * d * seg_len)) * moved
            prefix[group, r] = jnp.where(segment >= 1, pltpu.roll(scan, 1, 0), 0.0)
            end_now[r : r + 1, lanes] = scan[SEGS - 1 :, :]

    for j in range(share):

        @pl.when((pl.program_id(0) ^ place[0]) == j)
        def _(j=j):
            ends[j][...] = end_now[...]


def local_scan(place, streams, halo, short, rates, share):
    _, rows, chans = streams.shape
    order = rates.shape[0]
    wide = chans // share
    groups = wide // LANES
    seg_len = rows // SEGS
    pos_rows = TOP + SEGS * (seg_len + 1)
    end_shape = jax.ShapeDtypeStruct((order, wide), jnp.float32)
    return pl.pallas_call(
        functools.partial(local_scan_body, seg_len=seg_len, order=order, share=share),
        grid_spec=pltpu.PrefetchScalarGridSpec(
            num_scalar_prefetch=1,
            grid=(share,),
            in_specs=[
                pl.BlockSpec(memory_space=pltpu.HBM),
                pl.BlockSpec((3, 2, wide), lambda g, place: (0, 0, g)),
                pl.BlockSpec(memory_space=pltpu.HBM),
                pl.BlockSpec(memory_space=pltpu.HBM),
            ],
            out_specs=[pl.BlockSpec((order, wide), lambda g, place: (0, 0))] * share
            + [
                pl.BlockSpec((groups, rows, LANES), lambda g, place: (g, 0, 0)),
                pl.BlockSpec((groups, order, SEGS, LANES), lambda g, place: (g, 0, 0, 0)),
            ],
            scratch_shapes=[
                pltpu.VMEM((groups, pos_rows, LANES), jnp.float32),
                pltpu.VMEM((groups, pos_rows, LANES), jnp.float32),
                pltpu.VMEM((order, wide), jnp.float32),
                pltpu.VMEM((2, rows, chans), streams.dtype),
                pltpu.VMEM(short.shape, jnp.float32),
                pltpu.VMEM(rates.shape, jnp.float32),
                pltpu.SemaphoreType.DMA((share,)),
                pltpu.SemaphoreType.DMA((2,)),
            ],
        ),
        out_shape=[end_shape] * share
        + [
            jax.ShapeDtypeStruct((chans // LANES, rows, LANES), jnp.float32),
            jax.ShapeDtypeStruct((chans // LANES, order, SEGS, LANES), jnp.float32),
        ],
        compiler_params=pltpu.CompilerParams(vmem_limit_bytes=WHOLE_LIMIT),
        cost_estimate=estimate(rows * chans * 50, rows * chans * 10),
        name="local_scan",
    )(place, streams, halo, short, rates)


def plane_scan_body(place, rates, *rest, share, rows):
    ends = rest[:share]
    whole = rest[share]
    befores = rest[share + 1 : 2 * share + 1]
    by_place, before_place = rest[2 * share + 1 :]
    here = place[0]
    for j in range(share):
        by_place[here ^ j] = ends[j][...]
    decay = jnp.exp(rates[...] * (-1.0 * rows))
    state = jnp.zeros(rates.shape, jnp.float32)
    for at in range(share):
        before_place[at] = state
        state = decay * state + by_place[at]
    whole[...] = state
    for j in range(share):
        befores[j][...] = before_place[here ^ j]


def plane_scan(place, rates, ends, rows):
    share = len(ends)
    order, wide = ends[0].shape
    block = pl.BlockSpec((order, wide), lambda g, place: (0, 0))
    shape = jax.ShapeDtypeStruct((order, wide), jnp.float32)
    got = pl.pallas_call(
        functools.partial(plane_scan_body, share=share, rows=rows),
        grid_spec=pltpu.PrefetchScalarGridSpec(
            num_scalar_prefetch=1,
            grid=(1,),
            in_specs=[pl.BlockSpec((order, wide), lambda g, place: (0, place[0]))] + [block] * share,
            out_specs=[block] * (share + 1),
            scratch_shapes=[pltpu.VMEM((share, order, wide), jnp.float32)] * 2,
        ),
        out_shape=[shape] * (share + 1),
        compiler_params=pltpu.CompilerParams(vmem_limit_bytes=SMALL_LIMIT),
        cost_estimate=estimate(order * wide * 20, order * wide * 36),
        name="plane_scan",
    )(place, rates, *ends)
    return got[0], got[1:]


def line_scan_body(place, rates, *rest, share, rows, lines):
    befores = rest[:share]
    arrived = rest[share : share + lines]
    outs = rest[share + lines :]
    here = place[0]
    rate = rates[...] * (-1.0 * rows)
    decay = jnp.exp(rate * share)
    state = jnp.zeros(rate.shape, jnp.float32)
    for k in reversed(range(lines)):
        state = decay * state + arrived[k][...]
    for j in range(share):
        ahead = (here ^ j).astype(jnp.float32)
        outs[j][...] = befores[j][...] + jnp.exp(rate * ahead) * state


def line_scan(place, rates, befores, arrived, rows):
    share, lines = len(befores), len(arrived)
    order, wide = befores[0].shape
    block = pl.BlockSpec((order, wide), lambda g, place: (0, 0))
    return pl.pallas_call(
        functools.partial(line_scan_body, share=share, rows=rows, lines=lines),
        grid_spec=pltpu.PrefetchScalarGridSpec(
            num_scalar_prefetch=1,
            grid=(1,),
            in_specs=[pl.BlockSpec((order, wide), lambda g, place: (0, place[0]))]
            + [block] * (share + lines),
            out_specs=[block] * share,
        ),
        out_shape=[jax.ShapeDtypeStruct((order, wide), jnp.float32)] * share,
        compiler_params=pltpu.CompilerParams(vmem_limit_bytes=SMALL_LIMIT),
        cost_estimate=estimate(order * wide * 20, order * wide * 36),
        name="line_scan",
    )(place, rates, *befores, *arrived)


def hidden_body(place, query, halo, short, rates, coef, skip, gated, prefix, *rest, seg_len, order, share, first):
    starts = rest[:share]
    hidden = rest[share]
    query_pos, result_pos, start_by_place = rest[share + 1 :]
    pitch = seg_len + 1
    groups = gated.shape[0]
    now_at = pl.program_id(0) + first
    segment = lax.broadcasted_iota(jnp.int32, (SEGS, LANES), 0).astype(jnp.float32)

    @pl.when(pl.program_id(0) == 0)
    def _():
        for j in range(share):
            start_by_place[place[0] ^ j] = starts[j][...]

    for group in range(groups):
        lanes = slice(group * LANES, (group + 1) * LANES)
        lay_segments(query_pos, query, halo[0, :, lanes].astype(jnp.float32), seg_len, lanes, group)

    for group in range(groups):
        lanes = slice(group * LANES, (group + 1) * LANES)
        query_taps = taps(short, 0, lanes)
        gain = jnp.broadcast_to(skip[0:1, lanes], (SEGS, LANES))
        decay = [jnp.exp(-row(rates, r, lanes)) for r in range(order)]
        scale = [row(coef, r, lanes) for r in range(order)]
        states = []
        for r in range(order):
            ahead = jnp.exp(row(rates, r, lanes) * (segment * (-1.0 * seg_len)))
            before = jnp.broadcast_to(start_by_place[now_at, r : r + 1, lanes], (SEGS, LANES))
            states.append(prefix[group, r] + ahead * before)

        def step(i, carry, group=group, query_taps=query_taps, gain=gain, decay=decay, scale=scale):
            q1, q2, *states = carry
            q0 = strided(query_pos, group, TOP + i, pitch)
            now = gated[group, pl.ds(pl.multiple_of(i * SEGS, SEGS), SEGS), :]
            states = [d * h + now for d, h in zip(decay, states)]
            sums = [s * h for s, h in zip(scale, states)] + [gain * now]
            while len(sums) > 1:
                sums = [a + b for a, b in zip(sums[::2], sums[1::2])] + sums[len(sums) // 2 * 2 :]
            query_now = query_taps[0] * q0 + query_taps[1] * q1 + query_taps[2] * q2
            result_pos[group, pl.ds(TOP + i, SEGS, stride=pitch), :] = query_now * sums[0]
            return (q0, q1, *states)

        start = (
            strided(query_pos, group, TOP - 2, pitch),
            strided(query_pos, group, TOP - 3, pitch),
        ) + tuple(states)
        lax.fori_loop(0, seg_len, step, start, unroll=8)
        for s in range(SEGS):
            part = result_pos[group, TOP + s * pitch : TOP + s * pitch + seg_len, :]
            hidden[s * seg_len : (s + 1) * seg_len, lanes] = part.astype(hidden.dtype)


def hidden_rows(place, streams, halo, short, rates, coef, skip, gated, prefix, starts, part):
    _, rows, chans = streams.shape
    order = rates.shape[0]
    share = len(starts)
    wide = chans // share
    groups = wide // LANES
    seg_len = rows // SEGS
    steps = max(1, share // 2)
    first = part * steps
    pos_rows = TOP + SEGS * (seg_len + 1)
    return pl.pallas_call(
        functools.partial(hidden_body, seg_len=seg_len, order=order, share=share, first=first),
        grid_spec=pltpu.PrefetchScalarGridSpec(
            num_scalar_prefetch=1,
            grid=(steps,),
            in_specs=[
                pl.BlockSpec((1, rows, wide), lambda g, place: (0, 0, first + g)),
                pl.BlockSpec((3, 2, wide), lambda g, place: (0, 0, first + g)),
                pl.BlockSpec((3, 3, wide), lambda g, place: (0, 0, first + g)),
                pl.BlockSpec((order, wide), lambda g, place: (0, first + g)),
                pl.BlockSpec((order, wide), lambda g, place: (0, first + g)),
                pl.BlockSpec((1, wide), lambda g, place: (0, first + g)),
                pl.BlockSpec((groups, rows, LANES), lambda g, place: (first + g, 0, 0)),
                pl.BlockSpec((groups, order, SEGS, LANES), lambda g, place: (first + g, 0, 0, 0)),
            ]
            + [pl.BlockSpec((order, wide), lambda g, place: (0, 0))] * share,
            out_specs=pl.BlockSpec((rows, wide), lambda g, place: (0, g)),
            scratch_shapes=[
                pltpu.VMEM((groups, pos_rows, LANES), jnp.float32),
                pltpu.VMEM((groups, pos_rows, LANES), jnp.float32),
                pltpu.VMEM((share, order, wide), jnp.float32),
            ],
        ),
        out_shape=jax.ShapeDtypeStruct((rows, steps * wide), jnp.bfloat16),
        compiler_params=pltpu.CompilerParams(vmem_limit_bytes=VMEM_LIMIT),
        cost_estimate=estimate(rows * chans * 40, rows * chans * 5),
        name="hidden_rows",
    )(place, streams, halo, short, rates, coef, skip, gated, prefix, *starts)


def project_body(pick, *refs, rows_in, slots):
    out, chosen = refs[-2:]
    at = 0
    rows = []
    for count in rows_in:
        rows.append(refs[at : at + count])
        at += count
    width = chosen.shape[1]
    pieces = [jnp.concatenate([part[k][...] for part in rows], axis=0) for k in range(rows_in[0])]
    for slot, count in enumerate(slots):
        given = refs[at : at + count]
        at += count
        columns = given[0]
        if count == 2:

            @pl.when(pick[0] == 1)
            def _(given=given):
                chosen[...] = given[0][...]

            @pl.when(pick[0] != 1)
            def _(given=given):
                chosen[...] = given[1][...]

            columns = chosen
        total = 0.0
        start = 0
        for piece in pieces:
            depth = piece.shape[1]
            total += jnp.dot(piece, columns[start : start + depth, :], preferred_element_type=jnp.float32)
            start += depth
        out[:, slot * width : (slot + 1) * width] = total.astype(out.dtype)


def project(pick, rows, slots):
    flat = [piece for part in rows for piece in part] + [block for slot in slots for block in slot]
    count = sum(part[0].shape[0] for part in rows)
    depth, width = slots[0][0].shape
    return pl.pallas_call(
        functools.partial(
            project_body, rows_in=tuple(map(len, rows)), slots=tuple(map(len, slots))
        ),
        in_specs=[pl.BlockSpec(memory_space=pltpu.SMEM)]
        + [pl.BlockSpec(memory_space=pltpu.VMEM)] * len(flat),
        out_specs=pl.BlockSpec(memory_space=pltpu.VMEM),
        out_shape=jax.ShapeDtypeStruct((count, len(slots) * width), jnp.bfloat16),
        scratch_shapes=[pltpu.VMEM((depth, width), jnp.bfloat16)],
        compiler_params=pltpu.CompilerParams(vmem_limit_bytes=VMEM_LIMIT),
        cost_estimate=estimate(
            2 * count * depth * len(slots) * width,
            2 * (count * depth + len(slots) * width * (depth + count)),
        ),
        name="project",
    )(pick, *flat)


def assemble_body(place, *refs, kinds):
    out = refs[-1]
    width = refs[0].shape[1]
    at = 0
    for j, count in enumerate(kinds):
        given = refs[at : at + count]
        at += count
        column = pl.multiple_of((place[0] ^ j) * width, LANES)
        if count == 1:
            out[:, pl.ds(column, width)] = given[0][...]
            continue

        @pl.when(place[2] == 1)
        def _(given=given, column=column):
            out[:, pl.ds(column, width)] = given[0][...]

        @pl.when(place[2] != 1)
        def _(given=given, column=column):
            out[:, pl.ds(column, width)] = given[1][...]


def assemble(place, parts, blocks, width):
    flat = [piece for part in parts for piece in part]
    share = len(parts)
    rows = flat[0].shape[0]
    return pl.pallas_call(
        functools.partial(assemble_body, kinds=tuple(map(len, parts))),
        grid_spec=pltpu.PrefetchScalarGridSpec(
            num_scalar_prefetch=1,
            grid=(blocks,),
            in_specs=[pl.BlockSpec((rows, width), lambda b, place: (0, b ^ place[1]))] * len(flat),
            out_specs=pl.BlockSpec((rows, share * width), lambda b, place: (0, b)),
        ),
        out_shape=jax.ShapeDtypeStruct((rows, share * blocks * width), jnp.bfloat16),
        compiler_params=pltpu.CompilerParams(vmem_limit_bytes=VMEM_LIMIT),
        cost_estimate=estimate(0, 4 * rows * share * blocks * width),
        name="assemble",
    )(place, *flat)


def after(value, *others):
    return lax.optimization_barrier((value, *others))[0]


def send_planes(value, group, moves):
    pairs = [(a * group + e, b * group + e) for a, b in moves for e in range(group)]
    return lax.ppermute(value, "ctx", pairs)


def send_cores(value, count, moves):
    pairs = [(p * 2 + s, q * 2 + t) for at in range(count) for (p, s), (q, t) in moves(at)]
    return lax.ppermute(value, ("ctx", "tp"), pairs)


def plane_rows(hidden, count, group):
    if group != 4:
        return [hidden] + [[send_xor(part, count, group, j) for part in hidden] for j in range(1, group)]
    first, second = hidden
    first_1 = send_xor(first, count, group, 1)
    first_2 = send_xor(first, count, group, 2)
    second_2 = send_xor(second, count, group, 2)
    second_1 = send_xor(second, count, group, 1)
    first_3 = send_xor(first_1, count, group, 2)
    second_3 = send_xor(second_2, count, group, 1)
    return [[first, second], [first_1, second_1], [first_2, second_2], [first_3, second_3]]


def add_up(a, b):
    return (a.astype(jnp.float32) + b.astype(jnp.float32)).astype(jnp.bfloat16)


def project_4x4(out_weight, halo, states, hidden, count):
    group = 4
    here = lax.axis_index("ctx")
    half = lax.axis_index("tp")
    plane = here // group
    swap = [(0, 1), (1, 0), (2, 3), (3, 2)]
    inner = [(1, 2), (2, 1)]
    outward = [(1, 0), (2, 3)]
    own = after(out_weight, halo)
    by_1 = send_planes(own, group, swap)
    by_3_inner = send_planes(own, group, inner)
    by_2_inner = send_planes(after(by_1, states, by_3_inner), group, inner)
    by_2_outer = send_planes(after(by_3_inner, states), group, outward)
    rows = plane_rows(hidden, count, group)
    by_3_outer = send_planes(after(by_2_inner, by_2_outer, rows[1][0]), group, outward)
    near = [[own], [by_1]]
    far = [[by_2_inner, by_2_outer], [by_3_inner, by_3_outer]]

    pick = jnp.full((1,), (plane == 1) | (plane == 2), jnp.int32)
    size = hidden[0].shape[0]
    wide = 2 * out_weight.shape[1]

    def keeper(p):
        return p // group // 2

    def to_near(p):
        return [((p, 1 - keeper(p)), (p, keeper(p)))]

    def to_far(p):
        return [((p, keeper(p)), (p, 1 - keeper(p)))]

    def near_plane(j):
        return lambda p: [((p, keeper(p)), (p ^ j, keeper(p)))]

    def far_plane(j):
        return lambda p: [((p, 1 - keeper(p)), (p ^ j, 1 - keeper(p)))]

    near_part = project(pick, rows[:3], near)
    near_sum = [
        add_up(near_part[j * size : (j + 1) * size], taken)
        for j, taken in enumerate(jnp.split(send_cores(near_part, count, to_near), 3))
    ]
    near_got = [near_sum[0]] + [send_cores(near_sum[j], count, near_plane(j)) for j in (1, 2)]
    last_part = project(pick, rows[3:], near + far)
    last_taken = lax.ppermute(last_part, "tp", [(0, 1), (1, 0)])
    keeps_near = half == plane // 2
    last_sum = jnp.where(
        keeps_near,
        add_up(last_part[:, :wide], last_taken[:, :wide]),
        add_up(last_part[:, wide:], last_taken[:, wide:]),
    )
    last_got = send_xor(last_sum, count, group, 3)
    far_part = project(pick, rows[:3], far)
    far_sum = [
        add_up(far_part[j * size : (j + 1) * size], taken)
        for j, taken in enumerate(jnp.split(send_cores(far_part, count, to_far), 3))
    ]
    far_got = [far_sum[0]] + [send_cores(far_sum[j], count, far_plane(j)) for j in (1, 2)]
    parts = [[a, b] for a, b in zip(near_got, far_got)] + [[last_got]]
    place = jnp.stack([here % group, plane % 2, keeps_near.astype(here.dtype)]).astype(jnp.int32)
    return assemble(place, parts, 2, out_weight.shape[1])


def project_any(out_weight, halo, states, hidden, count):
    halves = lax.axis_size("tp")
    group = split_of(count)
    outer = count // group
    plane = lax.axis_index("ctx") // group
    size = hidden[0].shape[0]
    depth, width = out_weight.shape
    below, above = [after(out_weight, halo)], [after(out_weight, halo)]
    for k in range(1, outer):
        down, up = below[-1], above[-1]
        if k == 2:
            down, up = after(down, states), after(up, states)
        below.append(send_along(down, count, group, 1, k - 1))
        above.append(send_along(up, count, group, -1, k - 1))
    line = below[:0:-1] + above
    cols = lax.dynamic_slice_in_dim(jnp.stack(line), outer - 1 - plane, outer, 0)
    cols = jnp.moveaxis(cols, 0, 1).reshape(depth, outer * width)
    rows = plane_rows(hidden, count, group)
    held = jnp.concatenate([jnp.concatenate(part, axis=1) for part in rows], axis=0)
    partial = jnp.dot(held, cols, preferred_element_type=jnp.float32).astype(jnp.bfloat16)
    mixed = lax.psum_scatter(partial, "tp", scatter_dimension=1, tiled=True)
    mixed = jnp.split(mixed, group)
    mixed = [mixed[0]] + [send_xor(mixed[j], count, group, j) for j in range(1, group)]
    blocks = outer // halves
    stacked = jnp.stack(mixed).reshape(group, size, blocks, width)
    by_place = jnp.take(stacked, jnp.arange(group) ^ (lax.axis_index("ctx") % group), axis=0)
    return jnp.moveaxis(by_place, 0, 2).reshape(size, blocks * group * width)


def per_device(projected, short_filter, residues, rates, skip_gain, out_weight):
    count = lax.axis_size("ctx")
    halves = lax.axis_size("tp")
    here = lax.axis_index("ctx")
    rows, _, chans = projected.shape

    streams = jnp.transpose(projected, (1, 0, 2))
    halo = lax.ppermute(streams[:, -2:], "ctx", [(p, p + 1) for p in range(count - 1)])
    rates_t = rates.T
    coef_t = (residues * jnp.sqrt(-jnp.expm1(-2.0 * rates))).T

    share = min(split_of(count), chans // LANES, 4)
    lines = count // share
    spot = jnp.full((1,), here % share, jnp.int32)
    *ends, gated, prefix = local_scan(spot, streams, halo, short_filter, rates_t, share)
    ends = [ends[0]] + [send_xor(ends[j], count, share, j) for j in range(1, share)]
    whole, befores = plane_scan(spot, rates_t, ends, rows)
    arrived = [send_along(whole, count, share, k) for k in range(1, lines)]
    starts = line_scan(spot, rates_t, befores, arrived, rows)
    states = starts[0]
    starts = [starts[0]] + [send_xor(starts[j], count, share, j) for j in range(1, share)]
    hidden = [
        hidden_rows(
            spot, streams, halo, short_filter, rates_t, coef_t, skip_gain[None], gated, prefix, starts, part
        )
        for part in range(2)
    ]
    if count == 16 and halves == 2 and out_weight.shape[1] % LANES == 0:
        return project_4x4(out_weight, halo, states, hidden, count)
    return project_any(out_weight, halo, states, hidden, count)


def solution(mesh):
    return jax.shard_map(
        per_device,
        mesh=mesh,
        in_specs=(
            P("ctx", None, "tp"),
            P(None, None, "tp"),
            P("tp", None),
            P("tp", None),
            P("tp"),
            P("tp", "ctx"),
        ),
        out_specs=P("ctx", "tp"),
        check_vma=False,
    )
```

```python
import functools

import jax
import jax.numpy as jnp
from jax import lax
from jax.experimental import pallas as pl
from jax.experimental.pallas import tpu as pltpu
from jax.sharding import PartitionSpec as P

LANES = 128
SEGS = 8
TOP = 8
VMEM_LIMIT = 16 * 1024 * 1024
SMALL_LIMIT = 4 * 1024 * 1024
WHOLE_LIMIT = 50 * 1024 * 1024


def split_of(count):
    inner = 1
    while (2 * inner) ** 2 <= count and count % (2 * inner) == 0:
        inner *= 2
    return inner


def send_xor(value, count, group, step):
    pairs = [(p, p - p % group + ((p % group) ^ step)) for p in range(count)]
    return lax.ppermute(value, "ctx", pairs)


def send_along(value, count, group, steps, first=0):
    outer = count // group
    pairs = []
    for z in range(outer):
        if not 0 <= z + steps < outer:
            continue
        if (steps > 0 and z < first) or (steps < 0 and z > outer - 1 - first):
            continue
        pairs += [(z * group + e, (z + steps) * group + e) for e in range(group)]
    return lax.ppermute(value, "ctx", pairs)


def estimate(flops, bytes_accessed, transcendentals=0):
    return pl.CostEstimate(flops=flops, bytes_accessed=bytes_accessed, transcendentals=transcendentals)


def row(ref, r, lanes):
    return jnp.broadcast_to(ref[r : r + 1, lanes], (SEGS, LANES))


def lay_segments(dst, stream, halo, seg_len, lanes, group):
    pitch = seg_len + 1
    for s in range(SEGS):
        part = stream[0, s * seg_len : (s + 1) * seg_len, lanes].astype(jnp.float32)
        dst[group, TOP + s * pitch : TOP + s * pitch + seg_len, :] = part
    dst[group, TOP - 3 : TOP - 1, :] = halo


def taps(short, stream, lanes):
    return [jnp.broadcast_to(short[i, stream : stream + 1, lanes], (SEGS, LANES)) for i in range(3)]


def strided(ref, group, start, pitch):
    return ref[group, pl.ds(start, SEGS, stride=pitch), :]


def local_scan_body(place, streams, halo, short_all, rates_all, *rest, seg_len, order, share):
    ends = rest[:share]
    gated, prefix = rest[share : share + 2]
    key_pos, value_pos, end_now, held, short_held, rates_held, held_sem, small_sem = rest[share + 2 :]
    now_at = pl.program_id(0)
    wide = end_now.shape[1]
    small = [
        pltpu.make_async_copy(short_all, short_held, small_sem.at[0]),
        pltpu.make_async_copy(rates_all, rates_held, small_sem.at[1]),
    ]

    def stream_copy(at):
        columns = pl.ds(at * wide, wide)
        return pltpu.make_async_copy(
            streams.at[pl.ds(1, 2), :, columns], held.at[:, :, columns], held_sem.at[at]
        )

    @pl.when(now_at == 0)
    def _():
        stream_copy(0).start()
        for copy in small:
            copy.start()
        for at in range(1, share):
            stream_copy(at).start()
        for copy in small:
            copy.wait()

    for at in range(share):

        @pl.when(now_at == at)
        def _(at=at):
            stream_copy(at).wait()

    columns = pl.ds(pl.multiple_of(now_at * wide, LANES), wide)
    key = held.at[pl.ds(0, 1), :, columns]
    value = held.at[pl.ds(1, 1), :, columns]
    short = short_held.at[:, :, columns]
    rates = rates_held.at[:, columns]
    pitch = seg_len + 1
    groups = gated.shape[0]
    segment = lax.broadcasted_iota(jnp.int32, (SEGS, LANES), 0)
    for group in range(groups):
        lanes = slice(group * LANES, (group + 1) * LANES)
        lay_segments(key_pos, key, halo[1, :, lanes].astype(jnp.float32), seg_len, lanes, group)
        lay_segments(value_pos, value, halo[2, :, lanes].astype(jnp.float32), seg_len, lanes, group)

    for group in range(groups):
        lanes = slice(group * LANES, (group + 1) * LANES)
        key_taps = taps(short, 1, lanes)
        value_taps = taps(short, 2, lanes)
        decay = [jnp.exp(-row(rates, r, lanes)) for r in range(order)]

        def step(i, carry, group=group, key_taps=key_taps, value_taps=value_taps, decay=decay):
            k1, k2, v1, v2, *states = carry
            k0 = strided(key_pos, group, TOP + i, pitch)
            v0 = strided(value_pos, group, TOP + i, pitch)
            key_now = key_taps[0] * k0 + key_taps[1] * k1 + key_taps[2] * k2
            value_now = value_taps[0] * v0 + value_taps[1] * v1 + value_taps[2] * v2
            now = key_now * value_now
            gated[group, pl.ds(pl.multiple_of(i * SEGS, SEGS), SEGS), :] = now
            states = [d * h + now for d, h in zip(decay, states)]
            return (k0, k1, v0, v1, *states)

        zero = jnp.zeros((SEGS, LANES), jnp.float32)
        start = (
            strided(key_pos, group, TOP - 2, pitch),
            strided(key_pos, group, TOP - 3, pitch),
            strided(value_pos, group, TOP - 2, pitch),
            strided(value_pos, group, TOP - 3, pitch),
        ) + (zero,) * order
        states = lax.fori_loop(0, seg_len, step, start, unroll=8)[4:]
        for r in range(order):
            rate = row(rates, r, lanes)
            scan = states[r]
            for d in (1, 2, 4):
                moved = jnp.where(segment >= d, pltpu.roll(scan, d, 0), 0.0)
                scan = scan + jnp.exp(rate * (-1.0 * d * seg_len)) * moved
            prefix[group, r] = jnp.where(segment >= 1, pltpu.roll(scan, 1, 0), 0.0)
            end_now[r : r + 1, lanes] = scan[SEGS - 1 :, :]

    for j in range(share):

        @pl.when((pl.program_id(0) ^ place[0]) == j)
        def _(j=j):
            ends[j][...] = end_now[...]


def local_scan(place, streams, halo, short, rates, share):
    _, rows, chans = streams.shape
    order = rates.shape[0]
    wide = chans // share
    groups = wide // LANES
    seg_len = rows // SEGS
    pos_rows = TOP + SEGS * (seg_len + 1)
    end_shape = jax.ShapeDtypeStruct((order, wide), jnp.float32)
    return pl.pallas_call(
        functools.partial(local_scan_body, seg_len=seg_len, order=order, share=share),
        grid_spec=pltpu.PrefetchScalarGridSpec(
            num_scalar_prefetch=1,
            grid=(share,),
            in_specs=[
                pl.BlockSpec(memory_space=pltpu.HBM),
                pl.BlockSpec((3, 2, wide), lambda g, place: (0, 0, g)),
                pl.BlockSpec(memory_space=pltpu.HBM),
                pl.BlockSpec(memory_space=pltpu.HBM),
            ],
            out_specs=[pl.BlockSpec((order, wide), lambda g, place: (0, 0))] * share
            + [
                pl.BlockSpec((groups, rows, LANES), lambda g, place: (g, 0, 0)),
                pl.BlockSpec((groups, order, SEGS, LANES), lambda g, place: (g, 0, 0, 0)),
            ],
            scratch_shapes=[
                pltpu.VMEM((groups, pos_rows, LANES), jnp.float32),
                pltpu.VMEM((groups, pos_rows, LANES), jnp.float32),
                pltpu.VMEM((order, wide), jnp.float32),
                pltpu.VMEM((2, rows, chans), streams.dtype),
                pltpu.VMEM(short.shape, jnp.float32),
                pltpu.VMEM(rates.shape, jnp.float32),
                pltpu.SemaphoreType.DMA((share,)),
                pltpu.SemaphoreType.DMA((2,)),
            ],
        ),
        out_shape=[end_shape] * share
        + [
            jax.ShapeDtypeStruct((chans // LANES, rows, LANES), jnp.float32),
            jax.ShapeDtypeStruct((chans // LANES, order, SEGS, LANES), jnp.float32),
        ],
        compiler_params=pltpu.CompilerParams(vmem_limit_bytes=WHOLE_LIMIT),
        cost_estimate=estimate(rows * chans * 50, rows * chans * 10),
        name="local_scan",
    )(place, streams, halo, short, rates)


def plane_scan_body(place, rates, *rest, share, rows):
    ends = rest[:share]
    whole = rest[share]
    befores = rest[share + 1 : 2 * share + 1]
    by_place, before_place = rest[2 * share + 1 :]
    here = place[0]
    for j in range(share):
        by_place[here ^ j] = ends[j][...]
    decay = jnp.exp(rates[...] * (-1.0 * rows))
    state = jnp.zeros(rates.shape, jnp.float32)
    for at in range(share):
        before_place[at] = state
        state = decay * state + by_place[at]
    whole[...] = state
    for j in range(share):
        befores[j][...] = before_place[here ^ j]


def plane_scan(place, rates, ends, rows):
    share = len(ends)
    order, wide = ends[0].shape
    block = pl.BlockSpec((order, wide), lambda g, place: (0, 0))
    shape = jax.ShapeDtypeStruct((order, wide), jnp.float32)
    got = pl.pallas_call(
        functools.partial(plane_scan_body, share=share, rows=rows),
        grid_spec=pltpu.PrefetchScalarGridSpec(
            num_scalar_prefetch=1,
            grid=(1,),
            in_specs=[pl.BlockSpec((order, wide), lambda g, place: (0, place[0]))] + [block] * share,
            out_specs=[block] * (share + 1),
            scratch_shapes=[pltpu.VMEM((share, order, wide), jnp.float32)] * 2,
        ),
        out_shape=[shape] * (share + 1),
        compiler_params=pltpu.CompilerParams(vmem_limit_bytes=SMALL_LIMIT),
        cost_estimate=estimate(order * wide * 20, order * wide * 36),
        name="plane_scan",
    )(place, rates, *ends)
    return got[0], got[1:]


def line_scan_body(place, rates, *rest, share, rows, lines):
    befores = rest[:share]
    arrived = rest[share : share + lines]
    outs = rest[share + lines :]
    here = place[0]
    rate = rates[...] * (-1.0 * rows)
    decay = jnp.exp(rate * share)
    state = jnp.zeros(rate.shape, jnp.float32)
    for k in reversed(range(lines)):
        state = decay * state + arrived[k][...]
    for j in range(share):
        ahead = (here ^ j).astype(jnp.float32)
        outs[j][...] = befores[j][...] + jnp.exp(rate * ahead) * state


def line_scan(place, rates, befores, arrived, rows):
    share, lines = len(befores), len(arrived)
    order, wide = befores[0].shape
    block = pl.BlockSpec((order, wide), lambda g, place: (0, 0))
    return pl.pallas_call(
        functools.partial(line_scan_body, share=share, rows=rows, lines=lines),
        grid_spec=pltpu.PrefetchScalarGridSpec(
            num_scalar_prefetch=1,
            grid=(1,),
            in_specs=[pl.BlockSpec((order, wide), lambda g, place: (0, place[0]))]
            + [block] * (share + lines),
            out_specs=[block] * share,
        ),
        out_shape=[jax.ShapeDtypeStruct((order, wide), jnp.float32)] * share,
        compiler_params=pltpu.CompilerParams(vmem_limit_bytes=SMALL_LIMIT),
        cost_estimate=estimate(order * wide * 20, order * wide * 36),
        name="line_scan",
    )(place, rates, *befores, *arrived)


def hidden_body(place, query, halo, short, rates, coef, skip, gated, prefix, *rest, seg_len, order, share, first):
    starts = rest[:share]
    hidden = rest[share]
    query_pos, result_pos, start_by_place = rest[share + 1 :]
    pitch = seg_len + 1
    groups = gated.shape[0]
    now_at = pl.program_id(0) + first
    segment = lax.broadcasted_iota(jnp.int32, (SEGS, LANES), 0).astype(jnp.float32)

    @pl.when(pl.program_id(0) == 0)
    def _():
        for j in range(share):
            start_by_place[place[0] ^ j] = starts[j][...]

    for group in range(groups):
        lanes = slice(group * LANES, (group + 1) * LANES)
        lay_segments(query_pos, query, halo[0, :, lanes].astype(jnp.float32), seg_len, lanes, group)

    for group in range(groups):
        lanes = slice(group * LANES, (group + 1) * LANES)
        query_taps = taps(short, 0, lanes)
        gain = jnp.broadcast_to(skip[0:1, lanes], (SEGS, LANES))
        decay = [jnp.exp(-row(rates, r, lanes)) for r in range(order)]
        scale = [row(coef, r, lanes) for r in range(order)]
        states = []
        for r in range(order):
            ahead = jnp.exp(row(rates, r, lanes) * (segment * (-1.0 * seg_len)))
            before = jnp.broadcast_to(start_by_place[now_at, r : r + 1, lanes], (SEGS, LANES))
            states.append(prefix[group, r] + ahead * before)

        def step(i, carry, group=group, query_taps=query_taps, gain=gain, decay=decay, scale=scale):
            q1, q2, *states = carry
            q0 = strided(query_pos, group, TOP + i, pitch)
            now = gated[group, pl.ds(pl.multiple_of(i * SEGS, SEGS), SEGS), :]
            states = [d * h + now for d, h in zip(decay, states)]
            sums = [s * h for s, h in zip(scale, states)] + [gain * now]
            while len(sums) > 1:
                sums = [a + b for a, b in zip(sums[::2], sums[1::2])] + sums[len(sums) // 2 * 2 :]
            query_now = query_taps[0] * q0 + query_taps[1] * q1 + query_taps[2] * q2
            result_pos[group, pl.ds(TOP + i, SEGS, stride=pitch), :] = query_now * sums[0]
            return (q0, q1, *states)

        start = (
            strided(query_pos, group, TOP - 2, pitch),
            strided(query_pos, group, TOP - 3, pitch),
        ) + tuple(states)
        lax.fori_loop(0, seg_len, step, start, unroll=8)
        for s in range(SEGS):
            part = result_pos[group, TOP + s * pitch : TOP + s * pitch + seg_len, :]
            hidden[s * seg_len : (s + 1) * seg_len, lanes] = part.astype(hidden.dtype)


def hidden_rows(place, streams, halo, short, rates, coef, skip, gated, prefix, starts, part):
    _, rows, chans = streams.shape
    order = rates.shape[0]
    share = len(starts)
    wide = chans // share
    groups = wide // LANES
    seg_len = rows // SEGS
    steps = max(1, share // 2)
    first = part * steps
    pos_rows = TOP + SEGS * (seg_len + 1)
    return pl.pallas_call(
        functools.partial(hidden_body, seg_len=seg_len, order=order, share=share, first=first),
        grid_spec=pltpu.PrefetchScalarGridSpec(
            num_scalar_prefetch=1,
            grid=(steps,),
            in_specs=[
                pl.BlockSpec((1, rows, wide), lambda g, place: (0, 0, first + g)),
                pl.BlockSpec((3, 2, wide), lambda g, place: (0, 0, first + g)),
                pl.BlockSpec((3, 3, wide), lambda g, place: (0, 0, first + g)),
                pl.BlockSpec((order, wide), lambda g, place: (0, first + g)),
                pl.BlockSpec((order, wide), lambda g, place: (0, first + g)),
                pl.BlockSpec((1, wide), lambda g, place: (0, first + g)),
                pl.BlockSpec((groups, rows, LANES), lambda g, place: (first + g, 0, 0)),
                pl.BlockSpec((groups, order, SEGS, LANES), lambda g, place: (first + g, 0, 0, 0)),
            ]
            + [pl.BlockSpec((order, wide), lambda g, place: (0, 0))] * share,
            out_specs=pl.BlockSpec((rows, wide), lambda g, place: (0, g)),
            scratch_shapes=[
                pltpu.VMEM((groups, pos_rows, LANES), jnp.float32),
                pltpu.VMEM((groups, pos_rows, LANES), jnp.float32),
                pltpu.VMEM((share, order, wide), jnp.float32),
            ],
        ),
        out_shape=jax.ShapeDtypeStruct((rows, steps * wide), jnp.bfloat16),
        compiler_params=pltpu.CompilerParams(vmem_limit_bytes=VMEM_LIMIT),
        cost_estimate=estimate(rows * chans * 40, rows * chans * 5),
        name="hidden_rows",
    )(place, streams, halo, short, rates, coef, skip, gated, prefix, *starts)


def project_body(pick, *refs, rows_in, slots):
    out = refs[-1]
    at = 0
    rows = []
    for count in rows_in:
        rows.append(refs[at : at + count])
        at += count
    width = out.shape[1] // len(slots)

    def times(columns, slot):
        top = 0
        for part in rows:
            total = 0.0
            start = 0
            for piece in part:
                size, depth = piece.shape
                total += jnp.dot(
                    piece[...], columns[start : start + depth, :], preferred_element_type=jnp.float32
                )
                start += depth
            out[top : top + size, slot * width : (slot + 1) * width] = total.astype(out.dtype)
            top += size

    for slot, count in enumerate(slots):
        given = refs[at : at + count]
        at += count
        if count == 1:
            times(given[0], slot)
            continue

        @pl.when(pick[0] == 1)
        def _(given=given, slot=slot):
            times(given[0], slot)

        @pl.when(pick[0] != 1)
        def _(given=given, slot=slot):
            times(given[1], slot)


def project(pick, rows, slots):
    flat = [piece for part in rows for piece in part] + [block for slot in slots for block in slot]
    count = sum(part[0].shape[0] for part in rows)
    depth, width = slots[0][0].shape
    return pl.pallas_call(
        functools.partial(
            project_body, rows_in=tuple(map(len, rows)), slots=tuple(map(len, slots))
        ),
        in_specs=[pl.BlockSpec(memory_space=pltpu.SMEM)]
        + [pl.BlockSpec(memory_space=pltpu.VMEM)] * len(flat),
        out_specs=pl.BlockSpec(memory_space=pltpu.VMEM),
        out_shape=jax.ShapeDtypeStruct((count, len(slots) * width), jnp.bfloat16),
        compiler_params=pltpu.CompilerParams(vmem_limit_bytes=VMEM_LIMIT),
        cost_estimate=estimate(
            2 * count * depth * len(slots) * width,
            2 * (count * depth + len(slots) * width * (depth + count)),
        ),
        name="project",
    )(pick, *flat)


def assemble_body(place, *refs, kinds):
    out = refs[-1]
    width = refs[0].shape[1]
    at = 0
    for j, count in enumerate(kinds):
        given = refs[at : at + count]
        at += count
        column = pl.multiple_of((place[0] ^ j) * width, LANES)
        if count == 1:
            out[:, pl.ds(column, width)] = given[0][...]
            continue

        @pl.when(place[2] == 1)
        def _(given=given, column=column):
            out[:, pl.ds(column, width)] = given[0][...]

        @pl.when(place[2] != 1)
        def _(given=given, column=column):
            out[:, pl.ds(column, width)] = given[1][...]


def assemble(place, parts, blocks, width):
    flat = [piece for part in parts for piece in part]
    share = len(parts)
    rows = flat[0].shape[0]
    return pl.pallas_call(
        functools.partial(assemble_body, kinds=tuple(map(len, parts))),
        grid_spec=pltpu.PrefetchScalarGridSpec(
            num_scalar_prefetch=1,
            grid=(blocks,),
            in_specs=[pl.BlockSpec((rows, width), lambda b, place: (0, b ^ place[1]))] * len(flat),
            out_specs=pl.BlockSpec((rows, share * width), lambda b, place: (0, b)),
        ),
        out_shape=jax.ShapeDtypeStruct((rows, share * blocks * width), jnp.bfloat16),
        compiler_params=pltpu.CompilerParams(vmem_limit_bytes=VMEM_LIMIT),
        cost_estimate=estimate(0, 4 * rows * share * blocks * width),
        name="assemble",
    )(place, *flat)


def after(value, *others):
    return lax.optimization_barrier((value, *others))[0]


def send_planes(value, group, moves):
    pairs = [(a * group + e, b * group + e) for a, b in moves for e in range(group)]
    return lax.ppermute(value, "ctx", pairs)


def send_cores(value, count, moves):
    pairs = [(p * 2 + s, q * 2 + t) for at in range(count) for (p, s), (q, t) in moves(at)]
    return lax.ppermute(value, ("ctx", "tp"), pairs)


def plane_rows(hidden, count, group):
    if group != 4:
        return [hidden] + [[send_xor(part, count, group, j) for part in hidden] for j in range(1, group)]
    first, second = hidden
    first_1 = send_xor(first, count, group, 1)
    first_2 = send_xor(first, count, group, 2)
    second_2 = send_xor(second, count, group, 2)
    second_1 = send_xor(second, count, group, 1)
    first_3 = send_xor(first_1, count, group, 2)
    second_3 = send_xor(second_2, count, group, 1)
    return [[first, second], [first_1, second_1], [first_2, second_2], [first_3, second_3]]


def add_up_body(pick, a, b, *outs):
    size, width = outs[0].shape

    def add(columns):
        for j, out in enumerate(outs):
            rows = slice(j * size, (j + 1) * size)
            both = a[rows, columns].astype(jnp.float32) + b[rows, columns].astype(jnp.float32)
            out[...] = both.astype(out.dtype)

    if a.shape[1] == width:
        add(slice(None))
        return

    @pl.when(pick[0] == 1)
    def _():
        add(slice(0, width))

    @pl.when(pick[0] != 1)
    def _():
        add(slice(width, None))


def add_up(pick, a, b, parts, width):
    size = a.shape[0] // parts
    held = pl.BlockSpec(memory_space=pltpu.VMEM)
    return pl.pallas_call(
        add_up_body,
        in_specs=[pl.BlockSpec(memory_space=pltpu.SMEM), held, held],
        out_specs=[held] * parts,
        out_shape=[jax.ShapeDtypeStruct((size, width), a.dtype)] * parts,
        compiler_params=pltpu.CompilerParams(vmem_limit_bytes=VMEM_LIMIT),
        cost_estimate=estimate(parts * size * width, 6 * parts * size * width),
        name="add_up",
    )(pick, a, b)


def project_4x4(out_weight, halo, states, hidden, count):
    group = 4
    here = lax.axis_index("ctx")
    half = lax.axis_index("tp")
    plane = here // group
    swap = [(0, 1), (1, 0), (2, 3), (3, 2)]
    inner = [(1, 2), (2, 1)]
    outward = [(1, 0), (2, 3)]
    own = after(out_weight, halo)
    by_1 = send_planes(own, group, swap)
    by_3_inner = send_planes(own, group, inner)
    by_2_inner = send_planes(after(by_1, states, by_3_inner), group, inner)
    by_2_outer = send_planes(after(by_3_inner, states), group, outward)
    rows = plane_rows(hidden, count, group)
    by_3_outer = send_planes(after(by_2_inner, by_2_outer, rows[1][0], rows[2][0], hidden[1]), group, outward)
    near = [[own], [by_1]]
    far = [[by_2_inner, by_2_outer], [by_3_inner, by_3_outer]]

    pick = jnp.full((1,), (plane == 1) | (plane == 2), jnp.int32)
    size = hidden[0].shape[0]
    wide = 2 * out_weight.shape[1]

    def keeper(p):
        return p // group // 2

    def to_near(p):
        return [((p, 1 - keeper(p)), (p, keeper(p)))]

    def to_far(p):
        return [((p, keeper(p)), (p, 1 - keeper(p)))]

    def near_plane(j):
        return lambda p: [((p, keeper(p)), (p ^ j, keeper(p)))]

    def far_plane(j):
        return lambda p: [((p, 1 - keeper(p)), (p ^ j, 1 - keeper(p)))]

    keeps_near = half == plane // 2
    keeps = jnp.full((1,), keeps_near, jnp.int32)
    near_part = project(pick, rows[:3], near)
    near_sum = add_up(keeps, near_part, send_cores(near_part, count, to_near), 3, wide)
    near_got = [near_sum[0]] + [send_cores(near_sum[j], count, near_plane(j)) for j in (1, 2)]
    far_rows = [[after(piece, *near_sum) for piece in part] for part in rows[:3]]
    far_part = project(pick, far_rows, far)
    far_sum = add_up(keeps, far_part, send_cores(far_part, count, to_far), 3, wide)
    far_got = [far_sum[0]] + [send_cores(far_sum[j], count, far_plane(j)) for j in (1, 2)]
    last_rows = [[after(piece, *near_sum) for piece in part] for part in rows[3:]]
    last_part = project(pick, last_rows, near + far)
    last_taken = lax.ppermute(last_part, "tp", [(0, 1), (1, 0)])
    last_sum = add_up(keeps, last_part, last_taken, 1, wide)
    last_got = send_xor(last_sum[0], count, group, 3)
    parts = [[a, b] for a, b in zip(near_got, far_got)] + [[last_got]]
    place = jnp.stack([here % group, plane % 2, keeps_near.astype(here.dtype)]).astype(jnp.int32)
    return assemble(place, parts, 2, out_weight.shape[1])


def project_any(out_weight, halo, states, hidden, count):
    halves = lax.axis_size("tp")
    group = split_of(count)
    outer = count // group
    plane = lax.axis_index("ctx") // group
    size = hidden[0].shape[0]
    depth, width = out_weight.shape
    below, above = [after(out_weight, halo)], [after(out_weight, halo)]
    for k in range(1, outer):
        down, up = below[-1], above[-1]
        if k == 2:
            down, up = after(down, states), after(up, states)
        below.append(send_along(down, count, group, 1, k - 1))
        above.append(send_along(up, count, group, -1, k - 1))
    line = below[:0:-1] + above
    cols = lax.dynamic_slice_in_dim(jnp.stack(line), outer - 1 - plane, outer, 0)
    cols = jnp.moveaxis(cols, 0, 1).reshape(depth, outer * width)
    rows = plane_rows(hidden, count, group)
    held = jnp.concatenate([jnp.concatenate(part, axis=1) for part in rows], axis=0)
    partial = jnp.dot(held, cols, preferred_element_type=jnp.float32).astype(jnp.bfloat16)
    mixed = lax.psum_scatter(partial, "tp", scatter_dimension=1, tiled=True)
    mixed = jnp.split(mixed, group)
    mixed = [mixed[0]] + [send_xor(mixed[j], count, group, j) for j in range(1, group)]
    blocks = outer // halves
    stacked = jnp.stack(mixed).reshape(group, size, blocks, width)
    by_place = jnp.take(stacked, jnp.arange(group) ^ (lax.axis_index("ctx") % group), axis=0)
    return jnp.moveaxis(by_place, 0, 2).reshape(size, blocks * group * width)


def per_device(projected, short_filter, residues, rates, skip_gain, out_weight):
    count = lax.axis_size("ctx")
    halves = lax.axis_size("tp")
    here = lax.axis_index("ctx")
    rows, _, chans = projected.shape

    streams = jnp.transpose(projected, (1, 0, 2))
    tail = streams[:, -2:]
    halo = lax.ppermute(tail, "ctx", [(p, p + 1) for p in range(count - 1)])
    rates_t = rates.T
    coef_t = (residues * jnp.sqrt(-jnp.expm1(-2.0 * rates))).T

    share = min(split_of(count), chans // LANES, 4)
    lines = count // share
    spot = jnp.full((1,), here % share, jnp.int32)
    *ends, gated, prefix = local_scan(spot, streams, halo, short_filter, rates_t, share)
    ends = [ends[0]] + [send_xor(ends[j], count, share, j) for j in range(1, share)]
    whole, befores = plane_scan(spot, rates_t, ends, rows)
    arrived = [send_along(whole, count, share, k) for k in range(1, lines)]
    starts = line_scan(spot, rates_t, befores, arrived, rows)
    states = starts[0]
    starts = [starts[0]] + [send_xor(starts[j], count, share, j) for j in range(1, share)]
    hidden = [
        hidden_rows(
            spot, streams, halo, short_filter, rates_t, coef_t, skip_gain[None], gated, prefix, starts, part
        )
        for part in range(2)
    ]
    if count == 16 and halves == 2 and out_weight.shape[1] % LANES == 0:
        return project_4x4(out_weight, halo, states, hidden, count)
    return project_any(out_weight, halo, states, hidden, count)


def solution(mesh):
    return jax.shard_map(
        per_device,
        mesh=mesh,
        in_specs=(
            P("ctx", None, "tp"),
            P(None, None, "tp"),
            P("tp", None),
            P("tp", None),
            P("tp"),
            P("tp", "ctx"),
        ),
        out_specs=P("ctx", "tp"),
        check_vma=False,
    )
```

```python
import functools

import jax
import jax.numpy as jnp
from jax import lax
from jax.experimental import pallas as pl
from jax.experimental.pallas import tpu as pltpu
from jax.sharding import PartitionSpec as P

LANES = 128
SEGS = 8
TOP = 8
SPOT, MIDDLE, KEEPS, ODD = range(4)
VMEM_LIMIT = 16 * 1024 * 1024
SMALL_LIMIT = 4 * 1024 * 1024
WHOLE_LIMIT = 50 * 1024 * 1024


def split_of(count):
    inner = 1
    while (2 * inner) ** 2 <= count and count % (2 * inner) == 0:
        inner *= 2
    return inner


def send_xor(value, count, group, step):
    pairs = [(p, p - p % group + ((p % group) ^ step)) for p in range(count)]
    return lax.ppermute(value, "ctx", pairs)


def send_along(value, count, group, steps, first=0):
    outer = count // group
    pairs = []
    for z in range(outer):
        if not 0 <= z + steps < outer:
            continue
        if (steps > 0 and z < first) or (steps < 0 and z > outer - 1 - first):
            continue
        pairs += [(z * group + e, (z + steps) * group + e) for e in range(group)]
    return lax.ppermute(value, "ctx", pairs)


def estimate(flops, bytes_accessed, transcendentals=0):
    return pl.CostEstimate(flops=flops, bytes_accessed=bytes_accessed, transcendentals=transcendentals)


def row(ref, r, lanes):
    return jnp.broadcast_to(ref[r : r + 1, lanes], (SEGS, LANES))


def lay_segments(dst, stream, halo, seg_len, lanes, group):
    pitch = seg_len + 1
    for s in range(SEGS):
        part = stream[0, s * seg_len : (s + 1) * seg_len, lanes].astype(jnp.float32)
        dst[group, TOP + s * pitch : TOP + s * pitch + seg_len, :] = part
    dst[group, TOP - 3 : TOP - 1, :] = halo


def taps(short, stream, lanes):
    return [jnp.broadcast_to(short[i, stream : stream + 1, lanes], (SEGS, LANES)) for i in range(3)]


def strided(ref, group, start, pitch):
    return ref[group, pl.ds(start, SEGS, stride=pitch), :]


def local_scan_body(place, streams, halo, short_all, rates_all, *rest, seg_len, order, share):
    ends = rest[:share]
    gated, prefix = rest[share : share + 2]
    key_pos, value_pos, end_now, held, short_held, rates_held, held_sem, small_sem = rest[share + 2 :]
    now_at = pl.program_id(0)
    wide = end_now.shape[1]
    small = [
        pltpu.make_async_copy(short_all, short_held, small_sem.at[0]),
        pltpu.make_async_copy(rates_all, rates_held, small_sem.at[1]),
    ]

    def stream_copy(at):
        columns = pl.ds(at * wide, wide)
        return pltpu.make_async_copy(
            streams.at[pl.ds(1, 2), :, columns], held.at[:, :, columns], held_sem.at[at]
        )

    @pl.when(now_at == 0)
    def _():
        stream_copy(0).start()
        for copy in small:
            copy.start()
        for at in range(1, share):
            stream_copy(at).start()
        for copy in small:
            copy.wait()

    for at in range(share):

        @pl.when(now_at == at)
        def _(at=at):
            stream_copy(at).wait()

    columns = pl.ds(pl.multiple_of(now_at * wide, LANES), wide)
    key = held.at[pl.ds(0, 1), :, columns]
    value = held.at[pl.ds(1, 1), :, columns]
    short = short_held.at[:, :, columns]
    rates = rates_held.at[:, columns]
    pitch = seg_len + 1
    groups = gated.shape[0]
    segment = lax.broadcasted_iota(jnp.int32, (SEGS, LANES), 0)
    for group in range(groups):
        lanes = slice(group * LANES, (group + 1) * LANES)
        lay_segments(key_pos, key, halo[1, :, lanes].astype(jnp.float32), seg_len, lanes, group)
        lay_segments(value_pos, value, halo[2, :, lanes].astype(jnp.float32), seg_len, lanes, group)

    for group in range(groups):
        lanes = slice(group * LANES, (group + 1) * LANES)
        key_taps = taps(short, 1, lanes)
        value_taps = taps(short, 2, lanes)
        decay = [jnp.exp(-row(rates, r, lanes)) for r in range(order)]

        def step(i, carry, group=group, key_taps=key_taps, value_taps=value_taps, decay=decay):
            k1, k2, v1, v2, *states = carry
            k0 = strided(key_pos, group, TOP + i, pitch)
            v0 = strided(value_pos, group, TOP + i, pitch)
            key_now = key_taps[0] * k0 + key_taps[1] * k1 + key_taps[2] * k2
            value_now = value_taps[0] * v0 + value_taps[1] * v1 + value_taps[2] * v2
            now = key_now * value_now
            gated[group, pl.ds(pl.multiple_of(i * SEGS, SEGS), SEGS), :] = now
            states = [d * h + now for d, h in zip(decay, states)]
            return (k0, k1, v0, v1, *states)

        zero = jnp.zeros((SEGS, LANES), jnp.float32)
        start = (
            strided(key_pos, group, TOP - 2, pitch),
            strided(key_pos, group, TOP - 3, pitch),
            strided(value_pos, group, TOP - 2, pitch),
            strided(value_pos, group, TOP - 3, pitch),
        ) + (zero,) * order
        states = lax.fori_loop(0, seg_len, step, start, unroll=8)[4:]
        for r in range(order):
            rate = row(rates, r, lanes)
            scan = states[r]
            for d in (1, 2, 4):
                moved = jnp.where(segment >= d, pltpu.roll(scan, d, 0), 0.0)
                scan = scan + jnp.exp(rate * (-1.0 * d * seg_len)) * moved
            prefix[group, r] = jnp.where(segment >= 1, pltpu.roll(scan, 1, 0), 0.0)
            end_now[r : r + 1, lanes] = scan[SEGS - 1 :, :]

    for j in range(share):

        @pl.when((pl.program_id(0) ^ place[SPOT]) == j)
        def _(j=j):
            ends[j][...] = end_now[...]


def local_scan(place, streams, halo, short, rates, share):
    _, rows, chans = streams.shape
    order = rates.shape[0]
    wide = chans // share
    groups = wide // LANES
    seg_len = rows // SEGS
    pos_rows = TOP + SEGS * (seg_len + 1)
    end_shape = jax.ShapeDtypeStruct((order, wide), jnp.float32)
    return pl.pallas_call(
        functools.partial(local_scan_body, seg_len=seg_len, order=order, share=share),
        grid_spec=pltpu.PrefetchScalarGridSpec(
            num_scalar_prefetch=1,
            grid=(share,),
            in_specs=[
                pl.BlockSpec(memory_space=pltpu.HBM),
                pl.BlockSpec((3, 2, wide), lambda g, place: (0, 0, g)),
                pl.BlockSpec(memory_space=pltpu.HBM),
                pl.BlockSpec(memory_space=pltpu.HBM),
            ],
            out_specs=[pl.BlockSpec((order, wide), lambda g, place: (0, 0))] * share
            + [
                pl.BlockSpec((groups, rows, LANES), lambda g, place: (g, 0, 0)),
                pl.BlockSpec((groups, order, SEGS, LANES), lambda g, place: (g, 0, 0, 0)),
            ],
            scratch_shapes=[
                pltpu.VMEM((groups, pos_rows, LANES), jnp.float32),
                pltpu.VMEM((groups, pos_rows, LANES), jnp.float32),
                pltpu.VMEM((order, wide), jnp.float32),
                pltpu.VMEM((2, rows, chans), streams.dtype),
                pltpu.VMEM(short.shape, jnp.float32),
                pltpu.VMEM(rates.shape, jnp.float32),
                pltpu.SemaphoreType.DMA((share,)),
                pltpu.SemaphoreType.DMA((2,)),
            ],
        ),
        out_shape=[end_shape] * share
        + [
            jax.ShapeDtypeStruct((chans // LANES, rows, LANES), jnp.float32),
            jax.ShapeDtypeStruct((chans // LANES, order, SEGS, LANES), jnp.float32),
        ],
        compiler_params=pltpu.CompilerParams(vmem_limit_bytes=WHOLE_LIMIT),
        cost_estimate=estimate(rows * chans * 50, rows * chans * 10),
        name="local_scan",
    )(place, streams, halo, short, rates)


def plane_scan_body(place, rates, *rest, share, rows):
    ends = rest[:share]
    whole = rest[share]
    befores = rest[share + 1 : 2 * share + 1]
    by_place, before_place = rest[2 * share + 1 :]
    here = place[SPOT]
    for j in range(share):
        by_place[here ^ j] = ends[j][...]
    decay = jnp.exp(rates[...] * (-1.0 * rows))
    state = jnp.zeros(rates.shape, jnp.float32)
    for at in range(share):
        before_place[at] = state
        state = decay * state + by_place[at]
    whole[...] = state
    for j in range(share):
        befores[j][...] = before_place[here ^ j]


def plane_scan(place, rates, ends, rows):
    share = len(ends)
    order, wide = ends[0].shape
    block = pl.BlockSpec((order, wide), lambda g, place: (0, 0))
    shape = jax.ShapeDtypeStruct((order, wide), jnp.float32)
    got = pl.pallas_call(
        functools.partial(plane_scan_body, share=share, rows=rows),
        grid_spec=pltpu.PrefetchScalarGridSpec(
            num_scalar_prefetch=1,
            grid=(1,),
            in_specs=[pl.BlockSpec((order, wide), lambda g, place: (0, place[SPOT]))] + [block] * share,
            out_specs=[block] * (share + 1),
            scratch_shapes=[pltpu.VMEM((share, order, wide), jnp.float32)] * 2,
        ),
        out_shape=[shape] * (share + 1),
        compiler_params=pltpu.CompilerParams(vmem_limit_bytes=SMALL_LIMIT),
        cost_estimate=estimate(order * wide * 20, order * wide * 36),
        name="plane_scan",
    )(place, rates, *ends)
    return got[0], got[1:]


def line_scan_body(place, rates, *rest, share, rows, lines):
    befores = rest[:share]
    arrived = rest[share : share + lines]
    outs = rest[share + lines :]
    here = place[SPOT]
    rate = rates[...] * (-1.0 * rows)
    decay = jnp.exp(rate * share)
    state = jnp.zeros(rate.shape, jnp.float32)
    for k in reversed(range(lines)):
        state = decay * state + arrived[k][...]
    for j in range(share):
        ahead = (here ^ j).astype(jnp.float32)
        outs[j][...] = befores[j][...] + jnp.exp(rate * ahead) * state


def line_scan(place, rates, befores, arrived, rows):
    share, lines = len(befores), len(arrived)
    order, wide = befores[0].shape
    block = pl.BlockSpec((order, wide), lambda g, place: (0, 0))
    return pl.pallas_call(
        functools.partial(line_scan_body, share=share, rows=rows, lines=lines),
        grid_spec=pltpu.PrefetchScalarGridSpec(
            num_scalar_prefetch=1,
            grid=(1,),
            in_specs=[pl.BlockSpec((order, wide), lambda g, place: (0, place[SPOT]))]
            + [block] * (share + lines),
            out_specs=[block] * share,
        ),
        out_shape=[jax.ShapeDtypeStruct((order, wide), jnp.float32)] * share,
        compiler_params=pltpu.CompilerParams(vmem_limit_bytes=SMALL_LIMIT),
        cost_estimate=estimate(order * wide * 20, order * wide * 36),
        name="line_scan",
    )(place, rates, *befores, *arrived)


def hidden_body(place, query, halo, short, rates, coef, skip, gated, prefix, *rest, seg_len, order, share, first):
    starts = rest[:share]
    hidden = rest[share]
    query_pos, result_pos, start_by_place = rest[share + 1 :]
    pitch = seg_len + 1
    groups = gated.shape[0]
    now_at = pl.program_id(0) + first
    segment = lax.broadcasted_iota(jnp.int32, (SEGS, LANES), 0).astype(jnp.float32)

    @pl.when(pl.program_id(0) == 0)
    def _():
        for j in range(share):
            start_by_place[place[SPOT] ^ j] = starts[j][...]

    for group in range(groups):
        lanes = slice(group * LANES, (group + 1) * LANES)
        lay_segments(query_pos, query, halo[0, :, lanes].astype(jnp.float32), seg_len, lanes, group)

    for group in range(groups):
        lanes = slice(group * LANES, (group + 1) * LANES)
        query_taps = taps(short, 0, lanes)
        gain = jnp.broadcast_to(skip[0:1, lanes], (SEGS, LANES))
        decay = [jnp.exp(-row(rates, r, lanes)) for r in range(order)]
        scale = [row(coef, r, lanes) for r in range(order)]
        states = []
        for r in range(order):
            ahead = jnp.exp(row(rates, r, lanes) * (segment * (-1.0 * seg_len)))
            before = jnp.broadcast_to(start_by_place[now_at, r : r + 1, lanes], (SEGS, LANES))
            states.append(prefix[group, r] + ahead * before)

        def step(i, carry, group=group, query_taps=query_taps, gain=gain, decay=decay, scale=scale):
            q1, q2, *states = carry
            q0 = strided(query_pos, group, TOP + i, pitch)
            now = gated[group, pl.ds(pl.multiple_of(i * SEGS, SEGS), SEGS), :]
            states = [d * h + now for d, h in zip(decay, states)]
            sums = [s * h for s, h in zip(scale, states)] + [gain * now]
            while len(sums) > 1:
                sums = [a + b for a, b in zip(sums[::2], sums[1::2])] + sums[len(sums) // 2 * 2 :]
            query_now = query_taps[0] * q0 + query_taps[1] * q1 + query_taps[2] * q2
            result_pos[group, pl.ds(TOP + i, SEGS, stride=pitch), :] = query_now * sums[0]
            return (q0, q1, *states)

        start = (
            strided(query_pos, group, TOP - 2, pitch),
            strided(query_pos, group, TOP - 3, pitch),
        ) + tuple(states)
        lax.fori_loop(0, seg_len, step, start, unroll=8)
        for s in range(SEGS):
            part = result_pos[group, TOP + s * pitch : TOP + s * pitch + seg_len, :]
            hidden[s * seg_len : (s + 1) * seg_len, lanes] = part.astype(hidden.dtype)


def hidden_rows(place, streams, halo, short, rates, coef, skip, gated, prefix, starts, part):
    _, rows, chans = streams.shape
    order = rates.shape[0]
    share = len(starts)
    wide = chans // share
    groups = wide // LANES
    seg_len = rows // SEGS
    steps = max(1, share // 2)
    first = part * steps
    pos_rows = TOP + SEGS * (seg_len + 1)
    return pl.pallas_call(
        functools.partial(hidden_body, seg_len=seg_len, order=order, share=share, first=first),
        grid_spec=pltpu.PrefetchScalarGridSpec(
            num_scalar_prefetch=1,
            grid=(steps,),
            in_specs=[
                pl.BlockSpec((1, rows, wide), lambda g, place: (0, 0, first + g)),
                pl.BlockSpec((3, 2, wide), lambda g, place: (0, 0, first + g)),
                pl.BlockSpec((3, 3, wide), lambda g, place: (0, 0, first + g)),
                pl.BlockSpec((order, wide), lambda g, place: (0, first + g)),
                pl.BlockSpec((order, wide), lambda g, place: (0, first + g)),
                pl.BlockSpec((1, wide), lambda g, place: (0, first + g)),
                pl.BlockSpec((groups, rows, LANES), lambda g, place: (first + g, 0, 0)),
                pl.BlockSpec((groups, order, SEGS, LANES), lambda g, place: (first + g, 0, 0, 0)),
            ]
            + [pl.BlockSpec((order, wide), lambda g, place: (0, 0))] * share,
            out_specs=pl.BlockSpec((rows, wide), lambda g, place: (0, g)),
            scratch_shapes=[
                pltpu.VMEM((groups, pos_rows, LANES), jnp.float32),
                pltpu.VMEM((groups, pos_rows, LANES), jnp.float32),
                pltpu.VMEM((share, order, wide), jnp.float32),
            ],
        ),
        out_shape=jax.ShapeDtypeStruct((rows, steps * wide), jnp.bfloat16),
        compiler_params=pltpu.CompilerParams(vmem_limit_bytes=VMEM_LIMIT),
        cost_estimate=estimate(rows * chans * 40, rows * chans * 5),
        name="hidden_rows",
    )(place, streams, halo, short, rates, coef, skip, gated, prefix, *starts)


def project_body(place, *refs, rows_in, slots, sizes, made):
    outs = refs[-len(sizes) :]
    at = 0
    rows = []
    for count in rows_in:
        rows.append(refs[at : at + count])
        at += count
    width = outs[0].shape[1] // sizes[0]
    targets = [(out, e * width) for out, size in zip(outs, sizes) for e in range(size)]

    def times(columns, target):
        out, column = target
        top = 0
        for part in rows:
            total = 0.0
            start = 0
            for piece in part:
                size, depth = piece.shape
                total += jnp.dot(
                    piece[...], columns[start : start + depth, :], preferred_element_type=jnp.float32
                )
                start += depth
            out[top : top + size, column : column + width] = total.astype(out.dtype)
            top += size

    if made:
        outs[0][:, :width] = refs[-len(sizes) - 1][...]
        targets = targets[1:]
    for target, count in zip(targets, slots):
        given = refs[at : at + count]
        at += count
        if count == 1:
            times(given[0], target)
            continue

        @pl.when(place[MIDDLE] == 1)
        def _(given=given, target=target):
            times(given[0], target)

        @pl.when(place[MIDDLE] != 1)
        def _(given=given, target=target):
            times(given[1], target)


def project(place, rows, slots, sizes, made=None):
    flat = [piece for part in rows for piece in part] + [block for slot in slots for block in slot]
    flat += [] if made is None else [made]
    count = sum(part[0].shape[0] for part in rows)
    depth, width = slots[0][0].shape
    held = pl.BlockSpec(memory_space=pltpu.VMEM)
    return pl.pallas_call(
        functools.partial(
            project_body,
            rows_in=tuple(map(len, rows)),
            slots=tuple(map(len, slots)),
            sizes=sizes,
            made=made is not None,
        ),
        in_specs=[pl.BlockSpec(memory_space=pltpu.SMEM)] + [held] * len(flat),
        out_specs=[held] * len(sizes),
        out_shape=[jax.ShapeDtypeStruct((count, size * width), jnp.bfloat16) for size in sizes],
        compiler_params=pltpu.CompilerParams(vmem_limit_bytes=VMEM_LIMIT),
        cost_estimate=estimate(
            2 * count * depth * len(slots) * width,
            2 * (count * depth + len(slots) * width * (depth + count)),
        ),
        name="project",
    )(place, *flat)


def assemble_body(place, *refs, kinds):
    out = refs[-1]
    width = refs[0].shape[1]
    at = 0
    for j, count in enumerate(kinds):
        given = refs[at : at + count]
        at += count
        column = pl.multiple_of((place[SPOT] ^ j) * width, LANES)
        if count == 1:
            out[:, pl.ds(column, width)] = given[0][...]
            continue

        @pl.when(place[KEEPS] == 1)
        def _(given=given, column=column):
            out[:, pl.ds(column, width)] = given[0][...]

        @pl.when(place[KEEPS] != 1)
        def _(given=given, column=column):
            out[:, pl.ds(column, width)] = given[1][...]


def assemble(place, parts, blocks, width):
    flat = [piece for part in parts for piece in part]
    share = len(parts)
    rows = flat[0].shape[0]
    return pl.pallas_call(
        functools.partial(assemble_body, kinds=tuple(map(len, parts))),
        grid_spec=pltpu.PrefetchScalarGridSpec(
            num_scalar_prefetch=1,
            grid=(blocks,),
            in_specs=[pl.BlockSpec((rows, width), lambda b, place: (0, b ^ place[ODD]))] * len(flat),
            out_specs=pl.BlockSpec((rows, share * width), lambda b, place: (0, b)),
        ),
        out_shape=jax.ShapeDtypeStruct((rows, share * blocks * width), jnp.bfloat16),
        compiler_params=pltpu.CompilerParams(vmem_limit_bytes=VMEM_LIMIT),
        cost_estimate=estimate(0, 4 * rows * share * blocks * width),
        name="assemble",
    )(place, *flat)


def after(value, *others):
    return lax.optimization_barrier((value, *others))[0]


def send_planes(value, group, moves):
    pairs = [(a * group + e, b * group + e) for a, b in moves for e in range(group)]
    return lax.ppermute(value, "ctx", pairs)


def send_cores(value, count, moves):
    pairs = [(p * 2 + s, q * 2 + t) for at in range(count) for (p, s), (q, t) in moves(at)]
    return lax.ppermute(value, ("ctx", "tp"), pairs)


def plane_rows(hidden, count, group):
    if group != 4:
        return [hidden] + [[send_xor(part, count, group, j) for part in hidden] for j in range(1, group)]
    first, second = hidden
    first_1 = send_xor(first, count, group, 1)
    first_2 = send_xor(first, count, group, 2)
    second_2 = send_xor(second, count, group, 2)
    second_1 = send_xor(second, count, group, 1)
    first_3 = send_xor(first_1, count, group, 2)
    second_3 = send_xor(second_2, count, group, 1)
    return [[first, second], [first_1, second_1], [first_2, second_2], [first_3, second_3]]


def add_up_body(place, a, b, *outs):
    size, width = outs[0].shape

    def add(columns):
        for j, out in enumerate(outs):
            rows = slice(j * size, (j + 1) * size)
            both = a[rows, columns].astype(jnp.float32) + b[rows, columns].astype(jnp.float32)
            out[...] = both.astype(out.dtype)

    if a.shape[1] == width:
        add(slice(None))
        return

    @pl.when(place[KEEPS] == 1)
    def _():
        add(slice(0, width))

    @pl.when(place[KEEPS] != 1)
    def _():
        add(slice(width, None))


def add_up(place, a, b, parts, width):
    size = a.shape[0] // parts
    held = pl.BlockSpec(memory_space=pltpu.VMEM)
    return pl.pallas_call(
        add_up_body,
        in_specs=[pl.BlockSpec(memory_space=pltpu.SMEM), held, held],
        out_specs=[held] * parts,
        out_shape=[jax.ShapeDtypeStruct((size, width), a.dtype)] * parts,
        compiler_params=pltpu.CompilerParams(vmem_limit_bytes=VMEM_LIMIT),
        cost_estimate=estimate(parts * size * width, 6 * parts * size * width),
        name="add_up",
    )(place, a, b)


def project_4x4(place, out_weight, halo, states, hidden, count):
    group = 4
    swap = [(0, 1), (1, 0), (2, 3), (3, 2)]
    inner = [(1, 2), (2, 1)]
    outward = [(1, 0), (2, 3)]
    own = after(out_weight, halo)
    by_1 = send_planes(own, group, swap)
    by_3_inner = send_planes(own, group, inner)
    by_2_inner = send_planes(after(by_1, states, by_3_inner), group, inner)
    by_2_outer = send_planes(after(by_3_inner, states), group, outward)
    rows = plane_rows(hidden, count, group)
    by_3_outer = send_planes(after(by_2_inner, by_2_outer, rows[1][0], rows[2][0], hidden[1]), group, outward)
    near = [[own], [by_1]]
    far = [[by_2_inner, by_2_outer], [by_3_inner, by_3_outer]]

    size = hidden[0].shape[0]
    wide = 2 * out_weight.shape[1]

    def keeper(p):
        return p // group // 2

    def to_near(p):
        return [((p, 1 - keeper(p)), (p, keeper(p)))]

    def to_far(p):
        return [((p, keeper(p)), (p, 1 - keeper(p)))]

    def near_plane(j):
        return lambda p: [((p, keeper(p)), (p ^ j, keeper(p)))]

    def far_plane(j):
        return lambda p: [((p, 1 - keeper(p)), (p ^ j, 1 - keeper(p)))]

    near_part, far_first = project(place, rows[:3], near + far[:1], (2, 1))
    near_taken = send_cores(near_part, count, to_near)
    last_rows = [[piece for piece in part] for part in rows[3:]]
    last_part = project(place, last_rows, near + far, (4,))[0]
    last_taken = lax.ppermute(last_part, "tp", [(0, 1), (1, 0)])
    last_sum = add_up(place, last_part, last_taken, 1, wide)
    last_got = send_xor(last_sum[0], count, group, 3)
    far_rows = [[after(piece, last_part) for piece in part] for part in rows[:3]]
    far_part = project(place, far_rows, far[1:], (2,), far_first)[0]
    near_sum = add_up(place, after(near_part, last_sum[0]), near_taken, 3, wide)
    near_got = [near_sum[0]] + [send_cores(near_sum[j], count, near_plane(j)) for j in (1, 2)]
    far_sum = add_up(place, far_part, send_cores(far_part, count, to_far), 3, wide)
    far_got = [far_sum[0]] + [send_cores(far_sum[j], count, far_plane(j)) for j in (1, 2)]
    parts = [[a, b] for a, b in zip(near_got, far_got)] + [[last_got]]
    return assemble(place, parts, 2, out_weight.shape[1])


def project_any(out_weight, halo, states, hidden, count):
    halves = lax.axis_size("tp")
    group = split_of(count)
    outer = count // group
    plane = lax.axis_index("ctx") // group
    size = hidden[0].shape[0]
    depth, width = out_weight.shape
    below, above = [after(out_weight, halo)], [after(out_weight, halo)]
    for k in range(1, outer):
        down, up = below[-1], above[-1]
        if k == 2:
            down, up = after(down, states), after(up, states)
        below.append(send_along(down, count, group, 1, k - 1))
        above.append(send_along(up, count, group, -1, k - 1))
    line = below[:0:-1] + above
    cols = lax.dynamic_slice_in_dim(jnp.stack(line), outer - 1 - plane, outer, 0)
    cols = jnp.moveaxis(cols, 0, 1).reshape(depth, outer * width)
    rows = plane_rows(hidden, count, group)
    held = jnp.concatenate([jnp.concatenate(part, axis=1) for part in rows], axis=0)
    partial = jnp.dot(held, cols, preferred_element_type=jnp.float32).astype(jnp.bfloat16)
    mixed = lax.psum_scatter(partial, "tp", scatter_dimension=1, tiled=True)
    mixed = jnp.split(mixed, group)
    mixed = [mixed[0]] + [send_xor(mixed[j], count, group, j) for j in range(1, group)]
    blocks = outer // halves
    stacked = jnp.stack(mixed).reshape(group, size, blocks, width)
    by_place = jnp.take(stacked, jnp.arange(group) ^ (lax.axis_index("ctx") % group), axis=0)
    return jnp.moveaxis(by_place, 0, 2).reshape(size, blocks * group * width)


def per_device(projected, short_filter, residues, rates, skip_gain, out_weight):
    count = lax.axis_size("ctx")
    halves = lax.axis_size("tp")
    here = lax.axis_index("ctx")
    rows, _, chans = projected.shape

    streams = jnp.transpose(projected, (1, 0, 2))
    tail = streams[:, -2:]
    halo = lax.ppermute(tail, "ctx", [(p, p + 1) for p in range(count - 1)])
    rates_t = rates.T
    coef_t = (residues * jnp.sqrt(-jnp.expm1(-2.0 * rates))).T

    share = min(split_of(count), chans // LANES, 4)
    lines = count // share
    plane = here // share
    keeps = lax.axis_index("tp") == plane // 2
    place = jnp.stack([here % share, (plane == 1) | (plane == 2), keeps, plane % 2]).astype(jnp.int32)
    *ends, gated, prefix = local_scan(place, streams, halo, short_filter, rates_t, share)
    ends = [ends[0]] + [send_xor(ends[j], count, share, j) for j in range(1, share)]
    whole, befores = plane_scan(place, rates_t, ends, rows)
    arrived = [send_along(whole, count, share, k) for k in range(1, lines)]
    starts = line_scan(place, rates_t, befores, arrived, rows)
    states = starts[0]
    starts = [starts[0]] + [send_xor(starts[j], count, share, j) for j in range(1, share)]
    hidden = [
        hidden_rows(
            place, streams, halo, short_filter, rates_t, coef_t, skip_gain[None], gated, prefix, starts, part
        )
        for part in range(2)
    ]
    if count == 16 and halves == 2 and out_weight.shape[1] % LANES == 0:
        return project_4x4(place, out_weight, halo, states, hidden, count)
    return project_any(out_weight, halo, states, hidden, count)


def solution(mesh):
    return jax.shard_map(
        per_device,
        mesh=mesh,
        in_specs=(
            P("ctx", None, "tp"),
            P(None, None, "tp"),
            P("tp", None),
            P("tp", None),
            P("tp"),
            P("tp", "ctx"),
        ),
        out_specs=P("ctx", "tp"),
        check_vma=False,
    )
```

```python
import functools

import jax
import jax.numpy as jnp
from jax import lax
from jax.experimental import pallas as pl
from jax.experimental.pallas import tpu as pltpu
from jax.sharding import PartitionSpec as P

LANES = 128
SEGS = 8
TOP = 8
SPOT, MIDDLE, KEEPS, ODD = range(4)
VMEM_LIMIT = 16 * 1024 * 1024
SMALL_LIMIT = 4 * 1024 * 1024
WHOLE_LIMIT = 50 * 1024 * 1024


def split_of(count):
    inner = 1
    while (2 * inner) ** 2 <= count and count % (2 * inner) == 0:
        inner *= 2
    return inner


def send_xor(value, count, group, step):
    pairs = [(p, p - p % group + ((p % group) ^ step)) for p in range(count)]
    return lax.ppermute(value, "ctx", pairs)


def send_along(value, count, group, steps, first=0):
    outer = count // group
    pairs = []
    for z in range(outer):
        if not 0 <= z + steps < outer:
            continue
        if (steps > 0 and z < first) or (steps < 0 and z > outer - 1 - first):
            continue
        pairs += [(z * group + e, (z + steps) * group + e) for e in range(group)]
    return lax.ppermute(value, "ctx", pairs)


def estimate(flops, bytes_accessed, transcendentals=0):
    return pl.CostEstimate(flops=flops, bytes_accessed=bytes_accessed, transcendentals=transcendentals)


def row(ref, r, lanes):
    return jnp.broadcast_to(ref[r : r + 1, lanes], (SEGS, LANES))


def lay_segments(dst, stream, halo, seg_len, lanes, group):
    pitch = seg_len + 1
    for s in range(SEGS):
        part = stream[0, s * seg_len : (s + 1) * seg_len, lanes].astype(jnp.float32)
        dst[group, TOP + s * pitch : TOP + s * pitch + seg_len, :] = part
    dst[group, TOP - 3 : TOP - 1, :] = jnp.zeros((2, LANES), jnp.float32) if halo is None else halo


def taps(short, stream, lanes):
    return [jnp.broadcast_to(short[i, stream : stream + 1, lanes], (SEGS, LANES)) for i in range(3)]


def strided(ref, group, start, pitch):
    return ref[group, pl.ds(start, SEGS, stride=pitch), :]


LAST, FIRST = 6, 4


def first_gated(short, first, last):
    products = []
    for b, stream in enumerate((1, 2)):
        tap = [short[i, stream : stream + 1, :] for i in range(3)]
        now_0, now_1 = first[2 * b : 2 * b + 1], first[2 * b + 1 : 2 * b + 2]
        old_2, old_1 = last[2 * stream : 2 * stream + 1], last[2 * stream + 1 : 2 * stream + 2]
        products.append(
            (
                tap[0] * now_0 + tap[1] * old_1 + tap[2] * old_2,
                tap[0] * now_1 + tap[1] * now_0 + tap[2] * old_1,
            )
        )
    return products[0][0] * products[1][0], products[0][1] * products[1][1]


def end_share(short, rates, first, last, rows):
    gated_0, gated_1 = first_gated(short, first, last)
    return jnp.exp(rates * (1.0 - rows)) * gated_0 + jnp.exp(rates * (2.0 - rows)) * gated_1


def local_scan_body(place, streams, short_all, rates_all, *rest, seg_len, order, share):
    ends = rest[:share]
    gated, prefix = rest[share : share + 2]
    key_pos, value_pos, end_now, held, query_held, short_held, rates_held, held_sem, small_sem = rest[share + 2 :]
    now_at = pl.program_id(0)
    wide = end_now.shape[1]
    small = [
        pltpu.make_async_copy(short_all, short_held, small_sem.at[0]),
        pltpu.make_async_copy(rates_all, rates_held, small_sem.at[1]),
        pltpu.make_async_copy(
            streams.at[0, pl.ds(seg_len * SEGS - 16, 16), :], query_held, small_sem.at[2]
        ),
    ]

    def stream_copy(at):
        columns = pl.ds(at * wide, wide)
        return pltpu.make_async_copy(
            streams.at[pl.ds(1, 2), :, columns], held.at[:, :, columns], held_sem.at[at]
        )

    @pl.when(now_at == 0)
    def _():
        stream_copy(0).start()
        for copy in small:
            copy.start()
        for at in range(1, share):
            stream_copy(at).start()
        for copy in small:
            copy.wait()

    for at in range(share):

        @pl.when(now_at == at)
        def _(at=at):
            stream_copy(at).wait()

    columns = pl.ds(pl.multiple_of(now_at * wide, LANES), wide)
    key = held.at[pl.ds(0, 1), :, columns]
    value = held.at[pl.ds(1, 1), :, columns]
    short = short_held.at[:, :, columns]
    rates = rates_held.at[:, columns]
    pitch = seg_len + 1
    groups = gated.shape[0]
    segment = lax.broadcasted_iota(jnp.int32, (SEGS, LANES), 0)
    for group in range(groups):
        lanes = slice(group * LANES, (group + 1) * LANES)
        lay_segments(key_pos, key, None, seg_len, lanes, group)
        lay_segments(value_pos, value, None, seg_len, lanes, group)
    bottom = seg_len * SEGS - 2
    end_now[order : order + 2, :] = query_held[14:16, columns].astype(jnp.float32)
    for b, stream in enumerate((key, value)):
        at = order + 2 + 2 * b
        end_now[at : at + 2, :] = stream[0, bottom : bottom + 2, :].astype(jnp.float32)
        at = order + LAST + 2 * b
        end_now[at : at + 2, :] = stream[0, 0:2, :].astype(jnp.float32)

    for group in range(groups):
        lanes = slice(group * LANES, (group + 1) * LANES)
        key_taps = taps(short, 1, lanes)
        value_taps = taps(short, 2, lanes)
        decay = [jnp.exp(-row(rates, r, lanes)) for r in range(order)]

        def step(i, carry, early=False, group=group, key_taps=key_taps, value_taps=value_taps, decay=decay):
            k1, k2, v1, v2, *states = carry
            k0 = strided(key_pos, group, TOP + i, pitch)
            v0 = strided(value_pos, group, TOP + i, pitch)
            key_now = key_taps[0] * k0 + key_taps[1] * k1 + key_taps[2] * k2
            value_now = value_taps[0] * v0 + value_taps[1] * v1 + value_taps[2] * v2
            now = key_now * value_now
            if early:
                now = jnp.where(segment >= 1, now, 0.0)
            gated[group, pl.ds(pl.multiple_of(i * SEGS, SEGS), SEGS), :] = now
            states = [d * h + now for d, h in zip(decay, states)]
            return (k0, k1, v0, v1, *states)

        zero = jnp.zeros((SEGS, LANES), jnp.float32)
        start = (
            strided(key_pos, group, TOP - 2, pitch),
            strided(key_pos, group, TOP - 3, pitch),
            strided(value_pos, group, TOP - 2, pitch),
            strided(value_pos, group, TOP - 3, pitch),
        ) + (zero,) * order
        start = step(1, step(0, start, True), True)
        states = lax.fori_loop(2, seg_len, step, start, unroll=6)[4:]
        for r in range(order):
            rate = row(rates, r, lanes)
            scan = states[r]
            for d in (1, 2, 4):
                moved = jnp.where(segment >= d, pltpu.roll(scan, d, 0), 0.0)
                scan = scan + jnp.exp(rate * (-1.0 * d * seg_len)) * moved
            prefix[group, r] = jnp.where(segment >= 1, pltpu.roll(scan, 1, 0), 0.0)
            end_now[r : r + 1, lanes] = scan[SEGS - 1 :, :]

    for j in range(share):

        @pl.when((pl.program_id(0) ^ place[SPOT]) == j)
        def _(j=j):
            ends[j][...] = end_now[...]


def local_scan(place, streams, short, rates, share):
    _, rows, chans = streams.shape
    order = rates.shape[0]
    wide = chans // share
    groups = wide // LANES
    seg_len = rows // SEGS
    pos_rows = TOP + SEGS * (seg_len + 1)
    end_shape = jax.ShapeDtypeStruct((order + LAST + FIRST, wide), jnp.float32)
    return pl.pallas_call(
        functools.partial(local_scan_body, seg_len=seg_len, order=order, share=share),
        grid_spec=pltpu.PrefetchScalarGridSpec(
            num_scalar_prefetch=1,
            grid=(share,),
            in_specs=[
                pl.BlockSpec(memory_space=pltpu.HBM),
                pl.BlockSpec(memory_space=pltpu.HBM),
                pl.BlockSpec(memory_space=pltpu.HBM),
            ],
            out_specs=[pl.BlockSpec((order + LAST + FIRST, wide), lambda g, place: (0, 0))] * share
            + [
                pl.BlockSpec((groups, rows, LANES), lambda g, place: (g, 0, 0)),
                pl.BlockSpec((groups, order, SEGS, LANES), lambda g, place: (g, 0, 0, 0)),
            ],
            scratch_shapes=[
                pltpu.VMEM((groups, pos_rows, LANES), jnp.float32),
                pltpu.VMEM((groups, pos_rows, LANES), jnp.float32),
                pltpu.VMEM((order + LAST + FIRST, wide), jnp.float32),
                pltpu.VMEM((2, rows, chans), streams.dtype),
                pltpu.VMEM((16, chans), streams.dtype),
                pltpu.VMEM(short.shape, jnp.float32),
                pltpu.VMEM(rates.shape, jnp.float32),
                pltpu.SemaphoreType.DMA((share,)),
                pltpu.SemaphoreType.DMA((3,)),
            ],
        ),
        out_shape=[end_shape] * share
        + [
            jax.ShapeDtypeStruct((chans // LANES, rows, LANES), jnp.float32),
            jax.ShapeDtypeStruct((chans // LANES, order, SEGS, LANES), jnp.float32),
        ],
        compiler_params=pltpu.CompilerParams(vmem_limit_bytes=WHOLE_LIMIT),
        cost_estimate=estimate(rows * chans * 50, rows * chans * 10),
        name="local_scan",
    )(place, streams, short, rates)


def plane_scan_body(place, rates, short, *rest, share, rows):
    ends = rest[:share]
    whole = rest[share]
    befores = rest[share + 1 : 2 * share + 1]
    by_place, before_place = rest[2 * share + 1 :]
    order = rates.shape[0]
    here = place[SPOT]
    for j in range(share):
        by_place[here ^ j] = ends[j][...]
    rate = rates[...]
    decay = jnp.exp(rate * (-1.0 * rows))
    state = jnp.zeros(rate.shape, jnp.float32)
    for at in range(share):
        before_place[at, :order] = state
        state = decay * state + by_place[at, :order]
        if at > 0:
            last = by_place[at - 1, order : order + LAST]
            before_place[at, order:] = last
            state += end_share(short, rate, by_place[at, order + LAST :], last, rows)
    before_place[0, order:] = jnp.zeros((LAST, rate.shape[1]), jnp.float32)
    whole[:order] = state
    whole[order : order + LAST] = by_place[share - 1, order : order + LAST]
    whole[order + LAST :] = by_place[0, order + LAST :]
    for j in range(share):
        befores[j][...] = before_place[here ^ j]


def plane_scan(place, rates, short, ends, rows):
    share = len(ends)
    order = rates.shape[0]
    wide = ends[0].shape[1]
    block = pl.BlockSpec((order + LAST, wide), lambda g, place: (0, 0))
    edged = pl.BlockSpec((order + LAST + FIRST, wide), lambda g, place: (0, 0))
    shape = jax.ShapeDtypeStruct((order + LAST, wide), jnp.float32)
    got = pl.pallas_call(
        functools.partial(plane_scan_body, share=share, rows=rows),
        grid_spec=pltpu.PrefetchScalarGridSpec(
            num_scalar_prefetch=1,
            grid=(1,),
            in_specs=[
                pl.BlockSpec((order, wide), lambda g, place: (0, place[SPOT])),
                pl.BlockSpec((3, 3, wide), lambda g, place: (0, 0, place[SPOT])),
            ]
            + [edged] * share,
            out_specs=[edged] + [block] * share,
            scratch_shapes=[
                pltpu.VMEM((share, order + LAST + FIRST, wide), jnp.float32),
                pltpu.VMEM((share, order + LAST, wide), jnp.float32),
            ],
        ),
        out_shape=[jax.ShapeDtypeStruct((order + LAST + FIRST, wide), jnp.float32)] + [shape] * share,
        compiler_params=pltpu.CompilerParams(vmem_limit_bytes=SMALL_LIMIT),
        cost_estimate=estimate(order * wide * 20, order * wide * 36),
        name="plane_scan",
    )(place, rates, short, *ends)
    return got[0], got[1:]


def line_scan_body(place, rates, short, whole, *rest, share, rows, lines):
    befores = rest[:share]
    arrived = rest[share : share + lines]
    outs = rest[share + lines :]
    order = rates.shape[0]
    here = place[SPOT]
    rate = rates[...]
    planes = (whole,) + tuple(arrived)

    def last_rows(k):
        if k < lines:
            return planes[k + 1][order : order + LAST]
        return jnp.zeros((LAST, rate.shape[1]), jnp.float32)

    def first_share(k):
        return end_share(short, rate, planes[k][order + LAST :], last_rows(k), rows)

    state = jnp.zeros(rate.shape, jnp.float32)
    decay = jnp.exp(rate * (-1.0 * rows * share))
    later = jnp.exp(rate * (-1.0 * rows * (share - 1)))
    for k in reversed(range(1, lines + 1)):
        state = decay * state + planes[k][:order] + later * first_share(k)
    own = first_share(0)
    for j in range(share):
        at = (here ^ j).astype(jnp.float32)
        inside = jnp.minimum(at, 1.0)
        past = inside * jnp.exp(rate * (jnp.maximum(at - 1.0, 0.0) * (-1.0 * rows)))
        before = befores[j][:order]
        outs[j][:order] = before + jnp.exp(rate * (at * (-1.0 * rows))) * state + past * own
        outs[j][order:] = befores[j][order:] + (1.0 - inside) * last_rows(0)


def line_scan(place, rates, short, whole, befores, arrived, rows):
    share, lines = len(befores), len(arrived)
    order, wide = rates.shape[0], whole.shape[1]
    block = pl.BlockSpec((order + LAST, wide), lambda g, place: (0, 0))
    edged = pl.BlockSpec((order + LAST + FIRST, wide), lambda g, place: (0, 0))
    return pl.pallas_call(
        functools.partial(line_scan_body, share=share, rows=rows, lines=lines),
        grid_spec=pltpu.PrefetchScalarGridSpec(
            num_scalar_prefetch=1,
            grid=(1,),
            in_specs=[
                pl.BlockSpec((order, wide), lambda g, place: (0, place[SPOT])),
                pl.BlockSpec((3, 3, wide), lambda g, place: (0, 0, place[SPOT])),
                edged,
            ]
            + [block] * share
            + [edged] * lines,
            out_specs=[block] * share,
        ),
        out_shape=[jax.ShapeDtypeStruct((order + LAST, wide), jnp.float32)] * share,
        compiler_params=pltpu.CompilerParams(vmem_limit_bytes=SMALL_LIMIT),
        cost_estimate=estimate(order * wide * 20, order * wide * 36),
        name="line_scan",
    )(place, rates, short, whole, *befores, *arrived)


def hidden_body(place, query, top, short, rates, coef, skip, gated, prefix, *rest, seg_len, order, share, first):
    starts = rest[:share]
    hidden = rest[share]
    query_pos, result_pos, start_by_place = rest[share + 1 :]
    pitch = seg_len + 1
    groups = gated.shape[0]
    now_at = pl.program_id(0) + first
    segment = lax.broadcasted_iota(jnp.int32, (SEGS, LANES), 0).astype(jnp.float32)

    @pl.when(pl.program_id(0) == 0)
    def _():
        for j in range(share):
            start_by_place[place[SPOT] ^ j] = starts[j][...]

    for group in range(groups):
        lanes = slice(group * LANES, (group + 1) * LANES)
        ending = start_by_place[now_at, order : order + 2, lanes]
        lay_segments(query_pos, query, ending, seg_len, lanes, group)

    for group in range(groups):
        lanes = slice(group * LANES, (group + 1) * LANES)
        query_taps = taps(short, 0, lanes)
        gain = jnp.broadcast_to(skip[0:1, lanes], (SEGS, LANES))
        decay = [jnp.exp(-row(rates, r, lanes)) for r in range(order)]
        scale = [row(coef, r, lanes) for r in range(order)]
        first = jnp.concatenate([top[b, 0:2, lanes] for b in (1, 2)], axis=0).astype(jnp.float32)
        last = start_by_place[now_at, order:, lanes]
        early = [
            jnp.broadcast_to(value, (SEGS, LANES))
            for value in first_gated(short.at[:, :, lanes], first, last)
        ]
        states = []
        for r in range(order):
            rate = row(rates, r, lanes)
            ahead = jnp.exp(rate * (segment * (-1.0 * seg_len)))
            before = jnp.broadcast_to(start_by_place[now_at, r : r + 1, lanes], (SEGS, LANES))
            grown = jnp.exp(rate)
            before += jnp.where(segment >= 1.0, grown * (early[0] + grown * early[1]), 0.0)
            states.append(prefix[group, r] + ahead * before)

        def step(
            i, carry, late=None, group=group, query_taps=query_taps, gain=gain, decay=decay, scale=scale
        ):
            q1, q2, *states = carry
            q0 = strided(query_pos, group, TOP + i, pitch)
            now = gated[group, pl.ds(pl.multiple_of(i * SEGS, SEGS), SEGS), :]
            if late is not None:
                now = jnp.where(segment >= 1.0, now, late)
            states = [d * h + now for d, h in zip(decay, states)]
            sums = [s * h for s, h in zip(scale, states)] + [gain * now]
            while len(sums) > 1:
                sums = [a + b for a, b in zip(sums[::2], sums[1::2])] + sums[len(sums) // 2 * 2 :]
            query_now = query_taps[0] * q0 + query_taps[1] * q1 + query_taps[2] * q2
            result_pos[group, pl.ds(TOP + i, SEGS, stride=pitch), :] = query_now * sums[0]
            return (q0, q1, *states)

        start = (
            strided(query_pos, group, TOP - 2, pitch),
            strided(query_pos, group, TOP - 3, pitch),
        ) + tuple(states)
        start = step(1, step(0, start, early[0]), early[1])
        lax.fori_loop(2, seg_len, step, start, unroll=6)
        for s in range(SEGS):
            part = result_pos[group, TOP + s * pitch : TOP + s * pitch + seg_len, :]
            hidden[s * seg_len : (s + 1) * seg_len, lanes] = part.astype(hidden.dtype)


def hidden_rows(place, streams, short, rates, coef, skip, gated, prefix, starts, part):
    _, rows, chans = streams.shape
    order = rates.shape[0]
    share = len(starts)
    wide = chans // share
    groups = wide // LANES
    seg_len = rows // SEGS
    steps = max(1, share // 2)
    first = part * steps
    pos_rows = TOP + SEGS * (seg_len + 1)
    return pl.pallas_call(
        functools.partial(hidden_body, seg_len=seg_len, order=order, share=share, first=first),
        grid_spec=pltpu.PrefetchScalarGridSpec(
            num_scalar_prefetch=1,
            grid=(steps,),
            in_specs=[
                pl.BlockSpec((1, rows, wide), lambda g, place: (0, 0, first + g)),
                pl.BlockSpec((3, 16, wide), lambda g, place: (0, 0, first + g)),
                pl.BlockSpec((3, 3, wide), lambda g, place: (0, 0, first + g)),
                pl.BlockSpec((order, wide), lambda g, place: (0, first + g)),
                pl.BlockSpec((order, wide), lambda g, place: (0, first + g)),
                pl.BlockSpec((1, wide), lambda g, place: (0, first + g)),
                pl.BlockSpec((groups, rows, LANES), lambda g, place: (first + g, 0, 0)),
                pl.BlockSpec((groups, order, SEGS, LANES), lambda g, place: (first + g, 0, 0, 0)),
            ]
            + [pl.BlockSpec((order + LAST, wide), lambda g, place: (0, 0))] * share,
            out_specs=pl.BlockSpec((rows, wide), lambda g, place: (0, g)),
            scratch_shapes=[
                pltpu.VMEM((groups, pos_rows, LANES), jnp.float32),
                pltpu.VMEM((groups, pos_rows, LANES), jnp.float32),
                pltpu.VMEM((share, order + LAST, wide), jnp.float32),
            ],
        ),
        out_shape=jax.ShapeDtypeStruct((rows, steps * wide), jnp.bfloat16),
        compiler_params=pltpu.CompilerParams(vmem_limit_bytes=VMEM_LIMIT),
        cost_estimate=estimate(rows * chans * 40, rows * chans * 5),
        name="hidden_rows",
    )(place, streams, streams, short, rates, coef, skip, gated, prefix, *starts)


def project_body(place, *refs, rows_in, slots, sizes, made):
    outs = refs[-len(sizes) :]
    at = 0
    rows = []
    for count in rows_in:
        rows.append(refs[at : at + count])
        at += count
    width = outs[0].shape[1] // sizes[0]
    targets = [(out, e * width) for out, size in zip(outs, sizes) for e in range(size)]

    def times(columns, target):
        out, column = target
        top = 0
        for part in rows:
            total = 0.0
            start = 0
            for piece in part:
                size, depth = piece.shape
                total += jnp.dot(
                    piece[...], columns[start : start + depth, :], preferred_element_type=jnp.float32
                )
                start += depth
            out[top : top + size, column : column + width] = total.astype(out.dtype)
            top += size

    if made:
        outs[0][:, :width] = refs[-len(sizes) - 1][...]
        targets = targets[1:]
    for target, count in zip(targets, slots):
        given = refs[at : at + count]
        at += count
        if count == 1:
            times(given[0], target)
            continue

        @pl.when(place[MIDDLE] == 1)
        def _(given=given, target=target):
            times(given[0], target)

        @pl.when(place[MIDDLE] != 1)
        def _(given=given, target=target):
            times(given[1], target)


def project(place, rows, slots, sizes, made=None):
    flat = [piece for part in rows for piece in part] + [block for slot in slots for block in slot]
    flat += [] if made is None else [made]
    count = sum(part[0].shape[0] for part in rows)
    depth, width = slots[0][0].shape
    held = pl.BlockSpec(memory_space=pltpu.VMEM)
    return pl.pallas_call(
        functools.partial(
            project_body,
            rows_in=tuple(map(len, rows)),
            slots=tuple(map(len, slots)),
            sizes=sizes,
            made=made is not None,
        ),
        in_specs=[pl.BlockSpec(memory_space=pltpu.SMEM)] + [held] * len(flat),
        out_specs=[held] * len(sizes),
        out_shape=[jax.ShapeDtypeStruct((count, size * width), jnp.bfloat16) for size in sizes],
        compiler_params=pltpu.CompilerParams(vmem_limit_bytes=VMEM_LIMIT),
        cost_estimate=estimate(
            2 * count * depth * len(slots) * width,
            2 * (count * depth + len(slots) * width * (depth + count)),
        ),
        name="project",
    )(place, *flat)


def assemble_body(place, *refs):
    parts, out = refs[:-1], refs[-1]
    width = parts[0].shape[1]
    for j, part in enumerate(parts):
        column = pl.multiple_of((place[SPOT] ^ j) * width, LANES)
        out[:, pl.ds(column, width)] = part[...]


def assemble(place, parts, blocks, width):
    share = len(parts)
    rows = parts[0].shape[0]
    return pl.pallas_call(
        assemble_body,
        grid_spec=pltpu.PrefetchScalarGridSpec(
            num_scalar_prefetch=1,
            grid=(blocks,),
            in_specs=[pl.BlockSpec((rows, width), lambda b, place: (0, b ^ place[ODD]))] * share,
            out_specs=pl.BlockSpec((rows, share * width), lambda b, place: (0, b)),
        ),
        out_shape=jax.ShapeDtypeStruct((rows, share * blocks * width), jnp.bfloat16),
        compiler_params=pltpu.CompilerParams(vmem_limit_bytes=VMEM_LIMIT),
        cost_estimate=estimate(0, 4 * rows * share * blocks * width),
        name="assemble",
    )(place, *parts)


def after(value, *others):
    return lax.optimization_barrier((value, *others))[0]


def send_planes(value, group, moves):
    pairs = [(a * group + e, b * group + e) for a, b in moves for e in range(group)]
    return lax.ppermute(value, "ctx", pairs)


def send_cores(value, count, moves):
    pairs = [(p * 2 + s, q * 2 + t) for at in range(count) for (p, s), (q, t) in moves(at)]
    return lax.ppermute(value, ("ctx", "tp"), pairs)


def plane_rows(hidden, count, group):
    if group != 4:
        return [hidden] + [[send_xor(part, count, group, j) for part in hidden] for j in range(1, group)]
    first, second = hidden
    first_1 = send_xor(first, count, group, 1)
    first_2 = send_xor(first, count, group, 2)
    second_2 = send_xor(second, count, group, 2)
    second_1 = send_xor(second, count, group, 1)
    first_3 = send_xor(first_1, count, group, 2)
    second_3 = send_xor(second_2, count, group, 1)
    return [[first, second], [first_1, second_1], [first_2, second_2], [first_3, second_3]]


def add_up_body(place, *refs, pairs):
    outs = refs[2 * pairs :]
    size, width = outs[0].shape

    def add(pair, columns):
        a, b = refs[2 * pair : 2 * pair + 2]
        for j, out in enumerate(outs):
            rows = slice(j * size, (j + 1) * size)
            both = a[rows, columns].astype(jnp.float32) + b[rows, columns].astype(jnp.float32)
            out[...] = both.astype(out.dtype)

    total = refs[0].shape[1]

    @pl.when(place[KEEPS] == 1)
    def _():
        add(0, slice(0, width))

    @pl.when(place[KEEPS] != 1)
    def _():
        add(pairs - 1, slice(total - width, total))


def add_up(place, shares, parts, width):
    size = shares[0][0].shape[0] // parts
    dtype = shares[0][0].dtype
    held = pl.BlockSpec(memory_space=pltpu.VMEM)
    flat = [share for pair in shares for share in pair]
    return pl.pallas_call(
        functools.partial(add_up_body, pairs=len(shares)),
        in_specs=[pl.BlockSpec(memory_space=pltpu.SMEM)] + [held] * len(flat),
        out_specs=[held] * parts,
        out_shape=[jax.ShapeDtypeStruct((size, width), dtype)] * parts,
        compiler_params=pltpu.CompilerParams(vmem_limit_bytes=VMEM_LIMIT),
        cost_estimate=estimate(parts * size * width, 6 * parts * size * width),
        name="add_up",
    )(place, *flat)


def project_4x4(place, out_weight, states, hidden, count):
    group = 4
    swap = [(0, 1), (1, 0), (2, 3), (3, 2)]
    inner = [(1, 2), (2, 1)]
    outward = [(1, 0), (2, 3)]
    own = out_weight
    by_1 = send_planes(own, group, swap)
    by_3_inner = send_planes(own, group, inner)
    by_2_inner = send_planes(after(by_1, states, by_3_inner), group, inner)
    by_2_outer = send_planes(after(by_3_inner, states), group, outward)
    rows = plane_rows(hidden, count, group)
    by_3_outer = send_planes(after(by_2_inner, by_2_outer, rows[1][0], rows[2][0], hidden[1]), group, outward)
    near = [[own], [by_1]]
    far = [[by_2_inner, by_2_outer], [by_3_inner, by_3_outer]]

    size = hidden[0].shape[0]
    wide = 2 * out_weight.shape[1]

    def keeper(p):
        return p // group // 2

    def to_near(p):
        return [((p, 1 - keeper(p)), (p, keeper(p)))]

    def to_far(p):
        return [((p, keeper(p)), (p, 1 - keeper(p)))]

    near_part, far_first = project(place, rows[:3], near + far[:1], (2, 1))
    near_taken = send_cores(near_part, count, to_near)
    last_rows = [[piece for piece in part] for part in rows[3:]]
    last_part = project(place, last_rows, near + far, (4,))[0]
    last_taken = lax.ppermute(last_part, "tp", [(0, 1), (1, 0)])
    last_sum = add_up(place, [(last_part, last_taken)], 1, wide)[0]
    far_rows = [[after(piece, last_part) for piece in part] for part in rows[:3]]
    far_part = project(place, far_rows, far[1:], (2,), far_first)[0]
    far_taken = send_cores(far_part, count, to_far)
    mixed = [*add_up(place, [(near_part, near_taken), (far_part, far_taken)], 3, wide), last_sum]
    mixed = [mixed[0]] + [send_xor(mixed[j], count, group, j) for j in range(1, group)]
    return assemble(place, mixed, 2, out_weight.shape[1])


def project_any(out_weight, states, hidden, count):
    halves = lax.axis_size("tp")
    group = split_of(count)
    outer = count // group
    plane = lax.axis_index("ctx") // group
    size = hidden[0].shape[0]
    depth, width = out_weight.shape
    below, above = [out_weight], [out_weight]
    for k in range(1, outer):
        down, up = below[-1], above[-1]
        if k == 2:
            down, up = after(down, states), after(up, states)
        below.append(send_along(down, count, group, 1, k - 1))
        above.append(send_along(up, count, group, -1, k - 1))
    line = below[:0:-1] + above
    cols = lax.dynamic_slice_in_dim(jnp.stack(line), outer - 1 - plane, outer, 0)
    cols = jnp.moveaxis(cols, 0, 1).reshape(depth, outer * width)
    rows = plane_rows(hidden, count, group)
    held = jnp.concatenate([jnp.concatenate(part, axis=1) for part in rows], axis=0)
    partial = jnp.dot(held, cols, preferred_element_type=jnp.float32).astype(jnp.bfloat16)
    mixed = lax.psum_scatter(partial, "tp", scatter_dimension=1, tiled=True)
    mixed = jnp.split(mixed, group)
    mixed = [mixed[0]] + [send_xor(mixed[j], count, group, j) for j in range(1, group)]
    blocks = outer // halves
    stacked = jnp.stack(mixed).reshape(group, size, blocks, width)
    by_place = jnp.take(stacked, jnp.arange(group) ^ (lax.axis_index("ctx") % group), axis=0)
    return jnp.moveaxis(by_place, 0, 2).reshape(size, blocks * group * width)


def per_device(projected, short_filter, residues, rates, skip_gain, out_weight):
    count = lax.axis_size("ctx")
    halves = lax.axis_size("tp")
    here = lax.axis_index("ctx")
    rows, _, chans = projected.shape

    streams = jnp.transpose(projected, (1, 0, 2))
    rates_t = rates.T
    coef_t = (residues * jnp.sqrt(-jnp.expm1(-2.0 * rates))).T

    share = min(split_of(count), chans // LANES, 4)
    lines = count // share
    plane = here // share
    keeps = lax.axis_index("tp") == plane // 2
    place = jnp.stack([here % share, (plane == 1) | (plane == 2), keeps, plane % 2]).astype(jnp.int32)
    *ends, gated, prefix = local_scan(place, streams, short_filter, rates_t, share)
    ends = [ends[0]] + [send_xor(ends[j], count, share, j) for j in range(1, share)]
    whole, befores = plane_scan(place, rates_t, short_filter, ends, rows)
    arrived = [send_along(whole, count, share, k) for k in range(1, lines)]
    starts = line_scan(place, rates_t, short_filter, whole, befores, arrived, rows)
    states = starts[0]
    starts = [starts[0]] + [send_xor(starts[j], count, share, j) for j in range(1, share)]
    hidden = [
        hidden_rows(
            place, streams, short_filter, rates_t, coef_t, skip_gain[None], gated, prefix, starts, part
        )
        for part in range(2)
    ]
    if count == 16 and halves == 2 and out_weight.shape[1] % LANES == 0:
        return project_4x4(place, out_weight, states, hidden, count)
    return project_any(out_weight, states, hidden, count)


def solution(mesh):
    return jax.shard_map(
        per_device,
        mesh=mesh,
        in_specs=(
            P("ctx", None, "tp"),
            P(None, None, "tp"),
            P("tp", None),
            P("tp", None),
            P("tp"),
            P("tp", "ctx"),
        ),
        out_specs=P("ctx", "tp"),
        check_vma=False,
    )
```

```python
import functools

import jax
import jax.numpy as jnp
from jax import lax
from jax.experimental import pallas as pl
from jax.experimental.pallas import tpu as pltpu
from jax.sharding import PartitionSpec as P

LANES = 128
SEGS = 8
TOP = 8
SPOT, MIDDLE, KEEPS, ODD = range(4)
VMEM_LIMIT = 16 * 1024 * 1024
SMALL_LIMIT = 4 * 1024 * 1024
WHOLE_LIMIT = 50 * 1024 * 1024


def split_of(count):
    inner = 1
    while (2 * inner) ** 2 <= count and count % (2 * inner) == 0:
        inner *= 2
    return inner


def send_xor(value, count, group, step):
    pairs = [(p, p - p % group + ((p % group) ^ step)) for p in range(count)]
    return lax.ppermute(value, "ctx", pairs)


def send_along(value, count, group, steps, first=0):
    outer = count // group
    pairs = []
    for z in range(outer):
        if not 0 <= z + steps < outer:
            continue
        if (steps > 0 and z < first) or (steps < 0 and z > outer - 1 - first):
            continue
        pairs += [(z * group + e, (z + steps) * group + e) for e in range(group)]
    return lax.ppermute(value, "ctx", pairs)


def estimate(flops, bytes_accessed, transcendentals=0):
    return pl.CostEstimate(flops=flops, bytes_accessed=bytes_accessed, transcendentals=transcendentals)


def row(ref, r, lanes):
    return jnp.broadcast_to(ref[r : r + 1, lanes], (SEGS, LANES))


def lay_segments(dst, stream, halo, seg_len, lanes, group):
    pitch = seg_len + 1
    for s in range(SEGS):
        part = stream[0, s * seg_len : (s + 1) * seg_len, lanes].astype(jnp.float32)
        dst[group, TOP + s * pitch : TOP + s * pitch + seg_len, :] = part
    dst[group, TOP - 3 : TOP - 1, :] = jnp.zeros((2, LANES), jnp.float32) if halo is None else halo


def taps(short, stream, lanes):
    return [jnp.broadcast_to(short[i, stream : stream + 1, lanes], (SEGS, LANES)) for i in range(3)]


def strided(ref, group, start, pitch):
    return ref[group, pl.ds(start, SEGS, stride=pitch), :]


LAST, FIRST = 6, 4


def first_gated(short, first, last):
    products = []
    for b, stream in enumerate((1, 2)):
        tap = [short[i, stream : stream + 1, :] for i in range(3)]
        now_0, now_1 = first[2 * b : 2 * b + 1], first[2 * b + 1 : 2 * b + 2]
        old_2, old_1 = last[2 * stream : 2 * stream + 1], last[2 * stream + 1 : 2 * stream + 2]
        products.append(
            (
                tap[0] * now_0 + tap[1] * old_1 + tap[2] * old_2,
                tap[0] * now_1 + tap[1] * now_0 + tap[2] * old_1,
            )
        )
    return products[0][0] * products[1][0], products[0][1] * products[1][1]


def end_share(short, rates, first, last, rows):
    gated_0, gated_1 = first_gated(short, first, last)
    return jnp.exp(rates * (1.0 - rows)) * gated_0 + jnp.exp(rates * (2.0 - rows)) * gated_1


def local_scan_body(place, streams, short_all, rates_all, *rest, seg_len, order, share):
    ends = rest[:share]
    gated, prefix = rest[share : share + 2]
    key_pos, value_pos, end_now, held, query_held, short_held, rates_held, held_sem, small_sem = rest[share + 2 :]
    now_at = pl.program_id(0)
    wide = end_now.shape[1]
    small = [
        pltpu.make_async_copy(short_all, short_held, small_sem.at[0]),
        pltpu.make_async_copy(rates_all, rates_held, small_sem.at[1]),
        pltpu.make_async_copy(
            streams.at[0, pl.ds(seg_len * SEGS - 16, 16), :], query_held, small_sem.at[2]
        ),
    ]

    def stream_copy(at):
        columns = pl.ds(at * wide, wide)
        return pltpu.make_async_copy(
            streams.at[pl.ds(1, 2), :, columns], held.at[:, :, columns], held_sem.at[at]
        )

    @pl.when(now_at == 0)
    def _():
        stream_copy(0).start()
        for copy in small:
            copy.start()
        for at in range(1, share):
            stream_copy(at).start()
        for copy in small:
            copy.wait()

    for at in range(share):

        @pl.when(now_at == at)
        def _(at=at):
            stream_copy(at).wait()

    columns = pl.ds(pl.multiple_of(now_at * wide, LANES), wide)
    key = held.at[pl.ds(0, 1), :, columns]
    value = held.at[pl.ds(1, 1), :, columns]
    short = short_held.at[:, :, columns]
    rates = rates_held.at[:, columns]
    pitch = seg_len + 1
    groups = gated.shape[0]
    segment = lax.broadcasted_iota(jnp.int32, (SEGS, LANES), 0)
    for group in range(groups):
        lanes = slice(group * LANES, (group + 1) * LANES)
        lay_segments(key_pos, key, None, seg_len, lanes, group)
        lay_segments(value_pos, value, None, seg_len, lanes, group)
    bottom = seg_len * SEGS - 2
    end_now[order : order + 2, :] = query_held[14:16, columns].astype(jnp.float32)
    for b, stream in enumerate((key, value)):
        at = order + 2 + 2 * b
        end_now[at : at + 2, :] = stream[0, bottom : bottom + 2, :].astype(jnp.float32)
        at = order + LAST + 2 * b
        end_now[at : at + 2, :] = stream[0, 0:2, :].astype(jnp.float32)

    for group in range(groups):
        lanes = slice(group * LANES, (group + 1) * LANES)
        key_taps = taps(short, 1, lanes)
        value_taps = taps(short, 2, lanes)
        decay = [jnp.exp(-row(rates, r, lanes)) for r in range(order)]

        def step(i, carry, early=False, group=group, key_taps=key_taps, value_taps=value_taps, decay=decay):
            k1, k2, v1, v2, *states = carry
            k0 = strided(key_pos, group, TOP + i, pitch)
            v0 = strided(value_pos, group, TOP + i, pitch)
            key_now = key_taps[0] * k0 + key_taps[1] * k1 + key_taps[2] * k2
            value_now = value_taps[0] * v0 + value_taps[1] * v1 + value_taps[2] * v2
            now = key_now * value_now
            if early:
                now = jnp.where(segment >= 1, now, 0.0)
            gated[group, pl.ds(pl.multiple_of(i * SEGS, SEGS), SEGS), :] = now
            states = [d * h + now for d, h in zip(decay, states)]
            return (k0, k1, v0, v1, *states)

        zero = jnp.zeros((SEGS, LANES), jnp.float32)
        start = (
            strided(key_pos, group, TOP - 2, pitch),
            strided(key_pos, group, TOP - 3, pitch),
            strided(value_pos, group, TOP - 2, pitch),
            strided(value_pos, group, TOP - 3, pitch),
        ) + (zero,) * order
        start = step(1, step(0, start, True), True)
        states = lax.fori_loop(2, seg_len, step, start, unroll=6)[4:]
        for r in range(order):
            rate = row(rates, r, lanes)
            scan = states[r]
            for d in (1, 2, 4):
                moved = jnp.where(segment >= d, pltpu.roll(scan, d, 0), 0.0)
                scan = scan + jnp.exp(rate * (-1.0 * d * seg_len)) * moved
            prefix[group, r] = jnp.where(segment >= 1, pltpu.roll(scan, 1, 0), 0.0)
            end_now[r : r + 1, lanes] = scan[SEGS - 1 :, :]

    for j in range(share):

        @pl.when((pl.program_id(0) ^ place[SPOT]) == j)
        def _(j=j):
            ends[j][...] = end_now[...]


def local_scan(place, streams, short, rates, share):
    _, rows, chans = streams.shape
    order = rates.shape[0]
    wide = chans // share
    groups = wide // LANES
    seg_len = rows // SEGS
    pos_rows = TOP + SEGS * (seg_len + 1)
    end_shape = jax.ShapeDtypeStruct((order + LAST + FIRST, wide), jnp.float32)
    return pl.pallas_call(
        functools.partial(local_scan_body, seg_len=seg_len, order=order, share=share),
        grid_spec=pltpu.PrefetchScalarGridSpec(
            num_scalar_prefetch=1,
            grid=(share,),
            in_specs=[
                pl.BlockSpec(memory_space=pltpu.HBM),
                pl.BlockSpec(memory_space=pltpu.HBM),
                pl.BlockSpec(memory_space=pltpu.HBM),
            ],
            out_specs=[pl.BlockSpec((order + LAST + FIRST, wide), lambda g, place: (0, 0))] * share
            + [
                pl.BlockSpec((groups, rows, LANES), lambda g, place: (g, 0, 0)),
                pl.BlockSpec((groups, order, SEGS, LANES), lambda g, place: (g, 0, 0, 0)),
            ],
            scratch_shapes=[
                pltpu.VMEM((groups, pos_rows, LANES), jnp.float32),
                pltpu.VMEM((groups, pos_rows, LANES), jnp.float32),
                pltpu.VMEM((order + LAST + FIRST, wide), jnp.float32),
                pltpu.VMEM((2, rows, chans), streams.dtype),
                pltpu.VMEM((16, chans), streams.dtype),
                pltpu.VMEM(short.shape, jnp.float32),
                pltpu.VMEM(rates.shape, jnp.float32),
                pltpu.SemaphoreType.DMA((share,)),
                pltpu.SemaphoreType.DMA((3,)),
            ],
        ),
        out_shape=[end_shape] * share
        + [
            jax.ShapeDtypeStruct((chans // LANES, rows, LANES), jnp.float32),
            jax.ShapeDtypeStruct((chans // LANES, order, SEGS, LANES), jnp.float32),
        ],
        compiler_params=pltpu.CompilerParams(vmem_limit_bytes=WHOLE_LIMIT),
        cost_estimate=estimate(rows * chans * 50, rows * chans * 10),
        name="local_scan",
    )(place, streams, short, rates)


def plane_scan_body(place, rates, short, *rest, share, rows):
    ends = rest[:share]
    whole = rest[share]
    befores = rest[share + 1 : 2 * share + 1]
    by_place, before_place = rest[2 * share + 1 :]
    order = rates.shape[0]
    here = place[SPOT]
    for j in range(share):
        by_place[here ^ j] = ends[j][...]
    rate = rates[...]
    decay = jnp.exp(rate * (-1.0 * rows))
    state = jnp.zeros(rate.shape, jnp.float32)
    for at in range(share):
        before_place[at, :order] = state
        state = decay * state + by_place[at, :order]
        if at > 0:
            last = by_place[at - 1, order : order + LAST]
            before_place[at, order:] = last
            state += end_share(short, rate, by_place[at, order + LAST :], last, rows)
    before_place[0, order:] = jnp.zeros((LAST, rate.shape[1]), jnp.float32)
    whole[:order] = state
    whole[order : order + LAST] = by_place[share - 1, order : order + LAST]
    whole[order + LAST :] = by_place[0, order + LAST :]
    for j in range(share):
        befores[j][...] = before_place[here ^ j]


def plane_scan(place, rates, short, ends, rows):
    share = len(ends)
    order = rates.shape[0]
    wide = ends[0].shape[1]
    block = pl.BlockSpec((order + LAST, wide), lambda g, place: (0, 0))
    edged = pl.BlockSpec((order + LAST + FIRST, wide), lambda g, place: (0, 0))
    shape = jax.ShapeDtypeStruct((order + LAST, wide), jnp.float32)
    got = pl.pallas_call(
        functools.partial(plane_scan_body, share=share, rows=rows),
        grid_spec=pltpu.PrefetchScalarGridSpec(
            num_scalar_prefetch=1,
            grid=(1,),
            in_specs=[
                pl.BlockSpec((order, wide), lambda g, place: (0, place[SPOT])),
                pl.BlockSpec((3, 3, wide), lambda g, place: (0, 0, place[SPOT])),
            ]
            + [edged] * share,
            out_specs=[edged] + [block] * share,
            scratch_shapes=[
                pltpu.VMEM((share, order + LAST + FIRST, wide), jnp.float32),
                pltpu.VMEM((share, order + LAST, wide), jnp.float32),
            ],
        ),
        out_shape=[jax.ShapeDtypeStruct((order + LAST + FIRST, wide), jnp.float32)] + [shape] * share,
        compiler_params=pltpu.CompilerParams(vmem_limit_bytes=SMALL_LIMIT),
        cost_estimate=estimate(order * wide * 20, order * wide * 36),
        name="plane_scan",
    )(place, rates, short, *ends)
    return got[0], got[1:]


def line_scan_body(place, rates, short, whole, *rest, share, rows, lines):
    befores = rest[:share]
    arrived = rest[share : share + lines]
    outs = rest[share + lines :]
    order = rates.shape[0]
    here = place[SPOT]
    rate = rates[...]
    planes = (whole,) + tuple(arrived)

    def last_rows(k):
        if k < lines:
            return planes[k + 1][order : order + LAST]
        return jnp.zeros((LAST, rate.shape[1]), jnp.float32)

    def first_share(k):
        return end_share(short, rate, planes[k][order + LAST :], last_rows(k), rows)

    state = jnp.zeros(rate.shape, jnp.float32)
    decay = jnp.exp(rate * (-1.0 * rows * share))
    later = jnp.exp(rate * (-1.0 * rows * (share - 1)))
    for k in reversed(range(1, lines + 1)):
        state = decay * state + planes[k][:order] + later * first_share(k)
    own = first_share(0)
    for j in range(share):
        at = (here ^ j).astype(jnp.float32)
        inside = jnp.minimum(at, 1.0)
        past = inside * jnp.exp(rate * (jnp.maximum(at - 1.0, 0.0) * (-1.0 * rows)))
        before = befores[j][:order]
        outs[j][:order] = before + jnp.exp(rate * (at * (-1.0 * rows))) * state + past * own
        outs[j][order:] = befores[j][order:] + (1.0 - inside) * last_rows(0)


def line_scan(place, rates, short, whole, befores, arrived, rows):
    share, lines = len(befores), len(arrived)
    order, wide = rates.shape[0], whole.shape[1]
    block = pl.BlockSpec((order + LAST, wide), lambda g, place: (0, 0))
    edged = pl.BlockSpec((order + LAST + FIRST, wide), lambda g, place: (0, 0))
    return pl.pallas_call(
        functools.partial(line_scan_body, share=share, rows=rows, lines=lines),
        grid_spec=pltpu.PrefetchScalarGridSpec(
            num_scalar_prefetch=1,
            grid=(1,),
            in_specs=[
                pl.BlockSpec((order, wide), lambda g, place: (0, place[SPOT])),
                pl.BlockSpec((3, 3, wide), lambda g, place: (0, 0, place[SPOT])),
                edged,
            ]
            + [block] * share
            + [edged] * lines,
            out_specs=[block] * share,
        ),
        out_shape=[jax.ShapeDtypeStruct((order + LAST, wide), jnp.float32)] * share,
        compiler_params=pltpu.CompilerParams(vmem_limit_bytes=SMALL_LIMIT),
        cost_estimate=estimate(order * wide * 20, order * wide * 36),
        name="line_scan",
    )(place, rates, short, whole, *befores, *arrived)


def hidden_body(place, query, top, short, rates, coef, skip, gated, prefix, *rest, seg_len, order, share, first):
    starts = rest[:share]
    hidden = rest[share]
    query_pos, result_pos, start_by_place = rest[share + 1 :]
    pitch = seg_len + 1
    groups = gated.shape[0]
    now_at = pl.program_id(0) + first
    segment = lax.broadcasted_iota(jnp.int32, (SEGS, LANES), 0).astype(jnp.float32)

    @pl.when(pl.program_id(0) == 0)
    def _():
        for j in range(share):
            start_by_place[place[SPOT] ^ j] = starts[j][...]

    for group in range(groups):
        lanes = slice(group * LANES, (group + 1) * LANES)
        ending = start_by_place[now_at, order : order + 2, lanes]
        lay_segments(query_pos, query, ending, seg_len, lanes, group)

    for group in range(groups):
        lanes = slice(group * LANES, (group + 1) * LANES)
        query_taps = taps(short, 0, lanes)
        gain = jnp.broadcast_to(skip[0:1, lanes], (SEGS, LANES))
        decay = [jnp.exp(-row(rates, r, lanes)) for r in range(order)]
        scale = [row(coef, r, lanes) for r in range(order)]
        first = jnp.concatenate([top[b, 0:2, lanes] for b in (1, 2)], axis=0).astype(jnp.float32)
        last = start_by_place[now_at, order:, lanes]
        early = [
            jnp.broadcast_to(value, (SEGS, LANES))
            for value in first_gated(short.at[:, :, lanes], first, last)
        ]
        states = []
        for r in range(order):
            rate = row(rates, r, lanes)
            ahead = jnp.exp(rate * (segment * (-1.0 * seg_len)))
            before = jnp.broadcast_to(start_by_place[now_at, r : r + 1, lanes], (SEGS, LANES))
            grown = jnp.exp(rate)
            before += jnp.where(segment >= 1.0, grown * (early[0] + grown * early[1]), 0.0)
            states.append(prefix[group, r] + ahead * before)

        def step(
            i, carry, late=None, group=group, query_taps=query_taps, gain=gain, decay=decay, scale=scale
        ):
            q1, q2, *states = carry
            q0 = strided(query_pos, group, TOP + i, pitch)
            now = gated[group, pl.ds(pl.multiple_of(i * SEGS, SEGS), SEGS), :]
            if late is not None:
                now = jnp.where(segment >= 1.0, now, late)
            states = [d * h + now for d, h in zip(decay, states)]
            sums = [s * h for s, h in zip(scale, states)] + [gain * now]
            while len(sums) > 1:
                sums = [a + b for a, b in zip(sums[::2], sums[1::2])] + sums[len(sums) // 2 * 2 :]
            query_now = query_taps[0] * q0 + query_taps[1] * q1 + query_taps[2] * q2
            result_pos[group, pl.ds(TOP + i, SEGS, stride=pitch), :] = query_now * sums[0]
            return (q0, q1, *states)

        start = (
            strided(query_pos, group, TOP - 2, pitch),
            strided(query_pos, group, TOP - 3, pitch),
        ) + tuple(states)
        start = step(1, step(0, start, early[0]), early[1])
        lax.fori_loop(2, seg_len, step, start, unroll=6)
        for s in range(SEGS):
            part = result_pos[group, TOP + s * pitch : TOP + s * pitch + seg_len, :]
            hidden[s * seg_len : (s + 1) * seg_len, lanes] = part.astype(hidden.dtype)


def hidden_rows(place, streams, short, rates, coef, skip, gated, prefix, starts, part):
    _, rows, chans = streams.shape
    order = rates.shape[0]
    share = len(starts)
    wide = chans // share
    groups = wide // LANES
    seg_len = rows // SEGS
    steps = max(1, share // 2)
    first = part * steps
    pos_rows = TOP + SEGS * (seg_len + 1)
    return pl.pallas_call(
        functools.partial(hidden_body, seg_len=seg_len, order=order, share=share, first=first),
        grid_spec=pltpu.PrefetchScalarGridSpec(
            num_scalar_prefetch=1,
            grid=(steps,),
            in_specs=[
                pl.BlockSpec((1, rows, wide), lambda g, place: (0, 0, first + g)),
                pl.BlockSpec((3, 16, wide), lambda g, place: (0, 0, first + g)),
                pl.BlockSpec((3, 3, wide), lambda g, place: (0, 0, first + g)),
                pl.BlockSpec((order, wide), lambda g, place: (0, first + g)),
                pl.BlockSpec((order, wide), lambda g, place: (0, first + g)),
                pl.BlockSpec((1, wide), lambda g, place: (0, first + g)),
                pl.BlockSpec((groups, rows, LANES), lambda g, place: (first + g, 0, 0)),
                pl.BlockSpec((groups, order, SEGS, LANES), lambda g, place: (first + g, 0, 0, 0)),
            ]
            + [pl.BlockSpec((order + LAST, wide), lambda g, place: (0, 0))] * share,
            out_specs=pl.BlockSpec((rows, wide), lambda g, place: (0, g)),
            scratch_shapes=[
                pltpu.VMEM((groups, pos_rows, LANES), jnp.float32),
                pltpu.VMEM((groups, pos_rows, LANES), jnp.float32),
                pltpu.VMEM((share, order + LAST, wide), jnp.float32),
            ],
        ),
        out_shape=jax.ShapeDtypeStruct((rows, steps * wide), jnp.bfloat16),
        compiler_params=pltpu.CompilerParams(vmem_limit_bytes=VMEM_LIMIT),
        cost_estimate=estimate(rows * chans * 40, rows * chans * 5),
        name="hidden_rows",
    )(place, streams, streams, short, rates, coef, skip, gated, prefix, *starts)


def project_body(place, *refs, rows_in, slots):
    kept, sent = refs[-2:]
    at = 0
    rows = []
    for count in rows_in:
        rows.append(refs[at : at + count])
        at += count
    blocks = len(slots) // 2
    width = kept.shape[1] // blocks

    def times(columns, out, column):
        top = 0
        for part in rows:
            total = 0.0
            start = 0
            for piece in part:
                size, depth = piece.shape
                total += jnp.dot(
                    piece[...], columns[start : start + depth, :], preferred_element_type=jnp.float32
                )
                start += depth
            out[top : top + size, column : column + width] = total.astype(out.dtype)
            top += size

    for slot, count in enumerate(slots):
        given = refs[at : at + count]
        at += count
        far, block = divmod(slot, blocks)
        for out, keeps in ((kept, 1 - far), (sent, far)):
            for middle, columns in zip((1, 0), given):
                here = place[KEEPS] == keeps
                if count == 2:
                    here = here & (place[MIDDLE] == middle)

                @pl.when(here)
                def _(columns=columns, out=out, block=block):
                    times(columns, out, block * width)


def project(place, rows, slots):
    flat = [piece for part in rows for piece in part] + [block for slot in slots for block in slot]
    count = sum(part[0].shape[0] for part in rows)
    depth, width = slots[0][0].shape
    wide = len(slots) // 2 * width
    held = pl.BlockSpec(memory_space=pltpu.VMEM)
    return pl.pallas_call(
        functools.partial(
            project_body, rows_in=tuple(map(len, rows)), slots=tuple(map(len, slots))
        ),
        in_specs=[pl.BlockSpec(memory_space=pltpu.SMEM)] + [held] * len(flat),
        out_specs=[held] * 2,
        out_shape=[jax.ShapeDtypeStruct((count, wide), jnp.bfloat16)] * 2,
        compiler_params=pltpu.CompilerParams(vmem_limit_bytes=VMEM_LIMIT),
        cost_estimate=estimate(
            2 * count * depth * len(slots) * width,
            2 * (count * depth + len(slots) * width * (depth + count)),
        ),
        name="project",
    )(place, *flat)


def assemble_body(place, *refs):
    parts, out = refs[:-1], refs[-1]
    width = parts[0].shape[1]
    for j, part in enumerate(parts):
        column = pl.multiple_of((place[SPOT] ^ j) * width, LANES)
        out[:, pl.ds(column, width)] = part[...]


def assemble(place, parts, blocks, width):
    share = len(parts)
    rows = parts[0].shape[0]
    return pl.pallas_call(
        assemble_body,
        grid_spec=pltpu.PrefetchScalarGridSpec(
            num_scalar_prefetch=1,
            grid=(blocks,),
            in_specs=[pl.BlockSpec((rows, width), lambda b, place: (0, b ^ place[ODD]))] * share,
            out_specs=pl.BlockSpec((rows, share * width), lambda b, place: (0, b)),
        ),
        out_shape=jax.ShapeDtypeStruct((rows, share * blocks * width), jnp.bfloat16),
        compiler_params=pltpu.CompilerParams(vmem_limit_bytes=VMEM_LIMIT),
        cost_estimate=estimate(0, 4 * rows * share * blocks * width),
        name="assemble",
    )(place, *parts)


def after(value, *others):
    return lax.optimization_barrier((value, *others))[0]


def send_planes(value, group, moves):
    pairs = [(a * group + e, b * group + e) for a, b in moves for e in range(group)]
    return lax.ppermute(value, "ctx", pairs)


def plane_rows(hidden, count, group):
    if group != 4:
        return [hidden] + [[send_xor(part, count, group, j) for part in hidden] for j in range(1, group)]
    first, second = hidden
    first_1 = send_xor(first, count, group, 1)
    first_2 = send_xor(first, count, group, 2)
    second_2 = send_xor(after(second, first_2), count, group, 2)
    second_1 = send_xor(after(second, first_1), count, group, 1)
    first_3 = send_xor(first_1, count, group, 2)
    second_3 = send_xor(second_2, count, group, 1)
    return [[first, second], [first_1, second_1], [first_2, second_2], [first_3, second_3]]


def add_up_body(a, b, *outs):
    size = outs[0].shape[0]
    for j, out in enumerate(outs):
        rows = slice(j * size, (j + 1) * size)
        out[...] = (a[rows].astype(jnp.float32) + b[rows].astype(jnp.float32)).astype(out.dtype)


def add_up(a, b, parts):
    size, width = a.shape[0] // parts, a.shape[1]
    held = pl.BlockSpec(memory_space=pltpu.VMEM)
    return pl.pallas_call(
        add_up_body,
        in_specs=[held, held],
        out_specs=[held] * parts,
        out_shape=[jax.ShapeDtypeStruct((size, width), a.dtype)] * parts,
        compiler_params=pltpu.CompilerParams(vmem_limit_bytes=VMEM_LIMIT),
        cost_estimate=estimate(parts * size * width, 6 * parts * size * width),
        name="add_up",
    )(a, b)


def project_4x4(place, out_weight, states, hidden, count):
    group = 4
    swap = [(0, 1), (1, 0), (2, 3), (3, 2)]
    inner = [(1, 2), (2, 1)]
    outward = [(1, 0), (2, 3)]
    own = out_weight
    by_1 = send_planes(own, group, swap)
    by_3_inner = send_planes(own, group, inner)
    by_2_inner = send_planes(after(by_1, states, by_3_inner), group, inner)
    by_2_outer = send_planes(after(by_3_inner, states), group, outward)
    by_3_outer = send_planes(after(by_2_inner, by_2_outer, *hidden), group, outward)
    rows = plane_rows(hidden, count, group)
    blocks = [[own], [by_1], [by_2_inner, by_2_outer], [by_3_inner, by_3_outer]]

    def to_other(value):
        return lax.ppermute(value, "tp", [(0, 1), (1, 0)])

    kept, sent = project(place, rows[:3], blocks)
    taken = to_other(sent)
    last_kept, last_sent = project(place, rows[3:], blocks)
    last = add_up(last_kept, to_other(last_sent), 1)
    mixed = [*add_up(after(kept, *last), taken, 3), *last]
    mixed = [mixed[0]] + [send_xor(mixed[j], count, group, j) for j in range(1, group)]
    return assemble(place, mixed, 2, out_weight.shape[1])


def project_any(out_weight, states, hidden, count):
    halves = lax.axis_size("tp")
    group = split_of(count)
    outer = count // group
    plane = lax.axis_index("ctx") // group
    size = hidden[0].shape[0]
    depth, width = out_weight.shape
    below, above = [out_weight], [out_weight]
    for k in range(1, outer):
        down, up = below[-1], above[-1]
        if k == 2:
            down, up = after(down, states), after(up, states)
        below.append(send_along(down, count, group, 1, k - 1))
        above.append(send_along(up, count, group, -1, k - 1))
    line = below[:0:-1] + above
    cols = lax.dynamic_slice_in_dim(jnp.stack(line), outer - 1 - plane, outer, 0)
    cols = jnp.moveaxis(cols, 0, 1).reshape(depth, outer * width)
    rows = plane_rows(hidden, count, group)
    held = jnp.concatenate([jnp.concatenate(part, axis=1) for part in rows], axis=0)
    partial = jnp.dot(held, cols, preferred_element_type=jnp.float32).astype(jnp.bfloat16)
    mixed = lax.psum_scatter(partial, "tp", scatter_dimension=1, tiled=True)
    mixed = jnp.split(mixed, group)
    mixed = [mixed[0]] + [send_xor(mixed[j], count, group, j) for j in range(1, group)]
    blocks = outer // halves
    stacked = jnp.stack(mixed).reshape(group, size, blocks, width)
    by_place = jnp.take(stacked, jnp.arange(group) ^ (lax.axis_index("ctx") % group), axis=0)
    return jnp.moveaxis(by_place, 0, 2).reshape(size, blocks * group * width)


def per_device(projected, short_filter, residues, rates, skip_gain, out_weight):
    count = lax.axis_size("ctx")
    halves = lax.axis_size("tp")
    here = lax.axis_index("ctx")
    rows, _, chans = projected.shape

    streams = jnp.transpose(projected, (1, 0, 2))
    rates_t = rates.T
    coef_t = (residues * jnp.sqrt(-jnp.expm1(-2.0 * rates))).T

    share = min(split_of(count), chans // LANES, 4)
    lines = count // share
    plane = here // share
    keeps = lax.axis_index("tp") == plane // 2
    place = jnp.stack([here % share, (plane == 1) | (plane == 2), keeps, plane % 2]).astype(jnp.int32)
    *ends, gated, prefix = local_scan(place, streams, short_filter, rates_t, share)
    ends = [ends[0]] + [send_xor(ends[j], count, share, j) for j in range(1, share)]
    whole, befores = plane_scan(place, rates_t, short_filter, ends, rows)
    arrived = [send_along(whole, count, share, k) for k in range(1, lines)]
    starts = line_scan(place, rates_t, short_filter, whole, befores, arrived, rows)
    states = starts[0]
    starts = [starts[0]] + [send_xor(starts[j], count, share, j) for j in range(1, share)]
    hidden = [
        hidden_rows(
            place, streams, short_filter, rates_t, coef_t, skip_gain[None], gated, prefix, starts, part
        )
        for part in range(2)
    ]
    if count == 16 and halves == 2 and out_weight.shape[1] % LANES == 0:
        return project_4x4(place, out_weight, states, hidden, count)
    return project_any(out_weight, states, hidden, count)


def solution(mesh):
    return jax.shard_map(
        per_device,
        mesh=mesh,
        in_specs=(
            P("ctx", None, "tp"),
            P(None, None, "tp"),
            P("tp", None),
            P("tp", None),
            P("tp"),
            P("tp", "ctx"),
        ),
        out_specs=P("ctx", "tp"),
        check_vma=False,
    )
```

```python
import functools

import jax
import jax.numpy as jnp
from jax import lax
from jax.experimental import pallas as pl
from jax.experimental.pallas import tpu as pltpu
from jax.sharding import PartitionSpec as P

LANES = 128
SEGS = 8
TOP = 8
SPOT, MIDDLE, KEEPS, ODD = range(4)
VMEM_LIMIT = 16 * 1024 * 1024
SMALL_LIMIT = 4 * 1024 * 1024
WHOLE_LIMIT = 50 * 1024 * 1024


def split_of(count):
    inner = 1
    while (2 * inner) ** 2 <= count and count % (2 * inner) == 0:
        inner *= 2
    return inner


def send_xor(value, count, group, step):
    pairs = [(p, p - p % group + ((p % group) ^ step)) for p in range(count)]
    return lax.ppermute(value, "ctx", pairs)


def send_along(value, count, group, steps, first=0):
    outer = count // group
    pairs = []
    for z in range(outer):
        if not 0 <= z + steps < outer:
            continue
        if (steps > 0 and z < first) or (steps < 0 and z > outer - 1 - first):
            continue
        pairs += [(z * group + e, (z + steps) * group + e) for e in range(group)]
    return lax.ppermute(value, "ctx", pairs)


def estimate(flops, bytes_accessed, transcendentals=0):
    return pl.CostEstimate(flops=flops, bytes_accessed=bytes_accessed, transcendentals=transcendentals)


def row(ref, r, lanes):
    return jnp.broadcast_to(ref[r : r + 1, lanes], (SEGS, LANES))


def lay_segments(dst, stream, halo, seg_len, lanes, group):
    pitch = seg_len + 1
    for s in range(SEGS):
        part = stream[0, s * seg_len : (s + 1) * seg_len, lanes].astype(jnp.float32)
        dst[group, TOP + s * pitch : TOP + s * pitch + seg_len, :] = part
    dst[group, TOP - 3 : TOP - 1, :] = jnp.zeros((2, LANES), jnp.float32) if halo is None else halo


def taps(short, stream, lanes):
    return [jnp.broadcast_to(short[i, stream : stream + 1, lanes], (SEGS, LANES)) for i in range(3)]


def strided(ref, group, start, pitch):
    return ref[group, pl.ds(start, SEGS, stride=pitch), :]


LAST, FIRST = 6, 4


def first_gated(short, first, last):
    products = []
    for b, stream in enumerate((1, 2)):
        tap = [short[i, stream : stream + 1, :] for i in range(3)]
        now_0, now_1 = first[2 * b : 2 * b + 1], first[2 * b + 1 : 2 * b + 2]
        old_2, old_1 = last[2 * stream : 2 * stream + 1], last[2 * stream + 1 : 2 * stream + 2]
        products.append(
            (
                tap[0] * now_0 + tap[1] * old_1 + tap[2] * old_2,
                tap[0] * now_1 + tap[1] * now_0 + tap[2] * old_1,
            )
        )
    return products[0][0] * products[1][0], products[0][1] * products[1][1]


def end_share(short, rates, first, last, rows):
    gated_0, gated_1 = first_gated(short, first, last)
    return jnp.exp(rates * (1.0 - rows)) * gated_0 + jnp.exp(rates * (2.0 - rows)) * gated_1


def local_scan_body(place, streams, short_all, rates_all, *rest, seg_len, order, share):
    ends = rest[:share]
    gated, prefix = rest[share : share + 2]
    key_pos, value_pos, end_now, held, query_held, short_held, rates_held, held_sem, small_sem = rest[share + 2 :]
    now_at = pl.program_id(0)
    wide = end_now.shape[1]
    small = [
        pltpu.make_async_copy(short_all, short_held, small_sem.at[0]),
        pltpu.make_async_copy(rates_all, rates_held, small_sem.at[1]),
        pltpu.make_async_copy(
            streams.at[0, pl.ds(seg_len * SEGS - 16, 16), :], query_held, small_sem.at[2]
        ),
    ]

    def stream_copy(at):
        columns = pl.ds(at * wide, wide)
        return pltpu.make_async_copy(
            streams.at[pl.ds(1, 2), :, columns], held.at[:, :, columns], held_sem.at[at]
        )

    @pl.when(now_at == 0)
    def _():
        stream_copy(0).start()
        for copy in small:
            copy.start()
        for at in range(1, share):
            stream_copy(at).start()
        for copy in small:
            copy.wait()

    for at in range(share):

        @pl.when(now_at == at)
        def _(at=at):
            stream_copy(at).wait()

    columns = pl.ds(pl.multiple_of(now_at * wide, LANES), wide)
    key = held.at[pl.ds(0, 1), :, columns]
    value = held.at[pl.ds(1, 1), :, columns]
    short = short_held.at[:, :, columns]
    rates = rates_held.at[:, columns]
    pitch = seg_len + 1
    groups = gated.shape[0]
    segment = lax.broadcasted_iota(jnp.int32, (SEGS, LANES), 0)
    for group in range(groups):
        lanes = slice(group * LANES, (group + 1) * LANES)
        lay_segments(key_pos, key, None, seg_len, lanes, group)
        lay_segments(value_pos, value, None, seg_len, lanes, group)
    bottom = seg_len * SEGS - 2
    end_now[order : order + 2, :] = query_held[14:16, columns].astype(jnp.float32)
    for b, stream in enumerate((key, value)):
        at = order + 2 + 2 * b
        end_now[at : at + 2, :] = stream[0, bottom : bottom + 2, :].astype(jnp.float32)
        at = order + LAST + 2 * b
        end_now[at : at + 2, :] = stream[0, 0:2, :].astype(jnp.float32)

    for group in range(groups):
        lanes = slice(group * LANES, (group + 1) * LANES)
        key_taps = taps(short, 1, lanes)
        value_taps = taps(short, 2, lanes)
        decay = [jnp.exp(-row(rates, r, lanes)) for r in range(order)]

        def step(i, carry, early=False, group=group, key_taps=key_taps, value_taps=value_taps, decay=decay):
            k1, k2, v1, v2, *states = carry
            k0 = strided(key_pos, group, TOP + i, pitch)
            v0 = strided(value_pos, group, TOP + i, pitch)
            key_now = key_taps[0] * k0 + key_taps[1] * k1 + key_taps[2] * k2
            value_now = value_taps[0] * v0 + value_taps[1] * v1 + value_taps[2] * v2
            now = key_now * value_now
            if early:
                now = jnp.where(segment >= 1, now, 0.0)
            gated[group, pl.ds(pl.multiple_of(i * SEGS, SEGS), SEGS), :] = now
            states = [d * h + now for d, h in zip(decay, states)]
            return (k0, k1, v0, v1, *states)

        zero = jnp.zeros((SEGS, LANES), jnp.float32)
        start = (
            strided(key_pos, group, TOP - 2, pitch),
            strided(key_pos, group, TOP - 3, pitch),
            strided(value_pos, group, TOP - 2, pitch),
            strided(value_pos, group, TOP - 3, pitch),
        ) + (zero,) * order
        start = step(1, step(0, start, True), True)
        states = lax.fori_loop(2, seg_len, step, start, unroll=6)[4:]
        for r in range(order):
            rate = row(rates, r, lanes)
            scan = states[r]
            for d in (1, 2, 4):
                moved = jnp.where(segment >= d, pltpu.roll(scan, d, 0), 0.0)
                scan = scan + jnp.exp(rate * (-1.0 * d * seg_len)) * moved
            prefix[group, r] = jnp.where(segment >= 1, pltpu.roll(scan, 1, 0), 0.0)
            end_now[r : r + 1, lanes] = scan[SEGS - 1 :, :]

    for j in range(share):

        @pl.when((pl.program_id(0) ^ place[SPOT]) == j)
        def _(j=j):
            ends[j][...] = end_now[...]


def local_scan(place, streams, short, rates, share):
    _, rows, chans = streams.shape
    order = rates.shape[0]
    wide = chans // share
    groups = wide // LANES
    seg_len = rows // SEGS
    pos_rows = TOP + SEGS * (seg_len + 1)
    end_shape = jax.ShapeDtypeStruct((order + LAST + FIRST, wide), jnp.float32)
    return pl.pallas_call(
        functools.partial(local_scan_body, seg_len=seg_len, order=order, share=share),
        grid_spec=pltpu.PrefetchScalarGridSpec(
            num_scalar_prefetch=1,
            grid=(share,),
            in_specs=[
                pl.BlockSpec(memory_space=pltpu.HBM),
                pl.BlockSpec(memory_space=pltpu.HBM),
                pl.BlockSpec(memory_space=pltpu.HBM),
            ],
            out_specs=[pl.BlockSpec((order + LAST + FIRST, wide), lambda g, place: (0, 0))] * share
            + [
                pl.BlockSpec((groups, rows, LANES), lambda g, place: (g, 0, 0)),
                pl.BlockSpec((groups, order, SEGS, LANES), lambda g, place: (g, 0, 0, 0)),
            ],
            scratch_shapes=[
                pltpu.VMEM((groups, pos_rows, LANES), jnp.float32),
                pltpu.VMEM((groups, pos_rows, LANES), jnp.float32),
                pltpu.VMEM((order + LAST + FIRST, wide), jnp.float32),
                pltpu.VMEM((2, rows, chans), streams.dtype),
                pltpu.VMEM((16, chans), streams.dtype),
                pltpu.VMEM(short.shape, jnp.float32),
                pltpu.VMEM(rates.shape, jnp.float32),
                pltpu.SemaphoreType.DMA((share,)),
                pltpu.SemaphoreType.DMA((3,)),
            ],
        ),
        out_shape=[end_shape] * share
        + [
            jax.ShapeDtypeStruct((chans // LANES, rows, LANES), jnp.float32),
            jax.ShapeDtypeStruct((chans // LANES, order, SEGS, LANES), jnp.float32),
        ],
        compiler_params=pltpu.CompilerParams(vmem_limit_bytes=WHOLE_LIMIT),
        cost_estimate=estimate(rows * chans * 50, rows * chans * 10),
        name="local_scan",
    )(place, streams, short, rates)


def plane_scan_body(place, rates, short, *rest, share, rows):
    ends = rest[:share]
    whole = rest[share]
    befores = rest[share + 1 : 2 * share + 1]
    by_place, before_place = rest[2 * share + 1 :]
    order = rates.shape[0]
    here = place[SPOT]
    for j in range(share):
        by_place[here ^ j] = ends[j][...]
    rate = rates[...]
    decay = jnp.exp(rate * (-1.0 * rows))
    state = jnp.zeros(rate.shape, jnp.float32)
    for at in range(share):
        before_place[at, :order] = state
        state = decay * state + by_place[at, :order]
        if at > 0:
            last = by_place[at - 1, order : order + LAST]
            before_place[at, order:] = last
            state += end_share(short, rate, by_place[at, order + LAST :], last, rows)
    before_place[0, order:] = jnp.zeros((LAST, rate.shape[1]), jnp.float32)
    whole[:order] = state
    whole[order : order + LAST] = by_place[share - 1, order : order + LAST]
    whole[order + LAST :] = by_place[0, order + LAST :]
    for j in range(share):
        befores[j][...] = before_place[here ^ j]


def plane_scan(place, rates, short, ends, rows):
    share = len(ends)
    order = rates.shape[0]
    wide = ends[0].shape[1]
    block = pl.BlockSpec((order + LAST, wide), lambda g, place: (0, 0))
    edged = pl.BlockSpec((order + LAST + FIRST, wide), lambda g, place: (0, 0))
    shape = jax.ShapeDtypeStruct((order + LAST, wide), jnp.float32)
    got = pl.pallas_call(
        functools.partial(plane_scan_body, share=share, rows=rows),
        grid_spec=pltpu.PrefetchScalarGridSpec(
            num_scalar_prefetch=1,
            grid=(1,),
            in_specs=[
                pl.BlockSpec((order, wide), lambda g, place: (0, place[SPOT])),
                pl.BlockSpec((3, 3, wide), lambda g, place: (0, 0, place[SPOT])),
            ]
            + [edged] * share,
            out_specs=[edged] + [block] * share,
            scratch_shapes=[
                pltpu.VMEM((share, order + LAST + FIRST, wide), jnp.float32),
                pltpu.VMEM((share, order + LAST, wide), jnp.float32),
            ],
        ),
        out_shape=[jax.ShapeDtypeStruct((order + LAST + FIRST, wide), jnp.float32)] + [shape] * share,
        compiler_params=pltpu.CompilerParams(vmem_limit_bytes=SMALL_LIMIT),
        cost_estimate=estimate(order * wide * 20, order * wide * 36),
        name="plane_scan",
    )(place, rates, short, *ends)
    return got[0], got[1:]


def line_scan_body(place, rates, short, whole, *rest, share, rows, lines):
    befores = rest[:share]
    arrived = rest[share : share + lines]
    outs = rest[share + lines :]
    order = rates.shape[0]
    here = place[SPOT]
    rate = rates[...]
    planes = (whole,) + tuple(arrived)

    def last_rows(k):
        if k < lines:
            return planes[k + 1][order : order + LAST]
        return jnp.zeros((LAST, rate.shape[1]), jnp.float32)

    def first_share(k):
        return end_share(short, rate, planes[k][order + LAST :], last_rows(k), rows)

    state = jnp.zeros(rate.shape, jnp.float32)
    decay = jnp.exp(rate * (-1.0 * rows * share))
    later = jnp.exp(rate * (-1.0 * rows * (share - 1)))
    for k in reversed(range(1, lines + 1)):
        state = decay * state + planes[k][:order] + later * first_share(k)
    own = first_share(0)
    for j in range(share):
        at = (here ^ j).astype(jnp.float32)
        inside = jnp.minimum(at, 1.0)
        past = inside * jnp.exp(rate * (jnp.maximum(at - 1.0, 0.0) * (-1.0 * rows)))
        before = befores[j][:order]
        outs[j][:order] = before + jnp.exp(rate * (at * (-1.0 * rows))) * state + past * own
        outs[j][order:] = befores[j][order:] + (1.0 - inside) * last_rows(0)


def line_scan(place, rates, short, whole, befores, arrived, rows):
    share, lines = len(befores), len(arrived)
    order, wide = rates.shape[0], whole.shape[1]
    block = pl.BlockSpec((order + LAST, wide), lambda g, place: (0, 0))
    edged = pl.BlockSpec((order + LAST + FIRST, wide), lambda g, place: (0, 0))
    return pl.pallas_call(
        functools.partial(line_scan_body, share=share, rows=rows, lines=lines),
        grid_spec=pltpu.PrefetchScalarGridSpec(
            num_scalar_prefetch=1,
            grid=(1,),
            in_specs=[
                pl.BlockSpec((order, wide), lambda g, place: (0, place[SPOT])),
                pl.BlockSpec((3, 3, wide), lambda g, place: (0, 0, place[SPOT])),
                edged,
            ]
            + [block] * share
            + [edged] * lines,
            out_specs=[block] * share,
        ),
        out_shape=[jax.ShapeDtypeStruct((order + LAST, wide), jnp.float32)] * share,
        compiler_params=pltpu.CompilerParams(vmem_limit_bytes=SMALL_LIMIT),
        cost_estimate=estimate(order * wide * 20, order * wide * 36),
        name="line_scan",
    )(place, rates, short, whole, *befores, *arrived)


def hidden_body(place, query, top, short, rates, coef, skip, gated, prefix, *rest, seg_len, order, share, first):
    starts = rest[:share]
    hidden = rest[share]
    query_pos, result_pos, start_by_place = rest[share + 1 :]
    pitch = seg_len + 1
    groups = gated.shape[0]
    now_at = pl.program_id(0) + first
    segment = lax.broadcasted_iota(jnp.int32, (SEGS, LANES), 0).astype(jnp.float32)

    @pl.when(pl.program_id(0) == 0)
    def _():
        for j in range(share):
            start_by_place[place[SPOT] ^ j] = starts[j][...]

    for group in range(groups):
        lanes = slice(group * LANES, (group + 1) * LANES)
        ending = start_by_place[now_at, order : order + 2, lanes]
        lay_segments(query_pos, query, ending, seg_len, lanes, group)

    for group in range(groups):
        lanes = slice(group * LANES, (group + 1) * LANES)
        query_taps = taps(short, 0, lanes)
        gain = jnp.broadcast_to(skip[0:1, lanes], (SEGS, LANES))
        decay = [jnp.exp(-row(rates, r, lanes)) for r in range(order)]
        scale = [row(coef, r, lanes) for r in range(order)]
        first = jnp.concatenate([top[b, 0:2, lanes] for b in (1, 2)], axis=0).astype(jnp.float32)
        last = start_by_place[now_at, order:, lanes]
        early = [
            jnp.broadcast_to(value, (SEGS, LANES))
            for value in first_gated(short.at[:, :, lanes], first, last)
        ]
        states = []
        for r in range(order):
            rate = row(rates, r, lanes)
            ahead = jnp.exp(rate * (segment * (-1.0 * seg_len)))
            before = jnp.broadcast_to(start_by_place[now_at, r : r + 1, lanes], (SEGS, LANES))
            grown = jnp.exp(rate)
            before += jnp.where(segment >= 1.0, grown * (early[0] + grown * early[1]), 0.0)
            states.append(prefix[group, r] + ahead * before)

        def step(
            i, carry, late=None, group=group, query_taps=query_taps, gain=gain, decay=decay, scale=scale
        ):
            q1, q2, *states = carry
            q0 = strided(query_pos, group, TOP + i, pitch)
            now = gated[group, pl.ds(pl.multiple_of(i * SEGS, SEGS), SEGS), :]
            if late is not None:
                now = jnp.where(segment >= 1.0, now, late)
            states = [d * h + now for d, h in zip(decay, states)]
            sums = [s * h for s, h in zip(scale, states)] + [gain * now]
            while len(sums) > 1:
                sums = [a + b for a, b in zip(sums[::2], sums[1::2])] + sums[len(sums) // 2 * 2 :]
            query_now = query_taps[0] * q0 + query_taps[1] * q1 + query_taps[2] * q2
            result_pos[group, pl.ds(TOP + i, SEGS, stride=pitch), :] = query_now * sums[0]
            return (q0, q1, *states)

        start = (
            strided(query_pos, group, TOP - 2, pitch),
            strided(query_pos, group, TOP - 3, pitch),
        ) + tuple(states)
        start = step(1, step(0, start, early[0]), early[1])
        lax.fori_loop(2, seg_len, step, start, unroll=6)
        for s in range(SEGS):
            part = result_pos[group, TOP + s * pitch : TOP + s * pitch + seg_len, :]
            hidden[s * seg_len : (s + 1) * seg_len, lanes] = part.astype(hidden.dtype)


def hidden_rows(place, streams, short, rates, coef, skip, gated, prefix, starts, part):
    _, rows, chans = streams.shape
    order = rates.shape[0]
    share = len(starts)
    wide = chans // share
    groups = wide // LANES
    seg_len = rows // SEGS
    steps = max(1, share // 2)
    first = part * steps
    pos_rows = TOP + SEGS * (seg_len + 1)
    return pl.pallas_call(
        functools.partial(hidden_body, seg_len=seg_len, order=order, share=share, first=first),
        grid_spec=pltpu.PrefetchScalarGridSpec(
            num_scalar_prefetch=1,
            grid=(steps,),
            in_specs=[
                pl.BlockSpec((1, rows, wide), lambda g, place: (0, 0, first + g)),
                pl.BlockSpec((3, 16, wide), lambda g, place: (0, 0, first + g)),
                pl.BlockSpec((3, 3, wide), lambda g, place: (0, 0, first + g)),
                pl.BlockSpec((order, wide), lambda g, place: (0, first + g)),
                pl.BlockSpec((order, wide), lambda g, place: (0, first + g)),
                pl.BlockSpec((1, wide), lambda g, place: (0, first + g)),
                pl.BlockSpec((groups, rows, LANES), lambda g, place: (first + g, 0, 0)),
                pl.BlockSpec((groups, order, SEGS, LANES), lambda g, place: (first + g, 0, 0, 0)),
            ]
            + [pl.BlockSpec((order + LAST, wide), lambda g, place: (0, 0))] * share,
            out_specs=pl.BlockSpec((rows, wide), lambda g, place: (0, g)),
            scratch_shapes=[
                pltpu.VMEM((groups, pos_rows, LANES), jnp.float32),
                pltpu.VMEM((groups, pos_rows, LANES), jnp.float32),
                pltpu.VMEM((share, order + LAST, wide), jnp.float32),
            ],
        ),
        out_shape=jax.ShapeDtypeStruct((rows, steps * wide), jnp.bfloat16),
        compiler_params=pltpu.CompilerParams(vmem_limit_bytes=VMEM_LIMIT),
        cost_estimate=estimate(rows * chans * 40, rows * chans * 5),
        name="hidden_rows",
    )(place, streams, streams, short, rates, coef, skip, gated, prefix, *starts)


def project_body(place, *refs, rows_in, slots):
    kept, sent = refs[-2:]
    at = 0
    rows = []
    for count in rows_in:
        rows.append(refs[at : at + count])
        at += count
    blocks = 2
    width = kept.shape[1] // blocks

    def times(columns, out, column):
        times_into(rows, columns, out, column)

    def place_slot(given, block, far):
        for out, keeps in ((kept, 1 - far), (sent, far)):
            for middle, columns in zip((1, 0), given):
                here = place[KEEPS] == keeps
                if len(given) == 2:
                    here = here & (place[MIDDLE] == middle)

                @pl.when(here)
                def _(columns=columns, out=out):
                    times(columns, out, block * width)

    if len(slots) == 1:
        near, far_first = refs[-4:-2]
        for keeps, near_out, far_out in ((1, kept, sent), (0, sent, kept)):

            @pl.when(place[KEEPS] == keeps)
            def _(near_out=near_out, far_out=far_out):
                near_out[...] = near[...]
                far_out[:, :width] = far_first[...]

        place_slot(refs[at : at + slots[0]], 1, 1)
        return
    for slot, count in enumerate(slots):
        far, block = divmod(slot, blocks)
        place_slot(refs[at : at + count], block, far)
        at += count


def near_body(place, *refs, rows_in, slots):
    near, far_first = refs[-2:]
    at = 0
    rows = []
    for count in rows_in:
        rows.append(refs[at : at + count])
        at += count
    width = far_first.shape[1]
    for slot, count in enumerate(slots):
        out, column = (near, slot * width) if slot < 2 else (far_first, 0)
        for middle, columns in zip((1, 0), refs[at : at + count]):

            def put(columns=columns, out=out, column=column):
                times_into(rows, columns, out, column)

            if count == 1:
                put()
            else:
                pl.when(place[MIDDLE] == middle)(put)
        at += count


def times_into(rows, columns, out, column):
    width = columns.shape[1]
    top = 0
    for part in rows:
        total = 0.0
        start = 0
        for piece in part:
            size, depth = piece.shape
            total += jnp.dot(
                piece[...], columns[start : start + depth, :], preferred_element_type=jnp.float32
            )
            start += depth
        out[top : top + size, column : column + width] = total.astype(out.dtype)
        top += size


def project(place, rows, slots, made=None):
    flat = [piece for part in rows for piece in part] + [block for slot in slots for block in slot]
    flat += [] if made is None else list(made)
    count = sum(part[0].shape[0] for part in rows)
    depth, width = slots[0][0].shape
    widths = (2 * width, width) if len(slots) == 3 else (2 * width, 2 * width)
    held = pl.BlockSpec(memory_space=pltpu.VMEM)
    return pl.pallas_call(
        functools.partial(
            near_body if len(slots) == 3 else project_body,
            rows_in=tuple(map(len, rows)),
            slots=tuple(map(len, slots)),
        ),
        in_specs=[pl.BlockSpec(memory_space=pltpu.SMEM)] + [held] * len(flat),
        out_specs=[held] * 2,
        out_shape=[jax.ShapeDtypeStruct((count, wide), jnp.bfloat16) for wide in widths],
        compiler_params=pltpu.CompilerParams(vmem_limit_bytes=VMEM_LIMIT),
        cost_estimate=estimate(
            2 * count * depth * len(slots) * width,
            2 * (count * depth + len(slots) * width * (depth + count)),
        ),
        name="project",
    )(place, *flat)


def assemble_body(place, *refs):
    parts, out = refs[:-1], refs[-1]
    width = parts[0].shape[1]
    for j, part in enumerate(parts):
        column = pl.multiple_of((place[SPOT] ^ j) * width, LANES)
        out[:, pl.ds(column, width)] = part[...]


def assemble(place, parts, blocks, width):
    share = len(parts)
    rows = parts[0].shape[0]
    return pl.pallas_call(
        assemble_body,
        grid_spec=pltpu.PrefetchScalarGridSpec(
            num_scalar_prefetch=1,
            grid=(blocks,),
            in_specs=[pl.BlockSpec((rows, width), lambda b, place: (0, b ^ place[ODD]))] * share,
            out_specs=pl.BlockSpec((rows, share * width), lambda b, place: (0, b)),
        ),
        out_shape=jax.ShapeDtypeStruct((rows, share * blocks * width), jnp.bfloat16),
        compiler_params=pltpu.CompilerParams(vmem_limit_bytes=VMEM_LIMIT),
        cost_estimate=estimate(0, 4 * rows * share * blocks * width),
        name="assemble",
    )(place, *parts)


def after(value, *others):
    return lax.optimization_barrier((value, *others))[0]


def send_planes(value, group, moves):
    pairs = [(a * group + e, b * group + e) for a, b in moves for e in range(group)]
    return lax.ppermute(value, "ctx", pairs)


def plane_rows(hidden, count, group):
    if group != 4:
        return [hidden] + [[send_xor(part, count, group, j) for part in hidden] for j in range(1, group)]
    first, second = hidden
    first_1 = send_xor(first, count, group, 1)
    first_2 = send_xor(first, count, group, 2)
    second_2 = send_xor(second, count, group, 2)
    second_1 = send_xor(second, count, group, 1)
    first_3 = send_xor(first_1, count, group, 2)
    second_3 = send_xor(second_2, count, group, 1)
    return [[first, second], [first_1, second_1], [first_2, second_2], [first_3, second_3]]


def add_up_body(a, b, *outs):
    size = outs[0].shape[0]
    for j, out in enumerate(outs):
        rows = slice(j * size, (j + 1) * size)
        out[...] = (a[rows].astype(jnp.float32) + b[rows].astype(jnp.float32)).astype(out.dtype)


def add_up(a, b, parts):
    size, width = a.shape[0] // parts, a.shape[1]
    held = pl.BlockSpec(memory_space=pltpu.VMEM)
    return pl.pallas_call(
        add_up_body,
        in_specs=[held, held],
        out_specs=[held] * parts,
        out_shape=[jax.ShapeDtypeStruct((size, width), a.dtype)] * parts,
        compiler_params=pltpu.CompilerParams(vmem_limit_bytes=VMEM_LIMIT),
        cost_estimate=estimate(parts * size * width, 6 * parts * size * width),
        name="add_up",
    )(a, b)


def project_4x4(place, out_weight, states, hidden, count):
    group = 4
    swap = [(0, 1), (1, 0), (2, 3), (3, 2)]
    inner = [(1, 2), (2, 1)]
    outward = [(1, 0), (2, 3)]
    rows = plane_rows(hidden, count, group)
    own = out_weight
    by_1 = send_planes(own, group, swap)
    by_3_inner = send_planes(own, group, inner)
    by_2_inner = send_planes(after(by_1, states, by_3_inner), group, inner)
    by_2_outer = send_planes(after(by_3_inner, states), group, outward)
    by_3_outer = send_planes(after(by_2_inner, by_2_outer, rows[1][0], rows[2][0], hidden[1]), group, outward)
    blocks = [[own], [by_1], [by_2_inner, by_2_outer], [by_3_inner, by_3_outer]]

    def to_other(value):
        return lax.ppermute(value, "tp", [(0, 1), (1, 0)])

    made = project(place, rows[:3], blocks[:3])
    last_kept, last_sent = project(place, [[piece for piece in part] for part in rows[3:]], blocks)
    far_rows = [[after(piece, last_sent) for piece in part] for part in rows[:3]]
    kept, sent = project(place, far_rows, blocks[3:], made)
    taken = to_other(sent)
    last = add_up(last_kept, to_other(last_sent), 1)
    mixed = [*add_up(kept, taken, 3), *last]
    mixed = [mixed[0]] + [send_xor(mixed[j], count, group, j) for j in range(1, group)]
    return assemble(place, mixed, 2, out_weight.shape[1])


def project_any(out_weight, states, hidden, count):
    halves = lax.axis_size("tp")
    group = split_of(count)
    outer = count // group
    plane = lax.axis_index("ctx") // group
    size = hidden[0].shape[0]
    depth, width = out_weight.shape
    below, above = [out_weight], [out_weight]
    for k in range(1, outer):
        down, up = below[-1], above[-1]
        if k == 2:
            down, up = after(down, states), after(up, states)
        below.append(send_along(down, count, group, 1, k - 1))
        above.append(send_along(up, count, group, -1, k - 1))
    line = below[:0:-1] + above
    cols = lax.dynamic_slice_in_dim(jnp.stack(line), outer - 1 - plane, outer, 0)
    cols = jnp.moveaxis(cols, 0, 1).reshape(depth, outer * width)
    rows = plane_rows(hidden, count, group)
    held = jnp.concatenate([jnp.concatenate(part, axis=1) for part in rows], axis=0)
    partial = jnp.dot(held, cols, preferred_element_type=jnp.float32).astype(jnp.bfloat16)
    mixed = lax.psum_scatter(partial, "tp", scatter_dimension=1, tiled=True)
    mixed = jnp.split(mixed, group)
    mixed = [mixed[0]] + [send_xor(mixed[j], count, group, j) for j in range(1, group)]
    blocks = outer // halves
    stacked = jnp.stack(mixed).reshape(group, size, blocks, width)
    by_place = jnp.take(stacked, jnp.arange(group) ^ (lax.axis_index("ctx") % group), axis=0)
    return jnp.moveaxis(by_place, 0, 2).reshape(size, blocks * group * width)


def per_device(projected, short_filter, residues, rates, skip_gain, out_weight):
    count = lax.axis_size("ctx")
    halves = lax.axis_size("tp")
    here = lax.axis_index("ctx")
    rows, _, chans = projected.shape

    streams = jnp.transpose(projected, (1, 0, 2))
    rates_t = rates.T
    coef_t = (residues * jnp.sqrt(-jnp.expm1(-2.0 * rates))).T

    share = min(split_of(count), chans // LANES, 4)
    lines = count // share
    plane = here // share
    keeps = lax.axis_index("tp") == plane // 2
    place = jnp.stack([here % share, (plane == 1) | (plane == 2), keeps, plane % 2]).astype(jnp.int32)
    *ends, gated, prefix = local_scan(place, streams, short_filter, rates_t, share)
    ends = [ends[0]] + [send_xor(ends[j], count, share, j) for j in range(1, share)]
    whole, befores = plane_scan(place, rates_t, short_filter, ends, rows)
    arrived = [send_along(whole, count, share, k) for k in range(1, lines)]
    starts = line_scan(place, rates_t, short_filter, whole, befores, arrived, rows)
    states = starts[0]
    starts = [starts[0]] + [send_xor(starts[j], count, share, j) for j in range(1, share)]
    hidden = [
        hidden_rows(
            place, streams, short_filter, rates_t, coef_t, skip_gain[None], gated, prefix, starts, part
        )
        for part in range(2)
    ]
    if count == 16 and halves == 2 and out_weight.shape[1] % LANES == 0:
        return project_4x4(place, out_weight, states, hidden, count)
    return project_any(out_weight, states, hidden, count)


def solution(mesh):
    return jax.shard_map(
        per_device,
        mesh=mesh,
        in_specs=(
            P("ctx", None, "tp"),
            P(None, None, "tp"),
            P("tp", None),
            P("tp", None),
            P("tp"),
            P("tp", "ctx"),
        ),
        out_specs=P("ctx", "tp"),
        check_vma=False,
    )
```

```python
import functools

import jax
import jax.numpy as jnp
from jax import lax
from jax.experimental import pallas as pl
from jax.experimental.pallas import tpu as pltpu
from jax.sharding import PartitionSpec as P

LANES = 128
SEGS = 8
TOP = 8
SPOT, MIDDLE, KEEPS, ODD = range(4)
VMEM_LIMIT = 16 * 1024 * 1024
SMALL_LIMIT = 4 * 1024 * 1024
WHOLE_LIMIT = 50 * 1024 * 1024


def split_of(count):
    inner = 1
    while (2 * inner) ** 2 <= count and count % (2 * inner) == 0:
        inner *= 2
    return inner


def send_xor(value, count, group, step):
    pairs = [(p, p - p % group + ((p % group) ^ step)) for p in range(count)]
    return lax.ppermute(value, "ctx", pairs)


def send_along(value, count, group, steps, first=0):
    outer = count // group
    pairs = []
    for z in range(outer):
        if not 0 <= z + steps < outer:
            continue
        if (steps > 0 and z < first) or (steps < 0 and z > outer - 1 - first):
            continue
        pairs += [(z * group + e, (z + steps) * group + e) for e in range(group)]
    return lax.ppermute(value, "ctx", pairs)


def estimate(flops, bytes_accessed, transcendentals=0):
    return pl.CostEstimate(flops=flops, bytes_accessed=bytes_accessed, transcendentals=transcendentals)


def row(ref, r, lanes):
    return jnp.broadcast_to(ref[r : r + 1, lanes], (SEGS, LANES))


def lay_segments(dst, stream, halo, seg_len, lanes, group):
    pitch = seg_len + 1
    for s in range(SEGS):
        part = stream[0, s * seg_len : (s + 1) * seg_len, lanes].astype(jnp.float32)
        dst[group, TOP + s * pitch : TOP + s * pitch + seg_len, :] = part
    dst[group, TOP - 3 : TOP - 1, :] = jnp.zeros((2, LANES), jnp.float32) if halo is None else halo


def taps(short, stream, lanes):
    return [jnp.broadcast_to(short[i, stream : stream + 1, lanes], (SEGS, LANES)) for i in range(3)]


def strided(ref, group, start, pitch):
    return ref[group, pl.ds(start, SEGS, stride=pitch), :]


LAST, FIRST = 6, 4


def first_gated(short, first, last):
    products = []
    for b, stream in enumerate((1, 2)):
        tap = [short[i, stream : stream + 1, :] for i in range(3)]
        now_0, now_1 = first[2 * b : 2 * b + 1], first[2 * b + 1 : 2 * b + 2]
        old_2, old_1 = last[2 * stream : 2 * stream + 1], last[2 * stream + 1 : 2 * stream + 2]
        products.append(
            (
                tap[0] * now_0 + tap[1] * old_1 + tap[2] * old_2,
                tap[0] * now_1 + tap[1] * now_0 + tap[2] * old_1,
            )
        )
    return products[0][0] * products[1][0], products[0][1] * products[1][1]


def end_share(short, rates, first, last, rows):
    gated_0, gated_1 = first_gated(short, first, last)
    return jnp.exp(rates * (1.0 - rows)) * gated_0 + jnp.exp(rates * (2.0 - rows)) * gated_1


def local_scan_body(place, streams, short_all, rates_all, *rest, seg_len, order, share):
    ends = rest[:share]
    gated, prefix = rest[share : share + 2]
    key_pos, value_pos, end_now, held, query_held, short_held, rates_held, held_sem, small_sem = rest[share + 2 :]
    now_at = pl.program_id(0)
    wide = end_now.shape[1]
    small = [
        pltpu.make_async_copy(short_all, short_held, small_sem.at[0]),
        pltpu.make_async_copy(rates_all, rates_held, small_sem.at[1]),
        pltpu.make_async_copy(
            streams.at[0, pl.ds(seg_len * SEGS - 16, 16), :], query_held, small_sem.at[2]
        ),
    ]

    def stream_copy(at):
        columns = pl.ds(at * wide, wide)
        return pltpu.make_async_copy(
            streams.at[pl.ds(1, 2), :, columns], held.at[:, :, columns], held_sem.at[at]
        )

    @pl.when(now_at == 0)
    def _():
        stream_copy(0).start()
        for copy in small:
            copy.start()
        for at in range(1, share):
            stream_copy(at).start()
        for copy in small:
            copy.wait()

    for at in range(share):

        @pl.when(now_at == at)
        def _(at=at):
            stream_copy(at).wait()

    columns = pl.ds(pl.multiple_of(now_at * wide, LANES), wide)
    key = held.at[pl.ds(0, 1), :, columns]
    value = held.at[pl.ds(1, 1), :, columns]
    short = short_held.at[:, :, columns]
    rates = rates_held.at[:, columns]
    pitch = seg_len + 1
    groups = gated.shape[0]
    segment = lax.broadcasted_iota(jnp.int32, (SEGS, LANES), 0)
    for group in range(groups):
        lanes = slice(group * LANES, (group + 1) * LANES)
        lay_segments(key_pos, key, None, seg_len, lanes, group)
        lay_segments(value_pos, value, None, seg_len, lanes, group)
    bottom = seg_len * SEGS - 2
    end_now[order : order + 2, :] = query_held[14:16, columns].astype(jnp.float32)
    for b, stream in enumerate((key, value)):
        at = order + 2 + 2 * b
        end_now[at : at + 2, :] = stream[0, bottom : bottom + 2, :].astype(jnp.float32)
        at = order + LAST + 2 * b
        end_now[at : at + 2, :] = stream[0, 0:2, :].astype(jnp.float32)

    for group in range(groups):
        lanes = slice(group * LANES, (group + 1) * LANES)
        key_taps = taps(short, 1, lanes)
        value_taps = taps(short, 2, lanes)
        decay = [jnp.exp(-row(rates, r, lanes)) for r in range(order)]

        def step(i, carry, early=False, group=group, key_taps=key_taps, value_taps=value_taps, decay=decay):
            k1, k2, v1, v2, *states = carry
            k0 = strided(key_pos, group, TOP + i, pitch)
            v0 = strided(value_pos, group, TOP + i, pitch)
            key_now = key_taps[0] * k0 + key_taps[1] * k1 + key_taps[2] * k2
            value_now = value_taps[0] * v0 + value_taps[1] * v1 + value_taps[2] * v2
            now = key_now * value_now
            if early:
                now = jnp.where(segment >= 1, now, 0.0)
            gated[group, pl.ds(pl.multiple_of(i * SEGS, SEGS), SEGS), :] = now
            states = [d * h + now for d, h in zip(decay, states)]
            return (k0, k1, v0, v1, *states)

        zero = jnp.zeros((SEGS, LANES), jnp.float32)
        start = (
            strided(key_pos, group, TOP - 2, pitch),
            strided(key_pos, group, TOP - 3, pitch),
            strided(value_pos, group, TOP - 2, pitch),
            strided(value_pos, group, TOP - 3, pitch),
        ) + (zero,) * order
        start = step(1, step(0, start, True), True)
        states = lax.fori_loop(2, seg_len, step, start, unroll=6)[4:]
        for r in range(order):
            rate = row(rates, r, lanes)
            scan = states[r]
            for d in (1, 2, 4):
                moved = jnp.where(segment >= d, pltpu.roll(scan, d, 0), 0.0)
                scan = scan + jnp.exp(rate * (-1.0 * d * seg_len)) * moved
            prefix[group, r] = jnp.where(segment >= 1, pltpu.roll(scan, 1, 0), 0.0)
            end_now[r : r + 1, lanes] = scan[SEGS - 1 :, :]

    for j in range(share):

        @pl.when((pl.program_id(0) ^ place[SPOT]) == j)
        def _(j=j):
            ends[j][...] = end_now[...]


def local_scan(place, streams, short, rates, share):
    _, rows, chans = streams.shape
    order = rates.shape[0]
    wide = chans // share
    groups = wide // LANES
    seg_len = rows // SEGS
    pos_rows = TOP + SEGS * (seg_len + 1)
    end_shape = jax.ShapeDtypeStruct((order + LAST + FIRST, wide), jnp.float32)
    return pl.pallas_call(
        functools.partial(local_scan_body, seg_len=seg_len, order=order, share=share),
        grid_spec=pltpu.PrefetchScalarGridSpec(
            num_scalar_prefetch=1,
            grid=(share,),
            in_specs=[
                pl.BlockSpec(memory_space=pltpu.HBM),
                pl.BlockSpec(memory_space=pltpu.HBM),
                pl.BlockSpec(memory_space=pltpu.HBM),
            ],
            out_specs=[pl.BlockSpec((order + LAST + FIRST, wide), lambda g, place: (0, 0))] * share
            + [
                pl.BlockSpec((groups, rows, LANES), lambda g, place: (g, 0, 0)),
                pl.BlockSpec((groups, order, SEGS, LANES), lambda g, place: (g, 0, 0, 0)),
            ],
            scratch_shapes=[
                pltpu.VMEM((groups, pos_rows, LANES), jnp.float32),
                pltpu.VMEM((groups, pos_rows, LANES), jnp.float32),
                pltpu.VMEM((order + LAST + FIRST, wide), jnp.float32),
                pltpu.VMEM((2, rows, chans), streams.dtype),
                pltpu.VMEM((16, chans), streams.dtype),
                pltpu.VMEM(short.shape, jnp.float32),
                pltpu.VMEM(rates.shape, jnp.float32),
                pltpu.SemaphoreType.DMA((share,)),
                pltpu.SemaphoreType.DMA((3,)),
            ],
        ),
        out_shape=[end_shape] * share
        + [
            jax.ShapeDtypeStruct((chans // LANES, rows, LANES), jnp.float32),
            jax.ShapeDtypeStruct((chans // LANES, order, SEGS, LANES), jnp.float32),
        ],
        compiler_params=pltpu.CompilerParams(vmem_limit_bytes=WHOLE_LIMIT),
        cost_estimate=estimate(rows * chans * 50, rows * chans * 10),
        name="local_scan",
    )(place, streams, short, rates)


def plane_scan_body(place, rates, short, *rest, share, rows):
    ends = rest[:share]
    whole = rest[share]
    befores = rest[share + 1 : 2 * share + 1]
    by_place, before_place = rest[2 * share + 1 :]
    order = rates.shape[0]
    here = place[SPOT]
    for j in range(share):
        by_place[here ^ j] = ends[j][...]
    rate = rates[...]
    decay = jnp.exp(rate * (-1.0 * rows))
    state = jnp.zeros(rate.shape, jnp.float32)
    for at in range(share):
        before_place[at, :order] = state
        state = decay * state + by_place[at, :order]
        if at > 0:
            last = by_place[at - 1, order : order + LAST]
            before_place[at, order:] = last
            state += end_share(short, rate, by_place[at, order + LAST :], last, rows)
    before_place[0, order:] = jnp.zeros((LAST, rate.shape[1]), jnp.float32)
    whole[:order] = state
    whole[order : order + LAST] = by_place[share - 1, order : order + LAST]
    whole[order + LAST :] = by_place[0, order + LAST :]
    for j in range(share):
        befores[j][...] = before_place[here ^ j]


def plane_scan(place, rates, short, ends, rows):
    share = len(ends)
    order = rates.shape[0]
    wide = ends[0].shape[1]
    block = pl.BlockSpec((order + LAST, wide), lambda g, place: (0, 0))
    edged = pl.BlockSpec((order + LAST + FIRST, wide), lambda g, place: (0, 0))
    shape = jax.ShapeDtypeStruct((order + LAST, wide), jnp.float32)
    got = pl.pallas_call(
        functools.partial(plane_scan_body, share=share, rows=rows),
        grid_spec=pltpu.PrefetchScalarGridSpec(
            num_scalar_prefetch=1,
            grid=(1,),
            in_specs=[
                pl.BlockSpec((order, wide), lambda g, place: (0, place[SPOT])),
                pl.BlockSpec((3, 3, wide), lambda g, place: (0, 0, place[SPOT])),
            ]
            + [edged] * share,
            out_specs=[edged] + [block] * share,
            scratch_shapes=[
                pltpu.VMEM((share, order + LAST + FIRST, wide), jnp.float32),
                pltpu.VMEM((share, order + LAST, wide), jnp.float32),
            ],
        ),
        out_shape=[jax.ShapeDtypeStruct((order + LAST + FIRST, wide), jnp.float32)] + [shape] * share,
        compiler_params=pltpu.CompilerParams(vmem_limit_bytes=SMALL_LIMIT),
        cost_estimate=estimate(order * wide * 20, order * wide * 36),
        name="plane_scan",
    )(place, rates, short, *ends)
    return got[0], got[1:]


def line_scan_body(place, rates, short, whole, *rest, share, rows, lines):
    befores = rest[:share]
    arrived = rest[share : share + lines]
    outs = rest[share + lines :]
    order = rates.shape[0]
    here = place[SPOT]
    rate = rates[...]
    planes = (whole,) + tuple(arrived)

    def last_rows(k):
        if k < lines:
            return planes[k + 1][order : order + LAST]
        return jnp.zeros((LAST, rate.shape[1]), jnp.float32)

    def first_share(k):
        return end_share(short, rate, planes[k][order + LAST :], last_rows(k), rows)

    state = jnp.zeros(rate.shape, jnp.float32)
    decay = jnp.exp(rate * (-1.0 * rows * share))
    later = jnp.exp(rate * (-1.0 * rows * (share - 1)))
    for k in reversed(range(1, lines + 1)):
        state = decay * state + planes[k][:order] + later * first_share(k)
    own = first_share(0)
    for j in range(share):
        at = (here ^ j).astype(jnp.float32)
        inside = jnp.minimum(at, 1.0)
        past = inside * jnp.exp(rate * (jnp.maximum(at - 1.0, 0.0) * (-1.0 * rows)))
        before = befores[j][:order]
        outs[j][:order] = before + jnp.exp(rate * (at * (-1.0 * rows))) * state + past * own
        outs[j][order:] = befores[j][order:] + (1.0 - inside) * last_rows(0)


def line_scan(place, rates, short, whole, befores, arrived, rows):
    share, lines = len(befores), len(arrived)
    order, wide = rates.shape[0], whole.shape[1]
    block = pl.BlockSpec((order + LAST, wide), lambda g, place: (0, 0))
    edged = pl.BlockSpec((order + LAST + FIRST, wide), lambda g, place: (0, 0))
    return pl.pallas_call(
        functools.partial(line_scan_body, share=share, rows=rows, lines=lines),
        grid_spec=pltpu.PrefetchScalarGridSpec(
            num_scalar_prefetch=1,
            grid=(1,),
            in_specs=[
                pl.BlockSpec((order, wide), lambda g, place: (0, place[SPOT])),
                pl.BlockSpec((3, 3, wide), lambda g, place: (0, 0, place[SPOT])),
                edged,
            ]
            + [block] * share
            + [edged] * lines,
            out_specs=[block] * share,
        ),
        out_shape=[jax.ShapeDtypeStruct((order + LAST, wide), jnp.float32)] * share,
        compiler_params=pltpu.CompilerParams(vmem_limit_bytes=SMALL_LIMIT),
        cost_estimate=estimate(order * wide * 20, order * wide * 36),
        name="line_scan",
    )(place, rates, short, whole, *befores, *arrived)


def hidden_body(place, query, top, short, rates, coef, skip, gated, prefix, *rest, seg_len, order, share, first):
    starts = rest[:share]
    hidden = rest[share]
    query_pos, result_pos, start_by_place = rest[share + 1 :]
    pitch = seg_len + 1
    groups = gated.shape[0]
    now_at = pl.program_id(0) + first
    segment = lax.broadcasted_iota(jnp.int32, (SEGS, LANES), 0).astype(jnp.float32)

    @pl.when(pl.program_id(0) == 0)
    def _():
        for j in range(share):
            start_by_place[place[SPOT] ^ j] = starts[j][...]

    for group in range(groups):
        lanes = slice(group * LANES, (group + 1) * LANES)
        ending = start_by_place[now_at, order : order + 2, lanes]
        lay_segments(query_pos, query, ending, seg_len, lanes, group)

    for group in range(groups):
        lanes = slice(group * LANES, (group + 1) * LANES)
        query_taps = taps(short, 0, lanes)
        gain = jnp.broadcast_to(skip[0:1, lanes], (SEGS, LANES))
        decay = [jnp.exp(-row(rates, r, lanes)) for r in range(order)]
        scale = [row(coef, r, lanes) for r in range(order)]
        first = jnp.concatenate([top[b, 0:2, lanes] for b in (1, 2)], axis=0).astype(jnp.float32)
        last = start_by_place[now_at, order:, lanes]
        early = [
            jnp.broadcast_to(value, (SEGS, LANES))
            for value in first_gated(short.at[:, :, lanes], first, last)
        ]
        states = []
        for r in range(order):
            rate = row(rates, r, lanes)
            ahead = jnp.exp(rate * (segment * (-1.0 * seg_len)))
            before = jnp.broadcast_to(start_by_place[now_at, r : r + 1, lanes], (SEGS, LANES))
            grown = jnp.exp(rate)
            before += jnp.where(segment >= 1.0, grown * (early[0] + grown * early[1]), 0.0)
            states.append(prefix[group, r] + ahead * before)

        def step(
            i, carry, late=None, group=group, query_taps=query_taps, gain=gain, decay=decay, scale=scale
        ):
            q1, q2, *states = carry
            q0 = strided(query_pos, group, TOP + i, pitch)
            now = gated[group, pl.ds(pl.multiple_of(i * SEGS, SEGS), SEGS), :]
            if late is not None:
                now = jnp.where(segment >= 1.0, now, late)
            states = [d * h + now for d, h in zip(decay, states)]
            sums = [s * h for s, h in zip(scale, states)] + [gain * now]
            while len(sums) > 1:
                sums = [a + b for a, b in zip(sums[::2], sums[1::2])] + sums[len(sums) // 2 * 2 :]
            query_now = query_taps[0] * q0 + query_taps[1] * q1 + query_taps[2] * q2
            result_pos[group, pl.ds(TOP + i, SEGS, stride=pitch), :] = query_now * sums[0]
            return (q0, q1, *states)

        start = (
            strided(query_pos, group, TOP - 2, pitch),
            strided(query_pos, group, TOP - 3, pitch),
        ) + tuple(states)
        start = step(1, step(0, start, early[0]), early[1])
        lax.fori_loop(2, seg_len, step, start, unroll=6)
        for s in range(SEGS):
            part = result_pos[group, TOP + s * pitch : TOP + s * pitch + seg_len, :]
            hidden[s * seg_len : (s + 1) * seg_len, lanes] = part.astype(hidden.dtype)


def hidden_rows(place, streams, short, rates, coef, skip, gated, prefix, starts, part):
    _, rows, chans = streams.shape
    order = rates.shape[0]
    share = len(starts)
    wide = chans // share
    groups = wide // LANES
    seg_len = rows // SEGS
    steps = max(1, share // 2)
    first = part * steps
    pos_rows = TOP + SEGS * (seg_len + 1)
    return pl.pallas_call(
        functools.partial(hidden_body, seg_len=seg_len, order=order, share=share, first=first),
        grid_spec=pltpu.PrefetchScalarGridSpec(
            num_scalar_prefetch=1,
            grid=(steps,),
            in_specs=[
                pl.BlockSpec((1, rows, wide), lambda g, place: (0, 0, first + g)),
                pl.BlockSpec((3, 16, wide), lambda g, place: (0, 0, first + g)),
                pl.BlockSpec((3, 3, wide), lambda g, place: (0, 0, first + g)),
                pl.BlockSpec((order, wide), lambda g, place: (0, first + g)),
                pl.BlockSpec((order, wide), lambda g, place: (0, first + g)),
                pl.BlockSpec((1, wide), lambda g, place: (0, first + g)),
                pl.BlockSpec((groups, rows, LANES), lambda g, place: (first + g, 0, 0)),
                pl.BlockSpec((groups, order, SEGS, LANES), lambda g, place: (first + g, 0, 0, 0)),
            ]
            + [pl.BlockSpec((order + LAST, wide), lambda g, place: (0, 0))] * share,
            out_specs=pl.BlockSpec((rows, wide), lambda g, place: (0, g)),
            scratch_shapes=[
                pltpu.VMEM((groups, pos_rows, LANES), jnp.float32),
                pltpu.VMEM((groups, pos_rows, LANES), jnp.float32),
                pltpu.VMEM((share, order + LAST, wide), jnp.float32),
            ],
        ),
        out_shape=jax.ShapeDtypeStruct((rows, steps * wide), jnp.bfloat16),
        compiler_params=pltpu.CompilerParams(vmem_limit_bytes=VMEM_LIMIT),
        cost_estimate=estimate(rows * chans * 40, rows * chans * 5),
        name="hidden_rows",
    )(place, streams, streams, short, rates, coef, skip, gated, prefix, *starts)


def project_body(place, *refs, rows_in, slots):
    kept, sent = refs[-2:]
    at = 0
    rows, blocks = [], []
    for group, counts in ((rows, rows_in), (blocks, slots)):
        for count in counts:
            group.append(refs[at : at + count])
            at += count
    width = kept.shape[1] * 2 // len(slots)

    def all_blocks(keeps, middle):
        for slot, given in enumerate(blocks):
            columns = given[0 if middle else -1]
            far, block = divmod(slot, len(slots) // 2)
            out = sent if far == keeps else kept
            top = 0
            for part in rows:
                total = 0.0
                start = 0
                for piece in part:
                    size, depth = piece.shape
                    total += jnp.dot(
                        piece[...], columns[start : start + depth, :], preferred_element_type=jnp.float32
                    )
                    start += depth
                out[top : top + size, block * width : (block + 1) * width] = total.astype(out.dtype)
                top += size

    for keeps in (0, 1):
        for middle in (0, 1):
            here = (place[KEEPS] == keeps) & (place[MIDDLE] == middle)
            pl.when(here)(functools.partial(all_blocks, keeps, middle))


def project(place, rows, slots):
    flat = [piece for part in rows for piece in part] + [block for slot in slots for block in slot]
    count = sum(part[0].shape[0] for part in rows)
    depth, width = slots[0][0].shape
    wide = len(slots) // 2 * width
    held = pl.BlockSpec(memory_space=pltpu.VMEM)
    return pl.pallas_call(
        functools.partial(project_body, rows_in=tuple(map(len, rows)), slots=tuple(map(len, slots))),
        in_specs=[pl.BlockSpec(memory_space=pltpu.SMEM)] + [held] * len(flat),
        out_specs=[held] * 2,
        out_shape=[jax.ShapeDtypeStruct((count, wide), jnp.bfloat16)] * 2,
        compiler_params=pltpu.CompilerParams(vmem_limit_bytes=VMEM_LIMIT),
        cost_estimate=estimate(
            2 * count * depth * len(slots) * width,
            2 * (count * depth + len(slots) * width * (depth + count)),
        ),
        name="project",
    )(place, *flat)


def assemble_body(place, *refs):
    parts, out = refs[:-1], refs[-1]
    width = parts[0].shape[1]
    for j, part in enumerate(parts):
        column = pl.multiple_of((place[SPOT] ^ j) * width, LANES)
        out[:, pl.ds(column, width)] = part[...]


def assemble(place, parts, blocks, width):
    share = len(parts)
    rows = parts[0].shape[0]
    return pl.pallas_call(
        assemble_body,
        grid_spec=pltpu.PrefetchScalarGridSpec(
            num_scalar_prefetch=1,
            grid=(blocks,),
            in_specs=[pl.BlockSpec((rows, width), lambda b, place: (0, b ^ place[ODD]))] * share,
            out_specs=pl.BlockSpec((rows, share * width), lambda b, place: (0, b)),
        ),
        out_shape=jax.ShapeDtypeStruct((rows, share * blocks * width), jnp.bfloat16),
        compiler_params=pltpu.CompilerParams(vmem_limit_bytes=VMEM_LIMIT),
        cost_estimate=estimate(0, 4 * rows * share * blocks * width),
        name="assemble",
    )(place, *parts)


def after(value, *others):
    return lax.optimization_barrier((value, *others))[0]


def send_planes(value, group, moves):
    pairs = [(a * group + e, b * group + e) for a, b in moves for e in range(group)]
    return lax.ppermute(value, "ctx", pairs)


def plane_rows(hidden, count, group):
    if group != 4:
        return [hidden] + [[send_xor(part, count, group, j) for part in hidden] for j in range(1, group)]
    first, second = hidden
    first_1 = send_xor(first, count, group, 1)
    first_2 = send_xor(first, count, group, 2)
    second_2 = send_xor(after(second, first_2), count, group, 2)
    second_1 = send_xor(after(second, first_1), count, group, 1)
    first_3 = send_xor(first_1, count, group, 2)
    second_3 = send_xor(second_2, count, group, 1)
    return [[first, second], [first_1, second_1], [first_2, second_2], [first_3, second_3]]


def add_up_body(a, b, *outs):
    size = outs[0].shape[0]
    for j, out in enumerate(outs):
        rows = slice(j * size, (j + 1) * size)
        out[...] = (a[rows].astype(jnp.float32) + b[rows].astype(jnp.float32)).astype(out.dtype)


def add_up(a, b, parts):
    size, width = a.shape[0] // parts, a.shape[1]
    held = pl.BlockSpec(memory_space=pltpu.VMEM)
    return pl.pallas_call(
        add_up_body,
        in_specs=[held, held],
        out_specs=[held] * parts,
        out_shape=[jax.ShapeDtypeStruct((size, width), a.dtype)] * parts,
        compiler_params=pltpu.CompilerParams(vmem_limit_bytes=VMEM_LIMIT),
        cost_estimate=estimate(parts * size * width, 6 * parts * size * width),
        name="add_up",
    )(a, b)


def project_4x4(place, out_weight, whole, states, hidden, count):
    group = 4
    swap = [(0, 1), (1, 0), (2, 3), (3, 2)]
    inner = [(1, 2), (2, 1)]
    outward = [(1, 0), (2, 3)]
    rows = plane_rows(hidden, count, group)
    own = out_weight
    by_1 = send_planes(own, group, swap)
    by_3_inner = send_planes(own, group, inner)
    by_2_inner = send_planes(after(by_1, whole, by_3_inner), group, inner)
    by_2_outer = send_planes(after(by_3_inner, whole), group, outward)
    by_3_outer = send_planes(after(own, states), group, [(0, 3), (3, 0)])
    blocks = [[own], [by_1], [by_2_inner, by_2_outer], [by_3_inner, by_3_outer]]

    def to_other(value):
        return lax.ppermute(value, "tp", [(0, 1), (1, 0)])

    kept, sent = project(place, rows[:3], blocks)
    taken = to_other(sent)
    last_kept, last_sent = project(place, rows[3:], blocks)
    last = add_up(last_kept, to_other(last_sent), 1)
    mixed = [*add_up(after(kept, *last), taken, 3), *last]
    mixed = [mixed[0]] + [send_xor(mixed[j], count, group, j) for j in range(1, group)]
    return assemble(place, mixed, 2, out_weight.shape[1])


def project_any(out_weight, states, hidden, count):
    halves = lax.axis_size("tp")
    group = split_of(count)
    outer = count // group
    plane = lax.axis_index("ctx") // group
    size = hidden[0].shape[0]
    depth, width = out_weight.shape
    below, above = [out_weight], [out_weight]
    for k in range(1, outer):
        down, up = below[-1], above[-1]
        if k == 2:
            down, up = after(down, states), after(up, states)
        below.append(send_along(down, count, group, 1, k - 1))
        above.append(send_along(up, count, group, -1, k - 1))
    line = below[:0:-1] + above
    cols = lax.dynamic_slice_in_dim(jnp.stack(line), outer - 1 - plane, outer, 0)
    cols = jnp.moveaxis(cols, 0, 1).reshape(depth, outer * width)
    rows = plane_rows(hidden, count, group)
    held = jnp.concatenate([jnp.concatenate(part, axis=1) for part in rows], axis=0)
    partial = jnp.dot(held, cols, preferred_element_type=jnp.float32).astype(jnp.bfloat16)
    mixed = lax.psum_scatter(partial, "tp", scatter_dimension=1, tiled=True)
    mixed = jnp.split(mixed, group)
    mixed = [mixed[0]] + [send_xor(mixed[j], count, group, j) for j in range(1, group)]
    blocks = outer // halves
    stacked = jnp.stack(mixed).reshape(group, size, blocks, width)
    by_place = jnp.take(stacked, jnp.arange(group) ^ (lax.axis_index("ctx") % group), axis=0)
    return jnp.moveaxis(by_place, 0, 2).reshape(size, blocks * group * width)


def per_device(projected, short_filter, residues, rates, skip_gain, out_weight):
    count = lax.axis_size("ctx")
    halves = lax.axis_size("tp")
    here = lax.axis_index("ctx")
    rows, _, chans = projected.shape

    streams = jnp.transpose(projected, (1, 0, 2))
    rates_t = rates.T
    coef_t = (residues * jnp.sqrt(-jnp.expm1(-2.0 * rates))).T

    share = min(split_of(count), chans // LANES, 4)
    lines = count // share
    plane = here // share
    keeps = lax.axis_index("tp") == plane // 2
    place = jnp.stack([here % share, (plane == 1) | (plane == 2), keeps, plane % 2]).astype(jnp.int32)
    *ends, gated, prefix = local_scan(place, streams, short_filter, rates_t, share)
    ends = [ends[0]] + [send_xor(ends[j], count, share, j) for j in range(1, share)]
    whole, befores = plane_scan(place, rates_t, short_filter, ends, rows)
    arrived = [send_along(whole, count, share, k) for k in range(1, lines)]
    starts = line_scan(place, rates_t, short_filter, whole, befores, arrived, rows)
    states = starts[0]
    starts = [starts[0]] + [send_xor(starts[j], count, share, j) for j in range(1, share)]
    hidden = [
        hidden_rows(
            place, streams, short_filter, rates_t, coef_t, skip_gain[None], gated, prefix, starts, part
        )
        for part in range(2)
    ]
    if count == 16 and halves == 2 and out_weight.shape[1] % LANES == 0:
        return project_4x4(place, out_weight, whole, states, hidden, count)
    return project_any(out_weight, states, hidden, count)


def solution(mesh):
    return jax.shard_map(
        per_device,
        mesh=mesh,
        in_specs=(
            P("ctx", None, "tp"),
            P(None, None, "tp"),
            P("tp", None),
            P("tp", None),
            P("tp"),
            P("tp", "ctx"),
        ),
        out_specs=P("ctx", "tp"),
        check_vma=False,
    )
```

```python
import functools

import jax
import jax.numpy as jnp
from jax import lax
from jax.experimental import pallas as pl
from jax.experimental.pallas import tpu as pltpu
from jax.sharding import PartitionSpec as P

LANES = 128
SEGS = 8
TOP = 8
SPOT, MIDDLE, KEEPS, ODD = range(4)
VMEM_LIMIT = 16 * 1024 * 1024
SMALL_LIMIT = 4 * 1024 * 1024
WHOLE_LIMIT = 50 * 1024 * 1024


def split_of(count):
    inner = 1
    while (2 * inner) ** 2 <= count and count % (2 * inner) == 0:
        inner *= 2
    return inner


def send_xor(value, count, group, step):
    pairs = [(p, p - p % group + ((p % group) ^ step)) for p in range(count)]
    return lax.ppermute(value, "ctx", pairs)


def send_along(value, count, group, steps, first=0):
    outer = count // group
    pairs = []
    for z in range(outer):
        if not 0 <= z + steps < outer:
            continue
        if (steps > 0 and z < first) or (steps < 0 and z > outer - 1 - first):
            continue
        pairs += [(z * group + e, (z + steps) * group + e) for e in range(group)]
    return lax.ppermute(value, "ctx", pairs)


def estimate(flops, bytes_accessed, transcendentals=0):
    return pl.CostEstimate(flops=flops, bytes_accessed=bytes_accessed, transcendentals=transcendentals)


def row(ref, r, lanes):
    return jnp.broadcast_to(ref[r : r + 1, lanes], (SEGS, LANES))


def lay_segments(dst, stream, halo, seg_len, lanes, group):
    pitch = seg_len + 1
    for s in range(SEGS):
        part = stream[0, s * seg_len : (s + 1) * seg_len, lanes].astype(jnp.float32)
        dst[group, TOP + s * pitch : TOP + s * pitch + seg_len, :] = part
    dst[group, TOP - 3 : TOP - 1, :] = jnp.zeros((2, LANES), jnp.float32) if halo is None else halo


def taps(short, stream, lanes):
    return [jnp.broadcast_to(short[i, stream : stream + 1, lanes], (SEGS, LANES)) for i in range(3)]


def strided(ref, group, start, pitch):
    return ref[group, pl.ds(start, SEGS, stride=pitch), :]


LAST, FIRST = 6, 4


def first_gated(short, first, last):
    products = []
    for b, stream in enumerate((1, 2)):
        tap = [short[i, stream : stream + 1, :] for i in range(3)]
        now_0, now_1 = first[2 * b : 2 * b + 1], first[2 * b + 1 : 2 * b + 2]
        old_2, old_1 = last[2 * stream : 2 * stream + 1], last[2 * stream + 1 : 2 * stream + 2]
        products.append(
            (
                tap[0] * now_0 + tap[1] * old_1 + tap[2] * old_2,
                tap[0] * now_1 + tap[1] * now_0 + tap[2] * old_1,
            )
        )
    return products[0][0] * products[1][0], products[0][1] * products[1][1]


def end_share(short, rates, first, last, rows):
    gated_0, gated_1 = first_gated(short, first, last)
    return jnp.exp(rates * (1.0 - rows)) * gated_0 + jnp.exp(rates * (2.0 - rows)) * gated_1


def local_scan_body(place, streams, short_all, rates_all, *rest, seg_len, order, share):
    ends = rest[:share]
    gated, prefix = rest[share : share + 2]
    key_pos, value_pos, end_now, held, query_held, short_held, rates_held, held_sem, small_sem = rest[share + 2 :]
    now_at = pl.program_id(0)
    wide = end_now.shape[1]
    small = [
        pltpu.make_async_copy(short_all, short_held, small_sem.at[0]),
        pltpu.make_async_copy(rates_all, rates_held, small_sem.at[1]),
        pltpu.make_async_copy(
            streams.at[0, pl.ds(seg_len * SEGS - 16, 16), :], query_held, small_sem.at[2]
        ),
    ]

    def stream_copy(at):
        columns = pl.ds(at * wide, wide)
        return pltpu.make_async_copy(
            streams.at[pl.ds(1, 2), :, columns], held.at[:, :, columns], held_sem.at[at]
        )

    @pl.when(now_at == 0)
    def _():
        stream_copy(0).start()
        for copy in small:
            copy.start()
        for at in range(1, share):
            stream_copy(at).start()
        for copy in small:
            copy.wait()

    for at in range(share):

        @pl.when(now_at == at)
        def _(at=at):
            stream_copy(at).wait()

    columns = pl.ds(pl.multiple_of(now_at * wide, LANES), wide)
    key = held.at[pl.ds(0, 1), :, columns]
    value = held.at[pl.ds(1, 1), :, columns]
    short = short_held.at[:, :, columns]
    rates = rates_held.at[:, columns]
    pitch = seg_len + 1
    groups = gated.shape[0]
    segment = lax.broadcasted_iota(jnp.int32, (SEGS, LANES), 0)
    for group in range(groups):
        lanes = slice(group * LANES, (group + 1) * LANES)
        lay_segments(key_pos, key, None, seg_len, lanes, group)
        lay_segments(value_pos, value, None, seg_len, lanes, group)
    bottom = seg_len * SEGS - 2
    end_now[order : order + 2, :] = query_held[14:16, columns].astype(jnp.float32)
    for b, stream in enumerate((key, value)):
        at = order + 2 + 2 * b
        end_now[at : at + 2, :] = stream[0, bottom : bottom + 2, :].astype(jnp.float32)
        at = order + LAST + 2 * b
        end_now[at : at + 2, :] = stream[0, 0:2, :].astype(jnp.float32)

    for group in range(groups):
        lanes = slice(group * LANES, (group + 1) * LANES)
        key_taps = taps(short, 1, lanes)
        value_taps = taps(short, 2, lanes)
        decay = [jnp.exp(-row(rates, r, lanes)) for r in range(order)]

        def step(i, carry, early=False, group=group, key_taps=key_taps, value_taps=value_taps, decay=decay):
            k1, k2, v1, v2, *states = carry
            k0 = strided(key_pos, group, TOP + i, pitch)
            v0 = strided(value_pos, group, TOP + i, pitch)
            key_now = key_taps[0] * k0 + key_taps[1] * k1 + key_taps[2] * k2
            value_now = value_taps[0] * v0 + value_taps[1] * v1 + value_taps[2] * v2
            now = key_now * value_now
            if early:
                now = jnp.where(segment >= 1, now, 0.0)
            gated[group, pl.ds(pl.multiple_of(i * SEGS, SEGS), SEGS), :] = now
            states = [d * h + now for d, h in zip(decay, states)]
            return (k0, k1, v0, v1, *states)

        zero = jnp.zeros((SEGS, LANES), jnp.float32)
        start = (
            strided(key_pos, group, TOP - 2, pitch),
            strided(key_pos, group, TOP - 3, pitch),
            strided(value_pos, group, TOP - 2, pitch),
            strided(value_pos, group, TOP - 3, pitch),
        ) + (zero,) * order
        start = step(1, step(0, start, True), True)
        states = lax.fori_loop(2, seg_len, step, start, unroll=6)[4:]
        for r in range(order):
            rate = row(rates, r, lanes)
            scan = states[r]
            for d in (1, 2, 4):
                moved = jnp.where(segment >= d, pltpu.roll(scan, d, 0), 0.0)
                scan = scan + jnp.exp(rate * (-1.0 * d * seg_len)) * moved
            prefix[group, r] = jnp.where(segment >= 1, pltpu.roll(scan, 1, 0), 0.0)
            end_now[r : r + 1, lanes] = scan[SEGS - 1 :, :]

    for j in range(share):

        @pl.when((pl.program_id(0) ^ place[SPOT]) == j)
        def _(j=j):
            ends[j][...] = end_now[...]


def local_scan(place, streams, short, rates, share):
    _, rows, chans = streams.shape
    order = rates.shape[0]
    wide = chans // share
    groups = wide // LANES
    seg_len = rows // SEGS
    pos_rows = TOP + SEGS * (seg_len + 1)
    end_shape = jax.ShapeDtypeStruct((order + LAST + FIRST, wide), jnp.float32)
    return pl.pallas_call(
        functools.partial(local_scan_body, seg_len=seg_len, order=order, share=share),
        grid_spec=pltpu.PrefetchScalarGridSpec(
            num_scalar_prefetch=1,
            grid=(share,),
            in_specs=[
                pl.BlockSpec(memory_space=pltpu.HBM),
                pl.BlockSpec(memory_space=pltpu.HBM),
                pl.BlockSpec(memory_space=pltpu.HBM),
            ],
            out_specs=[pl.BlockSpec((order + LAST + FIRST, wide), lambda g, place: (0, 0))] * share
            + [
                pl.BlockSpec((groups, rows, LANES), lambda g, place: (g, 0, 0)),
                pl.BlockSpec((groups, order, SEGS, LANES), lambda g, place: (g, 0, 0, 0)),
            ],
            scratch_shapes=[
                pltpu.VMEM((groups, pos_rows, LANES), jnp.float32),
                pltpu.VMEM((groups, pos_rows, LANES), jnp.float32),
                pltpu.VMEM((order + LAST + FIRST, wide), jnp.float32),
                pltpu.VMEM((2, rows, chans), streams.dtype),
                pltpu.VMEM((16, chans), streams.dtype),
                pltpu.VMEM(short.shape, jnp.float32),
                pltpu.VMEM(rates.shape, jnp.float32),
                pltpu.SemaphoreType.DMA((share,)),
                pltpu.SemaphoreType.DMA((3,)),
            ],
        ),
        out_shape=[end_shape] * share
        + [
            jax.ShapeDtypeStruct((chans // LANES, rows, LANES), jnp.float32),
            jax.ShapeDtypeStruct((chans // LANES, order, SEGS, LANES), jnp.float32),
        ],
        compiler_params=pltpu.CompilerParams(vmem_limit_bytes=WHOLE_LIMIT),
        cost_estimate=estimate(rows * chans * 50, rows * chans * 10),
        name="local_scan",
    )(place, streams, short, rates)


def plane_scan_body(place, rates, short, *rest, share, rows):
    ends = rest[:share]
    whole = rest[share]
    befores = rest[share + 1 : 2 * share + 1]
    by_place, before_place = rest[2 * share + 1 :]
    order = rates.shape[0]
    here = place[SPOT]
    for j in range(share):
        by_place[here ^ j] = ends[j][...]
    rate = rates[...]
    decay = jnp.exp(rate * (-1.0 * rows))
    state = jnp.zeros(rate.shape, jnp.float32)
    for at in range(share):
        before_place[at, :order] = state
        state = decay * state + by_place[at, :order]
        if at > 0:
            last = by_place[at - 1, order : order + LAST]
            before_place[at, order:] = last
            state += end_share(short, rate, by_place[at, order + LAST :], last, rows)
    before_place[0, order:] = jnp.zeros((LAST, rate.shape[1]), jnp.float32)
    whole[:order] = state
    whole[order : order + LAST] = by_place[share - 1, order : order + LAST]
    whole[order + LAST :] = by_place[0, order + LAST :]
    for j in range(share):
        befores[j][...] = before_place[here ^ j]


def plane_scan(place, rates, short, ends, rows):
    share = len(ends)
    order = rates.shape[0]
    wide = ends[0].shape[1]
    block = pl.BlockSpec((order + LAST, wide), lambda g, place: (0, 0))
    edged = pl.BlockSpec((order + LAST + FIRST, wide), lambda g, place: (0, 0))
    shape = jax.ShapeDtypeStruct((order + LAST, wide), jnp.float32)
    got = pl.pallas_call(
        functools.partial(plane_scan_body, share=share, rows=rows),
        grid_spec=pltpu.PrefetchScalarGridSpec(
            num_scalar_prefetch=1,
            grid=(1,),
            in_specs=[
                pl.BlockSpec((order, wide), lambda g, place: (0, place[SPOT])),
                pl.BlockSpec((3, 3, wide), lambda g, place: (0, 0, place[SPOT])),
            ]
            + [edged] * share,
            out_specs=[edged] + [block] * share,
            scratch_shapes=[
                pltpu.VMEM((share, order + LAST + FIRST, wide), jnp.float32),
                pltpu.VMEM((share, order + LAST, wide), jnp.float32),
            ],
        ),
        out_shape=[jax.ShapeDtypeStruct((order + LAST + FIRST, wide), jnp.float32)] + [shape] * share,
        compiler_params=pltpu.CompilerParams(vmem_limit_bytes=SMALL_LIMIT),
        cost_estimate=estimate(order * wide * 20, order * wide * 36),
        name="plane_scan",
    )(place, rates, short, *ends)
    return got[0], got[1:]


def line_scan_body(place, rates, short, whole, *rest, share, rows, lines):
    befores = rest[:share]
    arrived = rest[share : share + lines]
    outs = rest[share + lines :]
    order = rates.shape[0]
    here = place[SPOT]
    rate = rates[...]
    planes = (whole,) + tuple(arrived)

    def last_rows(k):
        if k < lines:
            return planes[k + 1][order : order + LAST]
        return jnp.zeros((LAST, rate.shape[1]), jnp.float32)

    def first_share(k):
        return end_share(short, rate, planes[k][order + LAST :], last_rows(k), rows)

    state = jnp.zeros(rate.shape, jnp.float32)
    decay = jnp.exp(rate * (-1.0 * rows * share))
    later = jnp.exp(rate * (-1.0 * rows * (share - 1)))
    for k in reversed(range(1, lines + 1)):
        state = decay * state + planes[k][:order] + later * first_share(k)
    own = first_share(0)
    for j in range(share):
        at = (here ^ j).astype(jnp.float32)
        inside = jnp.minimum(at, 1.0)
        past = inside * jnp.exp(rate * (jnp.maximum(at - 1.0, 0.0) * (-1.0 * rows)))
        before = befores[j][:order]
        outs[j][:order] = before + jnp.exp(rate * (at * (-1.0 * rows))) * state + past * own
        outs[j][order:] = befores[j][order:] + (1.0 - inside) * last_rows(0)


def line_scan(place, rates, short, whole, befores, arrived, rows):
    share, lines = len(befores), len(arrived)
    order, wide = rates.shape[0], whole.shape[1]
    block = pl.BlockSpec((order + LAST, wide), lambda g, place: (0, 0))
    edged = pl.BlockSpec((order + LAST + FIRST, wide), lambda g, place: (0, 0))
    return pl.pallas_call(
        functools.partial(line_scan_body, share=share, rows=rows, lines=lines),
        grid_spec=pltpu.PrefetchScalarGridSpec(
            num_scalar_prefetch=1,
            grid=(1,),
            in_specs=[
                pl.BlockSpec((order, wide), lambda g, place: (0, place[SPOT])),
                pl.BlockSpec((3, 3, wide), lambda g, place: (0, 0, place[SPOT])),
                edged,
            ]
            + [block] * share
            + [edged] * lines,
            out_specs=[block] * share,
        ),
        out_shape=[jax.ShapeDtypeStruct((order + LAST, wide), jnp.float32)] * share,
        compiler_params=pltpu.CompilerParams(vmem_limit_bytes=SMALL_LIMIT),
        cost_estimate=estimate(order * wide * 20, order * wide * 36),
        name="line_scan",
    )(place, rates, short, whole, *befores, *arrived)


def hidden_body(place, query, top, short, rates, coef, skip, gated, prefix, *rest, seg_len, order, share, first):
    starts = rest[:share]
    hidden = rest[share]
    query_pos, result_pos, start_by_place = rest[share + 1 :]
    pitch = seg_len + 1
    groups = gated.shape[0]
    now_at = pl.program_id(0) + first
    segment = lax.broadcasted_iota(jnp.int32, (SEGS, LANES), 0).astype(jnp.float32)

    @pl.when(pl.program_id(0) == 0)
    def _():
        for j in range(share):
            start_by_place[place[SPOT] ^ j] = starts[j][...]

    for group in range(groups):
        lanes = slice(group * LANES, (group + 1) * LANES)
        ending = start_by_place[now_at, order : order + 2, lanes]
        lay_segments(query_pos, query, ending, seg_len, lanes, group)

    for group in range(groups):
        lanes = slice(group * LANES, (group + 1) * LANES)
        query_taps = taps(short, 0, lanes)
        gain = jnp.broadcast_to(skip[0:1, lanes], (SEGS, LANES))
        decay = [jnp.exp(-row(rates, r, lanes)) for r in range(order)]
        scale = [row(coef, r, lanes) for r in range(order)]
        first = jnp.concatenate([top[b, 0:2, lanes] for b in (1, 2)], axis=0).astype(jnp.float32)
        last = start_by_place[now_at, order:, lanes]
        early = [
            jnp.broadcast_to(value, (SEGS, LANES))
            for value in first_gated(short.at[:, :, lanes], first, last)
        ]
        states = []
        for r in range(order):
            rate = row(rates, r, lanes)
            ahead = jnp.exp(rate * (segment * (-1.0 * seg_len)))
            before = jnp.broadcast_to(start_by_place[now_at, r : r + 1, lanes], (SEGS, LANES))
            grown = jnp.exp(rate)
            before += jnp.where(segment >= 1.0, grown * (early[0] + grown * early[1]), 0.0)
            states.append(prefix[group, r] + ahead * before)

        def step(
            i, carry, late=None, group=group, query_taps=query_taps, gain=gain, decay=decay, scale=scale
        ):
            q1, q2, *states = carry
            q0 = strided(query_pos, group, TOP + i, pitch)
            now = gated[group, pl.ds(pl.multiple_of(i * SEGS, SEGS), SEGS), :]
            if late is not None:
                now = jnp.where(segment >= 1.0, now, late)
            states = [d * h + now for d, h in zip(decay, states)]
            sums = [s * h for s, h in zip(scale, states)] + [gain * now]
            while len(sums) > 1:
                sums = [a + b for a, b in zip(sums[::2], sums[1::2])] + sums[len(sums) // 2 * 2 :]
            query_now = query_taps[0] * q0 + query_taps[1] * q1 + query_taps[2] * q2
            result_pos[group, pl.ds(TOP + i, SEGS, stride=pitch), :] = query_now * sums[0]
            return (q0, q1, *states)

        start = (
            strided(query_pos, group, TOP - 2, pitch),
            strided(query_pos, group, TOP - 3, pitch),
        ) + tuple(states)
        start = step(1, step(0, start, early[0]), early[1])
        lax.fori_loop(2, seg_len, step, start, unroll=6)
        for s in range(SEGS):
            part = result_pos[group, TOP + s * pitch : TOP + s * pitch + seg_len, :]
            hidden[s * seg_len : (s + 1) * seg_len, lanes] = part.astype(hidden.dtype)


def hidden_rows(place, streams, short, rates, coef, skip, gated, prefix, starts, part):
    _, rows, chans = streams.shape
    order = rates.shape[0]
    share = len(starts)
    wide = chans // share
    groups = wide // LANES
    seg_len = rows // SEGS
    steps = max(1, share // 2)
    first = part * steps
    pos_rows = TOP + SEGS * (seg_len + 1)
    return pl.pallas_call(
        functools.partial(hidden_body, seg_len=seg_len, order=order, share=share, first=first),
        grid_spec=pltpu.PrefetchScalarGridSpec(
            num_scalar_prefetch=1,
            grid=(steps,),
            in_specs=[
                pl.BlockSpec((1, rows, wide), lambda g, place: (0, 0, first + g)),
                pl.BlockSpec((3, 16, wide), lambda g, place: (0, 0, first + g)),
                pl.BlockSpec((3, 3, wide), lambda g, place: (0, 0, first + g)),
                pl.BlockSpec((order, wide), lambda g, place: (0, first + g)),
                pl.BlockSpec((order, wide), lambda g, place: (0, first + g)),
                pl.BlockSpec((1, wide), lambda g, place: (0, first + g)),
                pl.BlockSpec((groups, rows, LANES), lambda g, place: (first + g, 0, 0)),
                pl.BlockSpec((groups, order, SEGS, LANES), lambda g, place: (first + g, 0, 0, 0)),
            ]
            + [pl.BlockSpec((order + LAST, wide), lambda g, place: (0, 0))] * share,
            out_specs=pl.BlockSpec((rows, wide), lambda g, place: (0, g)),
            scratch_shapes=[
                pltpu.VMEM((groups, pos_rows, LANES), jnp.float32),
                pltpu.VMEM((groups, pos_rows, LANES), jnp.float32),
                pltpu.VMEM((share, order + LAST, wide), jnp.float32),
            ],
        ),
        out_shape=jax.ShapeDtypeStruct((rows, steps * wide), jnp.bfloat16),
        compiler_params=pltpu.CompilerParams(vmem_limit_bytes=VMEM_LIMIT),
        cost_estimate=estimate(rows * chans * 40, rows * chans * 5),
        name="hidden_rows",
    )(place, streams, streams, short, rates, coef, skip, gated, prefix, *starts)


def times_into(rows, columns, out, column):
    width = columns.shape[1]
    top = 0
    for part in rows:
        total = 0.0
        start = 0
        for piece in part:
            size, depth = piece.shape
            total += jnp.dot(
                piece[...], columns[start : start + depth, :], preferred_element_type=jnp.float32
            )
            start += depth
        out[top : top + size, column : column + width] = total.astype(out.dtype)
        top += size


def operands(refs, rows_in, slots):
    at = 0
    rows, blocks = [], []
    for group, counts in ((rows, rows_in), (blocks, slots)):
        for count in counts:
            group.append(refs[at : at + count])
            at += count
    return rows, blocks


def near_body(place, *refs, rows_in, slots):
    near, far_first = refs[-2:]
    rows, blocks = operands(refs, rows_in, slots)
    width = far_first.shape[1]

    def all_blocks(middle):
        for slot, given in enumerate(blocks):
            out, column = (near, slot * width) if slot < 2 else (far_first, 0)
            times_into(rows, given[0 if middle else -1], out, column)

    for middle in (0, 1):
        pl.when(place[MIDDLE] == middle)(functools.partial(all_blocks, middle))


def project_body(place, *refs, rows_in, slots):
    near, far_first, kept, sent = refs[-4:]
    rows, blocks = operands(refs, rows_in, slots)
    made, width = far_first.shape

    def all_blocks(keeps, middle):
        outs = (kept, sent) if keeps else (sent, kept)
        outs[0][:made] = near[...]
        outs[1][:made, :width] = far_first[...]
        columns = [given[0 if middle else -1] for given in blocks]
        for slot, block in enumerate(columns):
            far, at = divmod(slot, 2)
            times_into(rows[-1:], block, outs[far].at[pl.ds(made, outs[far].shape[0] - made)], at * width)
        times_into(rows[:-1], columns[3], outs[1], width)

    for keeps in (0, 1):
        for middle in (0, 1):
            here = (place[KEEPS] == keeps) & (place[MIDDLE] == middle)
            pl.when(here)(functools.partial(all_blocks, keeps, middle))


def project(place, rows, slots, made=None):
    flat = [piece for part in rows for piece in part] + [block for slot in slots for block in slot]
    flat += [] if made is None else list(made)
    count = sum(part[0].shape[0] for part in rows)
    depth, width = slots[0][0].shape
    widths = (2 * width, width) if len(slots) == 3 else (2 * width, 2 * width)
    held = pl.BlockSpec(memory_space=pltpu.VMEM)
    return pl.pallas_call(
        functools.partial(
            near_body if len(slots) == 3 else project_body,
            rows_in=tuple(map(len, rows)),
            slots=tuple(map(len, slots)),
        ),
        in_specs=[pl.BlockSpec(memory_space=pltpu.SMEM)] + [held] * len(flat),
        out_specs=[held] * 2,
        out_shape=[jax.ShapeDtypeStruct((count, wide), jnp.bfloat16) for wide in widths],
        compiler_params=pltpu.CompilerParams(vmem_limit_bytes=VMEM_LIMIT),
        cost_estimate=estimate(
            2 * count * depth * len(slots) * width,
            2 * (count * depth + len(slots) * width * (depth + count)),
        ),
        name="project",
    )(place, *flat)


def assemble_body(place, *refs):
    parts, out = refs[:-1], refs[-1]
    width = parts[0].shape[1]
    for j, part in enumerate(parts):
        column = pl.multiple_of((place[SPOT] ^ j) * width, LANES)
        out[:, pl.ds(column, width)] = part[...]


def assemble(place, parts, blocks, width):
    share = len(parts)
    rows = parts[0].shape[0]
    return pl.pallas_call(
        assemble_body,
        grid_spec=pltpu.PrefetchScalarGridSpec(
            num_scalar_prefetch=1,
            grid=(blocks,),
            in_specs=[pl.BlockSpec((rows, width), lambda b, place: (0, b ^ place[ODD]))] * share,
            out_specs=pl.BlockSpec((rows, share * width), lambda b, place: (0, b)),
        ),
        out_shape=jax.ShapeDtypeStruct((rows, share * blocks * width), jnp.bfloat16),
        compiler_params=pltpu.CompilerParams(vmem_limit_bytes=VMEM_LIMIT),
        cost_estimate=estimate(0, 4 * rows * share * blocks * width),
        name="assemble",
    )(place, *parts)


def after(value, *others):
    return lax.optimization_barrier((value, *others))[0]


def send_planes(value, group, moves):
    pairs = [(a * group + e, b * group + e) for a, b in moves for e in range(group)]
    return lax.ppermute(value, "ctx", pairs)


def plane_rows(hidden, count, group):
    if group != 4:
        return [hidden] + [[send_xor(part, count, group, j) for part in hidden] for j in range(1, group)]
    first, second = hidden
    first_1 = send_xor(first, count, group, 1)
    first_2 = send_xor(first, count, group, 2)
    second_2 = send_xor(second, count, group, 2)
    second_1 = send_xor(second, count, group, 1)
    first_3 = send_xor(first_1, count, group, 2)
    second_3 = send_xor(second_2, count, group, 1)
    return [[first, second], [first_1, second_1], [first_2, second_2], [first_3, second_3]]


def add_up_body(a, b, *outs):
    size = outs[0].shape[0]
    for j, out in enumerate(outs):
        rows = slice(j * size, (j + 1) * size)
        out[...] = (a[rows].astype(jnp.float32) + b[rows].astype(jnp.float32)).astype(out.dtype)


def add_up(a, b, parts):
    size, width = a.shape[0] // parts, a.shape[1]
    held = pl.BlockSpec(memory_space=pltpu.VMEM)
    return pl.pallas_call(
        add_up_body,
        in_specs=[held, held],
        out_specs=[held] * parts,
        out_shape=[jax.ShapeDtypeStruct((size, width), a.dtype)] * parts,
        compiler_params=pltpu.CompilerParams(vmem_limit_bytes=VMEM_LIMIT),
        cost_estimate=estimate(parts * size * width, 6 * parts * size * width),
        name="add_up",
    )(a, b)


def project_4x4(place, out_weight, states, hidden, count):
    group = 4
    swap = [(0, 1), (1, 0), (2, 3), (3, 2)]
    inner = [(1, 2), (2, 1)]
    outward = [(1, 0), (2, 3)]
    rows = plane_rows(hidden, count, group)
    own = out_weight
    by_1 = send_planes(own, group, swap)
    by_3_inner = send_planes(own, group, inner)
    by_2_inner = send_planes(after(by_1, states, by_3_inner), group, inner)
    by_2_outer = send_planes(after(by_3_inner, states), group, outward)
    by_3_outer = send_planes(after(by_2_inner, by_2_outer, rows[1][0], rows[2][0], hidden[1]), group, outward)
    blocks = [[own], [by_1], [by_2_inner, by_2_outer], [by_3_inner, by_3_outer]]

    made = project(place, rows[:3], blocks[:3])
    kept, sent = project(place, rows, blocks, made)
    mixed = add_up(kept, lax.ppermute(sent, "tp", [(0, 1), (1, 0)]), group)
    mixed = [mixed[0]] + [send_xor(mixed[j], count, group, j) for j in range(1, group)]
    return assemble(place, mixed, 2, out_weight.shape[1])


def project_any(out_weight, states, hidden, count):
    halves = lax.axis_size("tp")
    group = split_of(count)
    outer = count // group
    plane = lax.axis_index("ctx") // group
    size = hidden[0].shape[0]
    depth, width = out_weight.shape
    below, above = [out_weight], [out_weight]
    for k in range(1, outer):
        down, up = below[-1], above[-1]
        if k == 2:
            down, up = after(down, states), after(up, states)
        below.append(send_along(down, count, group, 1, k - 1))
        above.append(send_along(up, count, group, -1, k - 1))
    line = below[:0:-1] + above
    cols = lax.dynamic_slice_in_dim(jnp.stack(line), outer - 1 - plane, outer, 0)
    cols = jnp.moveaxis(cols, 0, 1).reshape(depth, outer * width)
    rows = plane_rows(hidden, count, group)
    held = jnp.concatenate([jnp.concatenate(part, axis=1) for part in rows], axis=0)
    partial = jnp.dot(held, cols, preferred_element_type=jnp.float32).astype(jnp.bfloat16)
    mixed = lax.psum_scatter(partial, "tp", scatter_dimension=1, tiled=True)
    mixed = jnp.split(mixed, group)
    mixed = [mixed[0]] + [send_xor(mixed[j], count, group, j) for j in range(1, group)]
    blocks = outer // halves
    stacked = jnp.stack(mixed).reshape(group, size, blocks, width)
    by_place = jnp.take(stacked, jnp.arange(group) ^ (lax.axis_index("ctx") % group), axis=0)
    return jnp.moveaxis(by_place, 0, 2).reshape(size, blocks * group * width)


def per_device(projected, short_filter, residues, rates, skip_gain, out_weight):
    count = lax.axis_size("ctx")
    halves = lax.axis_size("tp")
    here = lax.axis_index("ctx")
    rows, _, chans = projected.shape

    streams = jnp.transpose(projected, (1, 0, 2))
    rates_t = rates.T
    coef_t = (residues * jnp.sqrt(-jnp.expm1(-2.0 * rates))).T

    share = min(split_of(count), chans // LANES, 4)
    lines = count // share
    plane = here // share
    keeps = lax.axis_index("tp") == plane // 2
    place = jnp.stack([here % share, (plane == 1) | (plane == 2), keeps, plane % 2]).astype(jnp.int32)
    *ends, gated, prefix = local_scan(place, streams, short_filter, rates_t, share)
    ends = [ends[0]] + [send_xor(ends[j], count, share, j) for j in range(1, share)]
    whole, befores = plane_scan(place, rates_t, short_filter, ends, rows)
    arrived = [send_along(whole, count, share, k) for k in range(1, lines)]
    starts = line_scan(place, rates_t, short_filter, whole, befores, arrived, rows)
    states = starts[0]
    starts = [starts[0]] + [send_xor(starts[j], count, share, j) for j in range(1, share)]
    hidden = [
        hidden_rows(
            place, streams, short_filter, rates_t, coef_t, skip_gain[None], gated, prefix, starts, part
        )
        for part in range(2)
    ]
    if count == 16 and halves == 2 and out_weight.shape[1] % LANES == 0:
        return project_4x4(place, out_weight, states, hidden, count)
    return project_any(out_weight, states, hidden, count)


def solution(mesh):
    return jax.shard_map(
        per_device,
        mesh=mesh,
        in_specs=(
            P("ctx", None, "tp"),
            P(None, None, "tp"),
            P("tp", None),
            P("tp", None),
            P("tp"),
            P("tp", "ctx"),
        ),
        out_specs=P("ctx", "tp"),
        check_vma=False,
    )
```

```python
import functools

import jax
import jax.numpy as jnp
from jax import lax
from jax.experimental import pallas as pl
from jax.experimental.pallas import tpu as pltpu
from jax.sharding import PartitionSpec as P

LANES = 128
SEGS = 8
TOP = 8
SPOT, MIDDLE, KEEPS, ODD = range(4)
VMEM_LIMIT = 16 * 1024 * 1024
SMALL_LIMIT = 4 * 1024 * 1024
WHOLE_LIMIT = 50 * 1024 * 1024


def split_of(count):
    inner = 1
    while (2 * inner) ** 2 <= count and count % (2 * inner) == 0:
        inner *= 2
    return inner


def send_xor(value, count, group, step):
    pairs = [(p, p - p % group + ((p % group) ^ step)) for p in range(count)]
    return lax.ppermute(value, "ctx", pairs)


def send_along(value, count, group, steps, first=0):
    outer = count // group
    pairs = []
    for z in range(outer):
        if not 0 <= z + steps < outer:
            continue
        if (steps > 0 and z < first) or (steps < 0 and z > outer - 1 - first):
            continue
        pairs += [(z * group + e, (z + steps) * group + e) for e in range(group)]
    return lax.ppermute(value, "ctx", pairs)


def estimate(flops, bytes_accessed, transcendentals=0):
    return pl.CostEstimate(flops=flops, bytes_accessed=bytes_accessed, transcendentals=transcendentals)


def row(ref, r, lanes):
    return jnp.broadcast_to(ref[r : r + 1, lanes], (SEGS, LANES))


def lay_segments(dst, stream, halo, seg_len, lanes, group):
    pitch = seg_len + 1
    for s in range(SEGS):
        part = stream[0, s * seg_len : (s + 1) * seg_len, lanes].astype(jnp.float32)
        dst[group, TOP + s * pitch : TOP + s * pitch + seg_len, :] = part
    dst[group, TOP - 3 : TOP - 1, :] = jnp.zeros((2, LANES), jnp.float32) if halo is None else halo


def taps(short, stream, lanes):
    return [jnp.broadcast_to(short[i, stream : stream + 1, lanes], (SEGS, LANES)) for i in range(3)]


def strided(ref, group, start, pitch):
    return ref[group, pl.ds(start, SEGS, stride=pitch), :]


LAST, FIRST = 6, 4


def first_gated(short, first, last):
    products = []
    for b, stream in enumerate((1, 2)):
        tap = [short[i, stream : stream + 1, :] for i in range(3)]
        now_0, now_1 = first[2 * b : 2 * b + 1], first[2 * b + 1 : 2 * b + 2]
        old_2, old_1 = last[2 * stream : 2 * stream + 1], last[2 * stream + 1 : 2 * stream + 2]
        products.append(
            (
                tap[0] * now_0 + tap[1] * old_1 + tap[2] * old_2,
                tap[0] * now_1 + tap[1] * now_0 + tap[2] * old_1,
            )
        )
    return products[0][0] * products[1][0], products[0][1] * products[1][1]


def end_share(short, rates, first, last, rows):
    gated_0, gated_1 = first_gated(short, first, last)
    return jnp.exp(rates * (1.0 - rows)) * gated_0 + jnp.exp(rates * (2.0 - rows)) * gated_1


def local_scan_body(place, streams, short_all, rates_all, *rest, seg_len, order, share):
    ends = rest[:share]
    gated, prefix = rest[share : share + 2]
    key_pos, value_pos, end_now, held, query_held, short_held, rates_held, held_sem, small_sem = rest[share + 2 :]
    now_at = pl.program_id(0)
    wide = end_now.shape[1]
    small = [
        pltpu.make_async_copy(short_all, short_held, small_sem.at[0]),
        pltpu.make_async_copy(rates_all, rates_held, small_sem.at[1]),
        pltpu.make_async_copy(
            streams.at[0, pl.ds(seg_len * SEGS - 16, 16), :], query_held, small_sem.at[2]
        ),
    ]

    def stream_copy(at):
        columns = pl.ds(at * wide, wide)
        return pltpu.make_async_copy(
            streams.at[pl.ds(1, 2), :, columns], held.at[:, :, columns], held_sem.at[at]
        )

    @pl.when(now_at == 0)
    def _():
        stream_copy(0).start()
        for copy in small:
            copy.start()
        for at in range(1, share):
            stream_copy(at).start()
        for copy in small:
            copy.wait()

    for at in range(share):

        @pl.when(now_at == at)
        def _(at=at):
            stream_copy(at).wait()

    columns = pl.ds(pl.multiple_of(now_at * wide, LANES), wide)
    key = held.at[pl.ds(0, 1), :, columns]
    value = held.at[pl.ds(1, 1), :, columns]
    short = short_held.at[:, :, columns]
    rates = rates_held.at[:, columns]
    pitch = seg_len + 1
    groups = gated.shape[0]
    segment = lax.broadcasted_iota(jnp.int32, (SEGS, LANES), 0)
    for group in range(groups):
        lanes = slice(group * LANES, (group + 1) * LANES)
        lay_segments(key_pos, key, None, seg_len, lanes, group)
        lay_segments(value_pos, value, None, seg_len, lanes, group)
    bottom = seg_len * SEGS - 2
    end_now[order : order + 2, :] = query_held[14:16, columns].astype(jnp.float32)
    for b, stream in enumerate((key, value)):
        at = order + 2 + 2 * b
        end_now[at : at + 2, :] = stream[0, bottom : bottom + 2, :].astype(jnp.float32)
        at = order + LAST + 2 * b
        end_now[at : at + 2, :] = stream[0, 0:2, :].astype(jnp.float32)

    for group in range(groups):
        lanes = slice(group * LANES, (group + 1) * LANES)
        key_taps = taps(short, 1, lanes)
        value_taps = taps(short, 2, lanes)
        decay = [jnp.exp(-row(rates, r, lanes)) for r in range(order)]

        def step(i, carry, early=False, group=group, key_taps=key_taps, value_taps=value_taps, decay=decay):
            k1, k2, v1, v2, *states = carry
            k0 = strided(key_pos, group, TOP + i, pitch)
            v0 = strided(value_pos, group, TOP + i, pitch)
            key_now = key_taps[0] * k0 + key_taps[1] * k1 + key_taps[2] * k2
            value_now = value_taps[0] * v0 + value_taps[1] * v1 + value_taps[2] * v2
            now = key_now * value_now
            if early:
                now = jnp.where(segment >= 1, now, 0.0)
            gated[group, pl.ds(pl.multiple_of(i * SEGS, SEGS), SEGS), :] = now
            states = [d * h + now for d, h in zip(decay, states)]
            return (k0, k1, v0, v1, *states)

        zero = jnp.zeros((SEGS, LANES), jnp.float32)
        start = (
            strided(key_pos, group, TOP - 2, pitch),
            strided(key_pos, group, TOP - 3, pitch),
            strided(value_pos, group, TOP - 2, pitch),
            strided(value_pos, group, TOP - 3, pitch),
        ) + (zero,) * order
        start = step(1, step(0, start, True), True)
        states = lax.fori_loop(2, seg_len, step, start, unroll=seg_len - 2)[4:]
        for r in range(order):
            rate = row(rates, r, lanes)
            scan = states[r]
            for d in (1, 2, 4):
                moved = jnp.where(segment >= d, pltpu.roll(scan, d, 0), 0.0)
                scan = scan + jnp.exp(rate * (-1.0 * d * seg_len)) * moved
            prefix[group, r] = jnp.where(segment >= 1, pltpu.roll(scan, 1, 0), 0.0)
            end_now[r : r + 1, lanes] = scan[SEGS - 1 :, :]

    for j in range(share):

        @pl.when((pl.program_id(0) ^ place[SPOT]) == j)
        def _(j=j):
            ends[j][...] = end_now[...]


def local_scan(place, streams, short, rates, share):
    _, rows, chans = streams.shape
    order = rates.shape[0]
    wide = chans // share
    groups = wide // LANES
    seg_len = rows // SEGS
    pos_rows = TOP + SEGS * (seg_len + 1)
    end_shape = jax.ShapeDtypeStruct((order + LAST + FIRST, wide), jnp.float32)
    return pl.pallas_call(
        functools.partial(local_scan_body, seg_len=seg_len, order=order, share=share),
        grid_spec=pltpu.PrefetchScalarGridSpec(
            num_scalar_prefetch=1,
            grid=(share,),
            in_specs=[
                pl.BlockSpec(memory_space=pltpu.HBM),
                pl.BlockSpec(memory_space=pltpu.HBM),
                pl.BlockSpec(memory_space=pltpu.HBM),
            ],
            out_specs=[pl.BlockSpec((order + LAST + FIRST, wide), lambda g, place: (0, 0))] * share
            + [
                pl.BlockSpec((groups, rows, LANES), lambda g, place: (g, 0, 0)),
                pl.BlockSpec((groups, order, SEGS, LANES), lambda g, place: (g, 0, 0, 0)),
            ],
            scratch_shapes=[
                pltpu.VMEM((groups, pos_rows, LANES), jnp.float32),
                pltpu.VMEM((groups, pos_rows, LANES), jnp.float32),
                pltpu.VMEM((order + LAST + FIRST, wide), jnp.float32),
                pltpu.VMEM((2, rows, chans), streams.dtype),
                pltpu.VMEM((16, chans), streams.dtype),
                pltpu.VMEM(short.shape, jnp.float32),
                pltpu.VMEM(rates.shape, jnp.float32),
                pltpu.SemaphoreType.DMA((share,)),
                pltpu.SemaphoreType.DMA((3,)),
            ],
        ),
        out_shape=[end_shape] * share
        + [
            jax.ShapeDtypeStruct((chans // LANES, rows, LANES), jnp.float32),
            jax.ShapeDtypeStruct((chans // LANES, order, SEGS, LANES), jnp.float32),
        ],
        compiler_params=pltpu.CompilerParams(vmem_limit_bytes=WHOLE_LIMIT),
        cost_estimate=estimate(rows * chans * 50, rows * chans * 10),
        name="local_scan",
    )(place, streams, short, rates)


def plane_scan_body(place, rates, short, *rest, share, rows):
    ends = rest[:share]
    whole = rest[share]
    befores = rest[share + 1 : 2 * share + 1]
    by_place, before_place = rest[2 * share + 1 :]
    order = rates.shape[0]
    here = place[SPOT]
    for j in range(share):
        by_place[here ^ j] = ends[j][...]
    rate = rates[...]
    decay = jnp.exp(rate * (-1.0 * rows))
    state = jnp.zeros(rate.shape, jnp.float32)
    for at in range(share):
        before_place[at, :order] = state
        state = decay * state + by_place[at, :order]
        if at > 0:
            last = by_place[at - 1, order : order + LAST]
            before_place[at, order:] = last
            state += end_share(short, rate, by_place[at, order + LAST :], last, rows)
    before_place[0, order:] = jnp.zeros((LAST, rate.shape[1]), jnp.float32)
    whole[:order] = state
    whole[order : order + LAST] = by_place[share - 1, order : order + LAST]
    whole[order + LAST :] = by_place[0, order + LAST :]
    for j in range(share):
        befores[j][...] = before_place[here ^ j]


def plane_scan(place, rates, short, ends, rows):
    share = len(ends)
    order = rates.shape[0]
    wide = ends[0].shape[1]
    block = pl.BlockSpec((order + LAST, wide), lambda g, place: (0, 0))
    edged = pl.BlockSpec((order + LAST + FIRST, wide), lambda g, place: (0, 0))
    shape = jax.ShapeDtypeStruct((order + LAST, wide), jnp.float32)
    got = pl.pallas_call(
        functools.partial(plane_scan_body, share=share, rows=rows),
        grid_spec=pltpu.PrefetchScalarGridSpec(
            num_scalar_prefetch=1,
            grid=(1,),
            in_specs=[
                pl.BlockSpec((order, wide), lambda g, place: (0, place[SPOT])),
                pl.BlockSpec((3, 3, wide), lambda g, place: (0, 0, place[SPOT])),
            ]
            + [edged] * share,
            out_specs=[edged] + [block] * share,
            scratch_shapes=[
                pltpu.VMEM((share, order + LAST + FIRST, wide), jnp.float32),
                pltpu.VMEM((share, order + LAST, wide), jnp.float32),
            ],
        ),
        out_shape=[jax.ShapeDtypeStruct((order + LAST + FIRST, wide), jnp.float32)] + [shape] * share,
        compiler_params=pltpu.CompilerParams(vmem_limit_bytes=SMALL_LIMIT),
        cost_estimate=estimate(order * wide * 20, order * wide * 36),
        name="plane_scan",
    )(place, rates, short, *ends)
    return got[0], got[1:]


def line_scan_body(place, rates, short, whole, *rest, share, rows, lines):
    befores = rest[:share]
    arrived = rest[share : share + lines]
    outs = rest[share + lines :]
    order = rates.shape[0]
    here = place[SPOT]
    rate = rates[...]
    planes = (whole,) + tuple(arrived)

    def last_rows(k):
        if k < lines:
            return planes[k + 1][order : order + LAST]
        return jnp.zeros((LAST, rate.shape[1]), jnp.float32)

    def first_share(k):
        return end_share(short, rate, planes[k][order + LAST :], last_rows(k), rows)

    state = jnp.zeros(rate.shape, jnp.float32)
    decay = jnp.exp(rate * (-1.0 * rows * share))
    later = jnp.exp(rate * (-1.0 * rows * (share - 1)))
    for k in reversed(range(1, lines + 1)):
        state = decay * state + planes[k][:order] + later * first_share(k)
    own = first_share(0)
    for j in range(share):
        at = (here ^ j).astype(jnp.float32)
        inside = jnp.minimum(at, 1.0)
        past = inside * jnp.exp(rate * (jnp.maximum(at - 1.0, 0.0) * (-1.0 * rows)))
        before = befores[j][:order]
        outs[j][:order] = before + jnp.exp(rate * (at * (-1.0 * rows))) * state + past * own
        outs[j][order:] = befores[j][order:] + (1.0 - inside) * last_rows(0)


def line_scan(place, rates, short, whole, befores, arrived, rows):
    share, lines = len(befores), len(arrived)
    order, wide = rates.shape[0], whole.shape[1]
    block = pl.BlockSpec((order + LAST, wide), lambda g, place: (0, 0))
    edged = pl.BlockSpec((order + LAST + FIRST, wide), lambda g, place: (0, 0))
    return pl.pallas_call(
        functools.partial(line_scan_body, share=share, rows=rows, lines=lines),
        grid_spec=pltpu.PrefetchScalarGridSpec(
            num_scalar_prefetch=1,
            grid=(1,),
            in_specs=[
                pl.BlockSpec((order, wide), lambda g, place: (0, place[SPOT])),
                pl.BlockSpec((3, 3, wide), lambda g, place: (0, 0, place[SPOT])),
                edged,
            ]
            + [block] * share
            + [edged] * lines,
            out_specs=[block] * share,
        ),
        out_shape=[jax.ShapeDtypeStruct((order + LAST, wide), jnp.float32)] * share,
        compiler_params=pltpu.CompilerParams(vmem_limit_bytes=SMALL_LIMIT),
        cost_estimate=estimate(order * wide * 20, order * wide * 36),
        name="line_scan",
    )(place, rates, short, whole, *befores, *arrived)


def hidden_body(place, query, top, short, rates, coef, skip, gated, prefix, *rest, seg_len, order, share, first):
    starts = rest[:share]
    hidden = rest[share]
    query_pos, result_pos, start_by_place = rest[share + 1 :]
    pitch = seg_len + 1
    groups = gated.shape[0]
    now_at = pl.program_id(0) + first
    segment = lax.broadcasted_iota(jnp.int32, (SEGS, LANES), 0).astype(jnp.float32)

    @pl.when(pl.program_id(0) == 0)
    def _():
        for j in range(share):
            start_by_place[place[SPOT] ^ j] = starts[j][...]

    for group in range(groups):
        lanes = slice(group * LANES, (group + 1) * LANES)
        ending = start_by_place[now_at, order : order + 2, lanes]
        lay_segments(query_pos, query, ending, seg_len, lanes, group)

    for group in range(groups):
        lanes = slice(group * LANES, (group + 1) * LANES)
        query_taps = taps(short, 0, lanes)
        gain = jnp.broadcast_to(skip[0:1, lanes], (SEGS, LANES))
        decay = [jnp.exp(-row(rates, r, lanes)) for r in range(order)]
        scale = [row(coef, r, lanes) for r in range(order)]
        first = jnp.concatenate([top[b, 0:2, lanes] for b in (1, 2)], axis=0).astype(jnp.float32)
        last = start_by_place[now_at, order:, lanes]
        early = [
            jnp.broadcast_to(value, (SEGS, LANES))
            for value in first_gated(short.at[:, :, lanes], first, last)
        ]
        states = []
        for r in range(order):
            rate = row(rates, r, lanes)
            ahead = jnp.exp(rate * (segment * (-1.0 * seg_len)))
            before = jnp.broadcast_to(start_by_place[now_at, r : r + 1, lanes], (SEGS, LANES))
            grown = jnp.exp(rate)
            before += jnp.where(segment >= 1.0, grown * (early[0] + grown * early[1]), 0.0)
            states.append(prefix[group, r] + ahead * before)

        def step(
            i, carry, late=None, group=group, query_taps=query_taps, gain=gain, decay=decay, scale=scale
        ):
            q1, q2, *states = carry
            q0 = strided(query_pos, group, TOP + i, pitch)
            now = gated[group, pl.ds(pl.multiple_of(i * SEGS, SEGS), SEGS), :]
            if late is not None:
                now = jnp.where(segment >= 1.0, now, late)
            states = [d * h + now for d, h in zip(decay, states)]
            sums = [s * h for s, h in zip(scale, states)] + [gain * now]
            while len(sums) > 1:
                sums = [a + b for a, b in zip(sums[::2], sums[1::2])] + sums[len(sums) // 2 * 2 :]
            query_now = query_taps[0] * q0 + query_taps[1] * q1 + query_taps[2] * q2
            result_pos[group, pl.ds(TOP + i, SEGS, stride=pitch), :] = query_now * sums[0]
            return (q0, q1, *states)

        start = (
            strided(query_pos, group, TOP - 2, pitch),
            strided(query_pos, group, TOP - 3, pitch),
        ) + tuple(states)
        start = step(1, step(0, start, early[0]), early[1])
        lax.fori_loop(2, seg_len, step, start, unroll=seg_len - 2)
        for s in range(SEGS):
            part = result_pos[group, TOP + s * pitch : TOP + s * pitch + seg_len, :]
            hidden[s * seg_len : (s + 1) * seg_len, lanes] = part.astype(hidden.dtype)


def hidden_rows(place, streams, short, rates, coef, skip, gated, prefix, starts, part):
    _, rows, chans = streams.shape
    order = rates.shape[0]
    share = len(starts)
    wide = chans // share
    groups = wide // LANES
    seg_len = rows // SEGS
    steps = max(1, share // 2)
    first = part * steps
    pos_rows = TOP + SEGS * (seg_len + 1)
    return pl.pallas_call(
        functools.partial(hidden_body, seg_len=seg_len, order=order, share=share, first=first),
        grid_spec=pltpu.PrefetchScalarGridSpec(
            num_scalar_prefetch=1,
            grid=(steps,),
            in_specs=[
                pl.BlockSpec((1, rows, wide), lambda g, place: (0, 0, first + g)),
                pl.BlockSpec((3, 16, wide), lambda g, place: (0, 0, first + g)),
                pl.BlockSpec((3, 3, wide), lambda g, place: (0, 0, first + g)),
                pl.BlockSpec((order, wide), lambda g, place: (0, first + g)),
                pl.BlockSpec((order, wide), lambda g, place: (0, first + g)),
                pl.BlockSpec((1, wide), lambda g, place: (0, first + g)),
                pl.BlockSpec((groups, rows, LANES), lambda g, place: (first + g, 0, 0)),
                pl.BlockSpec((groups, order, SEGS, LANES), lambda g, place: (first + g, 0, 0, 0)),
            ]
            + [pl.BlockSpec((order + LAST, wide), lambda g, place: (0, 0))] * share,
            out_specs=pl.BlockSpec((rows, wide), lambda g, place: (0, g)),
            scratch_shapes=[
                pltpu.VMEM((groups, pos_rows, LANES), jnp.float32),
                pltpu.VMEM((groups, pos_rows, LANES), jnp.float32),
                pltpu.VMEM((share, order + LAST, wide), jnp.float32),
            ],
        ),
        out_shape=jax.ShapeDtypeStruct((rows, steps * wide), jnp.bfloat16),
        compiler_params=pltpu.CompilerParams(vmem_limit_bytes=VMEM_LIMIT),
        cost_estimate=estimate(rows * chans * 40, rows * chans * 5),
        name="hidden_rows",
    )(place, streams, streams, short, rates, coef, skip, gated, prefix, *starts)


def times_into(rows, columns, out, column):
    width = columns.shape[1]
    top = 0
    for part in rows:
        total = 0.0
        start = 0
        for piece in part:
            size, depth = piece.shape
            total += jnp.dot(
                piece[...], columns[start : start + depth, :], preferred_element_type=jnp.float32
            )
            start += depth
        out[top : top + size, column : column + width] = total.astype(out.dtype)
        top += size


def operands(refs, rows_in, slots):
    at = 0
    rows, blocks = [], []
    for group, counts in ((rows, rows_in), (blocks, slots)):
        for count in counts:
            group.append(refs[at : at + count])
            at += count
    return rows, blocks


def near_body(place, *refs, rows_in, slots):
    near, far_first = refs[-2:]
    rows, blocks = operands(refs, rows_in, slots)
    width = far_first.shape[1]

    def all_blocks(middle):
        for slot, given in enumerate(blocks):
            out, column = (near, slot * width) if slot < 2 else (far_first, 0)
            times_into(rows, given[0 if middle else -1], out, column)

    for middle in (0, 1):
        pl.when(place[MIDDLE] == middle)(functools.partial(all_blocks, middle))


def project_body(place, *refs, rows_in, slots):
    near, far_first, kept, sent = refs[-4:]
    rows, blocks = operands(refs, rows_in, slots)
    made, width = far_first.shape

    def all_blocks(keeps, middle):
        outs = (kept, sent) if keeps else (sent, kept)
        outs[0][:made] = near[...]
        outs[1][:made, :width] = far_first[...]
        columns = [given[0 if middle else -1] for given in blocks]
        for slot, block in enumerate(columns):
            far, at = divmod(slot, 2)
            times_into(rows[-1:], block, outs[far].at[pl.ds(made, outs[far].shape[0] - made)], at * width)
        times_into(rows[:-1], columns[3], outs[1], width)

    for keeps in (0, 1):
        for middle in (0, 1):
            here = (place[KEEPS] == keeps) & (place[MIDDLE] == middle)
            pl.when(here)(functools.partial(all_blocks, keeps, middle))


def project(place, rows, slots, made=None):
    flat = [piece for part in rows for piece in part] + [block for slot in slots for block in slot]
    flat += [] if made is None else list(made)
    count = sum(part[0].shape[0] for part in rows)
    depth, width = slots[0][0].shape
    widths = (2 * width, width) if len(slots) == 3 else (2 * width, 2 * width)
    held = pl.BlockSpec(memory_space=pltpu.VMEM)
    return pl.pallas_call(
        functools.partial(
            near_body if len(slots) == 3 else project_body,
            rows_in=tuple(map(len, rows)),
            slots=tuple(map(len, slots)),
        ),
        in_specs=[pl.BlockSpec(memory_space=pltpu.SMEM)] + [held] * len(flat),
        out_specs=[held] * 2,
        out_shape=[jax.ShapeDtypeStruct((count, wide), jnp.bfloat16) for wide in widths],
        compiler_params=pltpu.CompilerParams(vmem_limit_bytes=VMEM_LIMIT),
        cost_estimate=estimate(
            2 * count * depth * len(slots) * width,
            2 * (count * depth + len(slots) * width * (depth + count)),
        ),
        name="project",
    )(place, *flat)


def assemble_body(place, *refs):
    parts, out = refs[:-1], refs[-1]
    blocks = 2
    width = parts[0].shape[1] // blocks
    for j, part in enumerate(parts):
        for b in range(blocks):
            column = ((b ^ place[ODD]) * len(parts) + (place[SPOT] ^ j)) * width
            out[:, pl.ds(pl.multiple_of(column, LANES), width)] = part[:, b * width : (b + 1) * width]


def assemble(place, parts, blocks, width):
    share = len(parts)
    rows = parts[0].shape[0]
    held = pl.BlockSpec(memory_space=pltpu.VMEM)
    return pl.pallas_call(
        assemble_body,
        in_specs=[pl.BlockSpec(memory_space=pltpu.SMEM)] + [held] * share,
        out_specs=held,
        out_shape=jax.ShapeDtypeStruct((rows, share * blocks * width), jnp.bfloat16),
        compiler_params=pltpu.CompilerParams(vmem_limit_bytes=VMEM_LIMIT),
        cost_estimate=estimate(0, 4 * rows * share * blocks * width),
        name="assemble",
    )(place, *parts)


def after(value, *others):
    return lax.optimization_barrier((value, *others))[0]


def send_planes(value, group, moves):
    pairs = [(a * group + e, b * group + e) for a, b in moves for e in range(group)]
    return lax.ppermute(value, "ctx", pairs)


def plane_rows(hidden, count, group):
    if group != 4:
        return [hidden] + [[send_xor(part, count, group, j) for part in hidden] for j in range(1, group)]
    first, second = hidden
    first_1 = send_xor(first, count, group, 1)
    first_2 = send_xor(first, count, group, 2)
    second_2 = send_xor(second, count, group, 2)
    second_1 = send_xor(second, count, group, 1)
    first_3 = send_xor(first_1, count, group, 2)
    second_3 = send_xor(second_2, count, group, 1)
    return [[first, second], [first_1, second_1], [first_2, second_2], [first_3, second_3]]


def add_up_body(a, b, *outs):
    size = outs[0].shape[0]
    for j, out in enumerate(outs):
        rows = slice(j * size, (j + 1) * size)
        out[...] = (a[rows].astype(jnp.float32) + b[rows].astype(jnp.float32)).astype(out.dtype)


def add_up(a, b, parts):
    size, width = a.shape[0] // parts, a.shape[1]
    held = pl.BlockSpec(memory_space=pltpu.VMEM)
    return pl.pallas_call(
        add_up_body,
        in_specs=[held, held],
        out_specs=[held] * parts,
        out_shape=[jax.ShapeDtypeStruct((size, width), a.dtype)] * parts,
        compiler_params=pltpu.CompilerParams(vmem_limit_bytes=VMEM_LIMIT),
        cost_estimate=estimate(parts * size * width, 6 * parts * size * width),
        name="add_up",
    )(a, b)


def project_4x4(place, out_weight, states, hidden, count):
    group = 4
    swap = [(0, 1), (1, 0), (2, 3), (3, 2)]
    inner = [(1, 2), (2, 1)]
    outward = [(1, 0), (2, 3)]
    rows = plane_rows(hidden, count, group)
    own = out_weight
    by_1 = send_planes(own, group, swap)
    by_3_inner = send_planes(own, group, inner)
    by_2_inner = send_planes(after(by_1, states, by_3_inner), group, inner)
    by_2_outer = send_planes(after(by_3_inner, states), group, outward)
    by_3_outer = send_planes(after(by_2_inner, by_2_outer, rows[1][0], rows[2][0], hidden[1]), group, outward)
    blocks = [[own], [by_1], [by_2_inner, by_2_outer], [by_3_inner, by_3_outer]]

    made = project(place, rows[:3], blocks[:3])
    kept, sent = project(place, rows, blocks, made)
    mixed = add_up(kept, lax.ppermute(sent, "tp", [(0, 1), (1, 0)]), group)
    mixed = [mixed[0]] + [send_xor(mixed[j], count, group, j) for j in range(1, group)]
    return assemble(place, mixed, 2, out_weight.shape[1])


def project_any(out_weight, states, hidden, count):
    halves = lax.axis_size("tp")
    group = split_of(count)
    outer = count // group
    plane = lax.axis_index("ctx") // group
    size = hidden[0].shape[0]
    depth, width = out_weight.shape
    below, above = [out_weight], [out_weight]
    for k in range(1, outer):
        down, up = below[-1], above[-1]
        if k == 2:
            down, up = after(down, states), after(up, states)
        below.append(send_along(down, count, group, 1, k - 1))
        above.append(send_along(up, count, group, -1, k - 1))
    line = below[:0:-1] + above
    cols = lax.dynamic_slice_in_dim(jnp.stack(line), outer - 1 - plane, outer, 0)
    cols = jnp.moveaxis(cols, 0, 1).reshape(depth, outer * width)
    rows = plane_rows(hidden, count, group)
    held = jnp.concatenate([jnp.concatenate(part, axis=1) for part in rows], axis=0)
    partial = jnp.dot(held, cols, preferred_element_type=jnp.float32).astype(jnp.bfloat16)
    mixed = lax.psum_scatter(partial, "tp", scatter_dimension=1, tiled=True)
    mixed = jnp.split(mixed, group)
    mixed = [mixed[0]] + [send_xor(mixed[j], count, group, j) for j in range(1, group)]
    blocks = outer // halves
    stacked = jnp.stack(mixed).reshape(group, size, blocks, width)
    by_place = jnp.take(stacked, jnp.arange(group) ^ (lax.axis_index("ctx") % group), axis=0)
    return jnp.moveaxis(by_place, 0, 2).reshape(size, blocks * group * width)


def per_device(projected, short_filter, residues, rates, skip_gain, out_weight):
    count = lax.axis_size("ctx")
    halves = lax.axis_size("tp")
    here = lax.axis_index("ctx")
    rows, _, chans = projected.shape

    streams = jnp.transpose(projected, (1, 0, 2))
    rates_t = rates.T
    coef_t = (residues * jnp.sqrt(-jnp.expm1(-2.0 * rates))).T

    share = min(split_of(count), chans // LANES, 4)
    lines = count // share
    plane = here // share
    keeps = lax.axis_index("tp") == plane // 2
    place = jnp.stack([here % share, (plane == 1) | (plane == 2), keeps, plane % 2]).astype(jnp.int32)
    *ends, gated, prefix = local_scan(place, streams, short_filter, rates_t, share)
    ends = [ends[0]] + [send_xor(ends[j], count, share, j) for j in range(1, share)]
    whole, befores = plane_scan(place, rates_t, short_filter, ends, rows)
    arrived = [send_along(whole, count, share, k) for k in range(1, lines)]
    starts = line_scan(place, rates_t, short_filter, whole, befores, arrived, rows)
    states = starts[0]
    starts = [starts[0]] + [send_xor(starts[j], count, share, j) for j in range(1, share)]
    hidden = [
        hidden_rows(
            place, streams, short_filter, rates_t, coef_t, skip_gain[None], gated, prefix, starts, part
        )
        for part in range(2)
    ]
    if count == 16 and halves == 2 and out_weight.shape[1] % LANES == 0:
        return project_4x4(place, out_weight, states, hidden, count)
    return project_any(out_weight, states, hidden, count)


def solution(mesh):
    return jax.shard_map(
        per_device,
        mesh=mesh,
        in_specs=(
            P("ctx", None, "tp"),
            P(None, None, "tp"),
            P("tp", None),
            P("tp", None),
            P("tp"),
            P("tp", "ctx"),
        ),
        out_specs=P("ctx", "tp"),
        check_vma=False,
    )
```

```python
import functools

import jax
import jax.numpy as jnp
from jax import lax
from jax.experimental import pallas as pl
from jax.experimental.pallas import tpu as pltpu
from jax.sharding import PartitionSpec as P

LANES = 128
SEGS = 8
TOP = 8
SPOT, MIDDLE, KEEPS, ODD = range(4)
VMEM_LIMIT = 16 * 1024 * 1024
SMALL_LIMIT = 4 * 1024 * 1024
WHOLE_LIMIT = 50 * 1024 * 1024


def split_of(count):
    inner = 1
    while (2 * inner) ** 2 <= count and count % (2 * inner) == 0:
        inner *= 2
    return inner


def send_xor(value, count, group, step):
    pairs = [(p, p - p % group + ((p % group) ^ step)) for p in range(count)]
    return lax.ppermute(value, "ctx", pairs)


def send_along(value, count, group, steps, first=0):
    outer = count // group
    pairs = []
    for z in range(outer):
        if not 0 <= z + steps < outer:
            continue
        if (steps > 0 and z < first) or (steps < 0 and z > outer - 1 - first):
            continue
        pairs += [(z * group + e, (z + steps) * group + e) for e in range(group)]
    return lax.ppermute(value, "ctx", pairs)


def estimate(flops, bytes_accessed, transcendentals=0):
    return pl.CostEstimate(flops=flops, bytes_accessed=bytes_accessed, transcendentals=transcendentals)


def row(ref, r, lanes):
    return jnp.broadcast_to(ref[r : r + 1, lanes], (SEGS, LANES))


def lay_segments(dst, stream, halo, seg_len, lanes, group):
    pitch = seg_len + 1
    for s in range(SEGS):
        part = stream[0, s * seg_len : (s + 1) * seg_len, lanes].astype(jnp.float32)
        dst[group, TOP + s * pitch : TOP + s * pitch + seg_len, :] = part
    dst[group, TOP - 3 : TOP - 1, :] = jnp.zeros((2, LANES), jnp.float32) if halo is None else halo


def taps(short, stream, lanes):
    return [jnp.broadcast_to(short[i, stream : stream + 1, lanes], (SEGS, LANES)) for i in range(3)]


def strided(ref, group, start, pitch):
    return ref[group, pl.ds(start, SEGS, stride=pitch), :]


LAST, FIRST = 6, 4


def first_gated(short, first, last):
    products = []
    for b, stream in enumerate((1, 2)):
        tap = [short[i, stream : stream + 1, :] for i in range(3)]
        now_0, now_1 = first[2 * b : 2 * b + 1], first[2 * b + 1 : 2 * b + 2]
        old_2, old_1 = last[2 * stream : 2 * stream + 1], last[2 * stream + 1 : 2 * stream + 2]
        products.append(
            (
                tap[0] * now_0 + tap[1] * old_1 + tap[2] * old_2,
                tap[0] * now_1 + tap[1] * now_0 + tap[2] * old_1,
            )
        )
    return products[0][0] * products[1][0], products[0][1] * products[1][1]


def end_share(short, rates, first, last, rows):
    gated_0, gated_1 = first_gated(short, first, last)
    return jnp.exp(rates * (1.0 - rows)) * gated_0 + jnp.exp(rates * (2.0 - rows)) * gated_1


def local_scan_body(place, streams, packed_all, *rest, seg_len, order, share):
    ends = rest[:share]
    gated, prefix = rest[share : share + 2]
    key_pos, value_pos, end_now, held, query_held, packed, held_sem, small_sem = rest[share + 2 :]
    now_at = pl.program_id(0)
    wide = end_now.shape[1]
    small = [
        pltpu.make_async_copy(packed_all, packed, small_sem.at[0]),
        pltpu.make_async_copy(
            streams.at[0, pl.ds(seg_len * SEGS - 16, 16), :], query_held, small_sem.at[1]
        ),
    ]

    def stream_copy(at):
        columns = pl.ds(at * wide, wide)
        return pltpu.make_async_copy(
            streams.at[pl.ds(1, 2), :, columns], held.at[:, :, columns], held_sem.at[at]
        )

    @pl.when(now_at == 0)
    def _():
        stream_copy(0).start()
        for copy in small:
            copy.start()
        for at in range(1, share):
            stream_copy(at).start()
        for copy in small:
            copy.wait()

    for at in range(share):

        @pl.when(now_at == at)
        def _(at=at):
            stream_copy(at).wait()

    columns = pl.ds(pl.multiple_of(now_at * wide, LANES), wide)
    key = held.at[pl.ds(0, 1), :, columns]
    value = held.at[pl.ds(1, 1), :, columns]
    rates = packed.at[pl.ds(0, order), columns]

    def stream_taps(stream, lanes):
        return [row(packed.at[:, columns], order + 3 * i + stream, lanes) for i in range(3)]

    pitch = seg_len + 1
    groups = gated.shape[0]
    segment = lax.broadcasted_iota(jnp.int32, (SEGS, LANES), 0)
    for group in range(groups):
        lanes = slice(group * LANES, (group + 1) * LANES)
        lay_segments(key_pos, key, None, seg_len, lanes, group)
        lay_segments(value_pos, value, None, seg_len, lanes, group)
    bottom = seg_len * SEGS - 2
    end_now[order : order + 2, :] = query_held[14:16, columns].astype(jnp.float32)
    for b, stream in enumerate((key, value)):
        at = order + 2 + 2 * b
        end_now[at : at + 2, :] = stream[0, bottom : bottom + 2, :].astype(jnp.float32)
        at = order + LAST + 2 * b
        end_now[at : at + 2, :] = stream[0, 0:2, :].astype(jnp.float32)

    for group in range(groups):
        lanes = slice(group * LANES, (group + 1) * LANES)
        key_taps = stream_taps(1, lanes)
        value_taps = stream_taps(2, lanes)
        decay = [jnp.exp(-row(rates, r, lanes)) for r in range(order)]

        def step(i, carry, early=False, group=group, key_taps=key_taps, value_taps=value_taps, decay=decay):
            k1, k2, v1, v2, *states = carry
            k0 = strided(key_pos, group, TOP + i, pitch)
            v0 = strided(value_pos, group, TOP + i, pitch)
            key_now = key_taps[0] * k0 + key_taps[1] * k1 + key_taps[2] * k2
            value_now = value_taps[0] * v0 + value_taps[1] * v1 + value_taps[2] * v2
            now = key_now * value_now
            if early:
                now = jnp.where(segment >= 1, now, 0.0)
            gated[group, pl.ds(pl.multiple_of(i * SEGS, SEGS), SEGS), :] = now
            states = [d * h + now for d, h in zip(decay, states)]
            return (k0, k1, v0, v1, *states)

        zero = jnp.zeros((SEGS, LANES), jnp.float32)
        start = (
            strided(key_pos, group, TOP - 2, pitch),
            strided(key_pos, group, TOP - 3, pitch),
            strided(value_pos, group, TOP - 2, pitch),
            strided(value_pos, group, TOP - 3, pitch),
        ) + (zero,) * order
        start = step(1, step(0, start, True), True)
        states = lax.fori_loop(2, seg_len, step, start, unroll=seg_len - 2)[4:]
        for r in range(order):
            rate = row(rates, r, lanes)
            scan = states[r]
            for d in (1, 2, 4):
                moved = jnp.where(segment >= d, pltpu.roll(scan, d, 0), 0.0)
                scan = scan + jnp.exp(rate * (-1.0 * d * seg_len)) * moved
            prefix[group, r] = jnp.where(segment >= 1, pltpu.roll(scan, 1, 0), 0.0)
            end_now[r : r + 1, lanes] = scan[SEGS - 1 :, :]

    for j in range(share):

        @pl.when((pl.program_id(0) ^ place[SPOT]) == j)
        def _(j=j):
            ends[j][...] = end_now[...]


def local_scan(place, streams, short, rates, share):
    _, rows, chans = streams.shape
    order = rates.shape[0]
    packed = jnp.concatenate([rates, *short], axis=0)
    wide = chans // share
    groups = wide // LANES
    seg_len = rows // SEGS
    pos_rows = TOP + SEGS * (seg_len + 1)
    end_shape = jax.ShapeDtypeStruct((order + LAST + FIRST, wide), jnp.float32)
    return pl.pallas_call(
        functools.partial(local_scan_body, seg_len=seg_len, order=order, share=share),
        grid_spec=pltpu.PrefetchScalarGridSpec(
            num_scalar_prefetch=1,
            grid=(share,),
            in_specs=[
                pl.BlockSpec(memory_space=pltpu.HBM),
                pl.BlockSpec(memory_space=pltpu.HBM),
            ],
            out_specs=[pl.BlockSpec((order + LAST + FIRST, wide), lambda g, place: (0, 0))] * share
            + [
                pl.BlockSpec((groups, rows, LANES), lambda g, place: (g, 0, 0)),
                pl.BlockSpec((groups, order, SEGS, LANES), lambda g, place: (g, 0, 0, 0)),
            ],
            scratch_shapes=[
                pltpu.VMEM((groups, pos_rows, LANES), jnp.float32),
                pltpu.VMEM((groups, pos_rows, LANES), jnp.float32),
                pltpu.VMEM((order + LAST + FIRST, wide), jnp.float32),
                pltpu.VMEM((2, rows, chans), streams.dtype),
                pltpu.VMEM((16, chans), streams.dtype),
                pltpu.VMEM(packed.shape, jnp.float32),
                pltpu.SemaphoreType.DMA((share,)),
                pltpu.SemaphoreType.DMA((2,)),
            ],
        ),
        out_shape=[end_shape] * share
        + [
            jax.ShapeDtypeStruct((chans // LANES, rows, LANES), jnp.float32),
            jax.ShapeDtypeStruct((chans // LANES, order, SEGS, LANES), jnp.float32),
        ],
        compiler_params=pltpu.CompilerParams(vmem_limit_bytes=WHOLE_LIMIT),
        cost_estimate=estimate(rows * chans * 50, rows * chans * 10),
        name="local_scan",
    )(place, streams, packed)


def plane_scan_body(place, rates, short, *rest, share, rows):
    ends = rest[:share]
    whole = rest[share]
    befores = rest[share + 1 : 2 * share + 1]
    by_place, before_place = rest[2 * share + 1 :]
    order = rates.shape[0]
    here = place[SPOT]
    for j in range(share):
        by_place[here ^ j] = ends[j][...]
    rate = rates[...]
    decay = jnp.exp(rate * (-1.0 * rows))
    state = jnp.zeros(rate.shape, jnp.float32)
    for at in range(share):
        before_place[at, :order] = state
        state = decay * state + by_place[at, :order]
        if at > 0:
            last = by_place[at - 1, order : order + LAST]
            before_place[at, order:] = last
            state += end_share(short, rate, by_place[at, order + LAST :], last, rows)
    before_place[0, order:] = jnp.zeros((LAST, rate.shape[1]), jnp.float32)
    whole[:order] = state
    whole[order : order + LAST] = by_place[share - 1, order : order + LAST]
    whole[order + LAST :] = by_place[0, order + LAST :]
    for j in range(share):
        befores[j][...] = before_place[here ^ j]


def plane_scan(place, rates, short, ends, rows):
    share = len(ends)
    order = rates.shape[0]
    wide = ends[0].shape[1]
    block = pl.BlockSpec((order + LAST, wide), lambda g, place: (0, 0))
    edged = pl.BlockSpec((order + LAST + FIRST, wide), lambda g, place: (0, 0))
    shape = jax.ShapeDtypeStruct((order + LAST, wide), jnp.float32)
    got = pl.pallas_call(
        functools.partial(plane_scan_body, share=share, rows=rows),
        grid_spec=pltpu.PrefetchScalarGridSpec(
            num_scalar_prefetch=1,
            grid=(1,),
            in_specs=[
                pl.BlockSpec((order, wide), lambda g, place: (0, place[SPOT])),
                pl.BlockSpec((3, 3, wide), lambda g, place: (0, 0, place[SPOT])),
            ]
            + [edged] * share,
            out_specs=[edged] + [block] * share,
            scratch_shapes=[
                pltpu.VMEM((share, order + LAST + FIRST, wide), jnp.float32),
                pltpu.VMEM((share, order + LAST, wide), jnp.float32),
            ],
        ),
        out_shape=[jax.ShapeDtypeStruct((order + LAST + FIRST, wide), jnp.float32)] + [shape] * share,
        compiler_params=pltpu.CompilerParams(vmem_limit_bytes=SMALL_LIMIT),
        cost_estimate=estimate(order * wide * 20, order * wide * 36),
        name="plane_scan",
    )(place, rates, short, *ends)
    return got[0], got[1:]


def line_scan_body(place, rates, short, whole, *rest, share, rows, lines):
    befores = rest[:share]
    arrived = rest[share : share + lines]
    outs = rest[share + lines :]
    order = rates.shape[0]
    here = place[SPOT]
    rate = rates[...]
    planes = (whole,) + tuple(arrived)

    def last_rows(k):
        if k < lines:
            return planes[k + 1][order : order + LAST]
        return jnp.zeros((LAST, rate.shape[1]), jnp.float32)

    def first_share(k):
        return end_share(short, rate, planes[k][order + LAST :], last_rows(k), rows)

    state = jnp.zeros(rate.shape, jnp.float32)
    decay = jnp.exp(rate * (-1.0 * rows * share))
    later = jnp.exp(rate * (-1.0 * rows * (share - 1)))
    for k in reversed(range(1, lines + 1)):
        state = decay * state + planes[k][:order] + later * first_share(k)
    own = first_share(0)
    for j in range(share):
        at = (here ^ j).astype(jnp.float32)
        inside = jnp.minimum(at, 1.0)
        past = inside * jnp.exp(rate * (jnp.maximum(at - 1.0, 0.0) * (-1.0 * rows)))
        before = befores[j][:order]
        outs[j][:order] = before + jnp.exp(rate * (at * (-1.0 * rows))) * state + past * own
        outs[j][order:] = befores[j][order:] + (1.0 - inside) * last_rows(0)


def line_scan(place, rates, short, whole, befores, arrived, rows):
    share, lines = len(befores), len(arrived)
    order, wide = rates.shape[0], whole.shape[1]
    block = pl.BlockSpec((order + LAST, wide), lambda g, place: (0, 0))
    edged = pl.BlockSpec((order + LAST + FIRST, wide), lambda g, place: (0, 0))
    return pl.pallas_call(
        functools.partial(line_scan_body, share=share, rows=rows, lines=lines),
        grid_spec=pltpu.PrefetchScalarGridSpec(
            num_scalar_prefetch=1,
            grid=(1,),
            in_specs=[
                pl.BlockSpec((order, wide), lambda g, place: (0, place[SPOT])),
                pl.BlockSpec((3, 3, wide), lambda g, place: (0, 0, place[SPOT])),
                edged,
            ]
            + [block] * share
            + [edged] * lines,
            out_specs=[block] * share,
        ),
        out_shape=[jax.ShapeDtypeStruct((order + LAST, wide), jnp.float32)] * share,
        compiler_params=pltpu.CompilerParams(vmem_limit_bytes=SMALL_LIMIT),
        cost_estimate=estimate(order * wide * 20, order * wide * 36),
        name="line_scan",
    )(place, rates, short, whole, *befores, *arrived)


def hidden_body(place, query, top, short, rates, coef, skip, gated, prefix, *rest, seg_len, order, share, first):
    starts = rest[:share]
    hidden = rest[share]
    query_pos, result_pos, start_by_place = rest[share + 1 :]
    pitch = seg_len + 1
    groups = gated.shape[0]
    now_at = pl.program_id(0) + first
    segment = lax.broadcasted_iota(jnp.int32, (SEGS, LANES), 0).astype(jnp.float32)

    @pl.when(pl.program_id(0) == 0)
    def _():
        for j in range(share):
            start_by_place[place[SPOT] ^ j] = starts[j][...]

    for group in range(groups):
        lanes = slice(group * LANES, (group + 1) * LANES)
        ending = start_by_place[now_at, order : order + 2, lanes]
        lay_segments(query_pos, query, ending, seg_len, lanes, group)

    for group in range(groups):
        lanes = slice(group * LANES, (group + 1) * LANES)
        query_taps = taps(short, 0, lanes)
        gain = jnp.broadcast_to(skip[0:1, lanes], (SEGS, LANES))
        decay = [jnp.exp(-row(rates, r, lanes)) for r in range(order)]
        scale = [row(coef, r, lanes) for r in range(order)]
        first = jnp.concatenate([top[b, 0:2, lanes] for b in (1, 2)], axis=0).astype(jnp.float32)
        last = start_by_place[now_at, order:, lanes]
        early = [
            jnp.broadcast_to(value, (SEGS, LANES))
            for value in first_gated(short.at[:, :, lanes], first, last)
        ]
        states = []
        for r in range(order):
            rate = row(rates, r, lanes)
            ahead = jnp.exp(rate * (segment * (-1.0 * seg_len)))
            before = jnp.broadcast_to(start_by_place[now_at, r : r + 1, lanes], (SEGS, LANES))
            grown = jnp.exp(rate)
            before += jnp.where(segment >= 1.0, grown * (early[0] + grown * early[1]), 0.0)
            states.append(prefix[group, r] + ahead * before)

        def step(
            i, carry, late=None, group=group, query_taps=query_taps, gain=gain, decay=decay, scale=scale
        ):
            q1, q2, *states = carry
            q0 = strided(query_pos, group, TOP + i, pitch)
            now = gated[group, pl.ds(pl.multiple_of(i * SEGS, SEGS), SEGS), :]
            if late is not None:
                now = jnp.where(segment >= 1.0, now, late)
            states = [d * h + now for d, h in zip(decay, states)]
            sums = [s * h for s, h in zip(scale, states)] + [gain * now]
            while len(sums) > 1:
                sums = [a + b for a, b in zip(sums[::2], sums[1::2])] + sums[len(sums) // 2 * 2 :]
            query_now = query_taps[0] * q0 + query_taps[1] * q1 + query_taps[2] * q2
            result_pos[group, pl.ds(TOP + i, SEGS, stride=pitch), :] = query_now * sums[0]
            return (q0, q1, *states)

        start = (
            strided(query_pos, group, TOP - 2, pitch),
            strided(query_pos, group, TOP - 3, pitch),
        ) + tuple(states)
        start = step(1, step(0, start, early[0]), early[1])
        lax.fori_loop(2, seg_len, step, start, unroll=seg_len - 2)
        for s in range(SEGS):
            part = result_pos[group, TOP + s * pitch : TOP + s * pitch + seg_len, :]
            hidden[s * seg_len : (s + 1) * seg_len, lanes] = part.astype(hidden.dtype)


def hidden_rows(place, streams, short, rates, coef, skip, gated, prefix, starts, part):
    _, rows, chans = streams.shape
    order = rates.shape[0]
    share = len(starts)
    wide = chans // share
    groups = wide // LANES
    seg_len = rows // SEGS
    steps = max(1, share // 2)
    first = part * steps
    pos_rows = TOP + SEGS * (seg_len + 1)
    return pl.pallas_call(
        functools.partial(hidden_body, seg_len=seg_len, order=order, share=share, first=first),
        grid_spec=pltpu.PrefetchScalarGridSpec(
            num_scalar_prefetch=1,
            grid=(steps,),
            in_specs=[
                pl.BlockSpec((1, rows, wide), lambda g, place: (0, 0, first + g)),
                pl.BlockSpec((3, 16, wide), lambda g, place: (0, 0, first + g)),
                pl.BlockSpec((3, 3, wide), lambda g, place: (0, 0, first + g)),
                pl.BlockSpec((order, wide), lambda g, place: (0, first + g)),
                pl.BlockSpec((order, wide), lambda g, place: (0, first + g)),
                pl.BlockSpec((1, wide), lambda g, place: (0, first + g)),
                pl.BlockSpec((groups, rows, LANES), lambda g, place: (first + g, 0, 0)),
                pl.BlockSpec((groups, order, SEGS, LANES), lambda g, place: (first + g, 0, 0, 0)),
            ]
            + [pl.BlockSpec((order + LAST, wide), lambda g, place: (0, 0))] * share,
            out_specs=pl.BlockSpec((rows, wide), lambda g, place: (0, g)),
            scratch_shapes=[
                pltpu.VMEM((groups, pos_rows, LANES), jnp.float32),
                pltpu.VMEM((groups, pos_rows, LANES), jnp.float32),
                pltpu.VMEM((share, order + LAST, wide), jnp.float32),
            ],
        ),
        out_shape=jax.ShapeDtypeStruct((rows, steps * wide), jnp.bfloat16),
        compiler_params=pltpu.CompilerParams(vmem_limit_bytes=VMEM_LIMIT),
        cost_estimate=estimate(rows * chans * 40, rows * chans * 5),
        name="hidden_rows",
    )(place, streams, streams, short, rates, coef, skip, gated, prefix, *starts)


def times_into(rows, columns, out, column):
    width = columns.shape[1]
    top = 0
    for part in rows:
        total = 0.0
        start = 0
        for piece in part:
            size, depth = piece.shape
            total += jnp.dot(
                piece[...], columns[start : start + depth, :], preferred_element_type=jnp.float32
            )
            start += depth
        out[top : top + size, column : column + width] = total.astype(out.dtype)
        top += size


def operands(refs, rows_in, slots):
    at = 0
    rows, blocks = [], []
    for group, counts in ((rows, rows_in), (blocks, slots)):
        for count in counts:
            group.append(refs[at : at + count])
            at += count
    return rows, blocks


def near_body(place, *refs, rows_in, slots):
    near, far_first = refs[-2:]
    rows, blocks = operands(refs, rows_in, slots)
    width = far_first.shape[1]

    def all_blocks(middle):
        for slot, given in enumerate(blocks):
            out, column = (near, slot * width) if slot < 2 else (far_first, 0)
            times_into(rows, given[0 if middle else -1], out, column)

    for middle in (0, 1):
        pl.when(place[MIDDLE] == middle)(functools.partial(all_blocks, middle))


def half_body(place, piece, *refs, slots):
    out = refs[-1]
    _, blocks = operands(refs, (), slots)
    depth, width = piece.shape[1], out.shape[1] // len(slots)

    def all_blocks(middle):
        for slot, given in enumerate(blocks):
            columns = given[0 if middle else -1]
            out[:, slot * width : (slot + 1) * width] = jnp.dot(
                piece[...], columns[:depth, :], preferred_element_type=jnp.float32
            )

    for middle in (0, 1):
        pl.when(place[MIDDLE] == middle)(functools.partial(all_blocks, middle))


def project_half(place, piece, slots):
    flat = [piece] + [block for slot in slots for block in slot]
    size, depth = piece.shape
    width = slots[0][0].shape[1]
    held = pl.BlockSpec(memory_space=pltpu.VMEM)
    return pl.pallas_call(
        functools.partial(half_body, slots=tuple(map(len, slots))),
        in_specs=[pl.BlockSpec(memory_space=pltpu.SMEM)] + [held] * len(flat),
        out_specs=held,
        out_shape=jax.ShapeDtypeStruct((size, len(slots) * width), jnp.float32),
        compiler_params=pltpu.CompilerParams(vmem_limit_bytes=VMEM_LIMIT),
        cost_estimate=estimate(2 * size * depth * len(slots) * width, 2 * depth * (size + len(slots) * width)),
        name="project_half",
    )(place, *flat)


def project_body(place, *refs, rows_in, slots):
    near, far_first, begun, kept, sent = refs[-5:]
    rows, blocks = operands(refs, rows_in, slots)
    made, width = far_first.shape

    def all_blocks(keeps, middle):
        outs = (kept, sent) if keeps else (sent, kept)
        outs[0][:made] = near[...]
        outs[1][:made, :width] = far_first[...]
        columns = [given[0 if middle else -1] for given in blocks]
        for slot, block in enumerate(columns):
            far, at = divmod(slot, 2)
            first, second = rows[-1]
            depth = first.shape[1]
            if slot < 3:
                total = begun[:, slot * width : (slot + 1) * width]
            else:
                total = jnp.dot(first[...], block[:depth, :], preferred_element_type=jnp.float32)
            total += jnp.dot(second[...], block[depth:, :], preferred_element_type=jnp.float32)
            outs[far][made:, at * width : (at + 1) * width] = total.astype(kept.dtype)
        times_into(rows[:-1], columns[3], outs[1], width)

    for keeps in (0, 1):
        for middle in (0, 1):
            here = (place[KEEPS] == keeps) & (place[MIDDLE] == middle)
            pl.when(here)(functools.partial(all_blocks, keeps, middle))


def project(place, rows, slots, made=None):
    flat = [piece for part in rows for piece in part] + [block for slot in slots for block in slot]
    flat += [] if made is None else list(made)
    count = sum(part[0].shape[0] for part in rows)
    depth, width = slots[0][0].shape
    widths = (2 * width, width) if len(slots) == 3 else (2 * width, 2 * width)
    held = pl.BlockSpec(memory_space=pltpu.VMEM)
    return pl.pallas_call(
        functools.partial(
            near_body if len(slots) == 3 else project_body,
            rows_in=tuple(map(len, rows)),
            slots=tuple(map(len, slots)),
        ),
        in_specs=[pl.BlockSpec(memory_space=pltpu.SMEM)] + [held] * len(flat),
        out_specs=[held] * 2,
        out_shape=[jax.ShapeDtypeStruct((count, wide), jnp.bfloat16) for wide in widths],
        compiler_params=pltpu.CompilerParams(vmem_limit_bytes=VMEM_LIMIT),
        cost_estimate=estimate(
            2 * count * depth * len(slots) * width,
            2 * (count * depth + len(slots) * width * (depth + count)),
        ),
        name="project",
    )(place, *flat)


def assemble_body(place, *refs):
    parts, out = refs[:-1], refs[-1]
    blocks = 2
    width = parts[0].shape[1] // blocks
    for j, part in enumerate(parts):
        for b in range(blocks):
            column = ((b ^ place[ODD]) * len(parts) + (place[SPOT] ^ j)) * width
            out[:, pl.ds(pl.multiple_of(column, LANES), width)] = part[:, b * width : (b + 1) * width]


def assemble(place, parts, blocks, width):
    share = len(parts)
    rows = parts[0].shape[0]
    held = pl.BlockSpec(memory_space=pltpu.VMEM)
    return pl.pallas_call(
        assemble_body,
        in_specs=[pl.BlockSpec(memory_space=pltpu.SMEM)] + [held] * share,
        out_specs=held,
        out_shape=jax.ShapeDtypeStruct((rows, share * blocks * width), jnp.bfloat16),
        compiler_params=pltpu.CompilerParams(vmem_limit_bytes=VMEM_LIMIT),
        cost_estimate=estimate(0, 4 * rows * share * blocks * width),
        name="assemble",
    )(place, *parts)


def after(value, *others):
    return lax.optimization_barrier((value, *others))[0]


def send_planes(value, group, moves):
    pairs = [(a * group + e, b * group + e) for a, b in moves for e in range(group)]
    return lax.ppermute(value, "ctx", pairs)


def plane_rows(hidden, count, group):
    if group != 4:
        return [hidden] + [[send_xor(part, count, group, j) for part in hidden] for j in range(1, group)]
    first, second = hidden
    first_1 = send_xor(first, count, group, 1)
    first_2 = send_xor(first, count, group, 2)
    second_2 = send_xor(second, count, group, 2)
    second_1 = send_xor(second, count, group, 1)
    first_3 = send_xor(first_1, count, group, 2)
    second_3 = send_xor(second_2, count, group, 1)
    return [[first, second], [first_1, second_1], [first_2, second_2], [first_3, second_3]]


def add_up_body(a, b, *outs):
    size = outs[0].shape[0]
    for j, out in enumerate(outs):
        rows = slice(j * size, (j + 1) * size)
        out[...] = (a[rows].astype(jnp.float32) + b[rows].astype(jnp.float32)).astype(out.dtype)


def add_up(a, b, parts):
    size, width = a.shape[0] // parts, a.shape[1]
    held = pl.BlockSpec(memory_space=pltpu.VMEM)
    return pl.pallas_call(
        add_up_body,
        in_specs=[held, held],
        out_specs=[held] * parts,
        out_shape=[jax.ShapeDtypeStruct((size, width), a.dtype)] * parts,
        compiler_params=pltpu.CompilerParams(vmem_limit_bytes=VMEM_LIMIT),
        cost_estimate=estimate(parts * size * width, 6 * parts * size * width),
        name="add_up",
    )(a, b)


def project_4x4(place, out_weight, states, hidden, count):
    group = 4
    swap = [(0, 1), (1, 0), (2, 3), (3, 2)]
    inner = [(1, 2), (2, 1)]
    outward = [(1, 0), (2, 3)]
    rows = plane_rows(hidden, count, group)
    own = out_weight
    by_1 = send_planes(own, group, swap)
    by_3_inner = send_planes(own, group, inner)
    by_2_inner = send_planes(after(by_1, states, by_3_inner), group, inner)
    by_2_outer = send_planes(after(by_3_inner, states), group, outward)
    by_3_outer = send_planes(after(by_2_inner, by_2_outer, rows[1][0], rows[2][0], hidden[1]), group, outward)
    blocks = [[own], [by_1], [by_2_inner, by_2_outer], [by_3_inner, by_3_outer]]

    made = project(place, rows[:3], blocks[:3])
    begun = project_half(place, rows[3][0], blocks[:3])
    kept, sent = project(place, rows, blocks, [*made, begun])
    mixed = add_up(kept, lax.ppermute(sent, "tp", [(0, 1), (1, 0)]), group)
    mixed = [mixed[0]] + [send_xor(mixed[j], count, group, j) for j in range(1, group)]
    return assemble(place, mixed, 2, out_weight.shape[1])


def project_any(out_weight, states, hidden, count):
    halves = lax.axis_size("tp")
    group = split_of(count)
    outer = count // group
    plane = lax.axis_index("ctx") // group
    size = hidden[0].shape[0]
    depth, width = out_weight.shape
    below, above = [out_weight], [out_weight]
    for k in range(1, outer):
        down, up = below[-1], above[-1]
        if k == 2:
            down, up = after(down, states), after(up, states)
        below.append(send_along(down, count, group, 1, k - 1))
        above.append(send_along(up, count, group, -1, k - 1))
    line = below[:0:-1] + above
    cols = lax.dynamic_slice_in_dim(jnp.stack(line), outer - 1 - plane, outer, 0)
    cols = jnp.moveaxis(cols, 0, 1).reshape(depth, outer * width)
    rows = plane_rows(hidden, count, group)
    held = jnp.concatenate([jnp.concatenate(part, axis=1) for part in rows], axis=0)
    partial = jnp.dot(held, cols, preferred_element_type=jnp.float32).astype(jnp.bfloat16)
    mixed = lax.psum_scatter(partial, "tp", scatter_dimension=1, tiled=True)
    mixed = jnp.split(mixed, group)
    mixed = [mixed[0]] + [send_xor(mixed[j], count, group, j) for j in range(1, group)]
    blocks = outer // halves
    stacked = jnp.stack(mixed).reshape(group, size, blocks, width)
    by_place = jnp.take(stacked, jnp.arange(group) ^ (lax.axis_index("ctx") % group), axis=0)
    return jnp.moveaxis(by_place, 0, 2).reshape(size, blocks * group * width)


def per_device(projected, short_filter, residues, rates, skip_gain, out_weight):
    count = lax.axis_size("ctx")
    halves = lax.axis_size("tp")
    here = lax.axis_index("ctx")
    rows, _, chans = projected.shape

    streams = jnp.transpose(projected, (1, 0, 2))
    rates_t = rates.T
    coef_t = (residues * jnp.sqrt(-jnp.expm1(-2.0 * rates))).T

    share = min(split_of(count), chans // LANES, 4)
    lines = count // share
    plane = here // share
    keeps = lax.axis_index("tp") == plane // 2
    place = jnp.stack([here % share, (plane == 1) | (plane == 2), keeps, plane % 2]).astype(jnp.int32)
    *ends, gated, prefix = local_scan(place, streams, short_filter, rates_t, share)
    ends = [ends[0]] + [send_xor(ends[j], count, share, j) for j in range(1, share)]
    whole, befores = plane_scan(place, rates_t, short_filter, ends, rows)
    arrived = [send_along(whole, count, share, k) for k in range(1, lines)]
    starts = line_scan(place, rates_t, short_filter, whole, befores, arrived, rows)
    states = starts[0]
    starts = [starts[0]] + [send_xor(starts[j], count, share, j) for j in range(1, share)]
    hidden = [
        hidden_rows(
            place, streams, short_filter, rates_t, coef_t, skip_gain[None], gated, prefix, starts, part
        )
        for part in range(2)
    ]
    if count == 16 and halves == 2 and out_weight.shape[1] % LANES == 0:
        return project_4x4(place, out_weight, states, hidden, count)
    return project_any(out_weight, states, hidden, count)


def solution(mesh):
    return jax.shard_map(
        per_device,
        mesh=mesh,
        in_specs=(
            P("ctx", None, "tp"),
            P(None, None, "tp"),
            P("tp", None),
            P("tp", None),
            P("tp"),
            P("tp", "ctx"),
        ),
        out_specs=P("ctx", "tp"),
        check_vma=False,
    )
```

```python
import functools

import jax
import jax.numpy as jnp
from jax import lax
from jax.experimental import pallas as pl
from jax.experimental.pallas import tpu as pltpu
from jax.sharding import PartitionSpec as P

LANES = 128
SEGS = 8
TOP = 8
SPOT, MIDDLE, KEEPS, ODD = range(4)
VMEM_LIMIT = 16 * 1024 * 1024
SMALL_LIMIT = 4 * 1024 * 1024
WHOLE_LIMIT = 50 * 1024 * 1024


def split_of(count):
    inner = 1
    while (2 * inner) ** 2 <= count and count % (2 * inner) == 0:
        inner *= 2
    return inner


def send_xor(value, count, group, step):
    pairs = [(p, p - p % group + ((p % group) ^ step)) for p in range(count)]
    return lax.ppermute(value, "ctx", pairs)


def send_along(value, count, group, steps, first=0):
    outer = count // group
    pairs = []
    for z in range(outer):
        if not 0 <= z + steps < outer:
            continue
        if (steps > 0 and z < first) or (steps < 0 and z > outer - 1 - first):
            continue
        pairs += [(z * group + e, (z + steps) * group + e) for e in range(group)]
    return lax.ppermute(value, "ctx", pairs)


def estimate(flops, bytes_accessed, transcendentals=0):
    return pl.CostEstimate(flops=flops, bytes_accessed=bytes_accessed, transcendentals=transcendentals)


def row(ref, r, lanes):
    return jnp.broadcast_to(ref[r : r + 1, lanes], (SEGS, LANES))


def lay_segments(dst, stream, halo, seg_len, lanes, group):
    pitch = seg_len + 1
    for s in range(SEGS):
        part = stream[0, s * seg_len : (s + 1) * seg_len, lanes].astype(jnp.float32)
        dst[group, TOP + s * pitch : TOP + s * pitch + seg_len, :] = part
    dst[group, TOP - 3 : TOP - 1, :] = jnp.zeros((2, LANES), jnp.float32) if halo is None else halo


def taps(short, stream, lanes):
    return [jnp.broadcast_to(short[i, stream : stream + 1, lanes], (SEGS, LANES)) for i in range(3)]


def strided(ref, group, start, pitch):
    return ref[group, pl.ds(start, SEGS, stride=pitch), :]


LAST, FIRST = 6, 4


def first_gated(short, first, last):
    products = []
    for b, stream in enumerate((1, 2)):
        tap = [short[i, stream : stream + 1, :] for i in range(3)]
        now_0, now_1 = first[2 * b : 2 * b + 1], first[2 * b + 1 : 2 * b + 2]
        old_2, old_1 = last[2 * stream : 2 * stream + 1], last[2 * stream + 1 : 2 * stream + 2]
        products.append(
            (
                tap[0] * now_0 + tap[1] * old_1 + tap[2] * old_2,
                tap[0] * now_1 + tap[1] * now_0 + tap[2] * old_1,
            )
        )
    return products[0][0] * products[1][0], products[0][1] * products[1][1]


def end_share(short, rates, first, last, rows):
    gated_0, gated_1 = first_gated(short, first, last)
    return jnp.exp(rates * (1.0 - rows)) * gated_0 + jnp.exp(rates * (2.0 - rows)) * gated_1


def local_scan_body(place, streams, short_all, rates_all, *rest, seg_len, order, share):
    ends = rest[:share]
    gated, prefix = rest[share : share + 2]
    key_pos, value_pos, end_now, table, held, query_held, short_held, rates_held, held_sem, small_sem = rest[share + 2 :]
    now_at = pl.program_id(0)
    wide = end_now.shape[1]
    small = [
        pltpu.make_async_copy(short_all, short_held, small_sem.at[0]),
        pltpu.make_async_copy(rates_all, rates_held, small_sem.at[1]),
        pltpu.make_async_copy(
            streams.at[0, pl.ds(seg_len * SEGS - 16, 16), :], query_held, small_sem.at[2]
        ),
    ]

    def stream_copy(at):
        columns = pl.ds(at * wide, wide)
        return pltpu.make_async_copy(
            streams.at[pl.ds(1, 2), :, columns], held.at[:, :, columns], held_sem.at[at]
        )

    @pl.when(now_at == 0)
    def _():
        stream_copy(0).start()
        for copy in small:
            copy.start()
        for at in range(1, share):
            stream_copy(at).start()
        for copy in small:
            copy.wait()

    for at in range(share):

        @pl.when(now_at == at)
        def _(at=at):
            stream_copy(at).wait()

    columns = pl.ds(pl.multiple_of(now_at * wide, LANES), wide)
    key = held.at[pl.ds(0, 1), :, columns]
    value = held.at[pl.ds(1, 1), :, columns]
    short = short_held.at[:, :, columns]
    rates = rates_held[:, columns]
    table[0] = jnp.exp(-rates)
    for e, d in enumerate((1, 2, 4)):
        table[1 + e] = jnp.exp(rates * (-1.0 * d * seg_len))
    pitch = seg_len + 1
    groups = gated.shape[0]
    segment = lax.broadcasted_iota(jnp.int32, (SEGS, LANES), 0)
    for group in range(groups):
        lanes = slice(group * LANES, (group + 1) * LANES)
        lay_segments(key_pos, key, None, seg_len, lanes, group)
        lay_segments(value_pos, value, None, seg_len, lanes, group)
    bottom = seg_len * SEGS - 2
    end_now[order : order + 2, :] = query_held[14:16, columns].astype(jnp.float32)
    for b, stream in enumerate((key, value)):
        at = order + 2 + 2 * b
        end_now[at : at + 2, :] = stream[0, bottom : bottom + 2, :].astype(jnp.float32)
        at = order + LAST + 2 * b
        end_now[at : at + 2, :] = stream[0, 0:2, :].astype(jnp.float32)

    for group in range(groups):
        lanes = slice(group * LANES, (group + 1) * LANES)
        key_taps = taps(short, 1, lanes)
        value_taps = taps(short, 2, lanes)
        decay = [row(table.at[0], r, lanes) for r in range(order)]

        def step(i, carry, early=False, group=group, key_taps=key_taps, value_taps=value_taps, decay=decay):
            k1, k2, v1, v2, *states = carry
            k0 = strided(key_pos, group, TOP + i, pitch)
            v0 = strided(value_pos, group, TOP + i, pitch)
            key_now = key_taps[0] * k0 + key_taps[1] * k1 + key_taps[2] * k2
            value_now = value_taps[0] * v0 + value_taps[1] * v1 + value_taps[2] * v2
            now = key_now * value_now
            if early:
                now = jnp.where(segment >= 1, now, 0.0)
            gated[group, pl.ds(pl.multiple_of(i * SEGS, SEGS), SEGS), :] = now
            states = [d * h + now for d, h in zip(decay, states)]
            return (k0, k1, v0, v1, *states)

        zero = jnp.zeros((SEGS, LANES), jnp.float32)
        start = (
            strided(key_pos, group, TOP - 2, pitch),
            strided(key_pos, group, TOP - 3, pitch),
            strided(value_pos, group, TOP - 2, pitch),
            strided(value_pos, group, TOP - 3, pitch),
        ) + (zero,) * order
        start = step(1, step(0, start, True), True)
        states = lax.fori_loop(2, seg_len, step, start, unroll=seg_len - 2)[4:]
        for r in range(order):
            scan = states[r]
            for e, d in enumerate((1, 2, 4)):
                moved = jnp.where(segment >= d, pltpu.roll(scan, d, 0), 0.0)
                scan = scan + row(table.at[1 + e], r, lanes) * moved
            prefix[group, r] = jnp.where(segment >= 1, pltpu.roll(scan, 1, 0), 0.0)
            end_now[r : r + 1, lanes] = scan[SEGS - 1 :, :]

    for j in range(share):

        @pl.when((pl.program_id(0) ^ place[SPOT]) == j)
        def _(j=j):
            ends[j][...] = end_now[...]


def local_scan(place, streams, short, rates, share):
    _, rows, chans = streams.shape
    order = rates.shape[0]
    wide = chans // share
    groups = wide // LANES
    seg_len = rows // SEGS
    pos_rows = TOP + SEGS * (seg_len + 1)
    end_shape = jax.ShapeDtypeStruct((order + LAST + FIRST, wide), jnp.float32)
    return pl.pallas_call(
        functools.partial(local_scan_body, seg_len=seg_len, order=order, share=share),
        grid_spec=pltpu.PrefetchScalarGridSpec(
            num_scalar_prefetch=1,
            grid=(share,),
            in_specs=[
                pl.BlockSpec(memory_space=pltpu.HBM),
                pl.BlockSpec(memory_space=pltpu.HBM),
                pl.BlockSpec(memory_space=pltpu.HBM),
            ],
            out_specs=[pl.BlockSpec((order + LAST + FIRST, wide), lambda g, place: (0, 0))] * share
            + [
                pl.BlockSpec((groups, rows, LANES), lambda g, place: (g, 0, 0)),
                pl.BlockSpec((groups, order, SEGS, LANES), lambda g, place: (g, 0, 0, 0)),
            ],
            scratch_shapes=[
                pltpu.VMEM((groups, pos_rows, LANES), jnp.float32),
                pltpu.VMEM((groups, pos_rows, LANES), jnp.float32),
                pltpu.VMEM((order + LAST + FIRST, wide), jnp.float32),
                pltpu.VMEM((4, order, wide), jnp.float32),
                pltpu.VMEM((2, rows, chans), streams.dtype),
                pltpu.VMEM((16, chans), streams.dtype),
                pltpu.VMEM(short.shape, jnp.float32),
                pltpu.VMEM(rates.shape, jnp.float32),
                pltpu.SemaphoreType.DMA((share,)),
                pltpu.SemaphoreType.DMA((3,)),
            ],
        ),
        out_shape=[end_shape] * share
        + [
            jax.ShapeDtypeStruct((chans // LANES, rows, LANES), jnp.float32),
            jax.ShapeDtypeStruct((chans // LANES, order, SEGS, LANES), jnp.float32),
        ],
        compiler_params=pltpu.CompilerParams(vmem_limit_bytes=WHOLE_LIMIT),
        cost_estimate=estimate(rows * chans * 50, rows * chans * 10),
        name="local_scan",
    )(place, streams, short, rates)


def plane_scan_body(place, rates, short, *rest, share, rows):
    ends = rest[:share]
    whole = rest[share]
    befores = rest[share + 1 : 2 * share + 1]
    by_place, before_place = rest[2 * share + 1 :]
    order = rates.shape[0]
    here = place[SPOT]
    for j in range(share):
        by_place[here ^ j] = ends[j][...]
    rate = rates[...]
    decay = jnp.exp(rate * (-1.0 * rows))
    state = jnp.zeros(rate.shape, jnp.float32)
    for at in range(share):
        before_place[at, :order] = state
        state = decay * state + by_place[at, :order]
        if at > 0:
            last = by_place[at - 1, order : order + LAST]
            before_place[at, order:] = last
            state += end_share(short, rate, by_place[at, order + LAST :], last, rows)
    before_place[0, order:] = jnp.zeros((LAST, rate.shape[1]), jnp.float32)
    whole[:order] = state
    whole[order : order + LAST] = by_place[share - 1, order : order + LAST]
    whole[order + LAST :] = by_place[0, order + LAST :]
    for j in range(share):
        befores[j][...] = before_place[here ^ j]


def plane_scan(place, rates, short, ends, rows):
    share = len(ends)
    order = rates.shape[0]
    wide = ends[0].shape[1]
    block = pl.BlockSpec((order + LAST, wide), lambda g, place: (0, 0))
    edged = pl.BlockSpec((order + LAST + FIRST, wide), lambda g, place: (0, 0))
    shape = jax.ShapeDtypeStruct((order + LAST, wide), jnp.float32)
    got = pl.pallas_call(
        functools.partial(plane_scan_body, share=share, rows=rows),
        grid_spec=pltpu.PrefetchScalarGridSpec(
            num_scalar_prefetch=1,
            grid=(1,),
            in_specs=[
                pl.BlockSpec((order, wide), lambda g, place: (0, place[SPOT])),
                pl.BlockSpec((3, 3, wide), lambda g, place: (0, 0, place[SPOT])),
            ]
            + [edged] * share,
            out_specs=[edged] + [block] * share,
            scratch_shapes=[
                pltpu.VMEM((share, order + LAST + FIRST, wide), jnp.float32),
                pltpu.VMEM((share, order + LAST, wide), jnp.float32),
            ],
        ),
        out_shape=[jax.ShapeDtypeStruct((order + LAST + FIRST, wide), jnp.float32)] + [shape] * share,
        compiler_params=pltpu.CompilerParams(vmem_limit_bytes=SMALL_LIMIT),
        cost_estimate=estimate(order * wide * 20, order * wide * 36),
        name="plane_scan",
    )(place, rates, short, *ends)
    return got[0], got[1:]


def line_scan_body(place, rates, short, whole, *rest, share, rows, lines):
    befores = rest[:share]
    arrived = rest[share : share + lines]
    outs = rest[share + lines :]
    order = rates.shape[0]
    here = place[SPOT]
    rate = rates[...]
    planes = (whole,) + tuple(arrived)

    def last_rows(k):
        if k < lines:
            return planes[k + 1][order : order + LAST]
        return jnp.zeros((LAST, rate.shape[1]), jnp.float32)

    def first_share(k):
        return end_share(short, rate, planes[k][order + LAST :], last_rows(k), rows)

    state = jnp.zeros(rate.shape, jnp.float32)
    decay = jnp.exp(rate * (-1.0 * rows * share))
    later = jnp.exp(rate * (-1.0 * rows * (share - 1)))
    for k in reversed(range(1, lines + 1)):
        state = decay * state + planes[k][:order] + later * first_share(k)
    own = first_share(0)
    for j in range(share):
        at = (here ^ j).astype(jnp.float32)
        inside = jnp.minimum(at, 1.0)
        past = inside * jnp.exp(rate * (jnp.maximum(at - 1.0, 0.0) * (-1.0 * rows)))
        before = befores[j][:order]
        outs[j][:order] = before + jnp.exp(rate * (at * (-1.0 * rows))) * state + past * own
        outs[j][order:] = befores[j][order:] + (1.0 - inside) * last_rows(0)


def line_scan(place, rates, short, whole, befores, arrived, rows):
    share, lines = len(befores), len(arrived)
    order, wide = rates.shape[0], whole.shape[1]
    block = pl.BlockSpec((order + LAST, wide), lambda g, place: (0, 0))
    edged = pl.BlockSpec((order + LAST + FIRST, wide), lambda g, place: (0, 0))
    return pl.pallas_call(
        functools.partial(line_scan_body, share=share, rows=rows, lines=lines),
        grid_spec=pltpu.PrefetchScalarGridSpec(
            num_scalar_prefetch=1,
            grid=(1,),
            in_specs=[
                pl.BlockSpec((order, wide), lambda g, place: (0, place[SPOT])),
                pl.BlockSpec((3, 3, wide), lambda g, place: (0, 0, place[SPOT])),
                edged,
            ]
            + [block] * share
            + [edged] * lines,
            out_specs=[block] * share,
        ),
        out_shape=[jax.ShapeDtypeStruct((order + LAST, wide), jnp.float32)] * share,
        compiler_params=pltpu.CompilerParams(vmem_limit_bytes=SMALL_LIMIT),
        cost_estimate=estimate(order * wide * 20, order * wide * 36),
        name="line_scan",
    )(place, rates, short, whole, *befores, *arrived)


def hidden_body(place, query, top, short, rates, coef, skip, gated, prefix, *rest, seg_len, order, share, first):
    starts = rest[:share]
    hidden = rest[share]
    query_pos, result_pos, start_by_place, table = rest[share + 1 :]
    pitch = seg_len + 1
    groups = gated.shape[0]
    now_at = pl.program_id(0) + first
    table[0] = jnp.exp(-rates[...])
    table[1] = jnp.exp(rates[...])
    segment = lax.broadcasted_iota(jnp.int32, (SEGS, LANES), 0).astype(jnp.float32)

    @pl.when(pl.program_id(0) == 0)
    def _():
        for j in range(share):
            start_by_place[place[SPOT] ^ j] = starts[j][...]

    for group in range(groups):
        lanes = slice(group * LANES, (group + 1) * LANES)
        ending = start_by_place[now_at, order : order + 2, lanes]
        lay_segments(query_pos, query, ending, seg_len, lanes, group)

    for group in range(groups):
        lanes = slice(group * LANES, (group + 1) * LANES)
        query_taps = taps(short, 0, lanes)
        gain = jnp.broadcast_to(skip[0:1, lanes], (SEGS, LANES))
        decay = [row(table.at[0], r, lanes) for r in range(order)]
        scale = [row(coef, r, lanes) for r in range(order)]
        first = jnp.concatenate([top[b, 0:2, lanes] for b in (1, 2)], axis=0).astype(jnp.float32)
        last = start_by_place[now_at, order:, lanes]
        early = [
            jnp.broadcast_to(value, (SEGS, LANES))
            for value in first_gated(short.at[:, :, lanes], first, last)
        ]
        states = []
        for r in range(order):
            rate = row(rates, r, lanes)
            ahead = jnp.exp(rate * (segment * (-1.0 * seg_len)))
            before = jnp.broadcast_to(start_by_place[now_at, r : r + 1, lanes], (SEGS, LANES))
            grown = row(table.at[1], r, lanes)
            before += jnp.where(segment >= 1.0, grown * (early[0] + grown * early[1]), 0.0)
            states.append(prefix[group, r] + ahead * before)

        def step(
            i, carry, late=None, group=group, query_taps=query_taps, gain=gain, decay=decay, scale=scale
        ):
            q1, q2, *states = carry
            q0 = strided(query_pos, group, TOP + i, pitch)
            now = gated[group, pl.ds(pl.multiple_of(i * SEGS, SEGS), SEGS), :]
            if late is not None:
                now = jnp.where(segment >= 1.0, now, late)
            states = [d * h + now for d, h in zip(decay, states)]
            sums = [s * h for s, h in zip(scale, states)] + [gain * now]
            while len(sums) > 1:
                sums = [a + b for a, b in zip(sums[::2], sums[1::2])] + sums[len(sums) // 2 * 2 :]
            query_now = query_taps[0] * q0 + query_taps[1] * q1 + query_taps[2] * q2
            result_pos[group, pl.ds(TOP + i, SEGS, stride=pitch), :] = query_now * sums[0]
            return (q0, q1, *states)

        start = (
            strided(query_pos, group, TOP - 2, pitch),
            strided(query_pos, group, TOP - 3, pitch),
        ) + tuple(states)
        start = step(1, step(0, start, early[0]), early[1])
        lax.fori_loop(2, seg_len, step, start, unroll=seg_len - 2)
        for s in range(SEGS):
            part = result_pos[group, TOP + s * pitch : TOP + s * pitch + seg_len, :]
            hidden[s * seg_len : (s + 1) * seg_len, lanes] = part.astype(hidden.dtype)


def hidden_rows(place, streams, short, rates, coef, skip, gated, prefix, starts, part):
    _, rows, chans = streams.shape
    order = rates.shape[0]
    share = len(starts)
    wide = chans // share
    groups = wide // LANES
    seg_len = rows // SEGS
    steps = max(1, share // 2)
    first = part * steps
    pos_rows = TOP + SEGS * (seg_len + 1)
    return pl.pallas_call(
        functools.partial(hidden_body, seg_len=seg_len, order=order, share=share, first=first),
        grid_spec=pltpu.PrefetchScalarGridSpec(
            num_scalar_prefetch=1,
            grid=(steps,),
            in_specs=[
                pl.BlockSpec((1, rows, wide), lambda g, place: (0, 0, first + g)),
                pl.BlockSpec((3, 16, wide), lambda g, place: (0, 0, first + g)),
                pl.BlockSpec((3, 3, wide), lambda g, place: (0, 0, first + g)),
                pl.BlockSpec((order, wide), lambda g, place: (0, first + g)),
                pl.BlockSpec((order, wide), lambda g, place: (0, first + g)),
                pl.BlockSpec((1, wide), lambda g, place: (0, first + g)),
                pl.BlockSpec((groups, rows, LANES), lambda g, place: (first + g, 0, 0)),
                pl.BlockSpec((groups, order, SEGS, LANES), lambda g, place: (first + g, 0, 0, 0)),
            ]
            + [pl.BlockSpec((order + LAST, wide), lambda g, place: (0, 0))] * share,
            out_specs=pl.BlockSpec((rows, wide), lambda g, place: (0, g)),
            scratch_shapes=[
                pltpu.VMEM((groups, pos_rows, LANES), jnp.float32),
                pltpu.VMEM((groups, pos_rows, LANES), jnp.float32),
                pltpu.VMEM((share, order + LAST, wide), jnp.float32),
                pltpu.VMEM((2, order, wide), jnp.float32),
            ],
        ),
        out_shape=jax.ShapeDtypeStruct((rows, steps * wide), jnp.bfloat16),
        compiler_params=pltpu.CompilerParams(vmem_limit_bytes=VMEM_LIMIT),
        cost_estimate=estimate(rows * chans * 40, rows * chans * 5),
        name="hidden_rows",
    )(place, streams, streams, short, rates, coef, skip, gated, prefix, *starts)


def times_into(rows, columns, out, column):
    width = columns.shape[1]
    top = 0
    for part in rows:
        total = 0.0
        start = 0
        for piece in part:
            size, depth = piece.shape
            total += jnp.dot(
                piece[...], columns[start : start + depth, :], preferred_element_type=jnp.float32
            )
            start += depth
        out[top : top + size, column : column + width] = total.astype(out.dtype)
        top += size


def operands(refs, rows_in, slots):
    at = 0
    rows, blocks = [], []
    for group, counts in ((rows, rows_in), (blocks, slots)):
        for count in counts:
            group.append(refs[at : at + count])
            at += count
    return rows, blocks


def near_body(place, *refs, rows_in, slots):
    near, far_first = refs[-2:]
    rows, blocks = operands(refs, rows_in, slots)
    width = far_first.shape[1]

    def all_blocks(middle):
        for slot, given in enumerate(blocks):
            out, column = (near, slot * width) if slot < 2 else (far_first, 0)
            times_into(rows, given[0 if middle else -1], out, column)

    for middle in (0, 1):
        pl.when(place[MIDDLE] == middle)(functools.partial(all_blocks, middle))


def project_body(place, *refs, rows_in, slots):
    near, far_first, kept, sent = refs[-4:]
    rows, blocks = operands(refs, rows_in, slots)
    made, width = far_first.shape

    def all_blocks(keeps, middle):
        outs = (kept, sent) if keeps else (sent, kept)
        outs[0][:made] = near[...]
        outs[1][:made, :width] = far_first[...]
        columns = [given[0 if middle else -1] for given in blocks]
        for slot, block in enumerate(columns):
            far, at = divmod(slot, 2)
            times_into(rows[-1:], block, outs[far].at[pl.ds(made, outs[far].shape[0] - made)], at * width)
        times_into(rows[:-1], columns[3], outs[1], width)

    for keeps in (0, 1):
        for middle in (0, 1):
            here = (place[KEEPS] == keeps) & (place[MIDDLE] == middle)
            pl.when(here)(functools.partial(all_blocks, keeps, middle))


def project(place, rows, slots, made=None):
    flat = [piece for part in rows for piece in part] + [block for slot in slots for block in slot]
    flat += [] if made is None else list(made)
    count = sum(part[0].shape[0] for part in rows)
    depth, width = slots[0][0].shape
    widths = (2 * width, width) if len(slots) == 3 else (2 * width, 2 * width)
    held = pl.BlockSpec(memory_space=pltpu.VMEM)
    return pl.pallas_call(
        functools.partial(
            near_body if len(slots) == 3 else project_body,
            rows_in=tuple(map(len, rows)),
            slots=tuple(map(len, slots)),
        ),
        in_specs=[pl.BlockSpec(memory_space=pltpu.SMEM)] + [held] * len(flat),
        out_specs=[held] * 2,
        out_shape=[jax.ShapeDtypeStruct((count, wide), jnp.bfloat16) for wide in widths],
        compiler_params=pltpu.CompilerParams(vmem_limit_bytes=VMEM_LIMIT),
        cost_estimate=estimate(
            2 * count * depth * len(slots) * width,
            2 * (count * depth + len(slots) * width * (depth + count)),
        ),
        name="project",
    )(place, *flat)


def assemble_body(place, *refs):
    parts, out = refs[:-1], refs[-1]
    blocks = 2
    width = parts[0].shape[1] // blocks
    for j, part in enumerate(parts):
        for b in range(blocks):
            column = ((b ^ place[ODD]) * len(parts) + (place[SPOT] ^ j)) * width
            out[:, pl.ds(pl.multiple_of(column, LANES), width)] = part[:, b * width : (b + 1) * width]


def assemble(place, parts, blocks, width):
    share = len(parts)
    rows = parts[0].shape[0]
    held = pl.BlockSpec(memory_space=pltpu.VMEM)
    return pl.pallas_call(
        assemble_body,
        in_specs=[pl.BlockSpec(memory_space=pltpu.SMEM)] + [held] * share,
        out_specs=held,
        out_shape=jax.ShapeDtypeStruct((rows, share * blocks * width), jnp.bfloat16),
        compiler_params=pltpu.CompilerParams(vmem_limit_bytes=VMEM_LIMIT),
        cost_estimate=estimate(0, 4 * rows * share * blocks * width),
        name="assemble",
    )(place, *parts)


def after(value, *others):
    return lax.optimization_barrier((value, *others))[0]


def send_planes(value, group, moves):
    pairs = [(a * group + e, b * group + e) for a, b in moves for e in range(group)]
    return lax.ppermute(value, "ctx", pairs)


def plane_rows(hidden, count, group):
    if group != 4:
        return [hidden] + [[send_xor(part, count, group, j) for part in hidden] for j in range(1, group)]
    first, second = hidden
    first_1 = send_xor(first, count, group, 1)
    first_2 = send_xor(first, count, group, 2)
    second_2 = send_xor(second, count, group, 2)
    second_1 = send_xor(second, count, group, 1)
    first_3 = send_xor(first_1, count, group, 2)
    second_3 = send_xor(second_2, count, group, 1)
    return [[first, second], [first_1, second_1], [first_2, second_2], [first_3, second_3]]


def add_up_body(a, b, *outs):
    size = outs[0].shape[0]
    for j, out in enumerate(outs):
        rows = slice(j * size, (j + 1) * size)
        out[...] = (a[rows].astype(jnp.float32) + b[rows].astype(jnp.float32)).astype(out.dtype)


def add_up(a, b, parts):
    size, width = a.shape[0] // parts, a.shape[1]
    held = pl.BlockSpec(memory_space=pltpu.VMEM)
    return pl.pallas_call(
        add_up_body,
        in_specs=[held, held],
        out_specs=[held] * parts,
        out_shape=[jax.ShapeDtypeStruct((size, width), a.dtype)] * parts,
        compiler_params=pltpu.CompilerParams(vmem_limit_bytes=VMEM_LIMIT),
        cost_estimate=estimate(parts * size * width, 6 * parts * size * width),
        name="add_up",
    )(a, b)


def project_4x4(place, out_weight, states, hidden, count):
    group = 4
    swap = [(0, 1), (1, 0), (2, 3), (3, 2)]
    inner = [(1, 2), (2, 1)]
    outward = [(1, 0), (2, 3)]
    rows = plane_rows(hidden, count, group)
    own = out_weight
    by_1 = send_planes(own, group, swap)
    by_3_inner = send_planes(own, group, inner)
    by_2_inner = send_planes(after(by_1, states, by_3_inner), group, inner)
    by_2_outer = send_planes(after(by_3_inner, states), group, outward)
    by_3_outer = send_planes(after(by_2_inner, by_2_outer, rows[1][0], rows[2][0], hidden[1]), group, outward)
    blocks = [[own], [by_1], [by_2_inner, by_2_outer], [by_3_inner, by_3_outer]]

    made = project(place, rows[:3], blocks[:3])
    kept, sent = project(place, rows, blocks, made)
    mixed = add_up(kept, lax.ppermute(sent, "tp", [(0, 1), (1, 0)]), group)
    mixed = [mixed[0]] + [send_xor(mixed[j], count, group, j) for j in range(1, group)]
    return assemble(place, mixed, 2, out_weight.shape[1])


def project_any(out_weight, states, hidden, count):
    halves = lax.axis_size("tp")
    group = split_of(count)
    outer = count // group
    plane = lax.axis_index("ctx") // group
    size = hidden[0].shape[0]
    depth, width = out_weight.shape
    below, above = [out_weight], [out_weight]
    for k in range(1, outer):
        down, up = below[-1], above[-1]
        if k == 2:
            down, up = after(down, states), after(up, states)
        below.append(send_along(down, count, group, 1, k - 1))
        above.append(send_along(up, count, group, -1, k - 1))
    line = below[:0:-1] + above
    cols = lax.dynamic_slice_in_dim(jnp.stack(line), outer - 1 - plane, outer, 0)
    cols = jnp.moveaxis(cols, 0, 1).reshape(depth, outer * width)
    rows = plane_rows(hidden, count, group)
    held = jnp.concatenate([jnp.concatenate(part, axis=1) for part in rows], axis=0)
    partial = jnp.dot(held, cols, preferred_element_type=jnp.float32).astype(jnp.bfloat16)
    mixed = lax.psum_scatter(partial, "tp", scatter_dimension=1, tiled=True)
    mixed = jnp.split(mixed, group)
    mixed = [mixed[0]] + [send_xor(mixed[j], count, group, j) for j in range(1, group)]
    blocks = outer // halves
    stacked = jnp.stack(mixed).reshape(group, size, blocks, width)
    by_place = jnp.take(stacked, jnp.arange(group) ^ (lax.axis_index("ctx") % group), axis=0)
    return jnp.moveaxis(by_place, 0, 2).reshape(size, blocks * group * width)


def per_device(projected, short_filter, residues, rates, skip_gain, out_weight):
    count = lax.axis_size("ctx")
    halves = lax.axis_size("tp")
    here = lax.axis_index("ctx")
    rows, _, chans = projected.shape

    streams = jnp.transpose(projected, (1, 0, 2))
    rates_t = rates.T
    coef_t = (residues * jnp.sqrt(-jnp.expm1(-2.0 * rates))).T

    share = min(split_of(count), chans // LANES, 4)
    lines = count // share
    plane = here // share
    keeps = lax.axis_index("tp") == plane // 2
    place = jnp.stack([here % share, (plane == 1) | (plane == 2), keeps, plane % 2]).astype(jnp.int32)
    *ends, gated, prefix = local_scan(place, streams, short_filter, rates_t, share)
    ends = [ends[0]] + [send_xor(ends[j], count, share, j) for j in range(1, share)]
    whole, befores = plane_scan(place, rates_t, short_filter, ends, rows)
    arrived = [send_along(whole, count, share, k) for k in range(1, lines)]
    starts = line_scan(place, rates_t, short_filter, whole, befores, arrived, rows)
    states = starts[0]
    starts = [starts[0]] + [send_xor(starts[j], count, share, j) for j in range(1, share)]
    hidden = [
        hidden_rows(
            place, streams, short_filter, rates_t, coef_t, skip_gain[None], gated, prefix, starts, part
        )
        for part in range(2)
    ]
    if count == 16 and halves == 2 and out_weight.shape[1] % LANES == 0:
        return project_4x4(place, out_weight, states, hidden, count)
    return project_any(out_weight, states, hidden, count)


def solution(mesh):
    return jax.shard_map(
        per_device,
        mesh=mesh,
        in_specs=(
            P("ctx", None, "tp"),
            P(None, None, "tp"),
            P("tp", None),
            P("tp", None),
            P("tp"),
            P("tp", "ctx"),
        ),
        out_specs=P("ctx", "tp"),
        check_vma=False,
    )
```

```python
import functools

import jax
import jax.numpy as jnp
from jax import lax
from jax.experimental import pallas as pl
from jax.experimental.pallas import tpu as pltpu
from jax.sharding import PartitionSpec as P

LANES = 128
SEGS = 8
TOP = 8
SPOT, MIDDLE, KEEPS, ODD = range(4)
VMEM_LIMIT = 16 * 1024 * 1024
SMALL_LIMIT = 4 * 1024 * 1024
WHOLE_LIMIT = 50 * 1024 * 1024


def split_of(count):
    inner = 1
    while (2 * inner) ** 2 <= count and count % (2 * inner) == 0:
        inner *= 2
    return inner


def send_xor(value, count, group, step):
    pairs = [(p, p - p % group + ((p % group) ^ step)) for p in range(count)]
    return lax.ppermute(value, "ctx", pairs)


def send_along(value, count, group, steps, first=0):
    outer = count // group
    pairs = []
    for z in range(outer):
        if not 0 <= z + steps < outer:
            continue
        if (steps > 0 and z < first) or (steps < 0 and z > outer - 1 - first):
            continue
        pairs += [(z * group + e, (z + steps) * group + e) for e in range(group)]
    return lax.ppermute(value, "ctx", pairs)


def estimate(flops, bytes_accessed, transcendentals=0):
    return pl.CostEstimate(flops=flops, bytes_accessed=bytes_accessed, transcendentals=transcendentals)


def row(ref, r, lanes):
    return jnp.broadcast_to(ref[r : r + 1, lanes], (SEGS, LANES))


def lay_segments(dst, stream, halo, seg_len, lanes, group):
    pitch = seg_len + 1
    for s in range(SEGS):
        part = stream[0, s * seg_len : (s + 1) * seg_len, lanes].astype(jnp.float32)
        dst[group, TOP + s * pitch : TOP + s * pitch + seg_len, :] = part
    dst[group, TOP - 3 : TOP - 1, :] = jnp.zeros((2, LANES), jnp.float32) if halo is None else halo


def taps(short, stream, lanes):
    return [jnp.broadcast_to(short[i, stream : stream + 1, lanes], (SEGS, LANES)) for i in range(3)]


def strided(ref, group, start, pitch):
    return ref[group, pl.ds(start, SEGS, stride=pitch), :]


LAST, FIRST = 6, 4


def first_gated(short, first, last):
    products = []
    for b, stream in enumerate((1, 2)):
        tap = [short[i, stream : stream + 1, :] for i in range(3)]
        now_0, now_1 = first[2 * b : 2 * b + 1], first[2 * b + 1 : 2 * b + 2]
        old_2, old_1 = last[2 * stream : 2 * stream + 1], last[2 * stream + 1 : 2 * stream + 2]
        products.append(
            (
                tap[0] * now_0 + tap[1] * old_1 + tap[2] * old_2,
                tap[0] * now_1 + tap[1] * now_0 + tap[2] * old_1,
            )
        )
    return products[0][0] * products[1][0], products[0][1] * products[1][1]


def end_share(short, rates, first, last, rows):
    gated_0, gated_1 = first_gated(short, first, last)
    return jnp.exp(rates * (1.0 - rows)) * gated_0 + jnp.exp(rates * (2.0 - rows)) * gated_1


def local_scan_body(place, streams, short_all, rates_all, *rest, seg_len, order, share):
    ends = rest[:share]
    gated, prefix = rest[share : share + 2]
    key_pos, value_pos, end_now, table, held, query_held, short_held, rates_held, held_sem, small_sem = rest[share + 2 :]
    now_at = pl.program_id(0)
    wide = end_now.shape[1]
    small = [
        pltpu.make_async_copy(short_all, short_held, small_sem.at[0]),
        pltpu.make_async_copy(rates_all, rates_held, small_sem.at[1]),
        pltpu.make_async_copy(
            streams.at[0, pl.ds(seg_len * SEGS - 16, 16), :], query_held, small_sem.at[2]
        ),
    ]

    def stream_copy(at):
        columns = pl.ds(at * wide, wide)
        return pltpu.make_async_copy(
            streams.at[pl.ds(1, 2), :, columns], held.at[:, :, columns], held_sem.at[at]
        )

    @pl.when(now_at == 0)
    def _():
        stream_copy(0).start()
        for copy in small:
            copy.start()
        for at in range(1, share):
            stream_copy(at).start()
        for copy in small:
            copy.wait()

    for at in range(share):

        @pl.when(now_at == at)
        def _(at=at):
            stream_copy(at).wait()

    columns = pl.ds(pl.multiple_of(now_at * wide, LANES), wide)
    key = held.at[pl.ds(0, 1), :, columns]
    value = held.at[pl.ds(1, 1), :, columns]
    short = short_held.at[:, :, columns]
    rates = rates_held[:, columns]
    table[0] = jnp.exp(-rates)
    for e, d in enumerate((1, 2, 4)):
        table[1 + e] = jnp.exp(rates * (-1.0 * d * seg_len))
    pitch = seg_len + 1
    groups = gated.shape[0]
    segment = lax.broadcasted_iota(jnp.int32, (SEGS, LANES), 0)
    for group in range(groups):
        lanes = slice(group * LANES, (group + 1) * LANES)
        lay_segments(key_pos, key, None, seg_len, lanes, group)
        lay_segments(value_pos, value, None, seg_len, lanes, group)
    bottom = seg_len * SEGS - 2
    end_now[order : order + 2, :] = query_held[14:16, columns].astype(jnp.float32)
    for b, stream in enumerate((key, value)):
        at = order + 2 + 2 * b
        end_now[at : at + 2, :] = stream[0, bottom : bottom + 2, :].astype(jnp.float32)
        at = order + LAST + 2 * b
        end_now[at : at + 2, :] = stream[0, 0:2, :].astype(jnp.float32)

    for group in range(groups):
        lanes = slice(group * LANES, (group + 1) * LANES)
        key_taps = taps(short, 1, lanes)
        value_taps = taps(short, 2, lanes)
        decay = [row(table.at[0], r, lanes) for r in range(order)]

        def step(i, carry, early=False, group=group, key_taps=key_taps, value_taps=value_taps, decay=decay):
            k1, k2, v1, v2, *states = carry
            k0 = strided(key_pos, group, TOP + i, pitch)
            v0 = strided(value_pos, group, TOP + i, pitch)
            key_now = key_taps[0] * k0 + key_taps[1] * k1 + key_taps[2] * k2
            value_now = value_taps[0] * v0 + value_taps[1] * v1 + value_taps[2] * v2
            now = key_now * value_now
            if early:
                now = jnp.where(segment >= 1, now, 0.0)
            gated[group, pl.ds(pl.multiple_of(i * SEGS, SEGS), SEGS), :] = now
            states = [d * h + now for d, h in zip(decay, states)]
            return (k0, k1, v0, v1, *states)

        zero = jnp.zeros((SEGS, LANES), jnp.float32)
        start = (
            strided(key_pos, group, TOP - 2, pitch),
            strided(key_pos, group, TOP - 3, pitch),
            strided(value_pos, group, TOP - 2, pitch),
            strided(value_pos, group, TOP - 3, pitch),
        ) + (zero,) * order
        start = step(1, step(0, start, True), True)
        states = lax.fori_loop(2, seg_len, step, start, unroll=seg_len - 2)[4:]
        for r in range(order):
            scan = states[r]
            for e, d in enumerate((1, 2, 4)):
                moved = jnp.where(segment >= d, pltpu.roll(scan, d, 0), 0.0)
                scan = scan + row(table.at[1 + e], r, lanes) * moved
            prefix[group, r] = jnp.where(segment >= 1, pltpu.roll(scan, 1, 0), 0.0)
            end_now[r : r + 1, lanes] = scan[SEGS - 1 :, :]

    for j in range(share):

        @pl.when((pl.program_id(0) ^ place[SPOT]) == j)
        def _(j=j):
            ends[j][...] = end_now[...]


def local_scan(place, streams, short, rates, share):
    _, rows, chans = streams.shape
    order = rates.shape[0]
    wide = chans // share
    groups = wide // LANES
    seg_len = rows // SEGS
    pos_rows = TOP + SEGS * (seg_len + 1)
    end_shape = jax.ShapeDtypeStruct((order + LAST + FIRST, wide), jnp.float32)
    return pl.pallas_call(
        functools.partial(local_scan_body, seg_len=seg_len, order=order, share=share),
        grid_spec=pltpu.PrefetchScalarGridSpec(
            num_scalar_prefetch=1,
            grid=(share,),
            in_specs=[
                pl.BlockSpec(memory_space=pltpu.HBM),
                pl.BlockSpec(memory_space=pltpu.HBM),
                pl.BlockSpec(memory_space=pltpu.HBM),
            ],
            out_specs=[pl.BlockSpec((order + LAST + FIRST, wide), lambda g, place: (0, 0))] * share
            + [
                pl.BlockSpec((groups, rows, LANES), lambda g, place: (g, 0, 0)),
                pl.BlockSpec((groups, order, SEGS, LANES), lambda g, place: (g, 0, 0, 0)),
            ],
            scratch_shapes=[
                pltpu.VMEM((groups, pos_rows, LANES), jnp.float32),
                pltpu.VMEM((groups, pos_rows, LANES), jnp.float32),
                pltpu.VMEM((order + LAST + FIRST, wide), jnp.float32),
                pltpu.VMEM((4, order, wide), jnp.float32),
                pltpu.VMEM((2, rows, chans), streams.dtype),
                pltpu.VMEM((16, chans), streams.dtype),
                pltpu.VMEM(short.shape, jnp.float32),
                pltpu.VMEM(rates.shape, jnp.float32),
                pltpu.SemaphoreType.DMA((share,)),
                pltpu.SemaphoreType.DMA((3,)),
            ],
        ),
        out_shape=[end_shape] * share
        + [
            jax.ShapeDtypeStruct((chans // LANES, rows, LANES), jnp.float32),
            jax.ShapeDtypeStruct((chans // LANES, order, SEGS, LANES), jnp.float32),
        ],
        compiler_params=pltpu.CompilerParams(vmem_limit_bytes=WHOLE_LIMIT),
        cost_estimate=estimate(rows * chans * 50, rows * chans * 10),
        name="local_scan",
    )(place, streams, short, rates)


def plane_scan_body(place, rates, short, *rest, share, rows):
    ends = rest[:share]
    whole = rest[share]
    befores = rest[share + 1 : 2 * share + 1]
    by_place, before_place = rest[2 * share + 1 :]
    order = rates.shape[0]
    here = place[SPOT]
    for j in range(share):
        by_place[here ^ j] = ends[j][...]
    rate = rates[...]
    decay = jnp.exp(rate * (-1.0 * rows))
    state = jnp.zeros(rate.shape, jnp.float32)
    for at in range(share):
        before_place[at, :order] = state
        state = decay * state + by_place[at, :order]
        if at > 0:
            last = by_place[at - 1, order : order + LAST]
            before_place[at, order:] = last
            state += end_share(short, rate, by_place[at, order + LAST :], last, rows)
    before_place[0, order:] = jnp.zeros((LAST, rate.shape[1]), jnp.float32)
    whole[:order] = state
    whole[order : order + LAST] = by_place[share - 1, order : order + LAST]
    whole[order + LAST :] = by_place[0, order + LAST :]
    for j in range(share):
        befores[j][...] = before_place[here ^ j]


def plane_scan(place, rates, short, ends, rows):
    share = len(ends)
    order = rates.shape[0]
    wide = ends[0].shape[1]
    block = pl.BlockSpec((order + LAST, wide), lambda g, place: (0, 0))
    edged = pl.BlockSpec((order + LAST + FIRST, wide), lambda g, place: (0, 0))
    shape = jax.ShapeDtypeStruct((order + LAST, wide), jnp.float32)
    got = pl.pallas_call(
        functools.partial(plane_scan_body, share=share, rows=rows),
        grid_spec=pltpu.PrefetchScalarGridSpec(
            num_scalar_prefetch=1,
            grid=(1,),
            in_specs=[
                pl.BlockSpec((order, wide), lambda g, place: (0, place[SPOT])),
                pl.BlockSpec((3, 3, wide), lambda g, place: (0, 0, place[SPOT])),
            ]
            + [edged] * share,
            out_specs=[edged] + [block] * share,
            scratch_shapes=[
                pltpu.VMEM((share, order + LAST + FIRST, wide), jnp.float32),
                pltpu.VMEM((share, order + LAST, wide), jnp.float32),
            ],
        ),
        out_shape=[jax.ShapeDtypeStruct((order + LAST + FIRST, wide), jnp.float32)] + [shape] * share,
        compiler_params=pltpu.CompilerParams(vmem_limit_bytes=SMALL_LIMIT),
        cost_estimate=estimate(order * wide * 20, order * wide * 36),
        name="plane_scan",
    )(place, rates, short, *ends)
    return got[0], got[1:]


def line_scan_body(place, rates, short, whole, *rest, share, rows, lines):
    befores = rest[:share]
    arrived = rest[share : share + lines]
    outs = rest[share + lines :]
    order = rates.shape[0]
    here = place[SPOT]
    rate = rates[...]
    planes = (whole,) + tuple(arrived)

    def last_rows(k):
        if k < lines:
            return planes[k + 1][order : order + LAST]
        return jnp.zeros((LAST, rate.shape[1]), jnp.float32)

    def first_share(k):
        return end_share(short, rate, planes[k][order + LAST :], last_rows(k), rows)

    state = jnp.zeros(rate.shape, jnp.float32)
    decay = jnp.exp(rate * (-1.0 * rows * share))
    later = jnp.exp(rate * (-1.0 * rows * (share - 1)))
    for k in reversed(range(1, lines + 1)):
        state = decay * state + planes[k][:order] + later * first_share(k)
    own = first_share(0)
    for j in range(share):
        at = (here ^ j).astype(jnp.float32)
        inside = jnp.minimum(at, 1.0)
        past = inside * jnp.exp(rate * (jnp.maximum(at - 1.0, 0.0) * (-1.0 * rows)))
        before = befores[j][:order]
        outs[j][:order] = before + jnp.exp(rate * (at * (-1.0 * rows))) * state + past * own
        outs[j][order:] = befores[j][order:] + (1.0 - inside) * last_rows(0)


def line_scan(place, rates, short, whole, befores, arrived, rows):
    share, lines = len(befores), len(arrived)
    order, wide = rates.shape[0], whole.shape[1]
    block = pl.BlockSpec((order + LAST, wide), lambda g, place: (0, 0))
    edged = pl.BlockSpec((order + LAST + FIRST, wide), lambda g, place: (0, 0))
    return pl.pallas_call(
        functools.partial(line_scan_body, share=share, rows=rows, lines=lines),
        grid_spec=pltpu.PrefetchScalarGridSpec(
            num_scalar_prefetch=1,
            grid=(1,),
            in_specs=[
                pl.BlockSpec((order, wide), lambda g, place: (0, place[SPOT])),
                pl.BlockSpec((3, 3, wide), lambda g, place: (0, 0, place[SPOT])),
                edged,
            ]
            + [block] * share
            + [edged] * lines,
            out_specs=[block] * share,
        ),
        out_shape=[jax.ShapeDtypeStruct((order + LAST, wide), jnp.float32)] * share,
        compiler_params=pltpu.CompilerParams(vmem_limit_bytes=SMALL_LIMIT),
        cost_estimate=estimate(order * wide * 20, order * wide * 36),
        name="line_scan",
    )(place, rates, short, whole, *befores, *arrived)


def hidden_body(place, query, top, short, rates, coef, skip, gated, prefix, *rest, seg_len, order, share, first):
    starts = rest[:share]
    hidden = rest[share]
    query_pos, result_pos, start_by_place, table = rest[share + 1 :]
    pitch = seg_len + 1
    groups = gated.shape[0]
    now_at = pl.program_id(0) + first
    table[0] = jnp.exp(-rates[...])
    table[1] = jnp.exp(rates[...])
    segment = lax.broadcasted_iota(jnp.int32, (SEGS, LANES), 0).astype(jnp.float32)

    @pl.when(pl.program_id(0) == 0)
    def _():
        for j in range(share):
            start_by_place[place[SPOT] ^ j] = starts[j][...]

    for group in range(groups):
        lanes = slice(group * LANES, (group + 1) * LANES)
        ending = start_by_place[now_at, order : order + 2, lanes]
        lay_segments(query_pos, query, ending, seg_len, lanes, group)

    for group in range(groups):
        lanes = slice(group * LANES, (group + 1) * LANES)
        query_taps = taps(short, 0, lanes)
        gain = jnp.broadcast_to(skip[0:1, lanes], (SEGS, LANES))
        decay = [row(table.at[0], r, lanes) for r in range(order)]
        scale = [row(coef, r, lanes) for r in range(order)]
        first = jnp.concatenate([top[b, 0:2, lanes] for b in (1, 2)], axis=0).astype(jnp.float32)
        last = start_by_place[now_at, order:, lanes]
        early = [
            jnp.broadcast_to(value, (SEGS, LANES))
            for value in first_gated(short.at[:, :, lanes], first, last)
        ]
        states = []
        for r in range(order):
            rate = row(rates, r, lanes)
            ahead = jnp.exp(rate * (segment * (-1.0 * seg_len)))
            before = jnp.broadcast_to(start_by_place[now_at, r : r + 1, lanes], (SEGS, LANES))
            grown = row(table.at[1], r, lanes)
            before += jnp.where(segment >= 1.0, grown * (early[0] + grown * early[1]), 0.0)
            states.append(prefix[group, r] + ahead * before)

        def step(
            i, carry, late=None, group=group, query_taps=query_taps, gain=gain, decay=decay, scale=scale
        ):
            q1, q2, *states = carry
            q0 = strided(query_pos, group, TOP + i, pitch)
            now = gated[group, pl.ds(pl.multiple_of(i * SEGS, SEGS), SEGS), :]
            if late is not None:
                now = jnp.where(segment >= 1.0, now, late)
            states = [d * h + now for d, h in zip(decay, states)]
            sums = [s * h for s, h in zip(scale, states)] + [gain * now]
            while len(sums) > 1:
                sums = [a + b for a, b in zip(sums[::2], sums[1::2])] + sums[len(sums) // 2 * 2 :]
            query_now = query_taps[0] * q0 + query_taps[1] * q1 + query_taps[2] * q2
            result_pos[group, pl.ds(TOP + i, SEGS, stride=pitch), :] = query_now * sums[0]
            return (q0, q1, *states)

        start = (
            strided(query_pos, group, TOP - 2, pitch),
            strided(query_pos, group, TOP - 3, pitch),
        ) + tuple(states)
        start = step(1, step(0, start, early[0]), early[1])
        lax.fori_loop(2, seg_len, step, start, unroll=seg_len - 2)
        for s in range(SEGS):
            part = result_pos[group, TOP + s * pitch : TOP + s * pitch + seg_len, :]
            hidden[s * seg_len : (s + 1) * seg_len, lanes] = part.astype(hidden.dtype)


def hidden_rows(place, streams, short, rates, coef, skip, gated, prefix, starts, part):
    _, rows, chans = streams.shape
    order = rates.shape[0]
    share = len(starts)
    wide = chans // share
    groups = wide // LANES
    seg_len = rows // SEGS
    steps = max(1, share // 2)
    first = part * steps
    pos_rows = TOP + SEGS * (seg_len + 1)
    return pl.pallas_call(
        functools.partial(hidden_body, seg_len=seg_len, order=order, share=share, first=first),
        grid_spec=pltpu.PrefetchScalarGridSpec(
            num_scalar_prefetch=1,
            grid=(steps,),
            in_specs=[
                pl.BlockSpec((1, rows, wide), lambda g, place: (0, 0, first + g)),
                pl.BlockSpec((3, 16, wide), lambda g, place: (0, 0, first + g)),
                pl.BlockSpec((3, 3, wide), lambda g, place: (0, 0, first + g)),
                pl.BlockSpec((order, wide), lambda g, place: (0, first + g)),
                pl.BlockSpec((order, wide), lambda g, place: (0, first + g)),
                pl.BlockSpec((1, wide), lambda g, place: (0, first + g)),
                pl.BlockSpec((groups, rows, LANES), lambda g, place: (first + g, 0, 0)),
                pl.BlockSpec((groups, order, SEGS, LANES), lambda g, place: (first + g, 0, 0, 0)),
            ]
            + [pl.BlockSpec((order + LAST, wide), lambda g, place: (0, 0))] * share,
            out_specs=pl.BlockSpec((rows, wide), lambda g, place: (0, g)),
            scratch_shapes=[
                pltpu.VMEM((groups, pos_rows, LANES), jnp.float32),
                pltpu.VMEM((groups, pos_rows, LANES), jnp.float32),
                pltpu.VMEM((share, order + LAST, wide), jnp.float32),
                pltpu.VMEM((2, order, wide), jnp.float32),
            ],
        ),
        out_shape=jax.ShapeDtypeStruct((rows, steps * wide), jnp.bfloat16),
        compiler_params=pltpu.CompilerParams(vmem_limit_bytes=VMEM_LIMIT),
        cost_estimate=estimate(rows * chans * 40, rows * chans * 5),
        name="hidden_rows",
    )(place, streams, streams, short, rates, coef, skip, gated, prefix, *starts)


def times_into(rows, columns, out, column):
    width = columns.shape[1]
    top = 0
    for part in rows:
        size = part[0].shape[0]
        joined = jnp.concatenate([piece[...] for piece in part], axis=1)
        total = jnp.dot(joined, columns[...], preferred_element_type=jnp.float32)
        out[top : top + size, column : column + width] = total.astype(out.dtype)
        top += size


def operands(refs, rows_in, slots):
    at = 0
    rows, blocks = [], []
    for group, counts in ((rows, rows_in), (blocks, slots)):
        for count in counts:
            group.append(refs[at : at + count])
            at += count
    return rows, blocks


def near_body(place, *refs, rows_in, slots):
    near, far_first = refs[-2:]
    rows, blocks = operands(refs, rows_in, slots)
    width = far_first.shape[1]

    def all_blocks(middle):
        for slot, given in enumerate(blocks):
            out, column = (near, slot * width) if slot < 2 else (far_first, 0)
            times_into(rows, given[0 if middle else -1], out, column)

    for middle in (0, 1):
        pl.when(place[MIDDLE] == middle)(functools.partial(all_blocks, middle))


def project_body(place, *refs, rows_in, slots):
    near, far_first, kept, sent = refs[-4:]
    rows, blocks = operands(refs, rows_in, slots)
    made, width = far_first.shape

    def all_blocks(keeps, middle):
        outs = (kept, sent) if keeps else (sent, kept)
        outs[0][:made] = near[...]
        outs[1][:made, :width] = far_first[...]
        columns = [given[0 if middle else -1] for given in blocks]
        for slot, block in enumerate(columns):
            far, at = divmod(slot, 2)
            times_into(rows[-1:], block, outs[far].at[pl.ds(made, outs[far].shape[0] - made)], at * width)
        times_into(rows[:-1], columns[3], outs[1], width)

    for keeps in (0, 1):
        for middle in (0, 1):
            here = (place[KEEPS] == keeps) & (place[MIDDLE] == middle)
            pl.when(here)(functools.partial(all_blocks, keeps, middle))


def project(place, rows, slots, made=None):
    flat = [piece for part in rows for piece in part] + [block for slot in slots for block in slot]
    flat += [] if made is None else list(made)
    count = sum(part[0].shape[0] for part in rows)
    depth, width = slots[0][0].shape
    widths = (2 * width, width) if len(slots) == 3 else (2 * width, 2 * width)
    held = pl.BlockSpec(memory_space=pltpu.VMEM)
    return pl.pallas_call(
        functools.partial(
            near_body if len(slots) == 3 else project_body,
            rows_in=tuple(map(len, rows)),
            slots=tuple(map(len, slots)),
        ),
        in_specs=[pl.BlockSpec(memory_space=pltpu.SMEM)] + [held] * len(flat),
        out_specs=[held] * 2,
        out_shape=[jax.ShapeDtypeStruct((count, wide), jnp.bfloat16) for wide in widths],
        compiler_params=pltpu.CompilerParams(vmem_limit_bytes=VMEM_LIMIT),
        cost_estimate=estimate(
            2 * count * depth * len(slots) * width,
            2 * (count * depth + len(slots) * width * (depth + count)),
        ),
        name="project",
    )(place, *flat)


def assemble_body(place, *refs):
    parts, out = refs[:-1], refs[-1]
    blocks = 2
    width = parts[0].shape[1] // blocks
    for j, part in enumerate(parts):
        for b in range(blocks):
            column = ((b ^ place[ODD]) * len(parts) + (place[SPOT] ^ j)) * width
            out[:, pl.ds(pl.multiple_of(column, LANES), width)] = part[:, b * width : (b + 1) * width]


def assemble(place, parts, blocks, width):
    share = len(parts)
    rows = parts[0].shape[0]
    held = pl.BlockSpec(memory_space=pltpu.VMEM)
    return pl.pallas_call(
        assemble_body,
        in_specs=[pl.BlockSpec(memory_space=pltpu.SMEM)] + [held] * share,
        out_specs=held,
        out_shape=jax.ShapeDtypeStruct((rows, share * blocks * width), jnp.bfloat16),
        compiler_params=pltpu.CompilerParams(vmem_limit_bytes=VMEM_LIMIT),
        cost_estimate=estimate(0, 4 * rows * share * blocks * width),
        name="assemble",
    )(place, *parts)


def after(value, *others):
    return lax.optimization_barrier((value, *others))[0]


def send_planes(value, group, moves):
    pairs = [(a * group + e, b * group + e) for a, b in moves for e in range(group)]
    return lax.ppermute(value, "ctx", pairs)


def plane_rows(hidden, count, group):
    if group != 4:
        return [hidden] + [[send_xor(part, count, group, j) for part in hidden] for j in range(1, group)]
    first, second = hidden
    first_1 = send_xor(first, count, group, 1)
    first_2 = send_xor(first, count, group, 2)
    second_2 = send_xor(second, count, group, 2)
    second_1 = send_xor(second, count, group, 1)
    first_3 = send_xor(first_1, count, group, 2)
    second_3 = send_xor(second_2, count, group, 1)
    return [[first, second], [first_1, second_1], [first_2, second_2], [first_3, second_3]]


def add_up_body(a, b, *outs):
    size = outs[0].shape[0]
    for j, out in enumerate(outs):
        rows = slice(j * size, (j + 1) * size)
        out[...] = (a[rows].astype(jnp.float32) + b[rows].astype(jnp.float32)).astype(out.dtype)


def add_up(a, b, parts):
    size, width = a.shape[0] // parts, a.shape[1]
    held = pl.BlockSpec(memory_space=pltpu.VMEM)
    return pl.pallas_call(
        add_up_body,
        in_specs=[held, held],
        out_specs=[held] * parts,
        out_shape=[jax.ShapeDtypeStruct((size, width), a.dtype)] * parts,
        compiler_params=pltpu.CompilerParams(vmem_limit_bytes=VMEM_LIMIT),
        cost_estimate=estimate(parts * size * width, 6 * parts * size * width),
        name="add_up",
    )(a, b)


def project_4x4(place, out_weight, states, hidden, count):
    group = 4
    swap = [(0, 1), (1, 0), (2, 3), (3, 2)]
    inner = [(1, 2), (2, 1)]
    outward = [(1, 0), (2, 3)]
    rows = plane_rows(hidden, count, group)
    own = out_weight
    by_1 = send_planes(own, group, swap)
    by_3_inner = send_planes(own, group, inner)
    by_2_inner = send_planes(after(by_1, states, by_3_inner), group, inner)
    by_2_outer = send_planes(after(by_3_inner, states), group, outward)
    by_3_outer = send_planes(after(by_2_inner, by_2_outer, rows[1][0], rows[2][0], hidden[1]), group, outward)
    blocks = [[own], [by_1], [by_2_inner, by_2_outer], [by_3_inner, by_3_outer]]

    made = project(place, rows[:3], blocks[:3])
    kept, sent = project(place, rows, blocks, made)
    mixed = add_up(kept, lax.ppermute(sent, "tp", [(0, 1), (1, 0)]), group)
    mixed = [mixed[0]] + [send_xor(mixed[j], count, group, j) for j in range(1, group)]
    return assemble(place, mixed, 2, out_weight.shape[1])


def project_any(out_weight, states, hidden, count):
    halves = lax.axis_size("tp")
    group = split_of(count)
    outer = count // group
    plane = lax.axis_index("ctx") // group
    size = hidden[0].shape[0]
    depth, width = out_weight.shape
    below, above = [out_weight], [out_weight]
    for k in range(1, outer):
        down, up = below[-1], above[-1]
        if k == 2:
            down, up = after(down, states), after(up, states)
        below.append(send_along(down, count, group, 1, k - 1))
        above.append(send_along(up, count, group, -1, k - 1))
    line = below[:0:-1] + above
    cols = lax.dynamic_slice_in_dim(jnp.stack(line), outer - 1 - plane, outer, 0)
    cols = jnp.moveaxis(cols, 0, 1).reshape(depth, outer * width)
    rows = plane_rows(hidden, count, group)
    held = jnp.concatenate([jnp.concatenate(part, axis=1) for part in rows], axis=0)
    partial = jnp.dot(held, cols, preferred_element_type=jnp.float32).astype(jnp.bfloat16)
    mixed = lax.psum_scatter(partial, "tp", scatter_dimension=1, tiled=True)
    mixed = jnp.split(mixed, group)
    mixed = [mixed[0]] + [send_xor(mixed[j], count, group, j) for j in range(1, group)]
    blocks = outer // halves
    stacked = jnp.stack(mixed).reshape(group, size, blocks, width)
    by_place = jnp.take(stacked, jnp.arange(group) ^ (lax.axis_index("ctx") % group), axis=0)
    return jnp.moveaxis(by_place, 0, 2).reshape(size, blocks * group * width)


def per_device(projected, short_filter, residues, rates, skip_gain, out_weight):
    count = lax.axis_size("ctx")
    halves = lax.axis_size("tp")
    here = lax.axis_index("ctx")
    rows, _, chans = projected.shape

    streams = jnp.transpose(projected, (1, 0, 2))
    rates_t = rates.T
    coef_t = (residues * jnp.sqrt(-jnp.expm1(-2.0 * rates))).T

    share = min(split_of(count), chans // LANES, 4)
    lines = count // share
    plane = here // share
    keeps = lax.axis_index("tp") == plane // 2
    place = jnp.stack([here % share, (plane == 1) | (plane == 2), keeps, plane % 2]).astype(jnp.int32)
    *ends, gated, prefix = local_scan(place, streams, short_filter, rates_t, share)
    ends = [ends[0]] + [send_xor(ends[j], count, share, j) for j in range(1, share)]
    whole, befores = plane_scan(place, rates_t, short_filter, ends, rows)
    arrived = [send_along(whole, count, share, k) for k in range(1, lines)]
    starts = line_scan(place, rates_t, short_filter, whole, befores, arrived, rows)
    states = starts[0]
    starts = [starts[0]] + [send_xor(starts[j], count, share, j) for j in range(1, share)]
    hidden = [
        hidden_rows(
            place, streams, short_filter, rates_t, coef_t, skip_gain[None], gated, prefix, starts, part
        )
        for part in range(2)
    ]
    if count == 16 and halves == 2 and out_weight.shape[1] % LANES == 0:
        return project_4x4(place, out_weight, states, hidden, count)
    return project_any(out_weight, states, hidden, count)


def solution(mesh):
    return jax.shard_map(
        per_device,
        mesh=mesh,
        in_specs=(
            P("ctx", None, "tp"),
            P(None, None, "tp"),
            P("tp", None),
            P("tp", None),
            P("tp"),
            P("tp", "ctx"),
        ),
        out_specs=P("ctx", "tp"),
        check_vma=False,
    )
```

```python
import functools

import jax
import jax.numpy as jnp
from jax import lax
from jax.experimental import pallas as pl
from jax.experimental.pallas import tpu as pltpu
from jax.sharding import PartitionSpec as P

LANES = 128
SEGS = 8
TOP = 8
SPOT, MIDDLE, KEEPS, ODD = range(4)
VMEM_LIMIT = 16 * 1024 * 1024
SMALL_LIMIT = 4 * 1024 * 1024
WHOLE_LIMIT = 50 * 1024 * 1024


def split_of(count):
    inner = 1
    while (2 * inner) ** 2 <= count and count % (2 * inner) == 0:
        inner *= 2
    return inner


def send_xor(value, count, group, step):
    pairs = [(p, p - p % group + ((p % group) ^ step)) for p in range(count)]
    return lax.ppermute(value, "ctx", pairs)


def send_along(value, count, group, steps, first=0):
    outer = count // group
    pairs = []
    for z in range(outer):
        if not 0 <= z + steps < outer:
            continue
        if (steps > 0 and z < first) or (steps < 0 and z > outer - 1 - first):
            continue
        pairs += [(z * group + e, (z + steps) * group + e) for e in range(group)]
    return lax.ppermute(value, "ctx", pairs)


def estimate(flops, bytes_accessed, transcendentals=0):
    return pl.CostEstimate(flops=flops, bytes_accessed=bytes_accessed, transcendentals=transcendentals)


def row(ref, r, lanes):
    return jnp.broadcast_to(ref[r : r + 1, lanes], (SEGS, LANES))


def lay_segments(dst, stream, halo, seg_len, lanes, group):
    pitch = seg_len + 1
    for s in range(SEGS):
        part = stream[0, s * seg_len : (s + 1) * seg_len, lanes].astype(jnp.float32)
        dst[group, TOP + s * pitch : TOP + s * pitch + seg_len, :] = part
    dst[group, TOP - 3 : TOP - 1, :] = jnp.zeros((2, LANES), jnp.float32) if halo is None else halo


def taps(short, stream, lanes):
    return [jnp.broadcast_to(short[i, stream : stream + 1, lanes], (SEGS, LANES)) for i in range(3)]


def strided(ref, group, start, pitch):
    return ref[group, pl.ds(start, SEGS, stride=pitch), :]


LAST, FIRST = 6, 4


def first_gated(short, first, last):
    products = []
    for b, stream in enumerate((1, 2)):
        tap = [short[i, stream : stream + 1, :] for i in range(3)]
        now_0, now_1 = first[2 * b : 2 * b + 1], first[2 * b + 1 : 2 * b + 2]
        old_2, old_1 = last[2 * stream : 2 * stream + 1], last[2 * stream + 1 : 2 * stream + 2]
        products.append(
            (
                tap[0] * now_0 + tap[1] * old_1 + tap[2] * old_2,
                tap[0] * now_1 + tap[1] * now_0 + tap[2] * old_1,
            )
        )
    return products[0][0] * products[1][0], products[0][1] * products[1][1]


def end_share(short, rates, first, last, rows):
    gated_0, gated_1 = first_gated(short, first, last)
    return jnp.exp(rates * (1.0 - rows)) * gated_0 + jnp.exp(rates * (2.0 - rows)) * gated_1


def local_scan_body(place, streams, short_all, rates_all, *rest, seg_len, order, share):
    ends = rest[:share]
    gated, prefix = rest[share : share + 2]
    key_pos, value_pos, end_now, table, held, query_held, short_held, rates_held, held_sem, small_sem = rest[share + 2 :]
    now_at = pl.program_id(0)
    wide = end_now.shape[1]
    small = [
        pltpu.make_async_copy(short_all, short_held, small_sem.at[0]),
        pltpu.make_async_copy(rates_all, rates_held, small_sem.at[1]),
        pltpu.make_async_copy(
            streams.at[0, pl.ds(seg_len * SEGS - 16, 16), :], query_held, small_sem.at[2]
        ),
    ]

    def stream_copy(at):
        columns = pl.ds(at * wide, wide)
        return pltpu.make_async_copy(
            streams.at[pl.ds(1, 2), :, columns], held.at[:, :, columns], held_sem.at[at]
        )

    @pl.when(now_at == 0)
    def _():
        stream_copy(0).start()
        for copy in small:
            copy.start()
        for at in range(1, share):
            stream_copy(at).start()
        for copy in small:
            copy.wait()

    for at in range(share):

        @pl.when(now_at == at)
        def _(at=at):
            stream_copy(at).wait()

    columns = pl.ds(pl.multiple_of(now_at * wide, LANES), wide)
    key = held.at[pl.ds(0, 1), :, columns]
    value = held.at[pl.ds(1, 1), :, columns]
    short = short_held.at[:, :, columns]
    rates = rates_held[:, columns]
    table[0] = jnp.exp(-rates)
    for e, d in enumerate((1, 2, 4)):
        table[1 + e] = jnp.exp(rates * (-1.0 * d * seg_len))
    pitch = seg_len + 1
    groups = gated.shape[0]
    segment = lax.broadcasted_iota(jnp.int32, (SEGS, LANES), 0)
    for group in range(groups):
        lanes = slice(group * LANES, (group + 1) * LANES)
        lay_segments(key_pos, key, None, seg_len, lanes, group)
        lay_segments(value_pos, value, None, seg_len, lanes, group)
    bottom = seg_len * SEGS - 2
    end_now[order : order + 2, :] = query_held[14:16, columns].astype(jnp.float32)
    for b, stream in enumerate((key, value)):
        at = order + 2 + 2 * b
        end_now[at : at + 2, :] = stream[0, bottom : bottom + 2, :].astype(jnp.float32)
        at = order + LAST + 2 * b
        end_now[at : at + 2, :] = stream[0, 0:2, :].astype(jnp.float32)

    for group in range(groups):
        lanes = slice(group * LANES, (group + 1) * LANES)
        key_taps = taps(short, 1, lanes)
        value_taps = taps(short, 2, lanes)
        decay = [row(table.at[0], r, lanes) for r in range(order)]

        def step(i, carry, early=False, group=group, key_taps=key_taps, value_taps=value_taps, decay=decay):
            k1, k2, v1, v2, *states = carry
            k0 = strided(key_pos, group, TOP + i, pitch)
            v0 = strided(value_pos, group, TOP + i, pitch)
            key_now = key_taps[0] * k0 + key_taps[1] * k1 + key_taps[2] * k2
            value_now = value_taps[0] * v0 + value_taps[1] * v1 + value_taps[2] * v2
            now = key_now * value_now
            if early:
                now = jnp.where(segment >= 1, now, 0.0)
            gated[group, pl.ds(pl.multiple_of(i * SEGS, SEGS), SEGS), :] = now
            states = [d * h + now for d, h in zip(decay, states)]
            return (k0, k1, v0, v1, *states)

        zero = jnp.zeros((SEGS, LANES), jnp.float32)
        start = (
            strided(key_pos, group, TOP - 2, pitch),
            strided(key_pos, group, TOP - 3, pitch),
            strided(value_pos, group, TOP - 2, pitch),
            strided(value_pos, group, TOP - 3, pitch),
        ) + (zero,) * order
        start = step(1, step(0, start, True), True)
        states = lax.fori_loop(2, seg_len, step, start, unroll=seg_len - 2)[4:]
        for r in range(order):
            scan = states[r]
            for e, d in enumerate((1, 2, 4)):
                moved = jnp.where(segment >= d, pltpu.roll(scan, d, 0), 0.0)
                scan = scan + row(table.at[1 + e], r, lanes) * moved
            prefix[group, r] = jnp.where(segment >= 1, pltpu.roll(scan, 1, 0), 0.0)
            end_now[r : r + 1, lanes] = scan[SEGS - 1 :, :]

    for j in range(share):

        @pl.when((pl.program_id(0) ^ place[SPOT]) == j)
        def _(j=j):
            ends[j][...] = end_now[...]


def local_scan(place, streams, short, rates, share):
    _, rows, chans = streams.shape
    order = rates.shape[0]
    wide = chans // share
    groups = wide // LANES
    seg_len = rows // SEGS
    pos_rows = TOP + SEGS * (seg_len + 1)
    end_shape = jax.ShapeDtypeStruct((order + LAST + FIRST, wide), jnp.float32)
    return pl.pallas_call(
        functools.partial(local_scan_body, seg_len=seg_len, order=order, share=share),
        grid_spec=pltpu.PrefetchScalarGridSpec(
            num_scalar_prefetch=1,
            grid=(share,),
            in_specs=[
                pl.BlockSpec(memory_space=pltpu.HBM),
                pl.BlockSpec(memory_space=pltpu.HBM),
                pl.BlockSpec(memory_space=pltpu.HBM),
            ],
            out_specs=[pl.BlockSpec((order + LAST + FIRST, wide), lambda g, place: (0, 0))] * share
            + [
                pl.BlockSpec((groups, rows, LANES), lambda g, place: (g, 0, 0)),
                pl.BlockSpec((groups, order, SEGS, LANES), lambda g, place: (g, 0, 0, 0)),
            ],
            scratch_shapes=[
                pltpu.VMEM((groups, pos_rows, LANES), jnp.float32),
                pltpu.VMEM((groups, pos_rows, LANES), jnp.float32),
                pltpu.VMEM((order + LAST + FIRST, wide), jnp.float32),
                pltpu.VMEM((4, order, wide), jnp.float32),
                pltpu.VMEM((2, rows, chans), streams.dtype),
                pltpu.VMEM((16, chans), streams.dtype),
                pltpu.VMEM(short.shape, jnp.float32),
                pltpu.VMEM(rates.shape, jnp.float32),
                pltpu.SemaphoreType.DMA((share,)),
                pltpu.SemaphoreType.DMA((3,)),
            ],
        ),
        out_shape=[end_shape] * share
        + [
            jax.ShapeDtypeStruct((chans // LANES, rows, LANES), jnp.float32),
            jax.ShapeDtypeStruct((chans // LANES, order, SEGS, LANES), jnp.float32),
        ],
        compiler_params=pltpu.CompilerParams(vmem_limit_bytes=WHOLE_LIMIT),
        cost_estimate=estimate(rows * chans * 50, rows * chans * 10),
        name="local_scan",
    )(place, streams, short, rates)


def plane_scan_body(place, rates, short, *rest, share, rows):
    ends = rest[:share]
    whole = rest[share]
    befores = rest[share + 1 : 2 * share + 1]
    by_place, before_place = rest[2 * share + 1 :]
    order = rates.shape[0]
    here = place[SPOT]
    for j in range(share):
        by_place[here ^ j] = ends[j][...]
    rate = rates[...]
    decay = jnp.exp(rate * (-1.0 * rows))
    state = jnp.zeros(rate.shape, jnp.float32)
    for at in range(share):
        before_place[at, :order] = state
        state = decay * state + by_place[at, :order]
        if at > 0:
            last = by_place[at - 1, order : order + LAST]
            before_place[at, order:] = last
            state += end_share(short, rate, by_place[at, order + LAST :], last, rows)
    before_place[0, order:] = jnp.zeros((LAST, rate.shape[1]), jnp.float32)
    whole[:order] = state
    whole[order : order + LAST] = by_place[share - 1, order : order + LAST]
    whole[order + LAST :] = by_place[0, order + LAST :]
    for j in range(share):
        befores[j][...] = before_place[here ^ j]


def plane_scan(place, rates, short, ends, rows):
    share = len(ends)
    order = rates.shape[0]
    wide = ends[0].shape[1]
    block = pl.BlockSpec((order + LAST, wide), lambda g, place: (0, 0))
    edged = pl.BlockSpec((order + LAST + FIRST, wide), lambda g, place: (0, 0))
    shape = jax.ShapeDtypeStruct((order + LAST, wide), jnp.float32)
    got = pl.pallas_call(
        functools.partial(plane_scan_body, share=share, rows=rows),
        grid_spec=pltpu.PrefetchScalarGridSpec(
            num_scalar_prefetch=1,
            grid=(1,),
            in_specs=[
                pl.BlockSpec((order, wide), lambda g, place: (0, place[SPOT])),
                pl.BlockSpec((3, 3, wide), lambda g, place: (0, 0, place[SPOT])),
            ]
            + [edged] * share,
            out_specs=[edged] + [block] * share,
            scratch_shapes=[
                pltpu.VMEM((share, order + LAST + FIRST, wide), jnp.float32),
                pltpu.VMEM((share, order + LAST, wide), jnp.float32),
            ],
        ),
        out_shape=[jax.ShapeDtypeStruct((order + LAST + FIRST, wide), jnp.float32)] + [shape] * share,
        compiler_params=pltpu.CompilerParams(vmem_limit_bytes=SMALL_LIMIT),
        cost_estimate=estimate(order * wide * 20, order * wide * 36),
        name="plane_scan",
    )(place, rates, short, *ends)
    return got[0], got[1:]


def line_scan_body(place, rates, short, whole, *rest, share, rows, lines):
    befores = rest[:share]
    arrived = rest[share : share + lines]
    outs = rest[share + lines :]
    order = rates.shape[0]
    here = place[SPOT]
    rate = rates[...]
    planes = (whole,) + tuple(arrived)

    def last_rows(k):
        if k < lines:
            return planes[k + 1][order : order + LAST]
        return jnp.zeros((LAST, rate.shape[1]), jnp.float32)

    def first_share(k):
        return end_share(short, rate, planes[k][order + LAST :], last_rows(k), rows)

    state = jnp.zeros(rate.shape, jnp.float32)
    decay = jnp.exp(rate * (-1.0 * rows * share))
    later = jnp.exp(rate * (-1.0 * rows * (share - 1)))
    for k in reversed(range(1, lines + 1)):
        state = decay * state + planes[k][:order] + later * first_share(k)
    own = first_share(0)
    for j in range(share):
        at = (here ^ j).astype(jnp.float32)
        inside = jnp.minimum(at, 1.0)
        past = inside * jnp.exp(rate * (jnp.maximum(at - 1.0, 0.0) * (-1.0 * rows)))
        before = befores[j][:order]
        outs[j][:order] = before + jnp.exp(rate * (at * (-1.0 * rows))) * state + past * own
        outs[j][order:] = befores[j][order:] + (1.0 - inside) * last_rows(0)


def line_scan(place, rates, short, whole, befores, arrived, rows):
    share, lines = len(befores), len(arrived)
    order, wide = rates.shape[0], whole.shape[1]
    block = pl.BlockSpec((order + LAST, wide), lambda g, place: (0, 0))
    edged = pl.BlockSpec((order + LAST + FIRST, wide), lambda g, place: (0, 0))
    return pl.pallas_call(
        functools.partial(line_scan_body, share=share, rows=rows, lines=lines),
        grid_spec=pltpu.PrefetchScalarGridSpec(
            num_scalar_prefetch=1,
            grid=(1,),
            in_specs=[
                pl.BlockSpec((order, wide), lambda g, place: (0, place[SPOT])),
                pl.BlockSpec((3, 3, wide), lambda g, place: (0, 0, place[SPOT])),
                edged,
            ]
            + [block] * share
            + [edged] * lines,
            out_specs=[block] * share,
        ),
        out_shape=[jax.ShapeDtypeStruct((order + LAST, wide), jnp.float32)] * share,
        compiler_params=pltpu.CompilerParams(vmem_limit_bytes=SMALL_LIMIT),
        cost_estimate=estimate(order * wide * 20, order * wide * 36),
        name="line_scan",
    )(place, rates, short, whole, *befores, *arrived)


def hidden_body(place, query, top, short, rates, coef, skip, gated, prefix, *rest, seg_len, order, share, first):
    starts = rest[:share]
    hidden = rest[share]
    query_pos, result_pos, start_by_place, table = rest[share + 1 :]
    pitch = seg_len + 1
    groups = gated.shape[0]
    now_at = pl.program_id(0) + first
    table[0] = jnp.exp(-rates[...])
    table[1] = jnp.exp(rates[...])
    segment = lax.broadcasted_iota(jnp.int32, (SEGS, LANES), 0).astype(jnp.float32)

    @pl.when(pl.program_id(0) == 0)
    def _():
        for j in range(share):
            start_by_place[place[SPOT] ^ j] = starts[j][...]

    for group in range(groups):
        lanes = slice(group * LANES, (group + 1) * LANES)
        ending = start_by_place[now_at, order : order + 2, lanes]
        lay_segments(query_pos, query, ending, seg_len, lanes, group)

    for group in range(groups):
        lanes = slice(group * LANES, (group + 1) * LANES)
        query_taps = taps(short, 0, lanes)
        gain = jnp.broadcast_to(skip[0:1, lanes], (SEGS, LANES))
        decay = [row(table.at[0], r, lanes) for r in range(order)]
        scale = [row(coef, r, lanes) for r in range(order)]
        first = jnp.concatenate([top[b, 0:2, lanes] for b in (1, 2)], axis=0).astype(jnp.float32)
        last = start_by_place[now_at, order:, lanes]
        early = [
            jnp.broadcast_to(value, (SEGS, LANES))
            for value in first_gated(short.at[:, :, lanes], first, last)
        ]
        states = []
        for r in range(order):
            rate = row(rates, r, lanes)
            ahead = jnp.exp(rate * (segment * (-1.0 * seg_len)))
            before = jnp.broadcast_to(start_by_place[now_at, r : r + 1, lanes], (SEGS, LANES))
            grown = row(table.at[1], r, lanes)
            before += jnp.where(segment >= 1.0, grown * (early[0] + grown * early[1]), 0.0)
            states.append(prefix[group, r] + ahead * before)

        def step(
            i, carry, late=None, group=group, query_taps=query_taps, gain=gain, decay=decay, scale=scale
        ):
            q1, q2, *states = carry
            q0 = strided(query_pos, group, TOP + i, pitch)
            now = gated[group, pl.ds(pl.multiple_of(i * SEGS, SEGS), SEGS), :]
            if late is not None:
                now = jnp.where(segment >= 1.0, now, late)
            states = [d * h + now for d, h in zip(decay, states)]
            sums = [s * h for s, h in zip(scale, states)] + [gain * now]
            while len(sums) > 1:
                sums = [a + b for a, b in zip(sums[::2], sums[1::2])] + sums[len(sums) // 2 * 2 :]
            query_now = query_taps[0] * q0 + query_taps[1] * q1 + query_taps[2] * q2
            result_pos[group, pl.ds(TOP + i, SEGS, stride=pitch), :] = query_now * sums[0]
            return (q0, q1, *states)

        start = (
            strided(query_pos, group, TOP - 2, pitch),
            strided(query_pos, group, TOP - 3, pitch),
        ) + tuple(states)
        start = step(1, step(0, start, early[0]), early[1])
        lax.fori_loop(2, seg_len, step, start, unroll=seg_len - 2)
        for s in range(SEGS):
            part = result_pos[group, TOP + s * pitch : TOP + s * pitch + seg_len, :]
            hidden[s * seg_len : (s + 1) * seg_len, lanes] = part.astype(hidden.dtype)


def hidden_rows(place, streams, short, rates, coef, skip, gated, prefix, starts, part):
    _, rows, chans = streams.shape
    order = rates.shape[0]
    share = len(starts)
    wide = chans // share
    groups = wide // LANES
    seg_len = rows // SEGS
    steps = max(1, share // 2)
    first = part * steps
    pos_rows = TOP + SEGS * (seg_len + 1)
    return pl.pallas_call(
        functools.partial(hidden_body, seg_len=seg_len, order=order, share=share, first=first),
        grid_spec=pltpu.PrefetchScalarGridSpec(
            num_scalar_prefetch=1,
            grid=(steps,),
            in_specs=[
                pl.BlockSpec((1, rows, wide), lambda g, place: (0, 0, first + g)),
                pl.BlockSpec((3, 16, wide), lambda g, place: (0, 0, first + g)),
                pl.BlockSpec((3, 3, wide), lambda g, place: (0, 0, first + g)),
                pl.BlockSpec((order, wide), lambda g, place: (0, first + g)),
                pl.BlockSpec((order, wide), lambda g, place: (0, first + g)),
                pl.BlockSpec((1, wide), lambda g, place: (0, first + g)),
                pl.BlockSpec((groups, rows, LANES), lambda g, place: (first + g, 0, 0)),
                pl.BlockSpec((groups, order, SEGS, LANES), lambda g, place: (first + g, 0, 0, 0)),
            ]
            + [pl.BlockSpec((order + LAST, wide), lambda g, place: (0, 0))] * share,
            out_specs=pl.BlockSpec((rows, wide), lambda g, place: (0, g)),
            scratch_shapes=[
                pltpu.VMEM((groups, pos_rows, LANES), jnp.float32),
                pltpu.VMEM((groups, pos_rows, LANES), jnp.float32),
                pltpu.VMEM((share, order + LAST, wide), jnp.float32),
                pltpu.VMEM((2, order, wide), jnp.float32),
            ],
        ),
        out_shape=jax.ShapeDtypeStruct((rows, steps * wide), jnp.bfloat16),
        compiler_params=pltpu.CompilerParams(vmem_limit_bytes=VMEM_LIMIT),
        cost_estimate=estimate(rows * chans * 40, rows * chans * 5),
        name="hidden_rows",
    )(place, streams, streams, short, rates, coef, skip, gated, prefix, *starts)


def times_into(rows, columns, out, column):
    width = columns.shape[1]
    top = 0
    for part in rows:
        size = part[0].shape[0]
        joined = jnp.concatenate([piece[...] for piece in part], axis=1)
        total = jnp.dot(joined, columns[...], preferred_element_type=jnp.float32)
        out[top : top + size, column : column + width] = total.astype(out.dtype)
        top += size


def operands(refs, rows_in, slots):
    at = 0
    rows, blocks = [], []
    for group, counts in ((rows, rows_in), (blocks, slots)):
        for count in counts:
            group.append(refs[at : at + count])
            at += count
    return rows, blocks


def near_body(place, *refs, rows_in, slots):
    near, far_first = refs[-2:]
    rows, blocks = operands(refs, rows_in, slots)
    width = far_first.shape[1]

    def all_blocks(middle):
        for slot, given in enumerate(blocks):
            out, column = (near, slot * width) if slot < 2 else (far_first, 0)
            times_into(rows, given[0 if middle else -1], out, column)

    for middle in (0, 1):
        pl.when(place[MIDDLE] == middle)(functools.partial(all_blocks, middle))


def project_body(place, *refs, rows_in, slots):
    near, far_first, kept, sent = refs[-4:]
    rows, blocks = operands(refs, rows_in, slots)
    made, width = far_first.shape

    def all_blocks(keeps, middle):
        outs = (kept, sent) if keeps else (sent, kept)
        outs[0][:made] = near[...]
        outs[1][:made, :width] = far_first[...]
        columns = [given[0 if middle else -1] for given in blocks]
        joined = jnp.concatenate([piece[...] for piece in rows[-1]], axis=1)
        together = jnp.concatenate([block[...] for block in columns], axis=1)
        total = jnp.dot(joined, together, preferred_element_type=jnp.float32).astype(kept.dtype)
        outs[0][made:] = total[:, : 2 * width]
        outs[1][made:] = total[:, 2 * width :]
        times_into(rows[:-1], columns[3], outs[1], width)

    for keeps in (0, 1):
        for middle in (0, 1):
            here = (place[KEEPS] == keeps) & (place[MIDDLE] == middle)
            pl.when(here)(functools.partial(all_blocks, keeps, middle))


def project(place, rows, slots, made=None):
    flat = [piece for part in rows for piece in part] + [block for slot in slots for block in slot]
    flat += [] if made is None else list(made)
    count = sum(part[0].shape[0] for part in rows)
    depth, width = slots[0][0].shape
    widths = (2 * width, width) if len(slots) == 3 else (2 * width, 2 * width)
    held = pl.BlockSpec(memory_space=pltpu.VMEM)
    return pl.pallas_call(
        functools.partial(
            near_body if len(slots) == 3 else project_body,
            rows_in=tuple(map(len, rows)),
            slots=tuple(map(len, slots)),
        ),
        in_specs=[pl.BlockSpec(memory_space=pltpu.SMEM)] + [held] * len(flat),
        out_specs=[held] * 2,
        out_shape=[jax.ShapeDtypeStruct((count, wide), jnp.bfloat16) for wide in widths],
        compiler_params=pltpu.CompilerParams(vmem_limit_bytes=VMEM_LIMIT),
        cost_estimate=estimate(
            2 * count * depth * len(slots) * width,
            2 * (count * depth + len(slots) * width * (depth + count)),
        ),
        name="project",
    )(place, *flat)


def assemble_body(place, *refs):
    parts, out = refs[:-1], refs[-1]
    blocks = 2
    width = parts[0].shape[1] // blocks
    for j, part in enumerate(parts):
        for b in range(blocks):
            column = ((b ^ place[ODD]) * len(parts) + (place[SPOT] ^ j)) * width
            out[:, pl.ds(pl.multiple_of(column, LANES), width)] = part[:, b * width : (b + 1) * width]


def assemble(place, parts, blocks, width):
    share = len(parts)
    rows = parts[0].shape[0]
    held = pl.BlockSpec(memory_space=pltpu.VMEM)
    return pl.pallas_call(
        assemble_body,
        in_specs=[pl.BlockSpec(memory_space=pltpu.SMEM)] + [held] * share,
        out_specs=held,
        out_shape=jax.ShapeDtypeStruct((rows, share * blocks * width), jnp.bfloat16),
        compiler_params=pltpu.CompilerParams(vmem_limit_bytes=VMEM_LIMIT),
        cost_estimate=estimate(0, 4 * rows * share * blocks * width),
        name="assemble",
    )(place, *parts)


def after(value, *others):
    return lax.optimization_barrier((value, *others))[0]


def send_planes(value, group, moves):
    pairs = [(a * group + e, b * group + e) for a, b in moves for e in range(group)]
    return lax.ppermute(value, "ctx", pairs)


def plane_rows(hidden, count, group):
    if group != 4:
        return [hidden] + [[send_xor(part, count, group, j) for part in hidden] for j in range(1, group)]
    first, second = hidden
    first_1 = send_xor(first, count, group, 1)
    first_2 = send_xor(first, count, group, 2)
    second_2 = send_xor(second, count, group, 2)
    second_1 = send_xor(second, count, group, 1)
    first_3 = send_xor(first_1, count, group, 2)
    second_3 = send_xor(second_2, count, group, 1)
    return [[first, second], [first_1, second_1], [first_2, second_2], [first_3, second_3]]


def add_up_body(a, b, *outs):
    size = outs[0].shape[0]
    for j, out in enumerate(outs):
        rows = slice(j * size, (j + 1) * size)
        out[...] = (a[rows].astype(jnp.float32) + b[rows].astype(jnp.float32)).astype(out.dtype)


def add_up(a, b, parts):
    size, width = a.shape[0] // parts, a.shape[1]
    held = pl.BlockSpec(memory_space=pltpu.VMEM)
    return pl.pallas_call(
        add_up_body,
        in_specs=[held, held],
        out_specs=[held] * parts,
        out_shape=[jax.ShapeDtypeStruct((size, width), a.dtype)] * parts,
        compiler_params=pltpu.CompilerParams(vmem_limit_bytes=VMEM_LIMIT),
        cost_estimate=estimate(parts * size * width, 6 * parts * size * width),
        name="add_up",
    )(a, b)


def project_4x4(place, out_weight, states, hidden, count):
    group = 4
    swap = [(0, 1), (1, 0), (2, 3), (3, 2)]
    inner = [(1, 2), (2, 1)]
    outward = [(1, 0), (2, 3)]
    rows = plane_rows(hidden, count, group)
    own = out_weight
    by_1 = send_planes(own, group, swap)
    by_3_inner = send_planes(own, group, inner)
    by_2_inner = send_planes(after(by_1, states, by_3_inner), group, inner)
    by_2_outer = send_planes(after(by_3_inner, states), group, outward)
    by_3_outer = send_planes(after(by_2_inner, by_2_outer, rows[1][0], rows[2][0], hidden[1]), group, outward)
    blocks = [[own], [by_1], [by_2_inner, by_2_outer], [by_3_inner, by_3_outer]]

    made = project(place, rows[:3], blocks[:3])
    kept, sent = project(place, rows, blocks, made)
    mixed = add_up(kept, lax.ppermute(sent, "tp", [(0, 1), (1, 0)]), group)
    mixed = [mixed[0]] + [send_xor(mixed[j], count, group, j) for j in range(1, group)]
    return assemble(place, mixed, 2, out_weight.shape[1])


def project_any(out_weight, states, hidden, count):
    halves = lax.axis_size("tp")
    group = split_of(count)
    outer = count // group
    plane = lax.axis_index("ctx") // group
    size = hidden[0].shape[0]
    depth, width = out_weight.shape
    below, above = [out_weight], [out_weight]
    for k in range(1, outer):
        down, up = below[-1], above[-1]
        if k == 2:
            down, up = after(down, states), after(up, states)
        below.append(send_along(down, count, group, 1, k - 1))
        above.append(send_along(up, count, group, -1, k - 1))
    line = below[:0:-1] + above
    cols = lax.dynamic_slice_in_dim(jnp.stack(line), outer - 1 - plane, outer, 0)
    cols = jnp.moveaxis(cols, 0, 1).reshape(depth, outer * width)
    rows = plane_rows(hidden, count, group)
    held = jnp.concatenate([jnp.concatenate(part, axis=1) for part in rows], axis=0)
    partial = jnp.dot(held, cols, preferred_element_type=jnp.float32).astype(jnp.bfloat16)
    mixed = lax.psum_scatter(partial, "tp", scatter_dimension=1, tiled=True)
    mixed = jnp.split(mixed, group)
    mixed = [mixed[0]] + [send_xor(mixed[j], count, group, j) for j in range(1, group)]
    blocks = outer // halves
    stacked = jnp.stack(mixed).reshape(group, size, blocks, width)
    by_place = jnp.take(stacked, jnp.arange(group) ^ (lax.axis_index("ctx") % group), axis=0)
    return jnp.moveaxis(by_place, 0, 2).reshape(size, blocks * group * width)


def per_device(projected, short_filter, residues, rates, skip_gain, out_weight):
    count = lax.axis_size("ctx")
    halves = lax.axis_size("tp")
    here = lax.axis_index("ctx")
    rows, _, chans = projected.shape

    streams = jnp.transpose(projected, (1, 0, 2))
    rates_t = rates.T
    coef_t = (residues * jnp.sqrt(-jnp.expm1(-2.0 * rates))).T

    share = min(split_of(count), chans // LANES, 4)
    lines = count // share
    plane = here // share
    keeps = lax.axis_index("tp") == plane // 2
    place = jnp.stack([here % share, (plane == 1) | (plane == 2), keeps, plane % 2]).astype(jnp.int32)
    *ends, gated, prefix = local_scan(place, streams, short_filter, rates_t, share)
    ends = [ends[0]] + [send_xor(ends[j], count, share, j) for j in range(1, share)]
    whole, befores = plane_scan(place, rates_t, short_filter, ends, rows)
    arrived = [send_along(whole, count, share, k) for k in range(1, lines)]
    starts = line_scan(place, rates_t, short_filter, whole, befores, arrived, rows)
    states = starts[0]
    starts = [starts[0]] + [send_xor(starts[j], count, share, j) for j in range(1, share)]
    hidden = [
        hidden_rows(
            place, streams, short_filter, rates_t, coef_t, skip_gain[None], gated, prefix, starts, part
        )
        for part in range(2)
    ]
    if count == 16 and halves == 2 and out_weight.shape[1] % LANES == 0:
        return project_4x4(place, out_weight, states, hidden, count)
    return project_any(out_weight, states, hidden, count)


def solution(mesh):
    return jax.shard_map(
        per_device,
        mesh=mesh,
        in_specs=(
            P("ctx", None, "tp"),
            P(None, None, "tp"),
            P("tp", None),
            P("tp", None),
            P("tp"),
            P("tp", "ctx"),
        ),
        out_specs=P("ctx", "tp"),
        check_vma=False,
    )
```

```python
import functools

import jax
import jax.numpy as jnp
from jax import lax
from jax.experimental import pallas as pl
from jax.experimental.pallas import tpu as pltpu
from jax.sharding import PartitionSpec as P

LANES = 128
SEGS = 8
TOP = 8
SPOT, MIDDLE, KEEPS, ODD = range(4)
VMEM_LIMIT = 16 * 1024 * 1024
SMALL_LIMIT = 4 * 1024 * 1024
WHOLE_LIMIT = 50 * 1024 * 1024


def split_of(count):
    inner = 1
    while (2 * inner) ** 2 <= count and count % (2 * inner) == 0:
        inner *= 2
    return inner


def send_xor(value, count, group, step):
    pairs = [(p, p - p % group + ((p % group) ^ step)) for p in range(count)]
    return lax.ppermute(value, "ctx", pairs)


def send_along(value, count, group, steps, first=0):
    outer = count // group
    pairs = []
    for z in range(outer):
        if not 0 <= z + steps < outer:
            continue
        if (steps > 0 and z < first) or (steps < 0 and z > outer - 1 - first):
            continue
        pairs += [(z * group + e, (z + steps) * group + e) for e in range(group)]
    return lax.ppermute(value, "ctx", pairs)


def estimate(flops, bytes_accessed, transcendentals=0):
    return pl.CostEstimate(flops=flops, bytes_accessed=bytes_accessed, transcendentals=transcendentals)


def row(ref, r, lanes):
    return jnp.broadcast_to(ref[r : r + 1, lanes], (SEGS, LANES))


def lay_segments(dst, stream, halo, seg_len, lanes, group):
    pitch = seg_len + 1
    for s in range(SEGS):
        part = stream[0, s * seg_len : (s + 1) * seg_len, lanes].astype(jnp.float32)
        dst[group, TOP + s * pitch : TOP + s * pitch + seg_len, :] = part
    dst[group, TOP - 3 : TOP - 1, :] = jnp.zeros((2, LANES), jnp.float32) if halo is None else halo


def taps(short, stream, lanes):
    return [jnp.broadcast_to(short[i, stream : stream + 1, lanes], (SEGS, LANES)) for i in range(3)]


def strided(ref, group, start, pitch):
    return ref[group, pl.ds(start, SEGS, stride=pitch), :]


LAST, FIRST = 6, 4


def first_gated(short, first, last):
    products = []
    for b, stream in enumerate((1, 2)):
        tap = [short[i, stream : stream + 1, :] for i in range(3)]
        now_0, now_1 = first[2 * b : 2 * b + 1], first[2 * b + 1 : 2 * b + 2]
        old_2, old_1 = last[2 * stream : 2 * stream + 1], last[2 * stream + 1 : 2 * stream + 2]
        products.append(
            (
                tap[0] * now_0 + tap[1] * old_1 + tap[2] * old_2,
                tap[0] * now_1 + tap[1] * now_0 + tap[2] * old_1,
            )
        )
    return products[0][0] * products[1][0], products[0][1] * products[1][1]


def end_share(short, rates, first, last, rows):
    gated_0, gated_1 = first_gated(short, first, last)
    return jnp.exp(rates * (1.0 - rows)) * gated_0 + jnp.exp(rates * (2.0 - rows)) * gated_1


def local_scan_body(place, streams, short_all, rates_all, *rest, seg_len, order, share):
    ends = rest[:share]
    gated, prefix = rest[share : share + 2]
    key_pos, value_pos, end_now, table, held, query_held, short_held, rates_held, held_sem, small_sem = rest[share + 2 :]
    now_at = pl.program_id(0)
    wide = end_now.shape[1]
    small = [
        pltpu.make_async_copy(short_all, short_held, small_sem.at[0]),
        pltpu.make_async_copy(rates_all, rates_held, small_sem.at[1]),
        pltpu.make_async_copy(
            streams.at[0, pl.ds(seg_len * SEGS - 16, 16), :], query_held, small_sem.at[2]
        ),
    ]

    def stream_copy(at):
        columns = pl.ds(at * wide, wide)
        return pltpu.make_async_copy(
            streams.at[pl.ds(1, 2), :, columns], held.at[:, :, columns], held_sem.at[at]
        )

    @pl.when(now_at == 0)
    def _():
        stream_copy(0).start()
        for copy in small:
            copy.start()
        for at in range(1, share):
            stream_copy(at).start()
        for copy in small:
            copy.wait()

    for at in range(share):

        @pl.when(now_at == at)
        def _(at=at):
            stream_copy(at).wait()

    columns = pl.ds(pl.multiple_of(now_at * wide, LANES), wide)
    key = held.at[pl.ds(0, 1), :, columns]
    value = held.at[pl.ds(1, 1), :, columns]
    short = short_held.at[:, :, columns]
    rates = rates_held[:, columns]
    table[0] = jnp.exp(-rates)
    for e, d in enumerate((1, 2, 4)):
        table[1 + e] = jnp.exp(rates * (-1.0 * d * seg_len))
    pitch = seg_len + 1
    groups = gated.shape[0]
    segment = lax.broadcasted_iota(jnp.int32, (SEGS, LANES), 0)
    for group in range(groups):
        lanes = slice(group * LANES, (group + 1) * LANES)
        lay_segments(key_pos, key, None, seg_len, lanes, group)
        lay_segments(value_pos, value, None, seg_len, lanes, group)
    bottom = seg_len * SEGS - 2
    end_now[order : order + 2, :] = query_held[14:16, columns].astype(jnp.float32)
    for b, stream in enumerate((key, value)):
        at = order + 2 + 2 * b
        end_now[at : at + 2, :] = stream[0, bottom : bottom + 2, :].astype(jnp.float32)
        at = order + LAST + 2 * b
        end_now[at : at + 2, :] = stream[0, 0:2, :].astype(jnp.float32)

    for group in range(groups):
        lanes = slice(group * LANES, (group + 1) * LANES)
        key_taps = taps(short, 1, lanes)
        value_taps = taps(short, 2, lanes)
        decay = [row(table.at[0], r, lanes) for r in range(order)]

        def step(i, carry, early=False, group=group, key_taps=key_taps, value_taps=value_taps, decay=decay):
            k1, k2, v1, v2, *states = carry
            k0 = strided(key_pos, group, TOP + i, pitch)
            v0 = strided(value_pos, group, TOP + i, pitch)
            key_now = key_taps[0] * k0 + key_taps[1] * k1 + key_taps[2] * k2
            value_now = value_taps[0] * v0 + value_taps[1] * v1 + value_taps[2] * v2
            now = key_now * value_now
            if early:
                now = jnp.where(segment >= 1, now, 0.0)
            gated[group, pl.ds(pl.multiple_of(i * SEGS, SEGS), SEGS), :] = now
            states = [d * h + now for d, h in zip(decay, states)]
            return (k0, k1, v0, v1, *states)

        zero = jnp.zeros((SEGS, LANES), jnp.float32)
        start = (
            strided(key_pos, group, TOP - 2, pitch),
            strided(key_pos, group, TOP - 3, pitch),
            strided(value_pos, group, TOP - 2, pitch),
            strided(value_pos, group, TOP - 3, pitch),
        ) + (zero,) * order
        start = step(1, step(0, start, True), True)
        states = lax.fori_loop(2, seg_len, step, start, unroll=seg_len - 2)[4:]
        for r in range(order):
            scan = states[r]
            for e, d in enumerate((1, 2, 4)):
                moved = jnp.where(segment >= d, pltpu.roll(scan, d, 0), 0.0)
                scan = scan + row(table.at[1 + e], r, lanes) * moved
            prefix[group, r] = jnp.where(segment >= 1, pltpu.roll(scan, 1, 0), 0.0)
            end_now[r : r + 1, lanes] = scan[SEGS - 1 :, :]

    for j in range(share):

        @pl.when((pl.program_id(0) ^ place[SPOT]) == j)
        def _(j=j):
            ends[j][...] = end_now[...]


def local_scan(place, streams, short, rates, share):
    _, rows, chans = streams.shape
    order = rates.shape[0]
    wide = chans // share
    groups = wide // LANES
    seg_len = rows // SEGS
    pos_rows = TOP + SEGS * (seg_len + 1)
    end_shape = jax.ShapeDtypeStruct((order + LAST + FIRST, wide), jnp.float32)
    return pl.pallas_call(
        functools.partial(local_scan_body, seg_len=seg_len, order=order, share=share),
        grid_spec=pltpu.PrefetchScalarGridSpec(
            num_scalar_prefetch=1,
            grid=(share,),
            in_specs=[
                pl.BlockSpec(memory_space=pltpu.HBM),
                pl.BlockSpec(memory_space=pltpu.HBM),
                pl.BlockSpec(memory_space=pltpu.HBM),
            ],
            out_specs=[pl.BlockSpec((order + LAST + FIRST, wide), lambda g, place: (0, 0))] * share
            + [
                pl.BlockSpec((groups, rows, LANES), lambda g, place: (g, 0, 0)),
                pl.BlockSpec((groups, order, SEGS, LANES), lambda g, place: (g, 0, 0, 0)),
            ],
            scratch_shapes=[
                pltpu.VMEM((groups, pos_rows, LANES), jnp.float32),
                pltpu.VMEM((groups, pos_rows, LANES), jnp.float32),
                pltpu.VMEM((order + LAST + FIRST, wide), jnp.float32),
                pltpu.VMEM((4, order, wide), jnp.float32),
                pltpu.VMEM((2, rows, chans), streams.dtype),
                pltpu.VMEM((16, chans), streams.dtype),
                pltpu.VMEM(short.shape, jnp.float32),
                pltpu.VMEM(rates.shape, jnp.float32),
                pltpu.SemaphoreType.DMA((share,)),
                pltpu.SemaphoreType.DMA((3,)),
            ],
        ),
        out_shape=[end_shape] * share
        + [
            jax.ShapeDtypeStruct((chans // LANES, rows, LANES), jnp.float32),
            jax.ShapeDtypeStruct((chans // LANES, order, SEGS, LANES), jnp.float32),
        ],
        compiler_params=pltpu.CompilerParams(vmem_limit_bytes=WHOLE_LIMIT),
        cost_estimate=estimate(rows * chans * 50, rows * chans * 10),
        name="local_scan",
    )(place, streams, short, rates)


def plane_scan_body(place, rates, short, *rest, share, rows):
    ends = rest[:share]
    whole = rest[share]
    befores = rest[share + 1 : 2 * share + 1]
    by_place, before_place = rest[2 * share + 1 :]
    order = rates.shape[0]
    here = place[SPOT]
    for j in range(share):
        by_place[here ^ j] = ends[j][...]
    rate = rates[...]
    decay = jnp.exp(rate * (-1.0 * rows))
    state = jnp.zeros(rate.shape, jnp.float32)
    for at in range(share):
        before_place[at, :order] = state
        state = decay * state + by_place[at, :order]
        if at > 0:
            last = by_place[at - 1, order : order + LAST]
            before_place[at, order:] = last
            state += end_share(short, rate, by_place[at, order + LAST :], last, rows)
    before_place[0, order:] = jnp.zeros((LAST, rate.shape[1]), jnp.float32)
    whole[:order] = state
    whole[order : order + LAST] = by_place[share - 1, order : order + LAST]
    whole[order + LAST :] = by_place[0, order + LAST :]
    for j in range(share):
        befores[j][...] = before_place[here ^ j]


def plane_scan(place, rates, short, ends, rows):
    share = len(ends)
    order = rates.shape[0]
    wide = ends[0].shape[1]
    block = pl.BlockSpec((order + LAST, wide), lambda g, place: (0, 0))
    edged = pl.BlockSpec((order + LAST + FIRST, wide), lambda g, place: (0, 0))
    shape = jax.ShapeDtypeStruct((order + LAST, wide), jnp.float32)
    got = pl.pallas_call(
        functools.partial(plane_scan_body, share=share, rows=rows),
        grid_spec=pltpu.PrefetchScalarGridSpec(
            num_scalar_prefetch=1,
            grid=(1,),
            in_specs=[
                pl.BlockSpec((order, wide), lambda g, place: (0, place[SPOT])),
                pl.BlockSpec((3, 3, wide), lambda g, place: (0, 0, place[SPOT])),
            ]
            + [edged] * share,
            out_specs=[edged] + [block] * share,
            scratch_shapes=[
                pltpu.VMEM((share, order + LAST + FIRST, wide), jnp.float32),
                pltpu.VMEM((share, order + LAST, wide), jnp.float32),
            ],
        ),
        out_shape=[jax.ShapeDtypeStruct((order + LAST + FIRST, wide), jnp.float32)] + [shape] * share,
        compiler_params=pltpu.CompilerParams(vmem_limit_bytes=SMALL_LIMIT),
        cost_estimate=estimate(order * wide * 20, order * wide * 36),
        name="plane_scan",
    )(place, rates, short, *ends)
    return got[0], got[1:]


def line_scan_body(place, rates, short, whole, *rest, share, rows, lines):
    befores = rest[:share]
    arrived = rest[share : share + lines]
    outs = rest[share + lines :]
    order = rates.shape[0]
    here = place[SPOT]
    rate = rates[...]
    planes = (whole,) + tuple(arrived)

    def last_rows(k):
        if k < lines:
            return planes[k + 1][order : order + LAST]
        return jnp.zeros((LAST, rate.shape[1]), jnp.float32)

    def first_share(k):
        return end_share(short, rate, planes[k][order + LAST :], last_rows(k), rows)

    state = jnp.zeros(rate.shape, jnp.float32)
    decay = jnp.exp(rate * (-1.0 * rows * share))
    later = jnp.exp(rate * (-1.0 * rows * (share - 1)))
    for k in reversed(range(1, lines + 1)):
        state = decay * state + planes[k][:order] + later * first_share(k)
    own = first_share(0)
    for j in range(share):
        at = (here ^ j).astype(jnp.float32)
        inside = jnp.minimum(at, 1.0)
        past = inside * jnp.exp(rate * (jnp.maximum(at - 1.0, 0.0) * (-1.0 * rows)))
        before = befores[j][:order]
        outs[j][:order] = before + jnp.exp(rate * (at * (-1.0 * rows))) * state + past * own
        outs[j][order:] = befores[j][order:] + (1.0 - inside) * last_rows(0)


def line_scan(place, rates, short, whole, befores, arrived, rows):
    share, lines = len(befores), len(arrived)
    order, wide = rates.shape[0], whole.shape[1]
    block = pl.BlockSpec((order + LAST, wide), lambda g, place: (0, 0))
    edged = pl.BlockSpec((order + LAST + FIRST, wide), lambda g, place: (0, 0))
    return pl.pallas_call(
        functools.partial(line_scan_body, share=share, rows=rows, lines=lines),
        grid_spec=pltpu.PrefetchScalarGridSpec(
            num_scalar_prefetch=1,
            grid=(1,),
            in_specs=[
                pl.BlockSpec((order, wide), lambda g, place: (0, place[SPOT])),
                pl.BlockSpec((3, 3, wide), lambda g, place: (0, 0, place[SPOT])),
                edged,
            ]
            + [block] * share
            + [edged] * lines,
            out_specs=[block] * share,
        ),
        out_shape=[jax.ShapeDtypeStruct((order + LAST, wide), jnp.float32)] * share,
        compiler_params=pltpu.CompilerParams(vmem_limit_bytes=SMALL_LIMIT),
        cost_estimate=estimate(order * wide * 20, order * wide * 36),
        name="line_scan",
    )(place, rates, short, whole, *befores, *arrived)


def hidden_body(place, query, top, short, rates, coef, skip, gated, prefix, *rest, seg_len, order, share, first):
    starts = rest[:share]
    hidden = rest[share]
    query_pos, result_pos, start_by_place, table = rest[share + 1 :]
    pitch = seg_len + 1
    groups = gated.shape[0]
    now_at = pl.program_id(0) + first
    table[0] = jnp.exp(-rates[...])
    table[1] = jnp.exp(rates[...])
    segment = lax.broadcasted_iota(jnp.int32, (SEGS, LANES), 0).astype(jnp.float32)

    @pl.when(pl.program_id(0) == 0)
    def _():
        for j in range(share):
            start_by_place[place[SPOT] ^ j] = starts[j][...]

    for group in range(groups):
        lanes = slice(group * LANES, (group + 1) * LANES)
        ending = start_by_place[now_at, order : order + 2, lanes]
        lay_segments(query_pos, query, ending, seg_len, lanes, group)

    for group in range(groups):
        lanes = slice(group * LANES, (group + 1) * LANES)
        query_taps = taps(short, 0, lanes)
        gain = jnp.broadcast_to(skip[0:1, lanes], (SEGS, LANES))
        decay = [row(table.at[0], r, lanes) for r in range(order)]
        scale = [row(coef, r, lanes) for r in range(order)]
        first = jnp.concatenate([top[b, 0:2, lanes] for b in (1, 2)], axis=0).astype(jnp.float32)
        last = start_by_place[now_at, order:, lanes]
        early = [
            jnp.broadcast_to(value, (SEGS, LANES))
            for value in first_gated(short.at[:, :, lanes], first, last)
        ]
        states = []
        for r in range(order):
            rate = row(rates, r, lanes)
            ahead = jnp.exp(rate * (segment * (-1.0 * seg_len)))
            before = jnp.broadcast_to(start_by_place[now_at, r : r + 1, lanes], (SEGS, LANES))
            grown = row(table.at[1], r, lanes)
            before += jnp.where(segment >= 1.0, grown * (early[0] + grown * early[1]), 0.0)
            states.append(prefix[group, r] + ahead * before)

        def step(
            i, carry, late=None, group=group, query_taps=query_taps, gain=gain, decay=decay, scale=scale
        ):
            q1, q2, *states = carry
            q0 = strided(query_pos, group, TOP + i, pitch)
            now = gated[group, pl.ds(pl.multiple_of(i * SEGS, SEGS), SEGS), :]
            if late is not None:
                now = jnp.where(segment >= 1.0, now, late)
            states = [d * h + now for d, h in zip(decay, states)]
            sums = [s * h for s, h in zip(scale, states)] + [gain * now]
            while len(sums) > 1:
                sums = [a + b for a, b in zip(sums[::2], sums[1::2])] + sums[len(sums) // 2 * 2 :]
            query_now = query_taps[0] * q0 + query_taps[1] * q1 + query_taps[2] * q2
            result_pos[group, pl.ds(TOP + i, SEGS, stride=pitch), :] = query_now * sums[0]
            return (q0, q1, *states)

        start = (
            strided(query_pos, group, TOP - 2, pitch),
            strided(query_pos, group, TOP - 3, pitch),
        ) + tuple(states)
        start = step(1, step(0, start, early[0]), early[1])
        lax.fori_loop(2, seg_len, step, start, unroll=seg_len - 2)
        for s in range(SEGS):
            part = result_pos[group, TOP + s * pitch : TOP + s * pitch + seg_len, :]
            hidden[s * seg_len : (s + 1) * seg_len, lanes] = part.astype(hidden.dtype)


def hidden_rows(place, streams, short, rates, coef, skip, gated, prefix, starts, part):
    _, rows, chans = streams.shape
    order = rates.shape[0]
    share = len(starts)
    wide = chans // share
    groups = wide // LANES
    seg_len = rows // SEGS
    steps = max(1, share // 2)
    first = part * steps
    pos_rows = TOP + SEGS * (seg_len + 1)
    return pl.pallas_call(
        functools.partial(hidden_body, seg_len=seg_len, order=order, share=share, first=first),
        grid_spec=pltpu.PrefetchScalarGridSpec(
            num_scalar_prefetch=1,
            grid=(steps,),
            in_specs=[
                pl.BlockSpec((1, rows, wide), lambda g, place: (0, 0, first + g)),
                pl.BlockSpec((3, 16, wide), lambda g, place: (0, 0, first + g)),
                pl.BlockSpec((3, 3, wide), lambda g, place: (0, 0, first + g)),
                pl.BlockSpec((order, wide), lambda g, place: (0, first + g)),
                pl.BlockSpec((order, wide), lambda g, place: (0, first + g)),
                pl.BlockSpec((1, wide), lambda g, place: (0, first + g)),
                pl.BlockSpec((groups, rows, LANES), lambda g, place: (first + g, 0, 0)),
                pl.BlockSpec((groups, order, SEGS, LANES), lambda g, place: (first + g, 0, 0, 0)),
            ]
            + [pl.BlockSpec((order + LAST, wide), lambda g, place: (0, 0))] * share,
            out_specs=pl.BlockSpec((rows, wide), lambda g, place: (0, g)),
            scratch_shapes=[
                pltpu.VMEM((groups, pos_rows, LANES), jnp.float32),
                pltpu.VMEM((groups, pos_rows, LANES), jnp.float32),
                pltpu.VMEM((share, order + LAST, wide), jnp.float32),
                pltpu.VMEM((2, order, wide), jnp.float32),
            ],
        ),
        out_shape=jax.ShapeDtypeStruct((rows, steps * wide), jnp.bfloat16),
        compiler_params=pltpu.CompilerParams(vmem_limit_bytes=VMEM_LIMIT),
        cost_estimate=estimate(rows * chans * 40, rows * chans * 5),
        name="hidden_rows",
    )(place, streams, streams, short, rates, coef, skip, gated, prefix, *starts)


def times_into(rows, columns, out, column):
    width = columns.shape[1]
    top = 0
    for part in rows:
        size = part[0].shape[0]
        joined = jnp.concatenate([piece[...] for piece in part], axis=1)
        total = jnp.dot(joined, columns[...], preferred_element_type=jnp.float32)
        out[top : top + size, column : column + width] = total.astype(out.dtype)
        top += size


def operands(refs, rows_in, slots):
    at = 0
    rows, blocks = [], []
    for group, counts in ((rows, rows_in), (blocks, slots)):
        for count in counts:
            group.append(refs[at : at + count])
            at += count
    return rows, blocks


def near_body(place, *refs, rows_in, slots):
    near, far_first = refs[-2:]
    rows, blocks = operands(refs, rows_in, slots)
    width = far_first.shape[1]

    def all_blocks(middle):
        for slot, given in enumerate(blocks):
            out, column = (near, slot * width) if slot < 2 else (far_first, 0)
            times_into(rows, given[0 if middle else -1], out, column)

    for middle in (0, 1):
        pl.when(place[MIDDLE] == middle)(functools.partial(all_blocks, middle))


def project_body(place, *refs, rows_in, slots):
    near, far_first, kept, sent = refs[-4:]
    rows, blocks = operands(refs, rows_in, slots)
    made, width = far_first.shape

    def all_blocks(keeps, middle):
        outs = (kept, sent) if keeps else (sent, kept)
        outs[0][:made] = near[...]
        outs[1][:made, :width] = far_first[...]
        columns = [given[0 if middle else -1] for given in blocks]
        joined = jnp.concatenate([piece[...] for piece in rows[-1]], axis=1)
        together = jnp.concatenate([block[...] for block in columns], axis=1)
        total = jnp.dot(joined, together, preferred_element_type=jnp.float32).astype(kept.dtype)
        outs[0][made:] = total[:, : 2 * width]
        outs[1][made:] = total[:, 2 * width :]
        pieces = [jnp.concatenate([part[k][...] for part in rows[:-1]], axis=0) for k in range(rows_in[0])]
        joined = jnp.concatenate(pieces, axis=1)
        total = jnp.dot(joined, columns[3][...], preferred_element_type=jnp.float32)
        outs[1][:made, width:] = total.astype(kept.dtype)

    for keeps in (0, 1):
        for middle in (0, 1):
            here = (place[KEEPS] == keeps) & (place[MIDDLE] == middle)
            pl.when(here)(functools.partial(all_blocks, keeps, middle))


def project(place, rows, slots, made=None):
    flat = [piece for part in rows for piece in part] + [block for slot in slots for block in slot]
    flat += [] if made is None else list(made)
    count = sum(part[0].shape[0] for part in rows)
    depth, width = slots[0][0].shape
    widths = (2 * width, width) if len(slots) == 3 else (2 * width, 2 * width)
    held = pl.BlockSpec(memory_space=pltpu.VMEM)
    return pl.pallas_call(
        functools.partial(
            near_body if len(slots) == 3 else project_body,
            rows_in=tuple(map(len, rows)),
            slots=tuple(map(len, slots)),
        ),
        in_specs=[pl.BlockSpec(memory_space=pltpu.SMEM)] + [held] * len(flat),
        out_specs=[held] * 2,
        out_shape=[jax.ShapeDtypeStruct((count, wide), jnp.bfloat16) for wide in widths],
        compiler_params=pltpu.CompilerParams(vmem_limit_bytes=VMEM_LIMIT),
        cost_estimate=estimate(
            2 * count * depth * len(slots) * width,
            2 * (count * depth + len(slots) * width * (depth + count)),
        ),
        name="project",
    )(place, *flat)


def assemble_body(place, *refs):
    parts, out = refs[:-1], refs[-1]
    blocks = 2
    width = parts[0].shape[1] // blocks
    for j, part in enumerate(parts):
        for b in range(blocks):
            column = ((b ^ place[ODD]) * len(parts) + (place[SPOT] ^ j)) * width
            out[:, pl.ds(pl.multiple_of(column, LANES), width)] = part[:, b * width : (b + 1) * width]


def assemble(place, parts, blocks, width):
    share = len(parts)
    rows = parts[0].shape[0]
    held = pl.BlockSpec(memory_space=pltpu.VMEM)
    return pl.pallas_call(
        assemble_body,
        in_specs=[pl.BlockSpec(memory_space=pltpu.SMEM)] + [held] * share,
        out_specs=held,
        out_shape=jax.ShapeDtypeStruct((rows, share * blocks * width), jnp.bfloat16),
        compiler_params=pltpu.CompilerParams(vmem_limit_bytes=VMEM_LIMIT),
        cost_estimate=estimate(0, 4 * rows * share * blocks * width),
        name="assemble",
    )(place, *parts)


def after(value, *others):
    return lax.optimization_barrier((value, *others))[0]


def send_planes(value, group, moves):
    pairs = [(a * group + e, b * group + e) for a, b in moves for e in range(group)]
    return lax.ppermute(value, "ctx", pairs)


def plane_rows(hidden, count, group):
    if group != 4:
        return [hidden] + [[send_xor(part, count, group, j) for part in hidden] for j in range(1, group)]
    first, second = hidden
    first_1 = send_xor(first, count, group, 1)
    first_2 = send_xor(first, count, group, 2)
    second_2 = send_xor(second, count, group, 2)
    second_1 = send_xor(second, count, group, 1)
    first_3 = send_xor(first_1, count, group, 2)
    second_3 = send_xor(second_2, count, group, 1)
    return [[first, second], [first_1, second_1], [first_2, second_2], [first_3, second_3]]


def add_up_body(a, b, *outs):
    size = outs[0].shape[0]
    for j, out in enumerate(outs):
        rows = slice(j * size, (j + 1) * size)
        out[...] = (a[rows].astype(jnp.float32) + b[rows].astype(jnp.float32)).astype(out.dtype)


def add_up(a, b, parts):
    size, width = a.shape[0] // parts, a.shape[1]
    held = pl.BlockSpec(memory_space=pltpu.VMEM)
    return pl.pallas_call(
        add_up_body,
        in_specs=[held, held],
        out_specs=[held] * parts,
        out_shape=[jax.ShapeDtypeStruct((size, width), a.dtype)] * parts,
        compiler_params=pltpu.CompilerParams(vmem_limit_bytes=VMEM_LIMIT),
        cost_estimate=estimate(parts * size * width, 6 * parts * size * width),
        name="add_up",
    )(a, b)


def project_4x4(place, out_weight, states, hidden, count):
    group = 4
    swap = [(0, 1), (1, 0), (2, 3), (3, 2)]
    inner = [(1, 2), (2, 1)]
    outward = [(1, 0), (2, 3)]
    rows = plane_rows(hidden, count, group)
    own = out_weight
    by_1 = send_planes(own, group, swap)
    by_3_inner = send_planes(own, group, inner)
    by_2_inner = send_planes(after(by_1, states, by_3_inner), group, inner)
    by_2_outer = send_planes(after(by_3_inner, states), group, outward)
    by_3_outer = send_planes(after(by_2_inner, by_2_outer, rows[1][0], rows[2][0], hidden[1]), group, outward)
    blocks = [[own], [by_1], [by_2_inner, by_2_outer], [by_3_inner, by_3_outer]]

    made = project(place, rows[:3], blocks[:3])
    kept, sent = project(place, rows, blocks, made)
    mixed = add_up(kept, lax.ppermute(sent, "tp", [(0, 1), (1, 0)]), group)
    mixed = [mixed[0]] + [send_xor(mixed[j], count, group, j) for j in range(1, group)]
    return assemble(place, mixed, 2, out_weight.shape[1])


def project_any(out_weight, states, hidden, count):
    halves = lax.axis_size("tp")
    group = split_of(count)
    outer = count // group
    plane = lax.axis_index("ctx") // group
    size = hidden[0].shape[0]
    depth, width = out_weight.shape
    below, above = [out_weight], [out_weight]
    for k in range(1, outer):
        down, up = below[-1], above[-1]
        if k == 2:
            down, up = after(down, states), after(up, states)
        below.append(send_along(down, count, group, 1, k - 1))
        above.append(send_along(up, count, group, -1, k - 1))
    line = below[:0:-1] + above
    cols = lax.dynamic_slice_in_dim(jnp.stack(line), outer - 1 - plane, outer, 0)
    cols = jnp.moveaxis(cols, 0, 1).reshape(depth, outer * width)
    rows = plane_rows(hidden, count, group)
    held = jnp.concatenate([jnp.concatenate(part, axis=1) for part in rows], axis=0)
    partial = jnp.dot(held, cols, preferred_element_type=jnp.float32).astype(jnp.bfloat16)
    mixed = lax.psum_scatter(partial, "tp", scatter_dimension=1, tiled=True)
    mixed = jnp.split(mixed, group)
    mixed = [mixed[0]] + [send_xor(mixed[j], count, group, j) for j in range(1, group)]
    blocks = outer // halves
    stacked = jnp.stack(mixed).reshape(group, size, blocks, width)
    by_place = jnp.take(stacked, jnp.arange(group) ^ (lax.axis_index("ctx") % group), axis=0)
    return jnp.moveaxis(by_place, 0, 2).reshape(size, blocks * group * width)


def per_device(projected, short_filter, residues, rates, skip_gain, out_weight):
    count = lax.axis_size("ctx")
    halves = lax.axis_size("tp")
    here = lax.axis_index("ctx")
    rows, _, chans = projected.shape

    streams = jnp.transpose(projected, (1, 0, 2))
    rates_t = rates.T
    coef_t = (residues * jnp.sqrt(-jnp.expm1(-2.0 * rates))).T

    share = min(split_of(count), chans // LANES, 4)
    lines = count // share
    plane = here // share
    keeps = lax.axis_index("tp") == plane // 2
    place = jnp.stack([here % share, (plane == 1) | (plane == 2), keeps, plane % 2]).astype(jnp.int32)
    *ends, gated, prefix = local_scan(place, streams, short_filter, rates_t, share)
    ends = [ends[0]] + [send_xor(ends[j], count, share, j) for j in range(1, share)]
    whole, befores = plane_scan(place, rates_t, short_filter, ends, rows)
    arrived = [send_along(whole, count, share, k) for k in range(1, lines)]
    starts = line_scan(place, rates_t, short_filter, whole, befores, arrived, rows)
    states = starts[0]
    starts = [starts[0]] + [send_xor(starts[j], count, share, j) for j in range(1, share)]
    hidden = [
        hidden_rows(
            place, streams, short_filter, rates_t, coef_t, skip_gain[None], gated, prefix, starts, part
        )
        for part in range(2)
    ]
    if count == 16 and halves == 2 and out_weight.shape[1] % LANES == 0:
        return project_4x4(place, out_weight, states, hidden, count)
    return project_any(out_weight, states, hidden, count)


def solution(mesh):
    return jax.shard_map(
        per_device,
        mesh=mesh,
        in_specs=(
            P("ctx", None, "tp"),
            P(None, None, "tp"),
            P("tp", None),
            P("tp", None),
            P("tp"),
            P("tp", "ctx"),
        ),
        out_specs=P("ctx", "tp"),
        check_vma=False,
    )
```
